32 devices in a mesh: face: 8 (over z, y), elem: 4 (over x, core).
Axes of the slice: x: 2, y: 2, z: 4, core: 2. Of those that a mesh axis runs over, the one named last changes fastest.
Arguments:
- trace_old: bfloat16 [2048, 128], P(('face', 'elem')), may hold values from -1.5 to 1.5
- new_owner: int32 [2048, 1], P(('face', 'elem')), may hold values from 0 to 7; in each aligned block of 64 rows (0 to 63, 64 to 127, ...) at most 16 rows name the same one
- mortar_tiles: bfloat16 [3072, 6144], P(('face', 'elem')), may hold values from -0.625 to 0.625
- mortar_owner: int32 [3072, 1], P(('face', 'elem')), may hold values from 0 to 7; in each aligned block of 96 rows (0 to 95, 96 to 191, ...) at most 24 rows name the same one
- mortar_coarse: int32 [3072], P(('face', 'elem')), may hold values from 0 to 15
- interior_rhs: bfloat16 [288, 512], P(('face', 'elem')), may hold values from -1.5 to 1.5
- local_inverse: bfloat16 [288, 512, 512], P(('face', 'elem')), may hold values from -0.25 to 0.25
- coupling: bfloat16 [288, 512, 384], P(('face', 'elem')), may hold values from -1.1953125 to 1.1953125
- connectivity: int32 [288, 3], P(('face', 'elem')), may hold values from 0 to 511
Outputs:
- schur_blocks: bfloat16 [288, 384, 384], P(('face', 'elem'))
- slot_residual: float32 [4096, 128], P(('face', 'elem'))
- coarse_blocks: float32 [512, 4096], P(('face', 'elem'))
The draws below stay inside these ranges and needn't reach their ends.
Inputs may be any that keep to these rules, and one draw needn't show every extreme that they name: `new_owner`: in each aligned block of 64 rows no owner is named by more than 16 rows, a bound that some block reaches. `mortar_owner`: in each aligned block of 96 rows no owner is named by more than 24 rows, a bound that some block reaches.
All inputs are finite; a program needn't handle non-finite values.
Results may differ from the reference program's by a relative error of at most 0.0075.
Values may be sent and summed in bfloat16 or wider, within the bound.
No kernel may reach another device: no remote copies, remote signals or barrier semaphores. Data moves between devices by JAX's collectives and lax.ppermute only.
A program may use at most 64 MiB of HBM per device.

```python
import math
import jax
import jax.numpy as jnp
import numpy as np
from jax import lax

FACE_COEFFS = 128
NI = 512
FACES_PER_ELEM = 3
MROW = 64
MCOL = 96
E_DEV = 9
ROWS_DEV = 64
M_DEV = 96
NC = 16
CAP = 16
MCAP = 24
PARTITION_SLOTS = 512
ROWS = 2048
TILES = 3072
ELEMENT_TOTAL = 288
N_FACE = 8
N_ELEM = 4


def plant(drawn, own_key, low, high):
    extent = drawn.shape
    place = [jax.random.randint(jax.random.fold_in(own_key, axis), (), 0, extent[axis]) for axis in range(len(extent))]
    drawn = drawn.at[tuple(place)].set(low)
    longest = extent.index(max(extent))
    place[longest] = (place[longest] + 1) % extent[longest]
    return drawn.at[tuple(place)].set(high)


def shard_levels(key, shape, cuts, low, high):
    def one(position, shards_of):
        heights = jax.random.uniform(jax.random.fold_in(jax.random.fold_in(key, 6), position), (shards_of,), jnp.float32, low / len(cuts), high / len(cuts))
        return jnp.repeat(jnp.exp(heights), shape[position] // shards_of).reshape((-1,) + (1,) * (len(shape) - position - 1))

    factor_of = one(*cuts[0])
    for cut in cuts[1:]:
        factor_of = factor_of * one(*cut)
    return factor_of


def deal_out(stream_key, own, number, rows, number_of, top, bound, slope):
    ranking = jax.random.permutation(stream_key, number_of)
    heavy_load, usual = load_shares(number_of, rows * top, bound, slope, True), load_shares(number_of, rows * top, bound, slope, False)
    places = jnp.arange(number_of)

    def named(lengths, offset_by):
        used = int((lengths > 0).sum())
        fixed = max(1, used // 4)
        moved = fixed + (places - fixed + offset_by * (used - fixed)) % max(1, number_of - fixed)
        return jnp.zeros((number_of,), jnp.int32).at[ranking[jnp.where(places < fixed, places, moved)]].set(jnp.asarray(lengths, jnp.int32))

    lengths = jnp.where(number % 4 == 0, named(heavy_load, number // 4), named(usual, number - number // 4 - 1))
    mixed = jax.random.permutation(jax.random.fold_in(own, 3), number_of)
    donor, receiver = mixed[0:number_of // 2 * 2:2], mixed[1:number_of // 2 * 2:2]
    margin = jnp.minimum(lengths[donor] - 1, bound - lengths[receiver]) // 2
    margin = jnp.where((donor == ranking[0]) | (receiver == ranking[0]) | (lengths[receiver] == 0), 0, jnp.maximum(margin, 0))
    moved = jax.random.randint(jax.random.fold_in(own, 4), (number_of // 2,), 0, 1 << 20) % (margin + 1)
    lengths = lengths.at[donor].add(-moved).at[receiver].add(moved)
    labels = jnp.searchsorted(jnp.cumsum(lengths), jnp.arange(rows * top), side="right").astype(jnp.int32)
    grid = labels.reshape(top, rows).T
    grid = grid[jax.random.permutation(jax.random.fold_in(own, 1), rows)]
    offset_by = jax.random.randint(jax.random.fold_in(own, 2), (rows, 1), 0, top)
    return jnp.take_along_axis(grid, (jnp.arange(top)[None, :] + offset_by) % top, axis=1)


def load_shares(number_of, total, bound, slope, full):
    portions = [(1 << 20) // math.isqrt(rank ** slope) + 1 for rank in range(1, number_of + 1)]
    largest = bound if full else min(bound, max(-(-total // number_of), total * portions[0] // sum(portions)))
    least = 1 if total - largest >= number_of - 1 else 0
    holding, rest = [largest] + [least] * (number_of - 1), total - largest - least * (number_of - 1)
    while rest > 0:
        free = [i for i in range(1, number_of) if holding[i] < largest] or [i for i in range(1, number_of) if holding[i] < bound]
        mass, remaining = sum([portions[i] for i in free]), rest
        for i in free:
            addition = min(bound - holding[i], max(1, remaining * portions[i] // mass), rest)
            holding[i] = holding[i] + addition
            rest = rest - addition
    return np.array(holding)


def gaussian(key, extent, deviation, reach, cuts=(), kind=jnp.bfloat16):
    entries = jax.random.normal(key, extent, jnp.float32) * deviation
    if len(cuts) > 0:
        entries = shard_levels(key, extent, cuts, -0.22, 0.18) * entries
    return jnp.clip(entries, min=-reach, max=reach).astype(kind)


def setup_inputs(seed: int = 0) -> dict:
    streams_of = jax.random.split(jax.random.key(seed), 10)
    trace_old = gaussian(streams_of[0], (ROWS, FACE_COEFFS), 0.25, 1.5, ((0, 32),))
    new_owner_keys = jax.random.split(jax.random.fold_in(streams_of[1], 1), ROWS // ROWS_DEV)
    new_owner_turns = jax.random.permutation(jax.random.fold_in(streams_of[1], 3), ROWS // ROWS_DEV)
    new_owner = jax.vmap(lambda own, number: deal_out(jax.random.fold_in(streams_of[1], 2), own, number, ROWS_DEV, N_FACE, 1, CAP, 2))(new_owner_keys, new_owner_turns).reshape((ROWS, 1))
    mortar_tiles = gaussian(streams_of[2], (TILES, MROW * MCOL), MCOL ** -0.5, 0.625, ((0, 32),))
    mortar_owner_keys = jax.random.split(jax.random.fold_in(streams_of[3], 1), TILES // M_DEV)
    mortar_owner_turns = jax.random.permutation(jax.random.fold_in(streams_of[3], 3), TILES // M_DEV)
    mortar_owner = jax.vmap(lambda own, number: deal_out(jax.random.fold_in(streams_of[3], 2), own, number, M_DEV, N_FACE, 1, MCAP, 2))(mortar_owner_keys, mortar_owner_turns).reshape((TILES, 1))
    mortar_coarse = plant(jax.random.randint(streams_of[4], (TILES,), 0, NC), jax.random.fold_in(streams_of[4], 1), 0, NC - 1).astype(jnp.int32)
    interior_rhs = gaussian(streams_of[5], (ELEMENT_TOTAL, NI), 0.25, 1.5, ((0, 32),))
    local_inverse = gaussian(streams_of[6], (ELEMENT_TOTAL, NI, NI), NI ** -0.5, 0.25, ((0, 32),))
    coupling = gaussian(streams_of[7], (ELEMENT_TOTAL, NI, FACES_PER_ELEM * FACE_COEFFS), 0.2, 1.1953125, ((0, 32),))
    connectivity = plant(jax.random.randint(streams_of[8], (ELEMENT_TOTAL, FACES_PER_ELEM), 0, PARTITION_SLOTS), jax.random.fold_in(streams_of[8], 1), 0, PARTITION_SLOTS - 1).astype(jnp.int32)
    return dict(trace_old=trace_old, new_owner=new_owner, mortar_tiles=mortar_tiles, mortar_owner=mortar_owner, mortar_coarse=mortar_coarse, interior_rhs=interior_rhs, local_inverse=local_inverse, coupling=coupling, connectivity=connectivity)


def place_rows(block_rows, block_owners, owner_count, capacity):
    slots_all = jnp.arange(owner_count, dtype=jnp.int32)
    onehot = (block_owners[:, None] == slots_all[None, :]).astype(jnp.int32)
    ranks = jnp.cumsum(onehot, axis=0) - onehot
    my_rank = jnp.sum(ranks * onehot, axis=1)
    target = block_owners * capacity + my_rank
    buffer_slots = jnp.arange(owner_count * capacity, dtype=jnp.int32)
    placing = (buffer_slots[:, None] == target[None, :]).astype(jnp.bfloat16)
    return jnp.dot(placing, block_rows, preferred_element_type=jnp.float32).astype(jnp.bfloat16)


def reference(trace_old, new_owner, mortar_tiles, mortar_owner, mortar_coarse, interior_rhs, local_inverse, coupling, connectivity):
    blocks = N_FACE * N_ELEM
    trace_blocks = trace_old.reshape(blocks, ROWS_DEV, FACE_COEFFS)
    owner_blocks = new_owner[:, 0].reshape(blocks, ROWS_DEV).astype(jnp.int32)
    slot_buffers = jax.vmap(lambda rows_in, owners_in: place_rows(rows_in, owners_in, N_FACE, CAP))(trace_blocks, owner_blocks)
    slot_buffers = slot_buffers.reshape(N_FACE, N_ELEM, N_FACE, CAP, FACE_COEFFS)
    lookup_table = jnp.transpose(slot_buffers, (2, 1, 0, 3, 4)).reshape(N_FACE, PARTITION_SLOTS, FACE_COEFFS)

    tile_blocks = mortar_tiles.reshape(blocks, M_DEV, MROW, MCOL)
    tile_owners = mortar_owner[:, 0].reshape(blocks, M_DEV).astype(jnp.int32)
    tile_coarse = mortar_coarse.reshape(blocks, M_DEV).astype(jnp.int32)
    block_elem = (jnp.arange(blocks, dtype=jnp.int32) % N_ELEM).astype(jnp.int32)

    def add_block(carried, inputs):
        tiles_in, owners_in, coarse_in, elem_in = inputs
        tiles_f = tiles_in.astype(jnp.float32)
        gram_blocks = jnp.einsum("tmn,tkn->tmk", tiles_f, tiles_f).reshape(M_DEV, MROW * MROW)
        segment = (owners_in * N_ELEM + elem_in) * NC + coarse_in
        summed = jax.ops.segment_sum(gram_blocks, segment, num_segments=N_FACE * N_ELEM * NC)
        return carried + summed, None

    start_blocks = jnp.zeros((N_FACE * N_ELEM * NC, MROW * MROW), jnp.float32)
    coarse_blocks, _ = lax.scan(add_block, start_blocks, (tile_blocks, tile_owners, tile_coarse, block_elem))

    per_part = N_ELEM * E_DEV

    def partition(inputs):
        rhs_in, inverse_in, coupling_in, connectivity_input, table_in = inputs
        inverse_f = inverse_in.astype(jnp.float32)
        coupling_f = coupling_in.astype(jnp.float32)
        weights = jnp.einsum("eik,ekt->eit", inverse_f, coupling_f).astype(jnp.bfloat16)
        weights_f = weights.astype(jnp.float32)
        schur = (-jnp.einsum("eit,eiu->etu", coupling_f, weights_f)).astype(jnp.bfloat16)
        lam_rows = jnp.take(table_in, connectivity_input.reshape(-1), axis=0).reshape(per_part, FACES_PER_ELEM * FACE_COEFFS)
        interior = jnp.einsum("eik,ek->ei", inverse_f, rhs_in.astype(jnp.float32))
        interior = interior - jnp.einsum("eit,et->ei", weights_f, lam_rows.astype(jnp.float32))
        interior = interior.astype(jnp.bfloat16)
        element_share = jnp.einsum("eit,ei->et", coupling_f, interior.astype(jnp.float32)).reshape(per_part * FACES_PER_ELEM, FACE_COEFFS)
        assembled_matrix = jax.ops.segment_sum(element_share, connectivity_input.reshape(-1), num_segments=PARTITION_SLOTS)
        return schur, table_in.astype(jnp.float32) - assembled_matrix

    schur_parts, residual_pieces = lax.map(partition, (
        interior_rhs.reshape(N_FACE, per_part, NI),
        local_inverse.reshape(N_FACE, per_part, NI, NI),
        coupling.reshape(N_FACE, per_part, NI, FACES_PER_ELEM * FACE_COEFFS),
        connectivity.reshape(N_FACE, per_part, FACES_PER_ELEM).astype(jnp.int32),
        lookup_table))
    schur_blocks = schur_parts.reshape(ELEMENT_TOTAL, FACES_PER_ELEM * FACE_COEFFS, FACES_PER_ELEM * FACE_COEFFS)
    slot_residual = residual_pieces.reshape(N_FACE * PARTITION_SLOTS, FACE_COEFFS)
    return schur_blocks, slot_residual, coarse_blocks
```

```python
import functools

import jax
import jax.numpy as jnp
from jax import lax
from jax.experimental import pallas as pl
from jax.experimental.pallas import tpu as pltpu
from jax.sharding import PartitionSpec as P

FACE_COEFFS = 128
FACES_PER_ELEM = 3
MROW = 64
MCOL = 96
NC = 16
HALF = MROW // 2
LANES = 128
DENSE = HALF * MROW // LANES
OWNER_ROWS = NC * (DENSE + 1)
SHARE_ROWS = 32
SLOT_BASE = 16

BF16 = jnp.bfloat16
F32 = jnp.float32
I32 = jnp.int32

NT = (((1,), (1,)), ((), ()))
TN = (((0,), (0,)), ((), ()))


def iota(shape, dim):
    return lax.broadcasted_iota(I32, shape, dim)


def dot(left, right, dims=(((1,), (0,)), ((), ()))):
    return lax.dot_general(left, right, dims, preferred_element_type=F32)


def place_kernel(elem_count, face_count, capacity, owner_ref, trace_ref, out_ref):
    owners = owner_ref[...]
    rows = owners.shape[1]
    hot = (iota((face_count, rows), 0) == owners).astype(F32)
    earlier = (iota((rows, rows), 0) < iota((rows, rows), 1)).astype(BF16)
    rank = jnp.sum(hot * dot(hot.astype(BF16), earlier), axis=0, keepdims=True).astype(I32)
    target = owners * capacity + rank
    slots = out_ref.shape[0]
    block = iota((slots, rows), 0)
    owner_of = block // (elem_count * capacity)
    wanted = owner_of * capacity + lax.rem(block, capacity)
    place = (wanted == target).astype(BF16)
    out_ref[...] = dot(place, trace_ref[...]).astype(BF16)


def gram_kernel(pairs_at_once, owner_ref, coarse_ref, tiles_ref, out_ref, rows_ref, acc_ref):
    tiles = tiles_ref.shape[0]
    acc_ref[...] = jnp.zeros_like(acc_ref)
    lane = iota((tiles, LANES), 1)
    inside = lane < MCOL
    for group in range(MROW // 4):
        base = group * 3 * LANES
        one, two, three = (
            tiles_ref[:, base + k * LANES : base + (k + 1) * LANES].astype(F32) for k in range(3)
        )
        rolled = (
            one,
            pltpu.roll(jnp.where(lane < 64, two, one), 32, 1),
            pltpu.roll(jnp.where(lane < 32, three, two), 64, 1),
            pltpu.roll(three, 96, 1),
        )
        for k in range(4):
            rows_ref[pl.ds(4 * group + k, tiles, stride=MROW), :] = jnp.where(
                inside, rolled[k], 0.0
            )

    row = iota((HALF, LANES), 0)
    column = lax.rem(iota((HALF, LANES), 1), MROW)
    swapped = (column > row) & (column < HALF)
    diagonal = column == row
    low = iota((DENSE, LANES), 1) < MROW
    low_wide = iota((MROW, LANES), 1) < MROW
    low_row = iota((1, LANES), 1) < MROW

    def step(index, carry):
        for k in range(pairs_at_once):
            pair = index * pairs_at_once + k
            start = pl.multiple_of(pair * LANES, LANES)
            both = rows_ref[pl.ds(start, LANES), :].astype(BF16)
            gram = dot(both, both, NT)
            side = jnp.where(low_wide, gram[:MROW], gram[MROW:])
            lower = pltpu.roll(side[HALF:], LANES - HALF, 1)
            packed = jnp.where(swapped, lower, side[:HALF])
            diag = jnp.sum(jnp.where(diagonal, lower, 0.0), axis=0, keepdims=True)
            turned = pltpu.roll(packed, MROW, 1)
            first = jnp.where(low, packed[:DENSE], turned[DENSE:])
            second = jnp.where(low, turned[:DENSE], packed[DENSE:])
            for tile, dense, own in ((0, first, low_row), (1, second, ~low_row)):
                owner = owner_ref[2 * pair + tile]
                coarse = coarse_ref[2 * pair + tile]
                here = pl.multiple_of(owner * OWNER_ROWS + coarse * DENSE, DENSE)
                acc_ref[pl.ds(here, DENSE), :] += dense
                there = owner * OWNER_ROWS + NC * DENSE + coarse
                acc_ref[pl.ds(there, 1), :] += jnp.where(own, diag, 0.0)
        return carry

    lax.fori_loop(0, tiles // 2 // pairs_at_once, step, 0)
    out_ref[...] = acc_ref[...].astype(BF16)


def table_position(slot, elem_count, face_count, capacity):
    part = face_count * capacity
    inner = lax.rem(slot, part)
    block = lax.div(inner, capacity) * elem_count + lax.div(slot, part)
    return block * capacity + lax.rem(inner, capacity)


def main_kernel(
    position_of,
    conn_ref,
    table_ref,
    rhs_ref,
    inverse_ref,
    coupling_ref,
    schur_ref,
    share_ref,
    rhs_wide_ref,
    rhs_turned_ref,
    lam_ref,
    columns_ref,
):
    element = pl.program_id(0)
    elements = rhs_ref.shape[0]
    faces = elements * FACES_PER_ELEM
    trace = FACES_PER_ELEM * FACE_COEFFS

    @pl.when(element == 0)
    def _():
        rhs_wide_ref[...] = jnp.zeros_like(rhs_wide_ref)
        rhs_wide_ref[0:elements, :] = rhs_ref[...].astype(F32)
        rhs_turned_ref[...] = rhs_wide_ref[...].T.astype(BF16)
        row = iota((SHARE_ROWS, LANES), 0)
        positions = jnp.full((SHARE_ROWS, LANES), -1, I32)
        for k in range(faces):
            positions = jnp.where(row == k, position_of(conn_ref[k]), positions)
        slots = table_ref.shape[0]
        lane = iota((SHARE_ROWS, LANES), 1)
        hot = jnp.concatenate(
            [positions == lane + base for base in range(0, slots, LANES)], axis=1
        )
        lam_ref[...] = dot(hot.astype(BF16), table_ref[...])
        columns_ref[...] = jnp.zeros_like(columns_ref)

    coupling = coupling_ref[0]
    wide = jnp.concatenate([coupling, rhs_turned_ref[...]], axis=1)
    weights = dot(inverse_ref[0], wide).astype(BF16)
    condensed = dot(coupling, weights, TN)
    schur_ref[0] = (-condensed[:, :trace]).astype(BF16)

    total = jnp.where(iota((trace, LANES), 1) == element, condensed[:, trace:], 0.0)
    for face in range(FACES_PER_ELEM):
        lam = lam_ref[pl.ds(element * FACES_PER_ELEM + face, 1), :]
        total = total - condensed[:, face * LANES : (face + 1) * LANES] * lam
    sums = jnp.sum(total, axis=1, keepdims=True)
    lane = iota((LANES, LANES), 1)
    columns = columns_ref[...]
    for face in range(FACES_PER_ELEM):
        columns = jnp.where(
            lane == element * FACES_PER_ELEM + face,
            sums[face * FACE_COEFFS : (face + 1) * FACE_COEFFS],
            columns,
        )
    columns_ref[...] = columns

    @pl.when(element == elements - 1)
    def _():
        shares = columns_ref[...].T[:SHARE_ROWS]
        row = iota((SHARE_ROWS, LANES), 0)
        lane = iota((1, LANES), 1)
        high = jnp.full((1, LANES), -1, I32)
        rest = jnp.zeros((1, LANES), I32)
        for k in range(faces):
            high = jnp.where(lane == k, lax.div(conn_ref[k], SLOT_BASE), high)
            rest = jnp.where(lane == k, lax.rem(conn_ref[k], SLOT_BASE), rest)
        shares = jnp.where(row == faces, high.astype(F32), shares)
        shares = jnp.where(row == faces + 1, rest.astype(F32), shares)
        share_ref[...] = shares.astype(BF16)


def residual_kernel(elem_count, capacity, faces, table_ref, *refs):
    share_refs, out_ref = refs[:-1], refs[-1]
    mine = lax.axis_index("elem")
    own = out_ref.shape[0]
    slots = table_ref.shape[0]
    place = iota((own, slots), 0)
    position = (lax.div(place, capacity) * elem_count + mine) * capacity + lax.rem(place, capacity)
    pick = (iota((own, slots), 1) == position).astype(BF16)
    total = dot(pick, table_ref[...])
    slot = (iota((own, SHARE_ROWS), 0) + mine * own).astype(F32)
    for share_ref in share_refs:
        shares = share_ref[...]
        names = shares.astype(F32)
        named = names[faces : faces + 1, :SHARE_ROWS] * SLOT_BASE
        named = named + names[faces + 1 : faces + 2, :SHARE_ROWS]
        total = total - dot((slot == named).astype(BF16), shares)
    out_ref[...] = total


def coarse_kernel(got_ref, out_ref, sum_ref, full_ref):
    total = got_ref[0].astype(F32)
    for k in range(1, got_ref.shape[0]):
        total = total + got_ref[k].astype(F32)
    sum_ref[...] = total

    lane = iota((HALF, LANES), 1)
    row = iota((HALF, LANES), 0)
    wide_row = iota((MROW, LANES), 0)
    wide_lane = iota((MROW, LANES), 1)
    top = wide_row < HALF
    held = (top & ((wide_lane <= wide_row) | (wide_lane >= HALF))) | (
        (~top) & (wide_lane >= wide_row)
    )
    for block in range(NC):
        dense = sum_ref[block * DENSE : (block + 1) * DENSE, :]
        upper = jnp.concatenate([dense, pltpu.roll(dense, MROW, 1)], axis=0)
        diag = sum_ref[NC * DENSE + block : NC * DENSE + block + 1, :]
        diag = pltpu.roll(diag + pltpu.roll(diag, MROW, 1), HALF, 1)
        lower = jnp.where(lane == row + HALF, diag, pltpu.roll(upper, HALF, 1))
        given = jnp.concatenate([upper, lower], axis=0)
        turned = jnp.concatenate([given, given], axis=0).T[:MROW]
        full_ref[block * MROW : (block + 1) * MROW, :] = jnp.where(held, given, turned)
    low = iota((NC, LANES), 1) < MROW
    for chunk in range(HALF):
        left = full_ref[pl.ds(2 * chunk, NC, stride=MROW), :]
        right = full_ref[pl.ds(2 * chunk + 1, NC, stride=MROW), :]
        out_ref[:, chunk * LANES : (chunk + 1) * LANES] = jnp.where(
            low, left, pltpu.roll(right, MROW, 1)
        )


def vmem(count):
    return [pl.BlockSpec(memory_space=pltpu.VMEM)] * count


def params(mib):
    return pltpu.CompilerParams(vmem_limit_bytes=mib << 20)


def shards(
    trace_old,
    new_owner,
    mortar_tiles,
    mortar_owner,
    mortar_coarse,
    interior_rhs,
    local_inverse,
    coupling,
    connectivity,
):
    face_count = lax.axis_size("face")
    elem_count = lax.axis_size("elem")
    row_count = trace_old.shape[0]
    tile_count = mortar_tiles.shape[0]
    elements, modes = interior_rhs.shape
    faces = elements * FACES_PER_ELEM
    trace = FACES_PER_ELEM * FACE_COEFFS
    capacity = max(2, 2 * row_count // face_count)
    devices = face_count * elem_count
    slots = devices * capacity
    own = slots // elem_count

    placed = pl.pallas_call(
        functools.partial(place_kernel, elem_count, face_count, capacity),
        out_shape=jax.ShapeDtypeStruct((slots, FACE_COEFFS), BF16),
        in_specs=vmem(2),
        out_specs=pl.BlockSpec(memory_space=pltpu.VMEM),
        name="place",
    )(new_owner.reshape(1, row_count), trace_old)
    table = lax.all_to_all(
        placed.reshape(devices, capacity, FACE_COEFFS), ("face", "elem"), 0, 0, tiled=True
    ).reshape(slots, FACE_COEFFS)

    half_grams = pl.pallas_call(
        functools.partial(gram_kernel, 6),
        out_shape=jax.ShapeDtypeStruct((face_count * OWNER_ROWS, LANES), BF16),
        in_specs=[pl.BlockSpec(memory_space=pltpu.SMEM)] * 2 + vmem(1),
        out_specs=pl.BlockSpec(memory_space=pltpu.VMEM),
        scratch_shapes=[
            pltpu.VMEM((tile_count * MROW, LANES), F32),
            pltpu.VMEM((face_count * OWNER_ROWS, LANES), F32),
        ],
        compiler_params=params(40),
        name="gram",
    )(mortar_owner.reshape(tile_count), mortar_coarse, mortar_tiles)
    got = lax.all_to_all(
        half_grams.reshape(face_count, OWNER_ROWS, LANES), "face", 0, 0, tiled=True
    )

    slots_named, _ = lax.optimization_barrier((connectivity.reshape(faces), half_grams))
    position_of = functools.partial(
        table_position, elem_count=elem_count, face_count=face_count, capacity=capacity
    )
    schur_blocks, shares = pl.pallas_call(
        functools.partial(main_kernel, position_of),
        out_shape=(
            jax.ShapeDtypeStruct((elements, trace, trace), BF16),
            jax.ShapeDtypeStruct((SHARE_ROWS, LANES), BF16),
        ),
        grid=(elements,),
        in_specs=[
            pl.BlockSpec(memory_space=pltpu.SMEM),
            pl.BlockSpec((slots, FACE_COEFFS), lambda e: (0, 0)),
            pl.BlockSpec((elements, modes), lambda e: (0, 0)),
            pl.BlockSpec((1, modes, modes), lambda e: (e, 0, 0)),
            pl.BlockSpec((1, modes, trace), lambda e: (e, 0, 0)),
        ],
        out_specs=(
            pl.BlockSpec((1, trace, trace), lambda e: (e, 0, 0)),
            pl.BlockSpec((SHARE_ROWS, LANES), lambda e: (0, 0)),
        ),
        scratch_shapes=[
            pltpu.VMEM((LANES, modes), F32),
            pltpu.VMEM((modes, LANES), BF16),
            pltpu.VMEM((SHARE_ROWS, LANES), F32),
            pltpu.VMEM((LANES, LANES), F32),
        ],
        compiler_params=params(32),
        cost_estimate=pl.CostEstimate(
            flops=2 * elements * modes * trace * (modes + trace),
            bytes_accessed=2 * elements * (modes * (modes + trace) + trace * trace),
            transcendentals=0,
        ),
        name="condense",
    )(slots_named, table, interior_rhs, local_inverse, coupling)

    all_shares = [shares]
    for shift in range(1, elem_count):
        pairs = [(k, (k + shift) % elem_count) for k in range(elem_count)]
        all_shares.append(lax.ppermute(shares, "elem", pairs))

    coarse_blocks = pl.pallas_call(
        coarse_kernel,
        out_shape=jax.ShapeDtypeStruct((NC, MROW * MROW), F32),
        in_specs=vmem(1),
        out_specs=pl.BlockSpec(memory_space=pltpu.VMEM),
        scratch_shapes=[
            pltpu.VMEM((OWNER_ROWS, LANES), F32),
            pltpu.VMEM((NC * MROW, LANES), F32),
        ],
        compiler_params=params(32),
        name="coarse",
    )(got)

    slot_residual = pl.pallas_call(
        functools.partial(residual_kernel, elem_count, capacity, faces),
        out_shape=jax.ShapeDtypeStruct((own, FACE_COEFFS), F32),
        in_specs=vmem(1 + elem_count),
        out_specs=pl.BlockSpec(memory_space=pltpu.VMEM),
        name="residual",
    )(table, *all_shares)
    return schur_blocks, slot_residual, coarse_blocks


def solution(mesh):
    return jax.shard_map(
        shards,
        mesh=mesh,
        in_specs=(
            P(("face", "elem"), None),
            P(("face", "elem"), None),
            P(("face", "elem"), None),
            P(("face", "elem"), None),
            P(("face", "elem")),
            P(("face", "elem"), None),
            P(("face", "elem"), None, None),
            P(("face", "elem"), None, None),
            P(("face", "elem"), None),
        ),
        out_specs=(
            P(("face", "elem"), None, None),
            P(("face", "elem"), None),
            P(("face", "elem"), None),
        ),
        check_vma=False,
    )
```

```python
import functools

import jax
import jax.numpy as jnp
from jax import lax
from jax.experimental import pallas as pl
from jax.experimental.pallas import tpu as pltpu
from jax.sharding import PartitionSpec as P

FACE_COEFFS = 128
FACES_PER_ELEM = 3
MROW = 64
MCOL = 96
NC = 16
HALF = MROW // 2
LANES = 128
DENSE = HALF * MROW // LANES
OWNER_ROWS = NC * (DENSE + 1)
SHARE_ROWS = 32
SLOT_BASE = 16
CHUNK = 16
PITCH = MROW + 8
BIG = 63
SMALL = 16

BF16 = jnp.bfloat16
F32 = jnp.float32
I32 = jnp.int32

NT = (((1,), (1,)), ((), ()))
TN = (((0,), (0,)), ((), ()))


def iota(shape, dim):
    return lax.broadcasted_iota(I32, shape, dim)


def dot(left, right, dims=(((1,), (0,)), ((), ()))):
    return lax.dot_general(left, right, dims, preferred_element_type=F32)


def place_rows(elem_count, face_count, capacity, owners, rows_in, slots):
    rows = owners.shape[1]
    hot = (iota((face_count, rows), 0) == owners).astype(F32)
    earlier = (iota((rows, rows), 0) < iota((rows, rows), 1)).astype(BF16)
    rank = jnp.sum(hot * dot(hot.astype(BF16), earlier), axis=0, keepdims=True).astype(I32)
    target = owners * capacity + rank
    block = iota((slots, rows), 0)
    wanted = lax.div(block, elem_count * capacity) * capacity + lax.rem(block, capacity)
    return dot((wanted == target).astype(BF16), rows_in).astype(BF16)


def send_kernel(
    elem_count,
    face_count,
    capacity,
    new_owner_ref,
    trace_ref,
    owner_hbm,
    coarse_hbm,
    tiles_hbm,
    placed_ref,
    out_ref,
    owner_ref,
    coarse_ref,
    tiles_ref,
    rows_ref,
    *more,
):
    accs, diags, sems = more[:2], more[2:4], more[4]
    tiles = tiles_ref.shape[0]
    copies = [
        pltpu.make_async_copy(owner_hbm, owner_ref, sems.at[0]),
        pltpu.make_async_copy(coarse_hbm, coarse_ref, sems.at[1]),
        pltpu.make_async_copy(tiles_hbm, tiles_ref, sems.at[2]),
    ]
    for copy in copies:
        copy.start()
    for ref in (*accs, *diags):
        ref[...] = jnp.zeros_like(ref)
    placed_ref[...] = place_rows(
        elem_count,
        face_count,
        capacity,
        new_owner_ref[...],
        trace_ref[...],
        placed_ref.shape[0],
    )
    for copy in copies:
        copy.wait()

    lane = iota((CHUNK, LANES), 1)
    inside = lane < MCOL
    row = iota((HALF, LANES), 0)
    column = lax.rem(iota((HALF, LANES), 1), MROW)
    swapped = (column > row) & (column < HALF)
    diagonal = column == row
    low = iota((DENSE, LANES), 1) < MROW
    low_wide = iota((MROW, LANES), 1) < MROW
    low_row = iota((1, LANES), 1) < MROW

    for chunk in range(tiles // CHUNK):
        first_tile = chunk * CHUNK
        for group in range(MROW // 4):
            base = group * 3 * LANES
            one, two, three = (
                tiles_ref[
                    first_tile : first_tile + CHUNK, base + k * LANES : base + (k + 1) * LANES
                ].astype(F32)
                for k in range(3)
            )
            rolled = (
                one,
                pltpu.roll(jnp.where(lane < 64, two, one), 32, 1),
                pltpu.roll(jnp.where(lane < 32, three, two), 64, 1),
                pltpu.roll(three, 96, 1),
            )
            for k in range(4):
                rows_ref[pl.ds(first_tile * PITCH + 4 * group + k, CHUNK, stride=PITCH), :] = (
                    jnp.where(inside, rolled[k], 0.0)
                )
        for tile in range(first_tile, first_tile + CHUNK, 2):
            both = jnp.concatenate(
                [
                    rows_ref[t * PITCH : t * PITCH + MROW, :].astype(BF16)
                    for t in (tile, tile + 1)
                ],
                axis=0,
            )
            gram = dot(both, both, NT)
            side = jnp.where(low_wide, gram[:MROW], gram[MROW:])
            lower = pltpu.roll(side[HALF:], LANES - HALF, 1)
            packed = jnp.where(swapped, lower, side[:HALF])
            diag = jnp.sum(jnp.where(diagonal, lower, 0.0), axis=0, keepdims=True)
            turned = pltpu.roll(packed, MROW, 1)
            dense = (
                jnp.where(low, packed[:DENSE], turned[DENSE:]),
                jnp.where(low, turned[:DENSE], packed[DENSE:]),
            )
            own = (jnp.where(low_row, diag, 0.0), jnp.where(low_row, 0.0, diag))
            for k in range(2):
                block = owner_ref[tile + k] * NC + coarse_ref[tile + k]
                here = pl.ds(pl.multiple_of(block * DENSE, DENSE), DENSE)
                accs[k][here, :] += dense[k]
                diags[k][pl.ds(block, 1), :] += own[k]
    for owner in range(face_count):
        start, size = owner * OWNER_ROWS, NC * DENSE
        here = slice(owner * size, (owner + 1) * size)
        out_ref[start : start + size, :] = (accs[0][here, :] + accs[1][here, :]).astype(BF16)
        here = slice(owner * NC, (owner + 1) * NC)
        out_ref[start + size : start + size + NC, :] = (
            diags[0][here, :] + diags[1][here, :]
        ).astype(BF16)


def table_position(slot, elem_count, face_count, capacity):
    part = face_count * capacity
    inner = lax.rem(slot, part)
    block = lax.div(inner, capacity) * elem_count + lax.div(slot, part)
    return block * capacity + lax.rem(inner, capacity)


def main_kernel(
    position_of,
    table_ref,
    conn_hbm,
    rhs_hbm,
    inverse_hbm,
    coupling_hbm,
    schur_hbm,
    share_ref,
    conn_ref,
    rhs_ref,
    inverse_ref,
    coupling_ref,
    schur_ref,
    rhs_wide_ref,
    rhs_turned_ref,
    lam_ref,
    sum_ref,
    weight_a_ref,
    weight_b_ref,
    turned_a_ref,
    turned_b_ref,
    small_sems,
    inverse_sems,
    coupling_sems,
    schur_sems,
):
    elements = rhs_ref.shape[0]
    faces = elements * FACES_PER_ELEM
    trace = FACES_PER_ELEM * FACE_COEFFS
    small = [
        pltpu.make_async_copy(conn_hbm, conn_ref, small_sems.at[0]),
        pltpu.make_async_copy(rhs_hbm, rhs_ref, small_sems.at[1]),
    ]
    for copy in small:
        copy.start()

    def bring(e):
        return (
            pltpu.make_async_copy(inverse_hbm.at[e], inverse_ref.at[e], inverse_sems.at[e]),
            pltpu.make_async_copy(coupling_hbm.at[e], coupling_ref.at[e], coupling_sems.at[e]),
        )

    def leave(e):
        return pltpu.make_async_copy(schur_ref.at[e], schur_hbm.at[e], schur_sems.at[e])

    for e in range(elements):
        for copy in bring(e):
            copy.start()
    for copy in small:
        copy.wait()

    rhs_wide_ref[...] = jnp.zeros_like(rhs_wide_ref)
    rhs_wide_ref[0:elements, :] = rhs_ref[...].astype(F32)
    rhs_turned_ref[...] = rhs_wide_ref[...].T.astype(BF16)
    row = iota((SHARE_ROWS, LANES), 0)
    lane = iota((SHARE_ROWS, LANES), 1)
    positions = jnp.full((SHARE_ROWS, LANES), -1, I32)
    for k in range(faces):
        slot = conn_ref[k % FACES_PER_ELEM, k // FACES_PER_ELEM]
        positions = jnp.where(row == k, position_of(slot), positions)
    slots = table_ref.shape[0]
    hot = jnp.concatenate([positions == lane + base for base in range(0, slots, LANES)], axis=1)
    lam_ref[...] = dot(hot.astype(BF16), table_ref[...])

    def solve(e, weight_ref, turned_ref):
        coupling = coupling_ref[e]
        wide = jnp.concatenate([coupling, rhs_turned_ref[...]], axis=1)
        weight_ref[...] = dot(inverse_ref[e], wide).astype(BF16)
        turned_ref[...] = coupling.T

    def condense(e, weight_ref, turned_ref):
        condensed = dot(turned_ref[...], weight_ref[...])
        schur = (-condensed[:, :trace]).astype(BF16)
        schur_ref[e] = schur
        lam = [lam_ref[pl.ds(e * FACES_PER_ELEM + a, 1), :] for a in range(FACES_PER_ELEM)]
        own = (iota((1, LANES), 1) == e).astype(F32)
        vector = jnp.broadcast_to(jnp.concatenate([*lam, own], axis=1), (16, trace + LANES))
        matrix = jnp.concatenate([schur, condensed[:, trace:].astype(BF16)], axis=1)
        share = dot(vector.astype(BF16), matrix, NT)
        for a in range(FACES_PER_ELEM):
            sum_ref[pl.ds(e * FACES_PER_ELEM + a, 1), :] = share[
                0:1, a * FACE_COEFFS : (a + 1) * FACE_COEFFS
            ]

    even = (weight_a_ref, turned_a_ref)
    odd = (weight_b_ref, turned_b_ref)

    def advance(e, there, here):
        for copy in bring(e):
            copy.wait()
        solve(e, *there)
        condense(e - 1, *here)
        leave(e - 1).start()

    for copy in bring(0):
        copy.wait()
    solve(0, *even)

    def two(index, carry):
        advance(2 * index + 1, odd, even)
        advance(2 * index + 2, even, odd)
        return carry

    lax.fori_loop(0, (elements - 1) // 2, two, 0)
    if elements % 2 == 0:
        advance(elements - 1, odd, even)
    condense(elements - 1, *(odd if elements % 2 == 0 else even))
    leave(elements - 1).start()

    lane = iota((1, LANES), 1)
    high = jnp.full((1, LANES), -1, I32)
    rest = jnp.zeros((1, LANES), I32)
    for k in range(faces):
        slot = conn_ref[k % FACES_PER_ELEM, k // FACES_PER_ELEM]
        high = jnp.where(lane == k, lax.div(slot, SLOT_BASE), high)
        rest = jnp.where(lane == k, lax.rem(slot, SLOT_BASE), rest)
    shares = jnp.where(row < faces, sum_ref[...], 0.0)
    shares = jnp.where(row == faces, high.astype(F32), shares)
    shares = jnp.where(row == faces + 1, rest.astype(F32), shares)
    share_ref[...] = shares.astype(BF16)
    for e in range(elements):
        leave(e).wait()


def residual(elem_count, capacity, faces, own, table_ref, share_refs):
    mine = lax.axis_index("elem")
    slots = table_ref.shape[0]
    place = iota((own, slots), 0)
    position = (lax.div(place, capacity) * elem_count + mine) * capacity + lax.rem(place, capacity)
    pick = (iota((own, slots), 1) == position).astype(BF16)
    total = dot(pick, table_ref[...])
    slot = (iota((own, SHARE_ROWS), 0) + mine * own).astype(F32)
    for share_ref in share_refs:
        shares = share_ref[...]
        names = shares.astype(F32)
        named = names[faces : faces + 1, :SHARE_ROWS] * SLOT_BASE
        named = named + names[faces + 1 : faces + 2, :SHARE_ROWS]
        total = total - dot((slot == named).astype(BF16), shares)
    return total


def finish_kernel(elem_count, capacity, faces, got_ref, table_ref, *refs):
    share_refs = refs[:elem_count]
    residual_ref, out_ref, sum_ref, full_ref = refs[elem_count:]
    residual_ref[...] = residual(
        elem_count, capacity, faces, residual_ref.shape[0], table_ref, share_refs
    )
    total = got_ref[0].astype(F32)
    for k in range(1, got_ref.shape[0]):
        total = total + got_ref[k].astype(F32)
    sum_ref[...] = total

    lane = iota((HALF, LANES), 1)
    row = iota((HALF, LANES), 0)
    wide_row = iota((MROW, LANES), 0)
    wide_lane = iota((MROW, LANES), 1)
    top = wide_row < HALF
    held = (top & ((wide_lane <= wide_row) | (wide_lane >= HALF))) | (
        (~top) & (wide_lane >= wide_row)
    )
    for block in range(NC):
        dense = sum_ref[block * DENSE : (block + 1) * DENSE, :]
        upper = jnp.concatenate([dense, pltpu.roll(dense, MROW, 1)], axis=0)
        diag = sum_ref[NC * DENSE + block : NC * DENSE + block + 1, :]
        diag = pltpu.roll(diag + pltpu.roll(diag, MROW, 1), HALF, 1)
        lower = jnp.where(lane == row + HALF, diag, pltpu.roll(upper, HALF, 1))
        given = jnp.concatenate([upper, lower], axis=0)
        turned = jnp.concatenate([given, given], axis=0).T[:MROW]
        full_ref[block * MROW : (block + 1) * MROW, :] = jnp.where(held, given, turned)
    low = iota((NC, LANES), 1) < MROW
    for chunk in range(HALF):
        left = full_ref[pl.ds(2 * chunk, NC, stride=MROW), :]
        right = full_ref[pl.ds(2 * chunk + 1, NC, stride=MROW), :]
        out_ref[:, chunk * LANES : (chunk + 1) * LANES] = jnp.where(
            low, left, pltpu.roll(right, MROW, 1)
        )


ANY = pl.BlockSpec(memory_space=pl.ANY)
VMEM = pl.BlockSpec(memory_space=pltpu.VMEM)


def params(mib):
    return pltpu.CompilerParams(vmem_limit_bytes=mib << 20)


def shards(
    trace_old,
    new_owner,
    mortar_tiles,
    mortar_owner,
    mortar_coarse,
    interior_rhs,
    local_inverse,
    coupling,
    connectivity,
):
    face_count = lax.axis_size("face")
    elem_count = lax.axis_size("elem")
    row_count = trace_old.shape[0]
    tile_count = mortar_tiles.shape[0]
    elements, modes = interior_rhs.shape
    faces = elements * FACES_PER_ELEM
    trace = FACES_PER_ELEM * FACE_COEFFS
    capacity = max(2, 2 * row_count // face_count)
    devices = face_count * elem_count
    slots = devices * capacity
    own = slots // elem_count

    placed, half_grams = pl.pallas_call(
        functools.partial(send_kernel, elem_count, face_count, capacity),
        out_shape=(
            jax.ShapeDtypeStruct((slots, FACE_COEFFS), BF16),
            jax.ShapeDtypeStruct((face_count * OWNER_ROWS, LANES), BF16),
        ),
        in_specs=[VMEM, VMEM, ANY, ANY, ANY],
        out_specs=(VMEM, VMEM),
        scratch_shapes=[
            pltpu.SMEM((tile_count,), I32),
            pltpu.SMEM((tile_count,), I32),
            pltpu.VMEM(mortar_tiles.shape, BF16),
            pltpu.VMEM((tile_count * PITCH, LANES), F32),
            pltpu.VMEM((face_count * NC * DENSE, LANES), F32),
            pltpu.VMEM((face_count * NC * DENSE, LANES), F32),
            pltpu.VMEM((face_count * NC, LANES), F32),
            pltpu.VMEM((face_count * NC, LANES), F32),
            pltpu.SemaphoreType.DMA((3,)),
        ],
        compiler_params=params(BIG),
        name="send",
    )(
        new_owner.reshape(1, row_count),
        trace_old,
        mortar_owner.reshape(tile_count),
        mortar_coarse,
        mortar_tiles,
    )
    table = lax.all_to_all(
        placed.reshape(devices, capacity, FACE_COEFFS), ("face", "elem"), 0, 0, tiled=True
    ).reshape(slots, FACE_COEFFS)
    got = lax.all_to_all(
        half_grams.reshape(face_count, OWNER_ROWS, LANES), "face", 0, 0, tiled=True
    )

    position_of = functools.partial(
        table_position, elem_count=elem_count, face_count=face_count, capacity=capacity
    )
    schur_blocks, shares = pl.pallas_call(
        functools.partial(main_kernel, position_of),
        out_shape=(
            jax.ShapeDtypeStruct((elements, trace, trace), BF16),
            jax.ShapeDtypeStruct((SHARE_ROWS, LANES), BF16),
        ),
        in_specs=[VMEM, ANY, ANY, ANY, ANY],
        out_specs=(ANY, VMEM),
        scratch_shapes=[
            pltpu.SMEM((FACES_PER_ELEM, elements), I32),
            pltpu.VMEM((elements, modes), BF16),
            pltpu.VMEM((elements, modes, modes), BF16),
            pltpu.VMEM((elements, modes, trace), BF16),
            pltpu.VMEM((elements, trace, trace), BF16),
            pltpu.VMEM((LANES, modes), F32),
            pltpu.VMEM((modes, LANES), BF16),
            pltpu.VMEM((SHARE_ROWS, LANES), F32),
            pltpu.VMEM((SHARE_ROWS, LANES), F32),
            pltpu.VMEM((modes, trace + LANES), BF16),
            pltpu.VMEM((modes, trace + LANES), BF16),
            pltpu.VMEM((trace, modes), BF16),
            pltpu.VMEM((trace, modes), BF16),
            pltpu.SemaphoreType.DMA((2,)),
            pltpu.SemaphoreType.DMA((elements,)),
            pltpu.SemaphoreType.DMA((elements,)),
            pltpu.SemaphoreType.DMA((elements,)),
        ],
        compiler_params=params(BIG),
        cost_estimate=pl.CostEstimate(
            flops=2 * elements * modes * trace * (modes + trace),
            bytes_accessed=2 * elements * (modes * (modes + trace) + trace * trace),
            transcendentals=0,
        ),
        name="condense",
    )(table, connectivity.T, interior_rhs, local_inverse, coupling)

    all_shares = [shares]
    for shift in range(1, elem_count):
        pairs = [(k, (k + shift) % elem_count) for k in range(elem_count)]
        all_shares.append(lax.ppermute(shares, "elem", pairs))

    slot_residual, coarse_blocks = pl.pallas_call(
        functools.partial(finish_kernel, elem_count, capacity, faces),
        out_shape=(
            jax.ShapeDtypeStruct((own, FACE_COEFFS), F32),
            jax.ShapeDtypeStruct((NC, MROW * MROW), F32),
        ),
        in_specs=[VMEM] * (2 + elem_count),
        out_specs=(VMEM, VMEM),
        scratch_shapes=[
            pltpu.VMEM((OWNER_ROWS, LANES), F32),
            pltpu.VMEM((NC * MROW, LANES), F32),
        ],
        compiler_params=params(SMALL),
        name="finish",
    )(got, table, *all_shares)
    return schur_blocks, slot_residual, coarse_blocks


def solution(mesh):
    return jax.shard_map(
        shards,
        mesh=mesh,
        in_specs=(
            P(("face", "elem"), None),
            P(("face", "elem"), None),
            P(("face", "elem"), None),
            P(("face", "elem"), None),
            P(("face", "elem")),
            P(("face", "elem"), None),
            P(("face", "elem"), None, None),
            P(("face", "elem"), None, None),
            P(("face", "elem"), None),
        ),
        out_specs=(
            P(("face", "elem"), None, None),
            P(("face", "elem"), None),
            P(("face", "elem"), None),
        ),
        check_vma=False,
    )
```

```python
import functools

import jax
import jax.numpy as jnp
from jax import lax
from jax.experimental import pallas as pl
from jax.experimental.pallas import tpu as pltpu
from jax.sharding import PartitionSpec as P

FACE_COEFFS = 128
FACES_PER_ELEM = 3
MROW = 64
MCOL = 96
NC = 16
HALF = MROW // 2
LANES = 128
DENSE = HALF * MROW // LANES
OWNER_ROWS = NC * (DENSE + 1)
SHARE_ROWS = 32
SLOT_BASE = 16
CHUNK = 16
AHEAD = 3
BIG = 62 << 20
PITCH = MROW + 8

BF16 = jnp.bfloat16
F32 = jnp.float32
I32 = jnp.int32

NT = (((1,), (1,)), ((), ()))
TN = (((0,), (0,)), ((), ()))


def iota(shape, dim):
    return lax.broadcasted_iota(I32, shape, dim)


def dot(left, right, dims=(((1,), (0,)), ((), ()))):
    return lax.dot_general(left, right, dims, preferred_element_type=F32)


def place_rows(elem_count, face_count, capacity, owners, rows_in, slots):
    rows = owners.shape[1]
    hot = (iota((face_count, rows), 0) == owners).astype(F32)
    earlier = (iota((rows, rows), 0) < iota((rows, rows), 1)).astype(BF16)
    rank = jnp.sum(hot * dot(hot.astype(BF16), earlier), axis=0, keepdims=True).astype(I32)
    target = owners * capacity + rank
    block = iota((slots, rows), 0)
    wanted = lax.div(block, elem_count * capacity) * capacity + lax.rem(block, capacity)
    return dot((wanted == target).astype(BF16), rows_in).astype(BF16)


def place_kernel(elem_count, face_count, capacity, new_owner_ref, trace_ref, placed_ref):
    placed_ref[...] = place_rows(
        elem_count,
        face_count,
        capacity,
        new_owner_ref[...],
        trace_ref[...],
        placed_ref.shape[0],
    )


def gram_kernel(
    face_count,
    owner_hbm,
    coarse_hbm,
    tiles_hbm,
    out_ref,
    owner_ref,
    coarse_ref,
    tiles_ref,
    rows_ref,
    *more,
):
    accs, diags, sems = more[:2], more[2:4], more[4]
    tiles = tiles_ref.shape[0]
    copies = [
        pltpu.make_async_copy(owner_hbm, owner_ref, sems.at[0]),
        pltpu.make_async_copy(coarse_hbm, coarse_ref, sems.at[1]),
        pltpu.make_async_copy(tiles_hbm, tiles_ref, sems.at[2]),
    ]
    for copy in copies:
        copy.start()
    for ref in (*accs, *diags):
        ref[...] = jnp.zeros_like(ref)
    for copy in copies:
        copy.wait()

    lane = iota((CHUNK, LANES), 1)
    inside = lane < MCOL
    row = iota((HALF, LANES), 0)
    column = lax.rem(iota((HALF, LANES), 1), MROW)
    swapped = (column > row) & (column < HALF)
    diagonal = column == row
    low = iota((DENSE, LANES), 1) < MROW
    low_wide = iota((MROW, LANES), 1) < MROW
    low_row = iota((1, LANES), 1) < MROW

    for chunk in range(tiles // CHUNK):
        first_tile = chunk * CHUNK
        for group in range(MROW // 4):
            base = group * 3 * LANES
            one, two, three = (
                tiles_ref[
                    first_tile : first_tile + CHUNK, base + k * LANES : base + (k + 1) * LANES
                ].astype(F32)
                for k in range(3)
            )
            rolled = (
                one,
                pltpu.roll(jnp.where(lane < 64, two, one), 32, 1),
                pltpu.roll(jnp.where(lane < 32, three, two), 64, 1),
                pltpu.roll(three, 96, 1),
            )
            for k in range(4):
                rows_ref[pl.ds(first_tile * PITCH + 4 * group + k, CHUNK, stride=PITCH), :] = (
                    jnp.where(inside, rolled[k], 0.0)
                )
        for tile in range(first_tile, first_tile + CHUNK, 2):
            both = jnp.concatenate(
                [
                    rows_ref[t * PITCH : t * PITCH + MROW, :].astype(BF16)
                    for t in (tile, tile + 1)
                ],
                axis=0,
            )
            gram = dot(both, both, NT)
            side = jnp.where(low_wide, gram[:MROW], gram[MROW:])
            lower = pltpu.roll(side[HALF:], LANES - HALF, 1)
            packed = jnp.where(swapped, lower, side[:HALF])
            diag = jnp.sum(jnp.where(diagonal, lower, 0.0), axis=0, keepdims=True)
            turned = pltpu.roll(packed, MROW, 1)
            dense = (
                jnp.where(low, packed[:DENSE], turned[DENSE:]),
                jnp.where(low, turned[:DENSE], packed[DENSE:]),
            )
            own = (jnp.where(low_row, diag, 0.0), jnp.where(low_row, 0.0, diag))
            for k in range(2):
                block = owner_ref[tile + k] * NC + coarse_ref[tile + k]
                here = pl.ds(pl.multiple_of(block * DENSE, DENSE), DENSE)
                accs[k][here, :] += dense[k]
                diags[k][pl.ds(block, 1), :] += own[k]
    for owner in range(face_count):
        start, size = owner * OWNER_ROWS, NC * DENSE
        here = slice(owner * size, (owner + 1) * size)
        out_ref[start : start + size, :] = (accs[0][here, :] + accs[1][here, :]).astype(BF16)
        here = slice(owner * NC, (owner + 1) * NC)
        out_ref[start + size : start + size + NC, :] = (
            diags[0][here, :] + diags[1][here, :]
        ).astype(BF16)


def table_position(slot, elem_count, face_count, capacity):
    part = face_count * capacity
    inner = lax.rem(slot, part)
    block = lax.div(inner, capacity) * elem_count + lax.div(slot, part)
    return block * capacity + lax.rem(inner, capacity)


def main_kernel(
    position_of,
    table_ref,
    conn_hbm,
    rhs_hbm,
    inverse_hbm,
    coupling_hbm,
    schur_hbm,
    share_ref,
    conn_ref,
    rhs_ref,
    inverse_ref,
    coupling_ref,
    schur_ref,
    rhs_wide_ref,
    rhs_turned_ref,
    lam_ref,
    sum_ref,
    weight_a_ref,
    weight_b_ref,
    turned_a_ref,
    turned_b_ref,
    small_sems,
    inverse_sems,
    coupling_sems,
    schur_sems,
):
    elements = rhs_ref.shape[0]
    faces = elements * FACES_PER_ELEM
    trace = FACES_PER_ELEM * FACE_COEFFS
    small = [
        pltpu.make_async_copy(rhs_hbm, rhs_ref, small_sems.at[0]),
        pltpu.make_async_copy(conn_hbm, conn_ref, small_sems.at[1]),
    ]
    for copy in small:
        copy.start()

    def bring(e):
        return (
            pltpu.make_async_copy(coupling_hbm.at[e], coupling_ref.at[e], coupling_sems.at[e]),
            pltpu.make_async_copy(inverse_hbm.at[e], inverse_ref.at[e], inverse_sems.at[e]),
        )

    def leave(e):
        return pltpu.make_async_copy(schur_ref.at[e], schur_hbm.at[e], schur_sems.at[e])

    for e in range(min(AHEAD, elements)):
        for copy in bring(e):
            copy.start()
    rhs_wide_ref[...] = jnp.zeros_like(rhs_wide_ref)
    for copy in small:
        copy.wait()
    rhs_wide_ref[0:elements, :] = rhs_ref[...].astype(F32)
    rhs_turned_ref[...] = rhs_wide_ref[...].T.astype(BF16)
    row = iota((SHARE_ROWS, LANES), 0)
    lane = iota((SHARE_ROWS, LANES), 1)
    positions = jnp.full((SHARE_ROWS, LANES), -1, I32)
    for k in range(faces):
        slot = conn_ref[k % FACES_PER_ELEM, k // FACES_PER_ELEM]
        positions = jnp.where(row == k, position_of(slot), positions)
    slots = table_ref.shape[0]
    hot = jnp.concatenate([positions == lane + base for base in range(0, slots, LANES)], axis=1)
    lam_ref[...] = dot(hot.astype(BF16), table_ref[...])

    def solve(e, weight_ref, turned_ref):
        coupling = coupling_ref[e]
        wide = jnp.concatenate([coupling, rhs_turned_ref[...]], axis=1)
        weight_ref[...] = dot(inverse_ref[e], wide).astype(BF16)
        turned_ref[...] = coupling.T

    def condense(e, weight_ref, turned_ref):
        condensed = dot(turned_ref[...], weight_ref[...])
        schur = (-condensed[:, :trace]).astype(BF16)
        schur_ref[e] = schur
        lam = [lam_ref[pl.ds(e * FACES_PER_ELEM + a, 1), :] for a in range(FACES_PER_ELEM)]
        own = (iota((1, LANES), 1) == e).astype(F32)
        vector = jnp.broadcast_to(jnp.concatenate([*lam, own], axis=1), (16, trace + LANES))
        matrix = jnp.concatenate([schur, condensed[:, trace:].astype(BF16)], axis=1)
        share = dot(vector.astype(BF16), matrix, NT)
        for a in range(FACES_PER_ELEM):
            sum_ref[pl.ds(e * FACES_PER_ELEM + a, 1), :] = share[
                0:1, a * FACE_COEFFS : (a + 1) * FACE_COEFFS
            ]

    even = (weight_a_ref, turned_a_ref)
    odd = (weight_b_ref, turned_b_ref)

    def advance(e, there, here):
        @pl.when(e + AHEAD - 1 < elements)
        def _():
            for copy in bring(e + AHEAD - 1):
                copy.start()

        for copy in bring(e):
            copy.wait()
        solve(e, *there)
        condense(e - 1, *here)
        leave(e - 1).start()

    for copy in bring(0):
        copy.wait()
    solve(0, *even)

    def two(index, carry):
        advance(2 * index + 1, odd, even)
        advance(2 * index + 2, even, odd)
        return carry

    lax.fori_loop(0, (elements - 1) // 2, two, 0)
    if elements % 2 == 0:
        advance(elements - 1, odd, even)
    condense(elements - 1, *(odd if elements % 2 == 0 else even))
    leave(elements - 1).start()

    lane = iota((1, LANES), 1)
    high = jnp.full((1, LANES), -1, I32)
    rest = jnp.zeros((1, LANES), I32)
    for k in range(faces):
        slot = conn_ref[k % FACES_PER_ELEM, k // FACES_PER_ELEM]
        high = jnp.where(lane == k, lax.div(slot, SLOT_BASE), high)
        rest = jnp.where(lane == k, lax.rem(slot, SLOT_BASE), rest)
    shares = jnp.where(row < faces, sum_ref[...], 0.0)
    shares = jnp.where(row == faces, high.astype(F32), shares)
    shares = jnp.where(row == faces + 1, rest.astype(F32), shares)
    share_ref[...] = shares.astype(BF16)
    for e in range(elements):
        leave(e).wait()


def residual(elem_count, capacity, faces, own, table_ref, share_refs):
    mine = lax.axis_index("elem")
    slots = table_ref.shape[0]
    place = iota((own, slots), 0)
    position = (lax.div(place, capacity) * elem_count + mine) * capacity + lax.rem(place, capacity)
    pick = (iota((own, slots), 1) == position).astype(BF16)
    total = dot(pick, table_ref[...])
    slot = (iota((own, SHARE_ROWS), 0) + mine * own).astype(F32)
    for share_ref in share_refs:
        shares = share_ref[...]
        names = shares.astype(F32)
        named = names[faces : faces + 1, :SHARE_ROWS] * SLOT_BASE
        named = named + names[faces + 1 : faces + 2, :SHARE_ROWS]
        total = total - dot((slot == named).astype(BF16), shares)
    return total


def finish_kernel(elem_count, capacity, faces, got_ref, table_ref, share_hbm, *refs):
    others = refs[: elem_count - 1]
    residual_ref, out_ref, sum_ref, full_ref, share_ref, sem = refs[elem_count - 1 :]
    copy = pltpu.make_async_copy(share_hbm, share_ref, sem)
    copy.start()
    total = got_ref[0].astype(F32)
    for k in range(1, got_ref.shape[0]):
        total = total + got_ref[k].astype(F32)
    sum_ref[...] = total

    lane = iota((HALF, LANES), 1)
    row = iota((HALF, LANES), 0)
    wide_row = iota((MROW, LANES), 0)
    wide_lane = iota((MROW, LANES), 1)
    top = wide_row < HALF
    held = (top & ((wide_lane <= wide_row) | (wide_lane >= HALF))) | (
        (~top) & (wide_lane >= wide_row)
    )
    for block in range(NC):
        dense = sum_ref[block * DENSE : (block + 1) * DENSE, :]
        upper = jnp.concatenate([dense, pltpu.roll(dense, MROW, 1)], axis=0)
        diag = sum_ref[NC * DENSE + block : NC * DENSE + block + 1, :]
        diag = pltpu.roll(diag + pltpu.roll(diag, MROW, 1), HALF, 1)
        lower = jnp.where(lane == row + HALF, diag, pltpu.roll(upper, HALF, 1))
        given = jnp.concatenate([upper, lower], axis=0)
        turned = jnp.concatenate([given, given], axis=0).T[:MROW]
        full_ref[block * MROW : (block + 1) * MROW, :] = jnp.where(held, given, turned)
    low = iota((NC, LANES), 1) < MROW
    for chunk in range(HALF):
        left = full_ref[pl.ds(2 * chunk, NC, stride=MROW), :]
        right = full_ref[pl.ds(2 * chunk + 1, NC, stride=MROW), :]
        out_ref[:, chunk * LANES : (chunk + 1) * LANES] = jnp.where(
            low, left, pltpu.roll(right, MROW, 1)
        )
    copy.wait()
    residual_ref[...] = residual(
        elem_count, capacity, faces, residual_ref.shape[0], table_ref, (share_ref, *others)
    )


ANY = pl.BlockSpec(memory_space=pl.ANY)
VMEM = pl.BlockSpec(memory_space=pltpu.VMEM)


def params(limit):
    return pltpu.CompilerParams(vmem_limit_bytes=limit)


def shards(
    trace_old,
    new_owner,
    mortar_tiles,
    mortar_owner,
    mortar_coarse,
    interior_rhs,
    local_inverse,
    coupling,
    connectivity,
):
    face_count = lax.axis_size("face")
    elem_count = lax.axis_size("elem")
    row_count = trace_old.shape[0]
    tile_count = mortar_tiles.shape[0]
    elements, modes = interior_rhs.shape
    faces = elements * FACES_PER_ELEM
    trace = FACES_PER_ELEM * FACE_COEFFS
    capacity = max(2, 2 * row_count // face_count)
    devices = face_count * elem_count
    slots = devices * capacity
    own = slots // elem_count

    placed = pl.pallas_call(
        functools.partial(place_kernel, elem_count, face_count, capacity),
        out_shape=jax.ShapeDtypeStruct((slots, FACE_COEFFS), BF16),
        in_specs=[VMEM, VMEM],
        out_specs=VMEM,
        compiler_params=params(BIG),
        name="place",
    )(new_owner.reshape(1, row_count), trace_old)
    table = lax.all_to_all(
        placed.reshape(devices, capacity, FACE_COEFFS), ("face", "elem"), 0, 0, tiled=True
    ).reshape(slots, FACE_COEFFS)

    blocks = face_count * NC
    sums_shape = (blocks * DENSE, LANES)
    half_grams = pl.pallas_call(
        functools.partial(gram_kernel, face_count),
        out_shape=jax.ShapeDtypeStruct((face_count * OWNER_ROWS, LANES), BF16),
        in_specs=[ANY, ANY, ANY],
        out_specs=VMEM,
        scratch_shapes=[
            pltpu.SMEM((tile_count,), I32),
            pltpu.SMEM((tile_count,), I32),
            pltpu.VMEM(mortar_tiles.shape, BF16),
            pltpu.VMEM((tile_count * PITCH, LANES), F32),
            pltpu.VMEM(sums_shape, F32),
            pltpu.VMEM(sums_shape, F32),
            pltpu.VMEM((blocks, LANES), F32),
            pltpu.VMEM((blocks, LANES), F32),
            pltpu.SemaphoreType.DMA((3,)),
        ],
        compiler_params=params(BIG),
        cost_estimate=pl.CostEstimate(
            flops=4 * tile_count * MROW * MROW * LANES, bytes_accessed=16 << 20, transcendentals=0
        ),
        name="gram",
    )(mortar_owner.reshape(tile_count), mortar_coarse, mortar_tiles)
    got = lax.all_to_all(
        half_grams.reshape(face_count, OWNER_ROWS, LANES), "face", 0, 0, tiled=True
    )

    slots_named, _ = lax.optimization_barrier((connectivity.T, half_grams))
    position_of = functools.partial(
        table_position, elem_count=elem_count, face_count=face_count, capacity=capacity
    )
    schur_blocks, shares = pl.pallas_call(
        functools.partial(main_kernel, position_of),
        out_shape=(
            jax.ShapeDtypeStruct((elements, trace, trace), BF16),
            jax.ShapeDtypeStruct((SHARE_ROWS, LANES), BF16),
        ),
        in_specs=[VMEM, ANY, ANY, ANY, ANY],
        out_specs=(ANY, VMEM),
        scratch_shapes=[
            pltpu.SMEM((FACES_PER_ELEM, elements), I32),
            pltpu.VMEM((elements, modes), BF16),
            pltpu.VMEM((elements, modes, modes), BF16),
            pltpu.VMEM((elements, modes, trace), BF16),
            pltpu.VMEM((elements, trace, trace), BF16),
            pltpu.VMEM((LANES, modes), F32),
            pltpu.VMEM((modes, LANES), BF16),
            pltpu.VMEM((SHARE_ROWS, LANES), F32),
            pltpu.VMEM((SHARE_ROWS, LANES), F32),
            pltpu.VMEM((modes, trace + LANES), BF16),
            pltpu.VMEM((modes, trace + LANES), BF16),
            pltpu.VMEM((trace, modes), BF16),
            pltpu.VMEM((trace, modes), BF16),
            pltpu.SemaphoreType.DMA((2,)),
            pltpu.SemaphoreType.DMA((elements,)),
            pltpu.SemaphoreType.DMA((elements,)),
            pltpu.SemaphoreType.DMA((elements,)),
        ],
        compiler_params=params(BIG),
        cost_estimate=pl.CostEstimate(
            flops=2 * elements * modes * trace * (modes + trace),
            bytes_accessed=2 * elements * (modes * (modes + trace) + trace * trace),
            transcendentals=0,
        ),
        name="condense",
    )(table, slots_named, interior_rhs, local_inverse, coupling)

    all_shares = [shares]
    for shift in range(1, elem_count):
        pairs = [(k, (k + shift) % elem_count) for k in range(elem_count)]
        all_shares.append(lax.ppermute(shares, "elem", pairs))

    slot_residual, coarse_blocks = pl.pallas_call(
        functools.partial(finish_kernel, elem_count, capacity, faces),
        out_shape=(
            jax.ShapeDtypeStruct((own, FACE_COEFFS), F32),
            jax.ShapeDtypeStruct((NC, MROW * MROW), F32),
        ),
        in_specs=[VMEM, VMEM, ANY] + [VMEM] * (elem_count - 1),
        out_specs=(VMEM, VMEM),
        scratch_shapes=[
            pltpu.VMEM((OWNER_ROWS, LANES), F32),
            pltpu.VMEM((NC * MROW, LANES), F32),
            pltpu.VMEM((SHARE_ROWS, LANES), BF16),
            pltpu.SemaphoreType.DMA,
        ],
        compiler_params=params(6 << 20),
        name="finish",
    )(got, table, *all_shares)
    return schur_blocks, slot_residual, coarse_blocks


def solution(mesh):
    return jax.shard_map(
        shards,
        mesh=mesh,
        in_specs=(
            P(("face", "elem"), None),
            P(("face", "elem"), None),
            P(("face", "elem"), None),
            P(("face", "elem"), None),
            P(("face", "elem")),
            P(("face", "elem"), None),
            P(("face", "elem"), None, None),
            P(("face", "elem"), None, None),
            P(("face", "elem"), None),
        ),
        out_specs=(
            P(("face", "elem"), None, None),
            P(("face", "elem"), None),
            P(("face", "elem"), None),
        ),
        check_vma=False,
    )
```

```python
import functools

import jax
import jax.numpy as jnp
from jax import lax
from jax.experimental import pallas as pl
from jax.experimental.pallas import tpu as pltpu
from jax.sharding import PartitionSpec as P

FACE_COEFFS = 128
FACES_PER_ELEM = 3
MROW = 64
MCOL = 96
NC = 16
HALF = MROW // 2
LANES = 128
DENSE = HALF * MROW // LANES
OWNER_ROWS = NC * (DENSE + 1)
PER_FACE = 16
NAMED = FACES_PER_ELEM * PER_FACE
SHARE_ROWS = NAMED + 16
SLOT_BASE = 16
CHUNK = 16
AHEAD = 3
BIG = 62 << 20
PITCH = MROW + 8

BF16 = jnp.bfloat16
F32 = jnp.float32
I32 = jnp.int32

NT = (((1,), (1,)), ((), ()))
TN = (((0,), (0,)), ((), ()))


def iota(shape, dim):
    return lax.broadcasted_iota(I32, shape, dim)


def dot(left, right, dims=(((1,), (0,)), ((), ()))):
    return lax.dot_general(left, right, dims, preferred_element_type=F32)


def place_kernel(face_count, capacity, owner_hbm, trace_hbm, placed_ref, owner_ref, trace_ref, sems):
    copies = [
        pltpu.make_async_copy(owner_hbm, owner_ref, sems.at[0]),
        pltpu.make_async_copy(trace_hbm, trace_ref, sems.at[1]),
    ]
    for copy in copies:
        copy.start()
    slots, rows = placed_ref.shape[0], trace_ref.shape[0]
    earlier = (iota((rows, rows), 0) < iota((rows, rows), 1)).astype(BF16)
    for copy in copies:
        copy.wait()
    owners = owner_ref[...]
    hot = (iota((face_count, rows), 0) == owners).astype(F32)
    rank = jnp.sum(hot * dot(hot.astype(BF16), earlier), axis=0, keepdims=True).astype(I32)
    place = (iota((slots, rows), 0) == owners * capacity + rank).astype(BF16)
    placed_ref[...] = dot(place, trace_ref[...]).astype(BF16)


def gram_kernel(
    face_count,
    owner_hbm,
    coarse_hbm,
    tiles_hbm,
    out_ref,
    owner_ref,
    coarse_ref,
    tiles_ref,
    rows_ref,
    *more,
):
    accs, diags, sems = more[:2], more[2:4], more[4]
    tiles = tiles_ref.shape[0]
    copies = [
        pltpu.make_async_copy(owner_hbm, owner_ref, sems.at[0]),
        pltpu.make_async_copy(coarse_hbm, coarse_ref, sems.at[1]),
        pltpu.make_async_copy(tiles_hbm, tiles_ref, sems.at[2]),
    ]
    for copy in copies:
        copy.start()
    for ref in (*accs, *diags):
        ref[...] = jnp.zeros_like(ref)
    for copy in copies:
        copy.wait()

    lane = iota((CHUNK, LANES), 1)
    inside = lane < MCOL
    row = iota((HALF, LANES), 0)
    column = lax.rem(iota((HALF, LANES), 1), MROW)
    swapped = (column > row) & (column < HALF)
    diagonal = column == row
    low = iota((DENSE, LANES), 1) < MROW
    low_wide = iota((MROW, LANES), 1) < MROW
    low_row = iota((1, LANES), 1) < MROW

    for chunk in range(tiles // CHUNK):
        first_tile = chunk * CHUNK
        for group in range(MROW // 4):
            base = group * 3 * LANES
            one, two, three = (
                tiles_ref[
                    first_tile : first_tile + CHUNK, base + k * LANES : base + (k + 1) * LANES
                ].astype(F32)
                for k in range(3)
            )
            rolled = (
                one,
                pltpu.roll(jnp.where(lane < 64, two, one), 32, 1),
                pltpu.roll(jnp.where(lane < 32, three, two), 64, 1),
                pltpu.roll(three, 96, 1),
            )
            for k in range(4):
                rows_ref[pl.ds(first_tile * PITCH + 4 * group + k, CHUNK, stride=PITCH), :] = (
                    jnp.where(inside, rolled[k], 0.0)
                )
        for tile in range(first_tile, first_tile + CHUNK, 2):
            both = jnp.concatenate(
                [
                    rows_ref[t * PITCH : t * PITCH + MROW, :].astype(BF16)
                    for t in (tile, tile + 1)
                ],
                axis=0,
            )
            gram = dot(both, both, NT)
            side = jnp.where(low_wide, gram[:MROW], gram[MROW:])
            lower = pltpu.roll(side[HALF:], LANES - HALF, 1)
            packed = jnp.where(swapped, lower, side[:HALF])
            diag = jnp.sum(jnp.where(diagonal, lower, 0.0), axis=0, keepdims=True)
            turned = pltpu.roll(packed, MROW, 1)
            dense = (
                jnp.where(low, packed[:DENSE], turned[DENSE:]),
                jnp.where(low, turned[:DENSE], packed[DENSE:]),
            )
            own = (jnp.where(low_row, diag, 0.0), jnp.where(low_row, 0.0, diag))
            for k in range(2):
                block = owner_ref[tile + k] * NC + coarse_ref[tile + k]
                here = pl.ds(pl.multiple_of(block * DENSE, DENSE), DENSE)
                accs[k][here, :] += dense[k]
                diags[k][pl.ds(block, 1), :] += own[k]
    for owner in range(face_count):
        start, size = owner * OWNER_ROWS, NC * DENSE
        here = slice(owner * size, (owner + 1) * size)
        out_ref[start : start + size, :] = (accs[0][here, :] + accs[1][here, :]).astype(BF16)
        here = slice(owner * NC, (owner + 1) * NC)
        out_ref[start + size : start + size + NC, :] = (
            diags[0][here, :] + diags[1][here, :]
        ).astype(BF16)


def main_kernel(
    elem_count,
    conn_hbm,
    rhs_hbm,
    inverse_hbm,
    coupling_hbm,
    *refs,
):
    tables_hbm = refs[:elem_count]
    (
        schur_hbm,
        share_ref,
        conn_ref,
        rhs_ref,
        table_ref,
        inverse_ref,
        coupling_ref,
        schur_ref,
        wide_ref,
        rhs_turned_ref,
        lam_turned_ref,
        sum_ref,
        weight_a_ref,
        weight_b_ref,
        turned_a_ref,
        turned_b_ref,
        small_sems,
        table_sems,
        inverse_sems,
        coupling_sems,
        schur_sems,
    ) = refs[elem_count:]
    elements = rhs_ref.shape[0]
    trace = FACES_PER_ELEM * FACE_COEFFS
    own = tables_hbm[0].shape[0]
    mine = lax.axis_index("elem")
    small = [
        pltpu.make_async_copy(rhs_hbm, rhs_ref, small_sems.at[0]),
        pltpu.make_async_copy(conn_hbm, conn_ref, small_sems.at[1]),
    ]
    for k in range(elem_count):
        there = table_ref.at[pl.ds(k * own, own)]
        small.append(pltpu.make_async_copy(tables_hbm[k], there, table_sems.at[k]))

    def bring(e):
        return (
            pltpu.make_async_copy(coupling_hbm.at[e], coupling_ref.at[e], coupling_sems.at[e]),
            pltpu.make_async_copy(inverse_hbm.at[e], inverse_ref.at[e], inverse_sems.at[e]),
        )

    def leave(e):
        return pltpu.make_async_copy(schur_ref.at[e], schur_hbm.at[e], schur_sems.at[e])

    for copy in small:
        copy.start()
    for e in range(min(AHEAD, elements)):
        for copy in bring(e):
            copy.start()
    wide_ref[...] = jnp.zeros_like(wide_ref)
    sum_ref[...] = jnp.zeros_like(sum_ref)
    for copy in small:
        copy.wait()
    wide_ref[0:elements, :] = rhs_ref[...].astype(F32)
    rhs_turned_ref[...] = wide_ref[...].T.astype(BF16)
    row = iota((PER_FACE, LANES), 0)
    lane = iota((PER_FACE, LANES), 1)
    slots = table_ref.shape[0]
    for a in range(FACES_PER_ELEM):
        positions = jnp.full((PER_FACE, LANES), -1, I32)
        for e in range(elements):
            slot = conn_ref[a, e]
            turn = lax.rem(mine + elem_count - lax.div(slot, own), elem_count)
            positions = jnp.where(row == e, turn * own + lax.rem(slot, own), positions)
        hot = jnp.concatenate([positions == lane + k for k in range(0, slots, LANES)], axis=1)
        wide_ref[0:PER_FACE, a * LANES : (a + 1) * LANES] = dot(hot.astype(BF16), table_ref[...])
    wide_ref[0:PER_FACE, trace:] = ((row == lane) & (row < elements)).astype(F32)
    lam_turned_ref[...] = wide_ref[...].T.astype(BF16)

    def solve(e, weight_ref, turned_ref):
        coupling = coupling_ref[e]
        wide = jnp.concatenate([coupling, rhs_turned_ref[...]], axis=1)
        weight_ref[...] = dot(inverse_ref[e], wide).astype(BF16)
        turned_ref[...] = coupling.T

    def condense(e, weight_ref, turned_ref):
        condensed = dot(turned_ref[...], weight_ref[...])
        schur = (-condensed[:, :trace]).astype(BF16)
        schur_ref[e] = schur
        matrix = jnp.concatenate([schur, condensed[:, trace:].astype(BF16)], axis=1)
        share = dot(matrix, lam_turned_ref[...])
        sum_ref[...] = jnp.where(iota((trace, LANES), 1) == e, share, sum_ref[...])

    even = (weight_a_ref, turned_a_ref)
    odd = (weight_b_ref, turned_b_ref)

    def advance(e, there, here):
        @pl.when(e + AHEAD - 1 < elements)
        def _():
            for copy in bring(e + AHEAD - 1):
                copy.start()

        for copy in bring(e):
            copy.wait()
        solve(e, *there)
        condense(e - 1, *here)
        leave(e - 1).start()

    for copy in bring(0):
        copy.wait()
    solve(0, *even)

    def two(index, carry):
        advance(2 * index + 1, odd, even)
        advance(2 * index + 2, even, odd)
        return carry

    lax.fori_loop(0, (elements - 1) // 2, two, 0)
    if elements % 2 == 0:
        advance(elements - 1, odd, even)
    condense(elements - 1, *(odd if elements % 2 == 0 else even))
    leave(elements - 1).start()

    lane = iota((1, LANES), 1)
    high = jnp.full((1, LANES), -1, I32)
    rest = jnp.zeros((1, LANES), I32)
    for a in range(FACES_PER_ELEM):
        here = slice(a * PER_FACE, (a + 1) * PER_FACE)
        shares = sum_ref[a * LANES : (a + 1) * LANES, :].T
        share_ref[here, :] = shares[:PER_FACE].astype(BF16)
        for e in range(elements):
            high = jnp.where(lane == a * PER_FACE + e, lax.div(conn_ref[a, e], SLOT_BASE), high)
            rest = jnp.where(lane == a * PER_FACE + e, lax.rem(conn_ref[a, e], SLOT_BASE), rest)
    names = jnp.where(row == 0, high, jnp.where(row == 1, rest, 0))
    share_ref[NAMED:, :] = names.astype(F32).astype(BF16)
    for e in range(elements):
        leave(e).wait()


def finish_kernel(elem_count, *refs):
    ins = refs[: 2 + elem_count]
    residual_ref, out_ref = refs[2 + elem_count : 4 + elem_count]
    got_ref, table_ref, shares_ref, sum_ref, full_ref, sems = refs[4 + elem_count :]
    places = [got_ref, table_ref] + [shares_ref.at[k] for k in range(elem_count)]
    copies = [
        pltpu.make_async_copy(ins[k], places[k], sems.at[k]) for k in range(2 + elem_count)
    ]
    for copy in copies:
        copy.start()
    copies[0].wait()
    total = got_ref[0].astype(F32)
    for k in range(1, got_ref.shape[0]):
        total = total + got_ref[k].astype(F32)
    sum_ref[...] = total

    lane = iota((HALF, LANES), 1)
    row = iota((HALF, LANES), 0)
    wide_row = iota((MROW, LANES), 0)
    wide_lane = iota((MROW, LANES), 1)
    top = wide_row < HALF
    held = (top & ((wide_lane <= wide_row) | (wide_lane >= HALF))) | (
        (~top) & (wide_lane >= wide_row)
    )
    for block in range(NC):
        dense = sum_ref[block * DENSE : (block + 1) * DENSE, :]
        upper = jnp.concatenate([dense, pltpu.roll(dense, MROW, 1)], axis=0)
        diag = sum_ref[NC * DENSE + block : NC * DENSE + block + 1, :]
        diag = pltpu.roll(diag + pltpu.roll(diag, MROW, 1), HALF, 1)
        lower = jnp.where(lane == row + HALF, diag, pltpu.roll(upper, HALF, 1))
        given = jnp.concatenate([upper, lower], axis=0)
        turned = jnp.concatenate([given, given], axis=0).T[:MROW]
        full_ref[block * MROW : (block + 1) * MROW, :] = jnp.where(held, given, turned)
    low = iota((NC, LANES), 1) < MROW
    for chunk in range(HALF):
        left = full_ref[pl.ds(2 * chunk, NC, stride=MROW), :]
        right = full_ref[pl.ds(2 * chunk + 1, NC, stride=MROW), :]
        out_ref[:, chunk * LANES : (chunk + 1) * LANES] = jnp.where(
            low, left, pltpu.roll(right, MROW, 1)
        )
    for copy in copies[1:]:
        copy.wait()
    own = residual_ref.shape[0]
    mine = lax.axis_index("elem")
    slot = (iota((own, SHARE_ROWS), 0) + mine * own).astype(F32)
    left = table_ref[...].astype(F32)
    for k in range(elem_count):
        names = shares_ref[k, NAMED:, :].astype(F32)
        named = (names[0:1] * SLOT_BASE + names[1:2])[:, :SHARE_ROWS]
        left = left - dot((slot == named).astype(BF16), shares_ref[k])
    residual_ref[...] = left


ANY = pl.BlockSpec(memory_space=pl.ANY)
VMEM = pl.BlockSpec(memory_space=pltpu.VMEM)


def params(limit):
    return pltpu.CompilerParams(vmem_limit_bytes=limit)


def around(block, elem_count):
    blocks = [block]
    for shift in range(1, elem_count):
        pairs = [(k, (k + shift) % elem_count) for k in range(elem_count)]
        blocks.append(lax.ppermute(block, "elem", pairs))
    return blocks


def shards(
    trace_old,
    new_owner,
    mortar_tiles,
    mortar_owner,
    mortar_coarse,
    interior_rhs,
    local_inverse,
    coupling,
    connectivity,
):
    face_count = lax.axis_size("face")
    elem_count = lax.axis_size("elem")
    row_count = trace_old.shape[0]
    tile_count = mortar_tiles.shape[0]
    elements, modes = interior_rhs.shape
    trace = FACES_PER_ELEM * FACE_COEFFS
    capacity = max(2, 2 * row_count // face_count)
    own = face_count * capacity

    placed = pl.pallas_call(
        functools.partial(place_kernel, face_count, capacity),
        out_shape=jax.ShapeDtypeStruct((own, FACE_COEFFS), BF16),
        in_specs=[ANY, ANY],
        out_specs=VMEM,
        scratch_shapes=[
            pltpu.VMEM((1, row_count), I32),
            pltpu.VMEM(trace_old.shape, BF16),
            pltpu.SemaphoreType.DMA((2,)),
        ],
        compiler_params=params(BIG),
        name="place",
    )(new_owner.reshape(1, row_count), trace_old)
    rows = lax.all_to_all(
        placed.reshape(face_count, capacity, FACE_COEFFS), "face", 0, 0, tiled=True
    ).reshape(own, FACE_COEFFS)
    tables = around(rows, elem_count)

    blocks = face_count * NC
    sums_shape = (blocks * DENSE, LANES)
    half_grams = pl.pallas_call(
        functools.partial(gram_kernel, face_count),
        out_shape=jax.ShapeDtypeStruct((face_count * OWNER_ROWS, LANES), BF16),
        in_specs=[ANY, ANY, ANY],
        out_specs=VMEM,
        scratch_shapes=[
            pltpu.SMEM((tile_count,), I32),
            pltpu.SMEM((tile_count,), I32),
            pltpu.VMEM(mortar_tiles.shape, BF16),
            pltpu.VMEM((tile_count * PITCH, LANES), F32),
            pltpu.VMEM(sums_shape, F32),
            pltpu.VMEM(sums_shape, F32),
            pltpu.VMEM((blocks, LANES), F32),
            pltpu.VMEM((blocks, LANES), F32),
            pltpu.SemaphoreType.DMA((3,)),
        ],
        compiler_params=params(BIG),
        cost_estimate=pl.CostEstimate(
            flops=4 * tile_count * MROW * MROW * LANES, bytes_accessed=16 << 20, transcendentals=0
        ),
        name="gram",
    )(mortar_owner.reshape(tile_count), mortar_coarse, mortar_tiles)
    got = lax.all_to_all(
        half_grams.reshape(face_count, OWNER_ROWS, LANES), "face", 0, 0, tiled=True
    )

    slots_named, _ = lax.optimization_barrier((connectivity.T, half_grams))
    schur_blocks, shares = pl.pallas_call(
        functools.partial(main_kernel, elem_count),
        out_shape=(
            jax.ShapeDtypeStruct((elements, trace, trace), BF16),
            jax.ShapeDtypeStruct((SHARE_ROWS, LANES), BF16),
        ),
        in_specs=[ANY] * (4 + elem_count),
        out_specs=(ANY, VMEM),
        scratch_shapes=[
            pltpu.SMEM((FACES_PER_ELEM, elements), I32),
            pltpu.VMEM((elements, modes), BF16),
            pltpu.VMEM((elem_count * own, FACE_COEFFS), BF16),
            pltpu.VMEM((elements, modes, modes), BF16),
            pltpu.VMEM((elements, modes, trace), BF16),
            pltpu.VMEM((elements, trace, trace), BF16),
            pltpu.VMEM((LANES, modes), F32),
            pltpu.VMEM((modes, LANES), BF16),
            pltpu.VMEM((trace + LANES, LANES), BF16),
            pltpu.VMEM((trace, LANES), F32),
            pltpu.VMEM((modes, trace + LANES), BF16),
            pltpu.VMEM((modes, trace + LANES), BF16),
            pltpu.VMEM((trace, modes), BF16),
            pltpu.VMEM((trace, modes), BF16),
            pltpu.SemaphoreType.DMA((2,)),
            pltpu.SemaphoreType.DMA((elem_count,)),
            pltpu.SemaphoreType.DMA((elements,)),
            pltpu.SemaphoreType.DMA((elements,)),
            pltpu.SemaphoreType.DMA((elements,)),
        ],
        compiler_params=params(BIG),
        cost_estimate=pl.CostEstimate(
            flops=2 * elements * modes * trace * (modes + trace),
            bytes_accessed=2 * elements * (modes * (modes + trace) + trace * trace),
            transcendentals=0,
        ),
        name="condense",
    )(slots_named, interior_rhs, local_inverse, coupling, *tables)

    slot_residual, coarse_blocks = pl.pallas_call(
        functools.partial(finish_kernel, elem_count),
        out_shape=(
            jax.ShapeDtypeStruct((own, FACE_COEFFS), F32),
            jax.ShapeDtypeStruct((NC, MROW * MROW), F32),
        ),
        in_specs=[ANY] * (2 + elem_count),
        out_specs=(VMEM, VMEM),
        scratch_shapes=[
            pltpu.VMEM(got.shape, BF16),
            pltpu.VMEM((own, FACE_COEFFS), BF16),
            pltpu.VMEM((elem_count, SHARE_ROWS, LANES), BF16),
            pltpu.VMEM((OWNER_ROWS, LANES), F32),
            pltpu.VMEM((NC * MROW, LANES), F32),
            pltpu.SemaphoreType.DMA((2 + elem_count,)),
        ],
        compiler_params=params(BIG),
        name="finish",
    )(got, rows, *around(shares, elem_count))
    return schur_blocks, slot_residual, coarse_blocks


def solution(mesh):
    return jax.shard_map(
        shards,
        mesh=mesh,
        in_specs=(
            P(("face", "elem"), None),
            P(("face", "elem"), None),
            P(("face", "elem"), None),
            P(("face", "elem"), None),
            P(("face", "elem")),
            P(("face", "elem"), None),
            P(("face", "elem"), None, None),
            P(("face", "elem"), None, None),
            P(("face", "elem"), None),
        ),
        out_specs=(
            P(("face", "elem"), None, None),
            P(("face", "elem"), None),
            P(("face", "elem"), None),
        ),
        check_vma=False,
    )
```

```python
import functools

import jax
import jax.numpy as jnp
from jax import lax
from jax.experimental import pallas as pl
from jax.experimental.pallas import tpu as pltpu
from jax.sharding import PartitionSpec as P

FACE_COEFFS = 128
FACES_PER_ELEM = 3
MROW = 64
MCOL = 96
NC = 16
HALF = MROW // 2
LANES = 128
DENSE = HALF * MROW // LANES
OWNER_ROWS = NC * (DENSE + 1)
PER_FACE = 16
NAMED = FACES_PER_ELEM * PER_FACE
SHARE_ROWS = NAMED + 16
SLOT_BASE = 16
CHUNK = 16
MOST_PAIRED = 8
BIG = 62 << 20
PITCH = MROW + 8

BF16 = jnp.bfloat16
F32 = jnp.float32
I32 = jnp.int32

NT = (((1,), (1,)), ((), ()))
TN = (((0,), (0,)), ((), ()))


def iota(shape, dim):
    return lax.broadcasted_iota(I32, shape, dim)


def dot(left, right, dims=(((1,), (0,)), ((), ()))):
    return lax.dot_general(left, right, dims, preferred_element_type=F32)


def place_kernel(elem_count, face_count, capacity, paired, *refs):
    owners_hbm, traces_hbm = refs[:elem_count], refs[elem_count : 2 * elem_count]
    out_refs = refs[2 * elem_count : -3]
    owner_ref, trace_ref, sems = refs[-3:]
    copies = []
    for k in range(elem_count):
        copies.append(
            pltpu.make_async_copy(owners_hbm[k], owner_ref.at[k], sems.at[k])
        )
        copies.append(
            pltpu.make_async_copy(traces_hbm[k], trace_ref.at[k], sems.at[elem_count + k])
        )
    for copy in copies:
        copy.start()
    mine = lax.axis_index("face") if paired else 0
    rows = trace_ref.shape[1]
    block = elem_count * capacity
    slots = face_count * block
    earlier = (iota((rows, rows), 0) < iota((rows, rows), 1)).astype(BF16)
    slot = iota((slots, rows), 0)
    for copy in copies:
        copy.wait()
    placed = jnp.zeros((slots, FACE_COEFFS), F32)
    for k in range(elem_count):
        owners = owner_ref[k]
        hot = (iota((face_count, rows), 0) == owners).astype(F32)
        rank = jnp.sum(hot * dot(hot.astype(BF16), earlier), axis=0, keepdims=True).astype(I32)
        target = ((owners ^ mine) * elem_count + k) * capacity + rank
        placed = placed + dot((slot == target).astype(BF16), trace_ref[k])
    each = slots // len(out_refs)
    for k, out_ref in enumerate(out_refs):
        out_ref[...] = placed[k * each : (k + 1) * each].astype(BF16)


def gram_kernel(face_count, paired, owner_hbm, coarse_hbm, tiles_hbm, *refs):
    out_refs, refs = refs[:-9], refs[-9:]
    owner_ref, coarse_ref, tiles_ref, rows_ref = refs[:4]
    accs, diags, sems = refs[4:6], refs[6:8], refs[8]
    mine = lax.axis_index("face") if paired else 0
    tiles = tiles_ref.shape[0]
    copies = [
        pltpu.make_async_copy(owner_hbm, owner_ref, sems.at[0]),
        pltpu.make_async_copy(coarse_hbm, coarse_ref, sems.at[1]),
        pltpu.make_async_copy(tiles_hbm, tiles_ref, sems.at[2]),
    ]
    for copy in copies:
        copy.start()
    for ref in (*accs, *diags):
        ref[...] = jnp.zeros_like(ref)
    for copy in copies:
        copy.wait()

    lane = iota((CHUNK, LANES), 1)
    inside = lane < MCOL
    row = iota((HALF, LANES), 0)
    column = lax.rem(iota((HALF, LANES), 1), MROW)
    swapped = (column > row) & (column < HALF)
    diagonal = column == row
    low = iota((DENSE, LANES), 1) < MROW
    low_wide = iota((MROW, LANES), 1) < MROW
    low_row = iota((1, LANES), 1) < MROW

    for chunk in range(tiles // CHUNK):
        first_tile = chunk * CHUNK
        for group in range(MROW // 4):
            base = group * 3 * LANES
            one, two, three = (
                tiles_ref[
                    first_tile : first_tile + CHUNK, base + k * LANES : base + (k + 1) * LANES
                ].astype(F32)
                for k in range(3)
            )
            rolled = (
                one,
                pltpu.roll(jnp.where(lane < 64, two, one), 32, 1),
                pltpu.roll(jnp.where(lane < 32, three, two), 64, 1),
                pltpu.roll(three, 96, 1),
            )
            for k in range(4):
                rows_ref[pl.ds(first_tile * PITCH + 4 * group + k, CHUNK, stride=PITCH), :] = (
                    jnp.where(inside, rolled[k], 0.0)
                )
        for tile in range(first_tile, first_tile + CHUNK, 2):
            both = jnp.concatenate(
                [
                    rows_ref[t * PITCH : t * PITCH + MROW, :].astype(BF16)
                    for t in (tile, tile + 1)
                ],
                axis=0,
            )
            gram = dot(both, both, NT)
            side = jnp.where(low_wide, gram[:MROW], gram[MROW:])
            lower = pltpu.roll(side[HALF:], LANES - HALF, 1)
            packed = jnp.where(swapped, lower, side[:HALF])
            diag = jnp.sum(jnp.where(diagonal, lower, 0.0), axis=0, keepdims=True)
            turned = pltpu.roll(packed, MROW, 1)
            dense = (
                jnp.where(low, packed[:DENSE], turned[DENSE:]),
                jnp.where(low, turned[:DENSE], packed[DENSE:]),
            )
            own = (jnp.where(low_row, diag, 0.0), jnp.where(low_row, 0.0, diag))
            for k in range(2):
                block = (owner_ref[tile + k] ^ mine) * NC + coarse_ref[tile + k]
                here = pl.ds(pl.multiple_of(block * DENSE, DENSE), DENSE)
                accs[k][here, :] += dense[k]
                diags[k][pl.ds(block, 1), :] += own[k]
    size = NC * DENSE
    for owner in range(face_count):
        out_ref, start = (out_refs[owner], 0) if paired else (out_refs[0], owner * OWNER_ROWS)
        here = slice(owner * size, (owner + 1) * size)
        out_ref[start : start + size, :] = (accs[0][here, :] + accs[1][here, :]).astype(BF16)
        here = slice(owner * NC, (owner + 1) * NC)
        out_ref[start + size : start + size + NC, :] = (
            diags[0][here, :] + diags[1][here, :]
        ).astype(BF16)


def main_kernel(
    elem_count,
    face_count,
    paired,
    conn_hbm,
    rhs_hbm,
    inverse_hbm,
    coupling_hbm,
    *refs,
):
    refs, tables_hbm = refs[-20:], refs[:-20]
    (
        schur_hbm,
        share_ref,
        own_ref,
        conn_ref,
        rhs_ref,
        table_ref,
        inverse_ref,
        coupling_ref,
        schur_ref,
        wide_ref,
        rhs_turned_ref,
        vector_ref,
        sum_ref,
        turned_a_ref,
        turned_b_ref,
        product_a_ref,
        product_b_ref,
        small_sems,
        block_sems,
        schur_sems,
    ) = refs
    elements = rhs_ref.shape[0]
    trace = FACES_PER_ELEM * FACE_COEFFS
    slots = table_ref.shape[0]
    own = own_ref.shape[0]
    capacity = own // face_count
    my_elem = lax.axis_index("elem")
    my_face = lax.axis_index("face") if paired else 0
    small = [
        pltpu.make_async_copy(rhs_hbm, rhs_ref, small_sems.at[0]),
        pltpu.make_async_copy(conn_hbm, conn_ref, small_sems.at[1]),
    ]
    each = slots // len(tables_hbm)
    for k, table_hbm in enumerate(tables_hbm):
        there = table_ref.at[pl.ds(k * each, each)]
        small.append(pltpu.make_async_copy(table_hbm, there, small_sems.at[2 + k]))

    def coupling_copy(e):
        return pltpu.make_async_copy(coupling_hbm.at[e], coupling_ref.at[e], block_sems.at[0, e])

    def inverse_copy(e):
        return pltpu.make_async_copy(inverse_hbm.at[e], inverse_ref.at[e], block_sems.at[1, e])

    def leave(e):
        return pltpu.make_async_copy(schur_ref.at[e], schur_hbm.at[e], schur_sems.at[e])

    coupling_copy(0).start()
    for copy in small:
        copy.start()
    inverse_copy(0).start()
    coupling_copy(1).start()
    inverse_copy(1).start()
    coupling_copy(2).start()

    def turn(e, turned_ref):
        turned_ref[...] = coupling_ref[e].T

    def first(e, turned_ref, product_ref):
        product_ref[...] = dot(turned_ref[...], inverse_ref[e]).astype(BF16)

    def second(e, product_ref):
        wide = jnp.concatenate([coupling_ref[e], rhs_turned_ref[...]], axis=1)
        condensed = dot(product_ref[...], wide)
        schur_ref[e] = (-condensed[:, :trace]).astype(BF16)
        total = condensed * vector_ref[pl.ds(e, 1), :]
        total = sum(total[:, k * LANES : (k + 1) * LANES] for k in range(FACES_PER_ELEM + 1))
        sums = jnp.sum(total, axis=1, keepdims=True)
        sum_ref[...] = jnp.where(iota((trace, LANES), 1) == e, sums, sum_ref[...])

    turned = (turned_a_ref, turned_b_ref)
    product = (product_a_ref, product_b_ref)

    def advance(e, parity, turning=True, finishing=True):
        if turning:
            @pl.when(e + 2 < elements)
            def _():
                inverse_copy(e + 2).start()

            @pl.when(e + 3 < elements)
            def _():
                coupling_copy(e + 3).start()

            coupling_copy(e + 1).wait()
        inverse_copy(e).wait()
        if turning:
            turn(e + 1, turned[1 - parity])
        first(e, turned[parity], product[parity])
        if finishing:
            second(e - 1, product[1 - parity])
            leave(e - 1).start()

    coupling_copy(0).wait()
    turn(0, turned[0])
    for copy in small:
        copy.wait()
    wide_ref[...] = jnp.zeros_like(wide_ref)
    sum_ref[...] = jnp.zeros_like(sum_ref)
    wide_ref[0:elements, :] = rhs_ref[...].astype(F32)
    rhs_turned_ref[...] = wide_ref[...].T.astype(BF16)
    row = iota((PER_FACE, LANES), 0)
    lane = iota((PER_FACE, LANES), 1)

    def position(elem, inner):
        face = lax.div(inner, capacity) ^ my_face
        return (face * elem_count + (elem ^ my_elem)) * capacity + lax.rem(inner, capacity)

    for a in range(FACES_PER_ELEM):
        positions = jnp.full((PER_FACE, LANES), -1, I32)
        for e in range(elements):
            slot = conn_ref[a, e]
            positions = jnp.where(
                row == e, position(lax.div(slot, own), lax.rem(slot, own)), positions
            )
        hot = jnp.concatenate([positions == lane + k for k in range(0, slots, LANES)], axis=1)
        lam = dot(hot.astype(BF16), table_ref[...])
        vector_ref[:, a * LANES : (a + 1) * LANES] = -lam
    vector_ref[:, trace:] = (row == lane).astype(F32)
    place = position(my_elem, iota((own, slots), 0))
    pick = (iota((own, slots), 1) == place).astype(BF16)
    own_ref[...] = dot(pick, table_ref[...]).astype(BF16)

    advance(0, 0, finishing=False)

    def two(index, carry):
        advance(2 * index + 1, 1)
        advance(2 * index + 2, 0)
        return carry

    pairs = (elements - 2) // 2
    lax.fori_loop(0, pairs, two, 0)
    for e in range(2 * pairs + 1, elements):
        advance(e, e % 2, turning=e + 1 < elements)
    second(elements - 1, product[(elements - 1) % 2])
    leave(elements - 1).start()

    lane = iota((1, LANES), 1)
    high = jnp.full((1, LANES), -1, I32)
    rest = jnp.zeros((1, LANES), I32)
    for a in range(FACES_PER_ELEM):
        here = slice(a * PER_FACE, (a + 1) * PER_FACE)
        shares = sum_ref[a * LANES : (a + 1) * LANES, :].T
        share_ref[here, :] = shares[:PER_FACE].astype(BF16)
        for e in range(elements):
            high = jnp.where(lane == a * PER_FACE + e, lax.div(conn_ref[a, e], SLOT_BASE), high)
            rest = jnp.where(lane == a * PER_FACE + e, lax.rem(conn_ref[a, e], SLOT_BASE), rest)
    names = jnp.where(row == 0, high, jnp.where(row == 1, rest, 0))
    share_ref[NAMED:, :] = names.astype(F32).astype(BF16)
    for e in range(elements):
        leave(e).wait()


def finish_kernel(elem_count, face_count, *refs):
    ins, refs = refs[:-8], refs[-8:]
    residual_ref, out_ref, got_ref, own_ref, shares_ref, sum_ref, full_ref, sems = refs
    places = [own_ref] + [shares_ref.at[k] for k in range(elem_count)]
    parts = len(ins) - len(places)
    each = face_count // parts
    places += [got_ref.at[pl.ds(k * each, each)] for k in range(parts)]
    copies = [pltpu.make_async_copy(ins[k], places[k], sems.at[k]) for k in range(len(ins))]
    for copy in copies[1 + elem_count :] + copies[: 1 + elem_count]:
        copy.start()
    for copy in copies[1 + elem_count :]:
        copy.wait()
    total = got_ref[0].astype(F32)
    for k in range(1, got_ref.shape[0]):
        total = total + got_ref[k].astype(F32)
    sum_ref[...] = total

    lane = iota((HALF, LANES), 1)
    row = iota((HALF, LANES), 0)
    wide_row = iota((MROW, LANES), 0)
    wide_lane = iota((MROW, LANES), 1)
    top = wide_row < HALF
    held = (top & ((wide_lane <= wide_row) | (wide_lane >= HALF))) | (
        (~top) & (wide_lane >= wide_row)
    )
    for block in range(NC):
        dense = sum_ref[block * DENSE : (block + 1) * DENSE, :]
        upper = jnp.concatenate([dense, pltpu.roll(dense, MROW, 1)], axis=0)
        diag = sum_ref[NC * DENSE + block : NC * DENSE + block + 1, :]
        diag = pltpu.roll(diag + pltpu.roll(diag, MROW, 1), HALF, 1)
        lower = jnp.where(lane == row + HALF, diag, pltpu.roll(upper, HALF, 1))
        given = jnp.concatenate([upper, lower], axis=0)
        turned = jnp.concatenate([given, given], axis=0).T[:MROW]
        full_ref[block * MROW : (block + 1) * MROW, :] = jnp.where(held, given, turned)
    low = iota((NC, LANES), 1) < MROW
    for chunk in range(HALF):
        left = full_ref[pl.ds(2 * chunk, NC, stride=MROW), :]
        right = full_ref[pl.ds(2 * chunk + 1, NC, stride=MROW), :]
        out_ref[:, chunk * LANES : (chunk + 1) * LANES] = jnp.where(
            low, left, pltpu.roll(right, MROW, 1)
        )
    for copy in copies[: 1 + elem_count]:
        copy.wait()
    own = residual_ref.shape[0]
    mine = lax.axis_index("elem")
    slot = (iota((own, SHARE_ROWS), 0) + mine * own).astype(F32)
    left = own_ref[...].astype(F32)
    for k in range(elem_count):
        names = shares_ref[k, NAMED:, :].astype(F32)
        named = (names[0:1] * SLOT_BASE + names[1:2])[:, :SHARE_ROWS]
        left = left - dot((slot == named).astype(BF16), shares_ref[k])
    residual_ref[...] = left


ANY = pl.BlockSpec(memory_space=pl.ANY)
VMEM = pl.BlockSpec(memory_space=pltpu.VMEM)


def params(limit):
    return pltpu.CompilerParams(vmem_limit_bytes=limit)


def around(block, axis):
    count = lax.axis_size(axis)
    return [block] + [
        lax.ppermute(block, axis, [(i, i ^ k) for i in range(count)]) for k in range(1, count)
    ]


def exchange(blocks, face_count):
    if len(blocks) == 1:
        block = blocks[0]
        shaped = block.reshape(face_count, -1, LANES)
        return [lax.all_to_all(shaped, "face", 0, 0, tiled=True)]
    return [blocks[0]] + [
        lax.ppermute(blocks[k], "face", [(i, i ^ k) for i in range(face_count)])
        for k in range(1, face_count)
    ]


def shards(
    trace_old,
    new_owner,
    mortar_tiles,
    mortar_owner,
    mortar_coarse,
    interior_rhs,
    local_inverse,
    coupling,
    connectivity,
):
    face_count = lax.axis_size("face")
    elem_count = lax.axis_size("elem")
    row_count = trace_old.shape[0]
    tile_count = mortar_tiles.shape[0]
    elements, modes = interior_rhs.shape
    trace = FACES_PER_ELEM * FACE_COEFFS
    capacity = max(2, 2 * row_count // face_count)
    own = face_count * capacity

    slots = own * elem_count
    paired = face_count <= MOST_PAIRED
    parts = face_count if paired else 1

    owners = around(new_owner.reshape(1, row_count), "elem")
    traces = around(trace_old, "elem")
    blocks = face_count * NC
    sums_shape = (blocks * DENSE, LANES)
    half_grams = pl.pallas_call(
        functools.partial(gram_kernel, face_count, paired),
        out_shape=[jax.ShapeDtypeStruct((blocks * (DENSE + 1) // parts, LANES), BF16)] * parts,
        in_specs=[ANY, ANY, ANY],
        out_specs=[VMEM] * parts,
        scratch_shapes=[
            pltpu.SMEM((tile_count,), I32),
            pltpu.SMEM((tile_count,), I32),
            pltpu.VMEM(mortar_tiles.shape, BF16),
            pltpu.VMEM((tile_count * PITCH, LANES), F32),
            pltpu.VMEM(sums_shape, F32),
            pltpu.VMEM(sums_shape, F32),
            pltpu.VMEM((blocks, LANES), F32),
            pltpu.VMEM((blocks, LANES), F32),
            pltpu.SemaphoreType.DMA((3,)),
        ],
        compiler_params=params(BIG),
        cost_estimate=pl.CostEstimate(
            flops=4 * tile_count * MROW * MROW * LANES, bytes_accessed=12 << 20, transcendentals=0
        ),
        name="gram",
    )(mortar_owner.reshape(tile_count), mortar_coarse, mortar_tiles)

    placed = pl.pallas_call(
        functools.partial(place_kernel, elem_count, face_count, capacity, paired),
        out_shape=[jax.ShapeDtypeStruct((slots // parts, FACE_COEFFS), BF16)] * parts,
        in_specs=[ANY] * (2 * elem_count),
        out_specs=[VMEM] * parts,
        scratch_shapes=[
            pltpu.VMEM((elem_count, 1, row_count), I32),
            pltpu.VMEM((elem_count, *trace_old.shape), BF16),
            pltpu.SemaphoreType.DMA((2 * elem_count,)),
        ],
        compiler_params=params(BIG),
        name="place",
    )(*owners, *traces)
    tables = exchange(placed, face_count)
    half_grams, _ = lax.optimization_barrier((half_grams, placed))
    got = exchange(half_grams, face_count)

    schur_blocks, shares, own_rows = pl.pallas_call(
        functools.partial(main_kernel, elem_count, face_count, paired),
        out_shape=(
            jax.ShapeDtypeStruct((elements, trace, trace), BF16),
            jax.ShapeDtypeStruct((SHARE_ROWS, LANES), BF16),
            jax.ShapeDtypeStruct((own, FACE_COEFFS), BF16),
        ),
        in_specs=[ANY] * (4 + parts),
        out_specs=(ANY, VMEM, VMEM),
        scratch_shapes=[
            pltpu.SMEM((FACES_PER_ELEM, elements), I32),
            pltpu.VMEM((elements, modes), BF16),
            pltpu.VMEM((slots, FACE_COEFFS), BF16),
            pltpu.VMEM((elements, modes, modes), BF16),
            pltpu.VMEM((elements, modes, trace), BF16),
            pltpu.VMEM((elements, trace, trace), BF16),
            pltpu.VMEM((LANES, modes), F32),
            pltpu.VMEM((modes, LANES), BF16),
            pltpu.VMEM((PER_FACE, trace + LANES), F32),
            pltpu.VMEM((trace, LANES), F32),
            pltpu.VMEM((trace, modes), BF16),
            pltpu.VMEM((trace, modes), BF16),
            pltpu.VMEM((trace, modes), BF16),
            pltpu.VMEM((trace, modes), BF16),
            pltpu.SemaphoreType.DMA((2 + parts,)),
            pltpu.SemaphoreType.DMA((2, elements)),
            pltpu.SemaphoreType.DMA((elements,)),
        ],
        compiler_params=params(BIG),
        cost_estimate=pl.CostEstimate(
            flops=2 * elements * modes * trace * (modes + trace),
            bytes_accessed=2 * elements * (modes * (modes + trace) + trace * trace),
            transcendentals=0,
        ),
        name="condense",
    )(
        connectivity.T,
        interior_rhs,
        local_inverse,
        coupling,
        *(table.reshape(slots // parts, FACE_COEFFS) for table in tables),
    )

    got_each = (face_count // parts, OWNER_ROWS, LANES)
    slot_residual, coarse_blocks = pl.pallas_call(
        functools.partial(finish_kernel, elem_count, face_count),
        out_shape=(
            jax.ShapeDtypeStruct((own, FACE_COEFFS), F32),
            jax.ShapeDtypeStruct((NC, MROW * MROW), F32),
        ),
        in_specs=[ANY] * (1 + elem_count + parts),
        out_specs=(VMEM, VMEM),
        scratch_shapes=[
            pltpu.VMEM((face_count, OWNER_ROWS, LANES), BF16),
            pltpu.VMEM((own, FACE_COEFFS), BF16),
            pltpu.VMEM((elem_count, SHARE_ROWS, LANES), BF16),
            pltpu.VMEM((OWNER_ROWS, LANES), F32),
            pltpu.VMEM((NC * MROW, LANES), F32),
            pltpu.SemaphoreType.DMA((1 + elem_count + parts,)),
        ],
        compiler_params=params(BIG),
        name="finish",
    )(own_rows, *around(shares, "elem"), *(part.reshape(got_each) for part in got))
    return schur_blocks, slot_residual, coarse_blocks


def solution(mesh):
    return jax.shard_map(
        shards,
        mesh=mesh,
        in_specs=(
            P(("face", "elem"), None),
            P(("face", "elem"), None),
            P(("face", "elem"), None),
            P(("face", "elem"), None),
            P(("face", "elem")),
            P(("face", "elem"), None),
            P(("face", "elem"), None, None),
            P(("face", "elem"), None, None),
            P(("face", "elem"), None),
        ),
        out_specs=(
            P(("face", "elem"), None, None),
            P(("face", "elem"), None),
            P(("face", "elem"), None),
        ),
        check_vma=False,
    )
```

```python
import functools

import jax
import jax.numpy as jnp
from jax import lax
from jax.experimental import pallas as pl
from jax.experimental.pallas import tpu as pltpu
from jax.sharding import PartitionSpec as P

FACE_COEFFS = 128
FACES_PER_ELEM = 3
MROW = 64
MCOL = 96
NC = 16
HALF = MROW // 2
LANES = 128
DENSE = HALF * MROW // LANES
OWNER_ROWS = NC * (DENSE + 1)
PER_FACE = 16
NAMED = FACES_PER_ELEM * PER_FACE
SHARE_ROWS = NAMED + 16
SLOT_BASE = 16
CHUNK = 16
EARLY = 5
BIG = 62 << 20
PITCH = MROW + 8

BF16 = jnp.bfloat16
F32 = jnp.float32
I32 = jnp.int32

NT = (((1,), (1,)), ((), ()))
TN = (((0,), (0,)), ((), ()))


def iota(shape, dim):
    return lax.broadcasted_iota(I32, shape, dim)


def dot(left, right, dims=(((1,), (0,)), ((), ()))):
    return lax.dot_general(left, right, dims, preferred_element_type=F32)


def place_kernel(elem_count, face_count, capacity, owner_hbm, trace_hbm, placed_ref, *refs):
    owner_ref, trace_ref, sems = refs
    copies = [
        pltpu.make_async_copy(owner_hbm, owner_ref, sems.at[0]),
        pltpu.make_async_copy(trace_hbm, trace_ref, sems.at[1]),
    ]
    for copy in copies:
        copy.start()
    slots, rows = placed_ref.shape[0], trace_ref.shape[0]
    earlier = (iota((rows, rows), 0) < iota((rows, rows), 1)).astype(BF16)
    slot = iota((slots, rows), 0)
    wanted = lax.div(slot, elem_count * capacity) * capacity + lax.rem(slot, capacity)
    for copy in copies:
        copy.wait()
    owners = owner_ref[...]
    hot = (iota((face_count, rows), 0) == owners).astype(F32)
    rank = jnp.sum(hot * dot(hot.astype(BF16), earlier), axis=0, keepdims=True).astype(I32)
    place = (wanted == owners * capacity + rank).astype(BF16)
    placed_ref[...] = dot(place, trace_ref[...]).astype(BF16)


class Element:
    def __init__(self, hbm, vmem, sems, turned, product, rhs_turned_ref):
        self.inverse_hbm, self.coupling_hbm = hbm
        self.inverse_ref, self.coupling_ref = vmem
        self.sems, self.turned, self.product = sems, turned, product
        self.rhs_turned_ref = rhs_turned_ref

    def coupling_copy(self, e, k):
        return pltpu.make_async_copy(
            self.coupling_hbm.at[e], self.coupling_ref.at[k], self.sems.at[0, k]
        )

    def inverse_copy(self, e, k):
        return pltpu.make_async_copy(
            self.inverse_hbm.at[e], self.inverse_ref.at[k], self.sems.at[1, k]
        )

    def turn(self, k):
        self.turned[k % 2][...] = self.coupling_ref[k].T

    def first(self, k):
        product = dot(self.turned[k % 2][...], self.inverse_ref[k])
        self.product[k % 2][...] = product.astype(BF16)

    def second(self, k):
        wide = jnp.concatenate([self.coupling_ref[k], self.rhs_turned_ref[...]], axis=1)
        return dot(self.product[k % 2][...], wide)


def turn_rhs(rhs_ref, wide_ref, rhs_turned_ref):
    wide_ref[...] = jnp.zeros_like(wide_ref)
    wide_ref[0 : rhs_ref.shape[0], :] = rhs_ref[...].astype(F32)
    rhs_turned_ref[...] = wide_ref[...].T.astype(BF16)


def gram_kernel(
    face_count,
    owner_hbm,
    coarse_hbm,
    tiles_hbm,
    rhs_hbm,
    inverse_hbm,
    coupling_hbm,
    out_ref,
    schur_hbm,
    solved_ref,
    owner_ref,
    coarse_ref,
    tiles_ref,
    rows_ref,
    acc_a_ref,
    acc_b_ref,
    diag_a_ref,
    diag_b_ref,
    rhs_ref,
    wide_ref,
    rhs_turned_ref,
    inverse_ref,
    coupling_ref,
    schur_ref,
    turned_a_ref,
    turned_b_ref,
    product_a_ref,
    product_b_ref,
    sems,
    block_sems,
    schur_sems,
):
    accs, diags = (acc_a_ref, acc_b_ref), (diag_a_ref, diag_b_ref)
    tiles = tiles_ref.shape[0]
    early, trace = schur_ref.shape[:2]
    element = Element(
        (inverse_hbm, coupling_hbm),
        (inverse_ref, coupling_ref),
        block_sems,
        (turned_a_ref, turned_b_ref),
        (product_a_ref, product_b_ref),
        rhs_turned_ref,
    )
    copies = [
        pltpu.make_async_copy(owner_hbm, owner_ref, sems.at[0]),
        pltpu.make_async_copy(coarse_hbm, coarse_ref, sems.at[1]),
        pltpu.make_async_copy(rhs_hbm, rhs_ref, sems.at[2]),
        pltpu.make_async_copy(tiles_hbm, tiles_ref, sems.at[3]),
    ]
    for copy in copies:
        copy.start()
    for e in range(2):
        element.coupling_copy(e, e).start()
        element.inverse_copy(e, e).start()
    element.coupling_copy(2, 2).start()
    for ref in (*accs, *diags, solved_ref):
        ref[...] = jnp.zeros_like(ref)
    for copy in copies:
        copy.wait()
    turn_rhs(rhs_ref, wide_ref, rhs_turned_ref)

    def leave(e):
        return pltpu.make_async_copy(schur_ref.at[e], schur_hbm.at[e], schur_sems.at[e])

    def solve(step):
        if step + 1 < early:
            element.turn(step + 1)
        if step < early:
            element.first(step)
        if 0 <= step - 1 < early:
            e = step - 1
            condensed = element.second(e)
            schur_ref[e] = (-condensed[:, :trace]).astype(BF16)
            solved_ref[...] = jnp.where(
                iota((trace, LANES), 1) == e, condensed[:, trace:], solved_ref[...]
            )

    lane = iota((CHUNK, LANES), 1)
    inside = lane < MCOL
    row = iota((HALF, LANES), 0)
    column = lax.rem(iota((HALF, LANES), 1), MROW)
    swapped = (column > row) & (column < HALF)
    diagonal = column == row
    low = iota((DENSE, LANES), 1) < MROW
    low_wide = iota((MROW, LANES), 1) < MROW
    low_row = iota((1, LANES), 1) < MROW

    element.coupling_copy(0, 0).wait()
    element.turn(0)
    for chunk in range(tiles // CHUNK):
        if chunk + 2 < early:
            element.inverse_copy(chunk + 2, chunk + 2).start()
        if chunk + 3 < early:
            element.coupling_copy(chunk + 3, chunk + 3).start()
        if chunk + 1 < early:
            element.coupling_copy(chunk + 1, chunk + 1).wait()
        if chunk < early:
            element.inverse_copy(chunk, chunk).wait()
        if 0 <= chunk - 2 < early:
            leave(chunk - 2).start()
        solve(chunk)
        first_tile = chunk * CHUNK
        for group in range(MROW // 4):
            base = group * 3 * LANES
            one, two, three = (
                tiles_ref[
                    first_tile : first_tile + CHUNK, base + k * LANES : base + (k + 1) * LANES
                ].astype(F32)
                for k in range(3)
            )
            rolled = (
                one,
                pltpu.roll(jnp.where(lane < 64, two, one), 32, 1),
                pltpu.roll(jnp.where(lane < 32, three, two), 64, 1),
                pltpu.roll(three, 96, 1),
            )
            for k in range(4):
                rows_ref[pl.ds(first_tile * PITCH + 4 * group + k, CHUNK, stride=PITCH), :] = (
                    jnp.where(inside, rolled[k], 0.0)
                )
        for tile in range(first_tile, first_tile + CHUNK, 2):
            both = jnp.concatenate(
                [
                    rows_ref[t * PITCH : t * PITCH + MROW, :].astype(BF16)
                    for t in (tile, tile + 1)
                ],
                axis=0,
            )
            gram = dot(both, both, NT)
            side = jnp.where(low_wide, gram[:MROW], gram[MROW:])
            lower = pltpu.roll(side[HALF:], LANES - HALF, 1)
            packed = jnp.where(swapped, lower, side[:HALF])
            diag = jnp.sum(jnp.where(diagonal, lower, 0.0), axis=0, keepdims=True)
            turned = pltpu.roll(packed, MROW, 1)
            dense = (
                jnp.where(low, packed[:DENSE], turned[DENSE:]),
                jnp.where(low, turned[:DENSE], packed[DENSE:]),
            )
            own = (jnp.where(low_row, diag, 0.0), jnp.where(low_row, 0.0, diag))
            for k in range(2):
                block = owner_ref[tile + k] * NC + coarse_ref[tile + k]
                here = pl.ds(pl.multiple_of(block * DENSE, DENSE), DENSE)
                accs[k][here, :] += dense[k]
                diags[k][pl.ds(block, 1), :] += own[k]
    size = NC * DENSE
    for owner in range(face_count):
        start = owner * OWNER_ROWS
        here = slice(owner * size, (owner + 1) * size)
        out_ref[start : start + size, :] = (accs[0][here, :] + accs[1][here, :]).astype(BF16)
        here = slice(owner * NC, (owner + 1) * NC)
        out_ref[start + size : start + size + NC, :] = (
            diags[0][here, :] + diags[1][here, :]
        ).astype(BF16)
    for e in range(max(tiles // CHUNK - 2, 0), early):
        leave(e).start()
    for e in range(early):
        leave(e).wait()


def main_kernel(
    elem_count,
    face_count,
    table_hbm,
    conn_hbm,
    rhs_hbm,
    inverse_hbm,
    coupling_hbm,
    schur_in_hbm,
    solved_hbm,
    schur_hbm,
    share_ref,
    own_ref,
    conn_ref,
    rhs_ref,
    table_ref,
    inverse_ref,
    coupling_ref,
    schur_ref,
    wide_ref,
    rhs_turned_ref,
    vector_ref,
    sum_ref,
    turned_a_ref,
    turned_b_ref,
    product_a_ref,
    product_b_ref,
    sems,
    block_sems,
    early_sems,
    schur_sems,
):
    elements = rhs_ref.shape[0]
    late = inverse_ref.shape[0]
    early = elements - late
    trace = FACES_PER_ELEM * FACE_COEFFS
    slots = table_ref.shape[0]
    own = own_ref.shape[0]
    capacity = own // face_count
    my_elem = lax.axis_index("elem")
    element = Element(
        (inverse_hbm, coupling_hbm),
        (inverse_ref, coupling_ref),
        block_sems,
        (turned_a_ref, turned_b_ref),
        (product_a_ref, product_b_ref),
        rhs_turned_ref,
    )
    copies = [
        pltpu.make_async_copy(rhs_hbm, rhs_ref, sems.at[0]),
        pltpu.make_async_copy(conn_hbm, conn_ref, sems.at[1]),
        pltpu.make_async_copy(table_hbm, table_ref, sems.at[2]),
        pltpu.make_async_copy(solved_hbm, sum_ref, sems.at[3]),
    ]

    def known(e):
        return pltpu.make_async_copy(schur_in_hbm.at[e], schur_ref.at[e], early_sems.at[e])

    def leave(k):
        e = early + k
        return pltpu.make_async_copy(schur_ref.at[e], schur_hbm.at[e], schur_sems.at[k])

    element.coupling_copy(early, 0).start()
    for copy in copies:
        copy.start()
    element.inverse_copy(early, 0).start()
    for k in range(1, late):
        element.coupling_copy(early + k, k).start()
        element.inverse_copy(early + k, k).start()
    for e in range(early):
        known(e).start()

    row = iota((PER_FACE, LANES), 0)
    lane = iota((PER_FACE, LANES), 1)
    first_lane = iota((1, LANES), 1)
    wide_lane = iota((trace, LANES), 1)
    for copy in copies:
        copy.wait()
    turn_rhs(rhs_ref, wide_ref, rhs_turned_ref)

    def position(elem, inner):
        face = lax.div(inner, capacity)
        return (face * elem_count + elem) * capacity + lax.rem(inner, capacity)

    high = jnp.full((1, LANES), -1, I32)
    rest = jnp.zeros((1, LANES), I32)
    for a in range(FACES_PER_ELEM):
        positions = jnp.full((PER_FACE, LANES), -1, I32)
        for e in range(elements):
            slot = conn_ref[a, e]
            here = position(lax.div(slot, own), lax.rem(slot, own))
            positions = jnp.where(row == e, here, positions)
            high = jnp.where(first_lane == a * PER_FACE + e, lax.div(slot, SLOT_BASE), high)
            rest = jnp.where(first_lane == a * PER_FACE + e, lax.rem(slot, SLOT_BASE), rest)
        hot = jnp.concatenate([positions == lane + k for k in range(0, slots, LANES)], axis=1)
        vector_ref[:, a * LANES : (a + 1) * LANES] = dot(hot.astype(BF16), table_ref[...])
    names = jnp.where(row == 0, high, jnp.where(row == 1, rest, 0))
    share_ref[NAMED:, :] = names.astype(F32).astype(BF16)
    place = position(my_elem, iota((own, slots), 0))
    pick = (iota((own, slots), 1) == place).astype(BF16)
    own_ref[...] = dot(pick, table_ref[...]).astype(BF16)

    def add(e, schur):
        total = schur * vector_ref[e : e + 1, :]
        total = sum(total[:, a * LANES : (a + 1) * LANES] for a in range(FACES_PER_ELEM))
        sums = jnp.sum(total, axis=1, keepdims=True)
        sum_ref[...] = sum_ref[...] + jnp.where(wide_lane == e, sums, 0.0)

    element.coupling_copy(early, 0).wait()
    element.turn(0)
    for step in range(late + 1):
        if step + 1 < late:
            element.coupling_copy(early + step + 1, step + 1).wait()
            element.turn(step + 1)
        if step < late:
            element.inverse_copy(early + step, step).wait()
            element.first(step)
        for e in range(step * early // (late + 1), (step + 1) * early // (late + 1)):
            known(e).wait()
            add(e, schur_ref[e].astype(F32))
        if step >= 1:
            k = step - 1
            e = early + k
            condensed = element.second(k)
            schur = -condensed[:, :trace]
            schur_ref[e] = schur.astype(BF16)
            leave(k).start()
            sum_ref[...] = jnp.where(wide_lane == e, condensed[:, trace:], sum_ref[...])
            add(e, schur)

    for a in range(FACES_PER_ELEM):
        shares = sum_ref[a * LANES : (a + 1) * LANES, :].T
        share_ref[a * PER_FACE : (a + 1) * PER_FACE, :] = shares[:PER_FACE].astype(BF16)
    for k in range(late):
        leave(k).wait()


def residual_kernel(elem_count, *refs):
    ins, (residual_ref, own_ref, shares_ref, sems) = refs[:-4], refs[-4:]
    places = [own_ref] + [shares_ref.at[k] for k in range(elem_count)]
    copies = [pltpu.make_async_copy(ins[k], places[k], sems.at[k]) for k in range(len(ins))]
    for copy in copies:
        copy.start()
    own = residual_ref.shape[0]
    mine = lax.axis_index("elem")
    slot = (iota((own, SHARE_ROWS), 0) + mine * own).astype(F32)
    for copy in copies:
        copy.wait()
    left = own_ref[...].astype(F32)
    for k in range(elem_count):
        names = shares_ref[k, NAMED:, :].astype(F32)
        named = (names[0:1] * SLOT_BASE + names[1:2])[:, :SHARE_ROWS]
        left = left - dot((slot == named).astype(BF16), shares_ref[k])
    residual_ref[...] = left


def coarse_kernel(got_hbm, out_ref, got_ref, sum_ref, full_ref, sem):
    copy = pltpu.make_async_copy(got_hbm, got_ref, sem)
    copy.start()
    copy.wait()
    total = got_ref[0].astype(F32)
    for k in range(1, got_ref.shape[0]):
        total = total + got_ref[k].astype(F32)
    sum_ref[...] = total

    lane = iota((HALF, LANES), 1)
    row = iota((HALF, LANES), 0)
    wide_row = iota((MROW, LANES), 0)
    wide_lane = iota((MROW, LANES), 1)
    top = wide_row < HALF
    held = (top & ((wide_lane <= wide_row) | (wide_lane >= HALF))) | (
        (~top) & (wide_lane >= wide_row)
    )
    for block in range(NC):
        dense = sum_ref[block * DENSE : (block + 1) * DENSE, :]
        upper = jnp.concatenate([dense, pltpu.roll(dense, MROW, 1)], axis=0)
        diag = sum_ref[NC * DENSE + block : NC * DENSE + block + 1, :]
        diag = pltpu.roll(diag + pltpu.roll(diag, MROW, 1), HALF, 1)
        lower = jnp.where(lane == row + HALF, diag, pltpu.roll(upper, HALF, 1))
        given = jnp.concatenate([upper, lower], axis=0)
        turned = jnp.concatenate([given, given], axis=0).T[:MROW]
        full_ref[block * MROW : (block + 1) * MROW, :] = jnp.where(held, given, turned)
    low = iota((NC, LANES), 1) < MROW
    for chunk in range(HALF):
        left = full_ref[pl.ds(2 * chunk, NC, stride=MROW), :]
        right = full_ref[pl.ds(2 * chunk + 1, NC, stride=MROW), :]
        out_ref[:, chunk * LANES : (chunk + 1) * LANES] = jnp.where(
            low, left, pltpu.roll(right, MROW, 1)
        )


ANY = pl.BlockSpec(memory_space=pl.ANY)
VMEM = pl.BlockSpec(memory_space=pltpu.VMEM)


def params(limit):
    return pltpu.CompilerParams(vmem_limit_bytes=limit)


def around(block, axis):
    count = lax.axis_size(axis)
    return [block] + [
        lax.ppermute(block, axis, [(i, i ^ k) for i in range(count)]) for k in range(1, count)
    ]


def shards(
    trace_old,
    new_owner,
    mortar_tiles,
    mortar_owner,
    mortar_coarse,
    interior_rhs,
    local_inverse,
    coupling,
    connectivity,
):
    face_count = lax.axis_size("face")
    elem_count = lax.axis_size("elem")
    row_count = trace_old.shape[0]
    tile_count = mortar_tiles.shape[0]
    elements, modes = interior_rhs.shape
    trace = FACES_PER_ELEM * FACE_COEFFS
    capacity = max(2, 2 * row_count // face_count)
    own = face_count * capacity

    slots = own * elem_count
    devices = face_count * elem_count
    early = min(EARLY, elements - 2)
    late = elements - early

    placed = pl.pallas_call(
        functools.partial(place_kernel, elem_count, face_count, capacity),
        out_shape=jax.ShapeDtypeStruct((slots, FACE_COEFFS), BF16),
        in_specs=[ANY, ANY],
        out_specs=VMEM,
        scratch_shapes=[
            pltpu.VMEM((1, row_count), I32),
            pltpu.VMEM(trace_old.shape, BF16),
            pltpu.SemaphoreType.DMA((2,)),
        ],
        compiler_params=params(BIG),
        name="place",
    )(new_owner.reshape(1, row_count), trace_old)
    table = lax.all_to_all(
        placed.reshape(devices, capacity, FACE_COEFFS), ("face", "elem"), 0, 0, tiled=True
    ).reshape(slots, FACE_COEFFS)

    stages = [
        pltpu.VMEM((trace, modes), BF16),
        pltpu.VMEM((trace, modes), BF16),
        pltpu.VMEM((trace, modes), BF16),
        pltpu.VMEM((trace, modes), BF16),
    ]
    blocks = face_count * NC
    sums_shape = (blocks * DENSE, LANES)
    schur_shape = jax.ShapeDtypeStruct((elements, trace, trace), BF16)
    half_grams, schur_early, solved = pl.pallas_call(
        functools.partial(gram_kernel, face_count),
        out_shape=(
            jax.ShapeDtypeStruct((blocks * (DENSE + 1), LANES), BF16),
            schur_shape,
            jax.ShapeDtypeStruct((trace, LANES), F32),
        ),
        in_specs=[ANY] * 6,
        out_specs=(VMEM, ANY, VMEM),
        scratch_shapes=[
            pltpu.SMEM((tile_count,), I32),
            pltpu.SMEM((tile_count,), I32),
            pltpu.VMEM(mortar_tiles.shape, BF16),
            pltpu.VMEM((tile_count * PITCH, LANES), F32),
            pltpu.VMEM(sums_shape, F32),
            pltpu.VMEM(sums_shape, F32),
            pltpu.VMEM((blocks, LANES), F32),
            pltpu.VMEM((blocks, LANES), F32),
            pltpu.VMEM((elements, modes), BF16),
            pltpu.VMEM((LANES, modes), F32),
            pltpu.VMEM((modes, LANES), BF16),
            pltpu.VMEM((early, modes, modes), BF16),
            pltpu.VMEM((early, modes, trace), BF16),
            pltpu.VMEM((early, trace, trace), BF16),
            *stages,
            pltpu.SemaphoreType.DMA((4,)),
            pltpu.SemaphoreType.DMA((2, early)),
            pltpu.SemaphoreType.DMA((early,)),
        ],
        compiler_params=params(BIG),
        cost_estimate=pl.CostEstimate(
            flops=2 * early * modes * trace * (modes + trace),
            bytes_accessed=16 << 20,
            transcendentals=0,
        ),
        name="gram",
    )(
        mortar_owner.reshape(tile_count),
        mortar_coarse,
        mortar_tiles,
        interior_rhs,
        local_inverse,
        coupling,
    )
    got = lax.all_to_all(
        half_grams.reshape(face_count, OWNER_ROWS, LANES), "face", 0, 0, tiled=True
    )

    schur_blocks, shares, own_rows = pl.pallas_call(
        functools.partial(main_kernel, elem_count, face_count),
        out_shape=(
            schur_shape,
            jax.ShapeDtypeStruct((SHARE_ROWS, LANES), BF16),
            jax.ShapeDtypeStruct((own, FACE_COEFFS), BF16),
        ),
        in_specs=[ANY] * 7,
        out_specs=(ANY, VMEM, VMEM),
        input_output_aliases={5: 0},
        scratch_shapes=[
            pltpu.SMEM((FACES_PER_ELEM, elements), I32),
            pltpu.VMEM((elements, modes), BF16),
            pltpu.VMEM((slots, FACE_COEFFS), BF16),
            pltpu.VMEM((late, modes, modes), BF16),
            pltpu.VMEM((late, modes, trace), BF16),
            pltpu.VMEM((elements, trace, trace), BF16),
            pltpu.VMEM((LANES, modes), F32),
            pltpu.VMEM((modes, LANES), BF16),
            pltpu.VMEM((PER_FACE, trace), F32),
            pltpu.VMEM((trace, LANES), F32),
            *stages,
            pltpu.SemaphoreType.DMA((4,)),
            pltpu.SemaphoreType.DMA((2, late)),
            pltpu.SemaphoreType.DMA((early,)),
            pltpu.SemaphoreType.DMA((late,)),
        ],
        compiler_params=params(BIG),
        cost_estimate=pl.CostEstimate(
            flops=2 * late * modes * trace * (modes + trace),
            bytes_accessed=16 << 20,
            transcendentals=0,
        ),
        name="condense",
    )(
        table,
        connectivity.T,
        interior_rhs,
        local_inverse,
        coupling,
        schur_early,
        solved,
    )

    all_shares = around(shares, "elem")
    coarse_blocks = pl.pallas_call(
        coarse_kernel,
        out_shape=jax.ShapeDtypeStruct((NC, MROW * MROW), F32),
        in_specs=[ANY],
        out_specs=VMEM,
        scratch_shapes=[
            pltpu.VMEM((face_count, OWNER_ROWS, LANES), BF16),
            pltpu.VMEM((OWNER_ROWS, LANES), F32),
            pltpu.VMEM((NC * MROW, LANES), F32),
            pltpu.SemaphoreType.DMA,
        ],
        compiler_params=params(BIG),
        name="coarse",
    )(got)
    own_rows, coarse_blocks = lax.optimization_barrier((own_rows, coarse_blocks))

    slot_residual = pl.pallas_call(
        functools.partial(residual_kernel, elem_count),
        out_shape=jax.ShapeDtypeStruct((own, FACE_COEFFS), F32),
        in_specs=[ANY] * (1 + elem_count),
        out_specs=VMEM,
        scratch_shapes=[
            pltpu.VMEM((own, FACE_COEFFS), BF16),
            pltpu.VMEM((elem_count, SHARE_ROWS, LANES), BF16),
            pltpu.SemaphoreType.DMA((1 + elem_count,)),
        ],
        compiler_params=params(BIG),
        name="residual",
    )(own_rows, *all_shares)
    return schur_blocks, slot_residual, coarse_blocks


def solution(mesh):
    return jax.shard_map(
        shards,
        mesh=mesh,
        in_specs=(
            P(("face", "elem"), None),
            P(("face", "elem"), None),
            P(("face", "elem"), None),
            P(("face", "elem"), None),
            P(("face", "elem")),
            P(("face", "elem"), None),
            P(("face", "elem"), None, None),
            P(("face", "elem"), None, None),
            P(("face", "elem"), None),
        ),
        out_specs=(
            P(("face", "elem"), None, None),
            P(("face", "elem"), None),
            P(("face", "elem"), None),
        ),
        check_vma=False,
    )
```

```python
import functools

import jax
import jax.numpy as jnp
from jax import lax
from jax.experimental import pallas as pl
from jax.experimental.pallas import tpu as pltpu
from jax.sharding import PartitionSpec as P

FACE_COEFFS = 128
FACES_PER_ELEM = 3
MROW = 64
MCOL = 96
NC = 16
HALF = MROW // 2
LANES = 128
DENSE = HALF * MROW // LANES
OWNER_ROWS = NC * (DENSE + 1)
PER_FACE = 16
NAMED = FACES_PER_ELEM * PER_FACE
SHARE_ROWS = NAMED + 16
SLOT_BASE = 16
CHUNK = 16
BIG = 62 << 20
SMALL = 12 << 20
PITCH = MROW + 8

BF16 = jnp.bfloat16
F32 = jnp.float32
I32 = jnp.int32

NT = (((1,), (1,)), ((), ()))
TN = (((0,), (0,)), ((), ()))


def iota(shape, dim):
    return lax.broadcasted_iota(I32, shape, dim)


def dot(left, right, dims=(((1,), (0,)), ((), ()))):
    return lax.dot_general(left, right, dims, preferred_element_type=F32)


def divided(value, by):
    shift = by.bit_length() - 1
    assert by == 1 << shift
    return value >> shift, value & (by - 1)


def place_kernel(elem_count, face_count, capacity, owner_hbm, trace_hbm, placed_ref, *refs):
    owner_ref, trace_ref, sems = refs
    copies = [
        pltpu.make_async_copy(owner_hbm, owner_ref, sems.at[0]),
        pltpu.make_async_copy(trace_hbm, trace_ref, sems.at[1]),
    ]
    for copy in copies:
        copy.start()
    slots, rows = placed_ref.shape[0], trace_ref.shape[0]
    earlier = (iota((rows, rows), 0) < iota((rows, rows), 1)).astype(BF16)
    slot = iota((slots, rows), 0)
    wanted = divided(slot, elem_count * capacity)[0] * capacity + divided(slot, capacity)[1]
    for copy in copies:
        copy.wait()
    owners = owner_ref[...]
    hot = (iota((face_count, rows), 0) == owners).astype(F32)
    rank = jnp.sum(hot * dot(hot.astype(BF16), earlier), axis=0, keepdims=True).astype(I32)
    place = (wanted == owners * capacity + rank).astype(BF16)
    placed_ref[...] = dot(place, trace_ref[...]).astype(BF16)


def turn_rhs(rhs_ref, wide_ref, rhs_turned_ref):
    wide_ref[...] = jnp.zeros_like(wide_ref)
    wide_ref[0 : rhs_ref.shape[0], :] = rhs_ref[...].astype(F32)
    rhs_turned_ref[...] = wide_ref[...].T.astype(BF16)


def gram_kernel(
    face_count,
    owner_hbm,
    coarse_hbm,
    tiles_hbm,
    out_ref,
    owner_ref,
    coarse_ref,
    tiles_ref,
    rows_ref,
    acc_a_ref,
    acc_b_ref,
    diag_a_ref,
    diag_b_ref,
    sems,
):
    accs, diags = (acc_a_ref, acc_b_ref), (diag_a_ref, diag_b_ref)
    tiles = tiles_ref.shape[0]
    copies = [
        pltpu.make_async_copy(owner_hbm, owner_ref, sems.at[0]),
        pltpu.make_async_copy(coarse_hbm, coarse_ref, sems.at[1]),
    ]
    chunks = []
    for chunk in range(tiles // CHUNK):
        here = pl.ds(chunk * CHUNK, CHUNK)
        chunks.append(
            pltpu.make_async_copy(tiles_hbm.at[here], tiles_ref.at[here], sems.at[2 + chunk])
        )
    for copy in copies + chunks:
        copy.start()
    for ref in (*accs, *diags):
        ref[...] = jnp.zeros_like(ref)
    for copy in copies:
        copy.wait()

    lane = iota((CHUNK, LANES), 1)
    inside = lane < MCOL
    row = iota((HALF, LANES), 0)
    column = divided(iota((HALF, LANES), 1), MROW)[1]
    swapped = (column > row) & (column < HALF)
    diagonal = column == row
    low = iota((DENSE, LANES), 1) < MROW
    low_wide = iota((MROW, LANES), 1) < MROW
    low_row = iota((1, LANES), 1) < MROW

    for chunk in range(tiles // CHUNK):
        chunks[chunk].wait()
        first_tile = chunk * CHUNK
        for group in range(MROW // 4):
            base = group * 3 * LANES
            one, two, three = (
                tiles_ref[
                    first_tile : first_tile + CHUNK, base + k * LANES : base + (k + 1) * LANES
                ].astype(F32)
                for k in range(3)
            )
            rolled = (
                one,
                pltpu.roll(jnp.where(lane < 64, two, one), 32, 1),
                pltpu.roll(jnp.where(lane < 32, three, two), 64, 1),
                pltpu.roll(three, 96, 1),
            )
            for k in range(4):
                rows_ref[pl.ds(first_tile * PITCH + 4 * group + k, CHUNK, stride=PITCH), :] = (
                    jnp.where(inside, rolled[k], 0.0)
                )
        for tile in range(first_tile, first_tile + CHUNK, 2):
            both = jnp.concatenate(
                [
                    rows_ref[t * PITCH : t * PITCH + MROW, :].astype(BF16)
                    for t in (tile, tile + 1)
                ],
                axis=0,
            )
            gram = dot(both, both, NT)
            side = jnp.where(low_wide, gram[:MROW], gram[MROW:])
            lower = pltpu.roll(side[HALF:], LANES - HALF, 1)
            packed = jnp.where(swapped, lower, side[:HALF])
            diag = jnp.sum(jnp.where(diagonal, lower, 0.0), axis=0, keepdims=True)
            turned = pltpu.roll(packed, MROW, 1)
            dense = (
                jnp.where(low, packed[:DENSE], turned[DENSE:]),
                jnp.where(low, turned[:DENSE], packed[DENSE:]),
            )
            own = (jnp.where(low_row, diag, 0.0), jnp.where(low_row, 0.0, diag))
            for k in range(2):
                block = owner_ref[tile + k] * NC + coarse_ref[tile + k]
                here = pl.ds(pl.multiple_of(block * DENSE, DENSE), DENSE)
                accs[k][here, :] += dense[k]
                diags[k][pl.ds(block, 1), :] += own[k]
    size = NC * DENSE
    for owner in range(face_count):
        start = owner * OWNER_ROWS
        here = slice(owner * size, (owner + 1) * size)
        out_ref[start : start + size, :] = (accs[0][here, :] + accs[1][here, :]).astype(BF16)
        here = slice(owner * NC, (owner + 1) * NC)
        out_ref[start + size : start + size + NC, :] = (
            diags[0][here, :] + diags[1][here, :]
        ).astype(BF16)


def main_kernel(
    elem_count,
    face_count,
    table_hbm,
    conn_hbm,
    rhs_hbm,
    inverse_hbm,
    coupling_hbm,
    schur_hbm,
    share_ref,
    own_ref,
    conn_ref,
    rhs_ref,
    table_ref,
    inverse_ref,
    coupling_ref,
    schur_ref,
    wide_ref,
    rhs_turned_ref,
    vector_ref,
    sum_ref,
    turned_a_ref,
    turned_b_ref,
    product_a_ref,
    product_b_ref,
    small_sems,
    block_sems,
    schur_sems,
):
    elements = rhs_ref.shape[0]
    trace = FACES_PER_ELEM * FACE_COEFFS
    slots = table_ref.shape[0]
    own = own_ref.shape[0]
    capacity = own // face_count
    my_elem = lax.axis_index("elem")
    small = [
        pltpu.make_async_copy(rhs_hbm, rhs_ref, small_sems.at[0]),
        pltpu.make_async_copy(conn_hbm, conn_ref, small_sems.at[1]),
        pltpu.make_async_copy(table_hbm, table_ref, small_sems.at[2]),
    ]

    def coupling_copy(e):
        return pltpu.make_async_copy(coupling_hbm.at[e], coupling_ref.at[e], block_sems.at[0, e])

    def inverse_copy(e):
        return pltpu.make_async_copy(inverse_hbm.at[e], inverse_ref.at[e], block_sems.at[1, e])

    def leave(e):
        return pltpu.make_async_copy(schur_ref.at[e], schur_hbm.at[e], schur_sems.at[e])

    coupling_copy(0).start()
    for copy in small:
        copy.start()
    inverse_copy(0).start()
    coupling_copy(1).start()
    inverse_copy(1).start()
    coupling_copy(2).start()

    def turn(e, turned_ref):
        turned_ref[...] = coupling_ref[e].T

    def first(e, turned_ref, product_ref):
        product_ref[...] = dot(turned_ref[...], inverse_ref[e]).astype(BF16)

    def second(e, product_ref):
        wide = jnp.concatenate([coupling_ref[e], rhs_turned_ref[...]], axis=1)
        condensed = dot(product_ref[...], wide)
        schur_ref[e] = (-condensed[:, :trace]).astype(BF16)
        total = condensed * vector_ref[pl.ds(e, 1), :]
        total = sum(total[:, k * LANES : (k + 1) * LANES] for k in range(FACES_PER_ELEM + 1))
        sums = jnp.sum(total, axis=1, keepdims=True)
        sum_ref[...] = jnp.where(iota((trace, LANES), 1) == e, sums, sum_ref[...])

    turned = (turned_a_ref, turned_b_ref)
    product = (product_a_ref, product_b_ref)

    def advance(e, parity, turning=True, finishing=True):
        if turning:
            @pl.when(e + 2 < elements)
            def _():
                inverse_copy(e + 2).start()

            @pl.when(e + 3 < elements)
            def _():
                coupling_copy(e + 3).start()

            coupling_copy(e + 1).wait()
        inverse_copy(e).wait()
        if turning:
            turn(e + 1, turned[1 - parity])
        first(e, turned[parity], product[parity])
        if finishing:
            second(e - 1, product[1 - parity])
            leave(e - 1).start()

    coupling_copy(0).wait()
    turn(0, turned[0])
    for copy in small:
        copy.wait()
    sum_ref[...] = jnp.zeros_like(sum_ref)
    turn_rhs(rhs_ref, wide_ref, rhs_turned_ref)
    row = iota((PER_FACE, LANES), 0)
    lane = iota((PER_FACE, LANES), 1)

    def position(elem, inner):
        face, rank = divided(inner, capacity)
        return (face * elem_count + elem) * capacity + rank

    first_lane = iota((1, LANES), 1)
    high = jnp.full((1, LANES), -1, I32)
    rest = jnp.zeros((1, LANES), I32)
    for a in range(FACES_PER_ELEM):
        positions = jnp.full((PER_FACE, LANES), -1, I32)
        for e in range(elements):
            slot = conn_ref[a, e]
            positions = jnp.where(row == e, position(*divided(slot, own)), positions)
            here = first_lane == a * PER_FACE + e
            quotient, remainder = divided(slot, SLOT_BASE)
            high = jnp.where(here, quotient, high)
            rest = jnp.where(here, remainder, rest)
        hot = jnp.concatenate([positions == lane + k for k in range(0, slots, LANES)], axis=1)
        lam = dot(hot.astype(BF16), table_ref[...])
        vector_ref[:, a * LANES : (a + 1) * LANES] = -lam
    vector_ref[:, trace:] = (row == lane).astype(F32)
    names = jnp.where(row == 0, high, jnp.where(row == 1, rest, 0))
    share_ref[NAMED:, :] = names.astype(F32).astype(BF16)
    place = position(my_elem, iota((own, slots), 0))
    pick = (iota((own, slots), 1) == place).astype(BF16)
    own_ref[...] = dot(pick, table_ref[...]).astype(BF16)

    advance(0, 0, finishing=False)

    def two(index, carry):
        advance(2 * index + 1, 1)
        advance(2 * index + 2, 0)
        return carry

    pairs = (elements - 2) // 2
    lax.fori_loop(0, pairs, two, 0)
    for e in range(2 * pairs + 1, elements):
        advance(e, e % 2, turning=e + 1 < elements)
    second(elements - 1, product[(elements - 1) % 2])
    leave(elements - 1).start()

    for a in range(FACES_PER_ELEM):
        shares = sum_ref[a * LANES : (a + 1) * LANES, :].T
        share_ref[a * PER_FACE : (a + 1) * PER_FACE, :] = shares[:PER_FACE].astype(BF16)
    for e in range(elements):
        leave(e).wait()


def residual_kernel(elem_count, *refs):
    ins, (residual_ref, own_ref, shares_ref, sems) = refs[:-4], refs[-4:]
    places = [own_ref] + [shares_ref.at[k] for k in range(elem_count)]
    copies = [pltpu.make_async_copy(ins[k], places[k], sems.at[k]) for k in range(len(ins))]
    for copy in copies:
        copy.start()
    own = residual_ref.shape[0]
    mine = lax.axis_index("elem")
    slot = (iota((own, SHARE_ROWS), 0) + mine * own).astype(F32)
    for copy in copies:
        copy.wait()
    left = own_ref[...].astype(F32)
    for k in range(elem_count):
        names = shares_ref[k, NAMED:, :].astype(F32)
        named = (names[0:1] * SLOT_BASE + names[1:2])[:, :SHARE_ROWS]
        left = left - dot((slot == named).astype(BF16), shares_ref[k])
    residual_ref[...] = left


def coarse_kernel(got_ref, out_ref, sum_ref, full_ref):
    total = got_ref[0].astype(F32)
    for k in range(1, got_ref.shape[0]):
        total = total + got_ref[k].astype(F32)
    sum_ref[...] = total

    lane = iota((HALF, LANES), 1)
    row = iota((HALF, LANES), 0)
    wide_row = iota((MROW, LANES), 0)
    wide_lane = iota((MROW, LANES), 1)
    top = wide_row < HALF
    held = (top & ((wide_lane <= wide_row) | (wide_lane >= HALF))) | (
        (~top) & (wide_lane >= wide_row)
    )
    for block in range(NC):
        dense = sum_ref[block * DENSE : (block + 1) * DENSE, :]
        upper = jnp.concatenate([dense, pltpu.roll(dense, MROW, 1)], axis=0)
        diag = sum_ref[NC * DENSE + block : NC * DENSE + block + 1, :]
        diag = pltpu.roll(diag + pltpu.roll(diag, MROW, 1), HALF, 1)
        lower = jnp.where(lane == row + HALF, diag, pltpu.roll(upper, HALF, 1))
        given = jnp.concatenate([upper, lower], axis=0)
        turned = jnp.concatenate([given, given], axis=0).T[:MROW]
        full_ref[block * MROW : (block + 1) * MROW, :] = jnp.where(held, given, turned)
    low = iota((NC, LANES), 1) < MROW
    for chunk in range(HALF):
        left = full_ref[pl.ds(2 * chunk, NC, stride=MROW), :]
        right = full_ref[pl.ds(2 * chunk + 1, NC, stride=MROW), :]
        out_ref[:, chunk * LANES : (chunk + 1) * LANES] = jnp.where(
            low, left, pltpu.roll(right, MROW, 1)
        )


ANY = pl.BlockSpec(memory_space=pl.ANY)
VMEM = pl.BlockSpec(memory_space=pltpu.VMEM)


def params(limit):
    return pltpu.CompilerParams(vmem_limit_bytes=limit)


def around(block, axis):
    count = lax.axis_size(axis)
    return [block] + [
        lax.ppermute(block, axis, [(i, i ^ k) for i in range(count)]) for k in range(1, count)
    ]


def shards(
    trace_old,
    new_owner,
    mortar_tiles,
    mortar_owner,
    mortar_coarse,
    interior_rhs,
    local_inverse,
    coupling,
    connectivity,
):
    face_count = lax.axis_size("face")
    elem_count = lax.axis_size("elem")
    row_count = trace_old.shape[0]
    tile_count = mortar_tiles.shape[0]
    elements, modes = interior_rhs.shape
    trace = FACES_PER_ELEM * FACE_COEFFS
    capacity = max(2, 2 * row_count // face_count)
    own = face_count * capacity

    slots = own * elem_count
    devices = face_count * elem_count

    placed = pl.pallas_call(
        functools.partial(place_kernel, elem_count, face_count, capacity),
        out_shape=jax.ShapeDtypeStruct((slots, FACE_COEFFS), BF16),
        in_specs=[ANY, ANY],
        out_specs=VMEM,
        scratch_shapes=[
            pltpu.VMEM((1, row_count), I32),
            pltpu.VMEM(trace_old.shape, BF16),
            pltpu.SemaphoreType.DMA((2,)),
        ],
        compiler_params=params(BIG),
        name="place",
    )(new_owner.reshape(1, row_count), trace_old)
    table = lax.all_to_all(
        placed.reshape(devices, capacity, FACE_COEFFS), ("face", "elem"), 0, 0, tiled=True
    ).reshape(slots, FACE_COEFFS)

    blocks = face_count * NC
    sums_shape = (blocks * DENSE, LANES)
    half_grams = pl.pallas_call(
        functools.partial(gram_kernel, face_count),
        out_shape=jax.ShapeDtypeStruct((blocks * (DENSE + 1), LANES), BF16),
        in_specs=[ANY] * 3,
        out_specs=VMEM,
        scratch_shapes=[
            pltpu.SMEM((tile_count,), I32),
            pltpu.SMEM((tile_count,), I32),
            pltpu.VMEM(mortar_tiles.shape, BF16),
            pltpu.VMEM((tile_count * PITCH, LANES), F32),
            pltpu.VMEM(sums_shape, F32),
            pltpu.VMEM(sums_shape, F32),
            pltpu.VMEM((blocks, LANES), F32),
            pltpu.VMEM((blocks, LANES), F32),
            pltpu.SemaphoreType.DMA((2 + tile_count // CHUNK,)),
        ],
        compiler_params=params(BIG),
        cost_estimate=pl.CostEstimate(
            flops=4 * tile_count * MROW * MROW * LANES, bytes_accessed=12 << 20, transcendentals=0
        ),
        name="gram",
    )(mortar_owner.reshape(tile_count), mortar_coarse, mortar_tiles)
    got = lax.all_to_all(
        half_grams.reshape(face_count, OWNER_ROWS, LANES), "face", 0, 0, tiled=True
    )

    slots_named, _ = lax.optimization_barrier((connectivity.T, half_grams))
    schur_blocks, shares, own_rows = pl.pallas_call(
        functools.partial(main_kernel, elem_count, face_count),
        out_shape=(
            jax.ShapeDtypeStruct((elements, trace, trace), BF16),
            jax.ShapeDtypeStruct((SHARE_ROWS, LANES), BF16),
            jax.ShapeDtypeStruct((own, FACE_COEFFS), BF16),
        ),
        in_specs=[ANY] * 5,
        out_specs=(ANY, VMEM, VMEM),
        scratch_shapes=[
            pltpu.SMEM((FACES_PER_ELEM, elements), I32),
            pltpu.VMEM((elements, modes), BF16),
            pltpu.VMEM((slots, FACE_COEFFS), BF16),
            pltpu.VMEM((elements, modes, modes), BF16),
            pltpu.VMEM((elements, modes, trace), BF16),
            pltpu.VMEM((elements, trace, trace), BF16),
            pltpu.VMEM((LANES, modes), F32),
            pltpu.VMEM((modes, LANES), BF16),
            pltpu.VMEM((PER_FACE, trace + LANES), F32),
            pltpu.VMEM((trace, LANES), F32),
            pltpu.VMEM((trace, modes), BF16),
            pltpu.VMEM((trace, modes), BF16),
            pltpu.VMEM((trace, modes), BF16),
            pltpu.VMEM((trace, modes), BF16),
            pltpu.SemaphoreType.DMA((3,)),
            pltpu.SemaphoreType.DMA((2, elements)),
            pltpu.SemaphoreType.DMA((elements,)),
        ],
        compiler_params=params(BIG),
        cost_estimate=pl.CostEstimate(
            flops=2 * elements * modes * trace * (modes + trace),
            bytes_accessed=2 * elements * (modes * (modes + trace) + trace * trace),
            transcendentals=0,
        ),
        name="condense",
    )(table, slots_named, interior_rhs, local_inverse, coupling)

    slot_residual = pl.pallas_call(
        functools.partial(residual_kernel, elem_count),
        out_shape=jax.ShapeDtypeStruct((own, FACE_COEFFS), F32),
        in_specs=[ANY] * (1 + elem_count),
        out_specs=VMEM,
        scratch_shapes=[
            pltpu.VMEM((own, FACE_COEFFS), BF16),
            pltpu.VMEM((elem_count, SHARE_ROWS, LANES), BF16),
            pltpu.SemaphoreType.DMA((1 + elem_count,)),
        ],
        compiler_params=params(SMALL),
        name="residual",
    )(own_rows, *around(shares, "elem"))

    got, slot_residual = lax.optimization_barrier((got, slot_residual))
    coarse_blocks = pl.pallas_call(
        coarse_kernel,
        out_shape=jax.ShapeDtypeStruct((NC, MROW * MROW), F32),
        in_specs=[VMEM],
        out_specs=VMEM,
        scratch_shapes=[
            pltpu.VMEM((OWNER_ROWS, LANES), F32),
            pltpu.VMEM((NC * MROW, LANES), F32),
        ],
        compiler_params=params(SMALL),
        name="coarse",
    )(got)
    return schur_blocks, slot_residual, coarse_blocks


def solution(mesh):
    return jax.shard_map(
        shards,
        mesh=mesh,
        in_specs=(
            P(("face", "elem"), None),
            P(("face", "elem"), None),
            P(("face", "elem"), None),
            P(("face", "elem"), None),
            P(("face", "elem")),
            P(("face", "elem"), None),
            P(("face", "elem"), None, None),
            P(("face", "elem"), None, None),
            P(("face", "elem"), None),
        ),
        out_specs=(
            P(("face", "elem"), None, None),
            P(("face", "elem"), None),
            P(("face", "elem"), None),
        ),
        check_vma=False,
    )
```

```python
import functools

import jax
import jax.numpy as jnp
from jax import lax
from jax.experimental import pallas as pl
from jax.experimental.pallas import tpu as pltpu
from jax.sharding import PartitionSpec as P

FACE_COEFFS = 128
FACES_PER_ELEM = 3
MROW = 64
MCOL = 96
NC = 16
HALF = MROW // 2
LANES = 128
DENSE = HALF * MROW // LANES
OWNER_ROWS = NC * (DENSE + 1)
PER_FACE = 16
NAMED = FACES_PER_ELEM * PER_FACE
SHARE_ROWS = NAMED + 16
SLOT_BASE = 16
CHUNK = 16
MOST_PAIRED = 8
BIG = 62 << 20
SMALL = 12 << 20
PITCH = MROW + 8

BF16 = jnp.bfloat16
F32 = jnp.float32
I32 = jnp.int32

NT = (((1,), (1,)), ((), ()))
TN = (((0,), (0,)), ((), ()))


def iota(shape, dim):
    return lax.broadcasted_iota(I32, shape, dim)


def dot(left, right, dims=(((1,), (0,)), ((), ()))):
    return lax.dot_general(left, right, dims, preferred_element_type=F32)


def divided(value, by):
    shift = by.bit_length() - 1
    assert by == 1 << shift
    return value >> shift, value & (by - 1)


def place_kernel(elem_count, face_count, capacity, owner_hbm, trace_hbm, placed_ref, *refs):
    owner_ref, trace_ref, sems = refs
    copies = [
        pltpu.make_async_copy(owner_hbm, owner_ref, sems.at[0]),
        pltpu.make_async_copy(trace_hbm, trace_ref, sems.at[1]),
    ]
    for copy in copies:
        copy.start()
    slots, rows = placed_ref.shape[0], trace_ref.shape[0]
    earlier = (iota((rows, rows), 0) < iota((rows, rows), 1)).astype(BF16)
    slot = iota((slots, rows), 0)
    wanted = divided(slot, elem_count * capacity)[0] * capacity + divided(slot, capacity)[1]
    for copy in copies:
        copy.wait()
    owners = owner_ref[...]
    hot = (iota((face_count, rows), 0) == owners).astype(F32)
    rank = jnp.sum(hot * dot(hot.astype(BF16), earlier), axis=0, keepdims=True).astype(I32)
    place = (wanted == owners * capacity + rank).astype(BF16)
    placed_ref[...] = dot(place, trace_ref[...]).astype(BF16)


def turn_rhs(rhs_ref, wide_ref, rhs_turned_ref):
    wide_ref[...] = jnp.zeros_like(wide_ref)
    wide_ref[0 : rhs_ref.shape[0], :] = rhs_ref[...].astype(F32)
    rhs_turned_ref[...] = wide_ref[...].T.astype(BF16)


def gram_kernel(face_count, paired, owner_hbm, coarse_hbm, tiles_hbm, *refs):
    out_refs, refs = refs[:-9], refs[-9:]
    owner_ref, coarse_ref, tiles_ref, rows_ref = refs[:4]
    accs, diags, sems = refs[4:6], refs[6:8], refs[8]

    def place_of(owner):
        if not paired:
            return owner
        other = owner ^ lax.axis_index("face")
        return (other & 1) * (face_count // 2) + (other >> 1)

    tiles = tiles_ref.shape[0]
    copies = [
        pltpu.make_async_copy(owner_hbm, owner_ref, sems.at[0]),
        pltpu.make_async_copy(coarse_hbm, coarse_ref, sems.at[1]),
    ]
    copies.append(pltpu.make_async_copy(tiles_hbm, tiles_ref, sems.at[2]))
    for copy in copies:
        copy.start()
    for ref in (*accs, *diags):
        ref[...] = jnp.zeros_like(ref)
    for copy in copies:
        copy.wait()

    lane = iota((CHUNK, LANES), 1)
    inside = lane < MCOL
    row = iota((HALF, LANES), 0)
    column = divided(iota((HALF, LANES), 1), MROW)[1]
    swapped = (column > row) & (column < HALF)
    diagonal = column == row
    low = iota((DENSE, LANES), 1) < MROW
    low_wide = iota((MROW, LANES), 1) < MROW
    low_row = iota((1, LANES), 1) < MROW

    for chunk in range(tiles // CHUNK):
        first_tile = chunk * CHUNK
        for group in range(MROW // 4):
            base = group * 3 * LANES
            one, two, three = (
                tiles_ref[
                    first_tile : first_tile + CHUNK, base + k * LANES : base + (k + 1) * LANES
                ].astype(F32)
                for k in range(3)
            )
            rolled = (
                one,
                pltpu.roll(jnp.where(lane < 64, two, one), 32, 1),
                pltpu.roll(jnp.where(lane < 32, three, two), 64, 1),
                pltpu.roll(three, 96, 1),
            )
            for k in range(4):
                rows_ref[pl.ds(first_tile * PITCH + 4 * group + k, CHUNK, stride=PITCH), :] = (
                    jnp.where(inside, rolled[k], 0.0)
                )
        for tile in range(first_tile, first_tile + CHUNK, 2):
            both = jnp.concatenate(
                [
                    rows_ref[t * PITCH : t * PITCH + MROW, :].astype(BF16)
                    for t in (tile, tile + 1)
                ],
                axis=0,
            )
            gram = dot(both, both, NT)
            side = jnp.where(low_wide, gram[:MROW], gram[MROW:])
            lower = pltpu.roll(side[HALF:], LANES - HALF, 1)
            packed = jnp.where(swapped, lower, side[:HALF])
            diag = jnp.sum(jnp.where(diagonal, lower, 0.0), axis=0, keepdims=True)
            turned = pltpu.roll(packed, MROW, 1)
            dense = (
                jnp.where(low, packed[:DENSE], turned[DENSE:]),
                jnp.where(low, turned[:DENSE], packed[DENSE:]),
            )
            own = (jnp.where(low_row, diag, 0.0), jnp.where(low_row, 0.0, diag))
            for k in range(2):
                block = place_of(owner_ref[tile + k]) * NC + coarse_ref[tile + k]
                here = pl.ds(pl.multiple_of(block * DENSE, DENSE), DENSE)
                accs[k][here, :] += dense[k]
                diags[k][pl.ds(block, 1), :] += own[k]
    size = NC * DENSE
    each = face_count // len(out_refs)
    for owner in range(face_count):
        out_ref, start = out_refs[owner // each], owner % each * OWNER_ROWS
        here = slice(owner * size, (owner + 1) * size)
        out_ref[start : start + size, :] = (accs[0][here, :] + accs[1][here, :]).astype(BF16)
        here = slice(owner * NC, (owner + 1) * NC)
        out_ref[start + size : start + size + NC, :] = (
            diags[0][here, :] + diags[1][here, :]
        ).astype(BF16)


def join_kernel(kept_ref, came_ref, *out_refs):
    for k, out_ref in enumerate(out_refs):
        here = slice(k * OWNER_ROWS, (k + 1) * OWNER_ROWS)
        total = kept_ref[here, :].astype(F32) + came_ref[here, :].astype(F32)
        out_ref[...] = total.astype(BF16)


def main_kernel(
    rhs_hbm,
    inverse_hbm,
    coupling_hbm,
    schur_hbm,
    solved_ref,
    rhs_ref,
    inverse_ref,
    coupling_ref,
    schur_ref,
    wide_ref,
    rhs_turned_ref,
    turned_a_ref,
    turned_b_ref,
    product_a_ref,
    product_b_ref,
    small_sem,
    block_sems,
    schur_sems,
):
    elements = rhs_ref.shape[0]
    trace = FACES_PER_ELEM * FACE_COEFFS
    wide_lane = iota((trace, LANES), 1)
    small = pltpu.make_async_copy(rhs_hbm, rhs_ref, small_sem)

    def coupling_copy(e):
        return pltpu.make_async_copy(coupling_hbm.at[e], coupling_ref.at[e], block_sems.at[0, e])

    def inverse_copy(e):
        return pltpu.make_async_copy(inverse_hbm.at[e], inverse_ref.at[e], block_sems.at[1, e])

    def leave(e):
        return pltpu.make_async_copy(schur_ref.at[e], schur_hbm.at[e], schur_sems.at[e])

    coupling_copy(0).start()
    small.start()
    inverse_copy(0).start()
    coupling_copy(1).start()
    inverse_copy(1).start()
    coupling_copy(2).start()

    def turn(e, turned_ref):
        turned_ref[...] = coupling_ref[e].T

    def first(e, turned_ref, product_ref):
        product_ref[...] = dot(turned_ref[...], inverse_ref[e]).astype(BF16)

    def second(e, product_ref):
        wide = jnp.concatenate([coupling_ref[e], rhs_turned_ref[...]], axis=1)
        condensed = dot(product_ref[...], wide)
        schur_ref[e] = (-condensed[:, :trace]).astype(BF16)
        solved_ref[...] = jnp.where(wide_lane == e, condensed[:, trace:], solved_ref[...])

    turned = (turned_a_ref, turned_b_ref)
    product = (product_a_ref, product_b_ref)

    def advance(e, parity, turning=True, finishing=True):
        if turning:

            @pl.when(e + 2 < elements)
            def _():
                inverse_copy(e + 2).start()

            @pl.when(e + 3 < elements)
            def _():
                coupling_copy(e + 3).start()

            coupling_copy(e + 1).wait()
        inverse_copy(e).wait()
        if turning:
            turn(e + 1, turned[1 - parity])
        first(e, turned[parity], product[parity])
        if finishing:
            second(e - 1, product[1 - parity])
            leave(e - 1).start()

    solved_ref[...] = jnp.zeros_like(solved_ref)
    coupling_copy(0).wait()
    small.wait()
    turn(0, turned[0])
    turn_rhs(rhs_ref, wide_ref, rhs_turned_ref)
    advance(0, 0, finishing=False)

    def two(index, carry):
        advance(2 * index + 1, 1)
        advance(2 * index + 2, 0)
        return carry

    pairs = (elements - 2) // 2
    lax.fori_loop(0, pairs, two, 0)
    for e in range(2 * pairs + 1, elements):
        advance(e, e % 2, turning=e + 1 < elements)
    second(elements - 1, product[(elements - 1) % 2])
    leave(elements - 1).start()
    for e in range(elements):
        leave(e).wait()


def share_kernel(
    elem_count,
    face_count,
    table_hbm,
    conn_hbm,
    schur_hbm,
    solved_hbm,
    share_ref,
    own_ref,
    table_ref,
    conn_ref,
    schur_ref,
    vector_ref,
    sum_ref,
    sems,
    schur_sems,
):
    elements = schur_ref.shape[0]
    trace = FACES_PER_ELEM * FACE_COEFFS
    slots = table_ref.shape[0]
    own = own_ref.shape[0]
    capacity = own // face_count
    my_elem = lax.axis_index("elem")
    copies = [
        pltpu.make_async_copy(conn_hbm, conn_ref, sems.at[0]),
        pltpu.make_async_copy(table_hbm, table_ref, sems.at[1]),
        pltpu.make_async_copy(solved_hbm, sum_ref, sems.at[2]),
    ]
    parts = [
        pltpu.make_async_copy(schur_hbm.at[e], schur_ref.at[e], schur_sems.at[e])
        for e in range(elements)
    ]
    for copy in copies + parts:
        copy.start()
    for copy in copies:
        copy.wait()

    row = iota((PER_FACE, LANES), 0)
    lane = iota((PER_FACE, LANES), 1)
    first_lane = iota((1, LANES), 1)
    wide_lane = iota((trace, LANES), 1)

    def position(elem, inner):
        face, rank = divided(inner, capacity)
        return (face * elem_count + elem) * capacity + rank

    high = jnp.full((1, LANES), -1, I32)
    rest = jnp.zeros((1, LANES), I32)
    for a in range(FACES_PER_ELEM):
        positions = jnp.full((PER_FACE, LANES), -1, I32)
        for e in range(elements):
            slot = conn_ref[a, e]
            positions = jnp.where(row == e, position(*divided(slot, own)), positions)
            here = first_lane == a * PER_FACE + e
            quotient, remainder = divided(slot, SLOT_BASE)
            high = jnp.where(here, quotient, high)
            rest = jnp.where(here, remainder, rest)
        hot = jnp.concatenate([positions == lane + k for k in range(0, slots, LANES)], axis=1)
        vector_ref[:, a * LANES : (a + 1) * LANES] = dot(hot.astype(BF16), table_ref[...])
    names = jnp.where(row == 0, high, jnp.where(row == 1, rest, 0))
    share_ref[NAMED:, :] = names.astype(F32).astype(BF16)
    place = position(my_elem, iota((own, slots), 0))
    pick = (iota((own, slots), 1) == place).astype(BF16)
    own_ref[...] = dot(pick, table_ref[...]).astype(BF16)

    for copy in parts:
        copy.wait()
    columns = sum_ref[...]
    for e in range(elements):
        total = sum(
            schur_ref[e, :, a * LANES : (a + 1) * LANES].astype(F32)
            * vector_ref[e : e + 1, a * LANES : (a + 1) * LANES]
            for a in range(FACES_PER_ELEM)
        )
        sums = jnp.sum(total, axis=1, keepdims=True)
        columns = columns + jnp.where(wide_lane == e, sums, 0.0)
    for a in range(FACES_PER_ELEM):
        shares = columns[a * LANES : (a + 1) * LANES, :].T
        share_ref[a * PER_FACE : (a + 1) * PER_FACE, :] = shares[:PER_FACE].astype(BF16)


def less_shares(left, share_ref):
    own = left.shape[0]
    slot = (iota((own, SHARE_ROWS), 0) + lax.axis_index("elem") * own).astype(F32)
    names = share_ref[NAMED:, :].astype(F32)
    named = (names[0:1] * SLOT_BASE + names[1:2])[:, :SHARE_ROWS]
    return left - dot((slot == named).astype(BF16), share_ref[...])


def residual_kernel(left_ref, *refs):
    share_refs, residual_ref = refs[:-1], refs[-1]
    left = left_ref[...]
    for share_ref in share_refs:
        left = less_shares(left, share_ref)
    residual_ref[...] = left


def coarse_kernel(own_ref, share_ref, *refs):
    got_refs, (left_ref, out_ref, sum_ref, full_ref) = refs[:-4], refs[-4:]
    left_ref[...] = less_shares(own_ref[...].astype(F32), share_ref)
    sum_ref[...] = sum(
        got_ref[k : k + OWNER_ROWS, :].astype(F32)
        for got_ref in got_refs
        for k in range(0, got_ref.shape[0], OWNER_ROWS)
    )

    lane = iota((HALF, LANES), 1)
    row = iota((HALF, LANES), 0)
    wide_row = iota((MROW, LANES), 0)
    wide_lane = iota((MROW, LANES), 1)
    top = wide_row < HALF
    held = (top & ((wide_lane <= wide_row) | (wide_lane >= HALF))) | (
        (~top) & (wide_lane >= wide_row)
    )
    for block in range(NC):
        dense = sum_ref[block * DENSE : (block + 1) * DENSE, :]
        upper = jnp.concatenate([dense, pltpu.roll(dense, MROW, 1)], axis=0)
        diag = sum_ref[NC * DENSE + block : NC * DENSE + block + 1, :]
        diag = pltpu.roll(diag + pltpu.roll(diag, MROW, 1), HALF, 1)
        lower = jnp.where(lane == row + HALF, diag, pltpu.roll(upper, HALF, 1))
        given = jnp.concatenate([upper, lower], axis=0)
        turned = jnp.concatenate([given, given], axis=0).T[:MROW]
        full_ref[block * MROW : (block + 1) * MROW, :] = jnp.where(held, given, turned)
    low = iota((NC, LANES), 1) < MROW
    for chunk in range(HALF):
        left = full_ref[pl.ds(2 * chunk, NC, stride=MROW), :]
        right = full_ref[pl.ds(2 * chunk + 1, NC, stride=MROW), :]
        out_ref[:, chunk * LANES : (chunk + 1) * LANES] = jnp.where(
            low, left, pltpu.roll(right, MROW, 1)
        )


ANY = pl.BlockSpec(memory_space=pl.ANY)
VMEM = pl.BlockSpec(memory_space=pltpu.VMEM)


def cost(flops, bytes_accessed):
    return pl.CostEstimate(flops=flops, bytes_accessed=bytes_accessed, transcendentals=0)


def params(limit):
    return pltpu.CompilerParams(vmem_limit_bytes=limit)


def around(block, axis):
    count = lax.axis_size(axis)
    return [block] + [
        lax.ppermute(block, axis, [(i, i ^ k) for i in range(count)]) for k in range(1, count)
    ]


def shards(
    trace_old,
    new_owner,
    mortar_tiles,
    mortar_owner,
    mortar_coarse,
    interior_rhs,
    local_inverse,
    coupling,
    connectivity,
):
    face_count = lax.axis_size("face")
    elem_count = lax.axis_size("elem")
    row_count = trace_old.shape[0]
    tile_count = mortar_tiles.shape[0]
    elements, modes = interior_rhs.shape
    trace = FACES_PER_ELEM * FACE_COEFFS
    capacity = max(2, 2 * row_count // face_count)
    own = face_count * capacity

    slots = own * elem_count
    devices = face_count * elem_count
    paired = face_count <= MOST_PAIRED
    sides = 2 if paired else 1

    blocks = face_count * NC
    sums_shape = (blocks * DENSE, LANES)
    half_grams = pl.pallas_call(
        functools.partial(gram_kernel, face_count, paired),
        out_shape=[jax.ShapeDtypeStruct((blocks * (DENSE + 1) // sides, LANES), BF16)] * sides,
        in_specs=[ANY] * 3,
        out_specs=[VMEM] * sides,
        scratch_shapes=[
            pltpu.SMEM((tile_count,), I32),
            pltpu.SMEM((tile_count,), I32),
            pltpu.VMEM(mortar_tiles.shape, BF16),
            pltpu.VMEM((tile_count * PITCH, LANES), F32),
            pltpu.VMEM(sums_shape, F32),
            pltpu.VMEM(sums_shape, F32),
            pltpu.VMEM((blocks, LANES), F32),
            pltpu.VMEM((blocks, LANES), F32),
            pltpu.SemaphoreType.DMA((3,)),
        ],
        compiler_params=params(BIG),
        cost_estimate=cost(4 * tile_count * MROW * MROW * LANES, 12 << 20),
        name="gram",
    )(mortar_owner.reshape(tile_count), mortar_coarse, mortar_tiles)
    if paired:
        came = lax.ppermute(half_grams[1], "face", [(i, i ^ 1) for i in range(face_count)])

    owners, _ = lax.optimization_barrier((new_owner.reshape(1, row_count), half_grams[0]))
    placed = pl.pallas_call(
        functools.partial(place_kernel, elem_count, face_count, capacity),
        out_shape=jax.ShapeDtypeStruct((slots, FACE_COEFFS), BF16),
        in_specs=[ANY, ANY],
        out_specs=VMEM,
        scratch_shapes=[
            pltpu.VMEM((1, row_count), I32),
            pltpu.VMEM(trace_old.shape, BF16),
            pltpu.SemaphoreType.DMA((2,)),
        ],
        compiler_params=params(BIG),
        name="place",
    )(owners, trace_old)
    table = lax.all_to_all(
        placed.reshape(devices, capacity, FACE_COEFFS), ("face", "elem"), 0, 0, tiled=True
    ).reshape(slots, FACE_COEFFS)

    if paired:
        kept, _ = lax.optimization_barrier((half_grams[0], placed))
        joined = pl.pallas_call(
            join_kernel,
            out_shape=[jax.ShapeDtypeStruct((OWNER_ROWS, LANES), BF16)] * (face_count // 2),
            in_specs=[VMEM] * 2,
            out_specs=[VMEM] * (face_count // 2),
            compiler_params=params(SMALL),
            cost_estimate=cost(0, 4 << 20),
            name="join",
        )(kept, came)
        got = [joined[0]] + [
            lax.ppermute(joined[k], "face", [(i, i ^ (2 * k)) for i in range(face_count)])
            for k in range(1, face_count // 2)
        ]
        before = joined[0]
    else:
        blocked = half_grams[0].reshape(face_count, OWNER_ROWS, LANES)
        got = [lax.all_to_all(blocked, "face", 0, 0, tiled=True).reshape(-1, LANES)]
        before = half_grams[0]

    rhs, _ = lax.optimization_barrier((interior_rhs, before))
    schur_blocks, solved = pl.pallas_call(
        main_kernel,
        out_shape=(
            jax.ShapeDtypeStruct((elements, trace, trace), BF16),
            jax.ShapeDtypeStruct((trace, LANES), F32),
        ),
        in_specs=[ANY] * 3,
        out_specs=(ANY, VMEM),
        scratch_shapes=[
            pltpu.VMEM((elements, modes), BF16),
            pltpu.VMEM((elements, modes, modes), BF16),
            pltpu.VMEM((elements, modes, trace), BF16),
            pltpu.VMEM((elements, trace, trace), BF16),
            pltpu.VMEM((LANES, modes), F32),
            pltpu.VMEM((modes, LANES), BF16),
            pltpu.VMEM((trace, modes), BF16),
            pltpu.VMEM((trace, modes), BF16),
            pltpu.VMEM((trace, modes), BF16),
            pltpu.VMEM((trace, modes), BF16),
            pltpu.SemaphoreType.DMA,
            pltpu.SemaphoreType.DMA((2, elements)),
            pltpu.SemaphoreType.DMA((elements,)),
        ],
        compiler_params=params(BIG),
        cost_estimate=cost(
            2 * elements * modes * trace * (modes + trace),
            2 * elements * (modes * (modes + trace) + trace * trace),
        ),
        name="condense",
    )(rhs, local_inverse, coupling)

    shares, own_rows = pl.pallas_call(
        functools.partial(share_kernel, elem_count, face_count),
        out_shape=(
            jax.ShapeDtypeStruct((SHARE_ROWS, LANES), BF16),
            jax.ShapeDtypeStruct((own, FACE_COEFFS), BF16),
        ),
        in_specs=[ANY] * 4,
        out_specs=(VMEM, VMEM),
        scratch_shapes=[
            pltpu.VMEM((slots, FACE_COEFFS), BF16),
            pltpu.SMEM((FACES_PER_ELEM, elements), I32),
            pltpu.VMEM((elements, trace, trace), BF16),
            pltpu.VMEM((PER_FACE, trace), F32),
            pltpu.VMEM((trace, LANES), F32),
            pltpu.SemaphoreType.DMA((3,)),
            pltpu.SemaphoreType.DMA((elements,)),
        ],
        compiler_params=params(BIG),
        cost_estimate=cost(0, 8 << 20),
        name="share",
    )(table, connectivity.T, schur_blocks, solved)

    all_shares = around(shares, "elem")
    left, coarse_blocks = pl.pallas_call(
        coarse_kernel,
        out_shape=(
            jax.ShapeDtypeStruct((own, FACE_COEFFS), F32),
            jax.ShapeDtypeStruct((NC, MROW * MROW), F32),
        ),
        in_specs=[VMEM] * (2 + len(got)),
        out_specs=(VMEM, VMEM),
        scratch_shapes=[
            pltpu.VMEM((OWNER_ROWS, LANES), F32),
            pltpu.VMEM((NC * MROW, LANES), F32),
        ],
        compiler_params=params(SMALL),
        cost_estimate=cost(0, 8 << 20),
        name="coarse",
    )(own_rows, shares, *got)
    slot_residual = pl.pallas_call(
        residual_kernel,
        out_shape=jax.ShapeDtypeStruct((own, FACE_COEFFS), F32),
        in_specs=[VMEM] * elem_count,
        out_specs=VMEM,
        compiler_params=params(SMALL),
        name="residual",
    )(left, *all_shares[1:])
    return schur_blocks, slot_residual, coarse_blocks


def solution(mesh):
    return jax.shard_map(
        shards,
        mesh=mesh,
        in_specs=(
            P(("face", "elem"), None),
            P(("face", "elem"), None),
            P(("face", "elem"), None),
            P(("face", "elem"), None),
            P(("face", "elem")),
            P(("face", "elem"), None),
            P(("face", "elem"), None, None),
            P(("face", "elem"), None, None),
            P(("face", "elem"), None),
        ),
        out_specs=(
            P(("face", "elem"), None, None),
            P(("face", "elem"), None),
            P(("face", "elem"), None),
        ),
        check_vma=False,
    )
```

```python
import functools

import jax
import jax.numpy as jnp
from jax import lax
from jax.experimental import pallas as pl
from jax.experimental.pallas import tpu as pltpu
from jax.sharding import PartitionSpec as P

FACE_COEFFS = 128
FACES_PER_ELEM = 3
MROW = 64
MCOL = 96
NC = 16
HALF = MROW // 2
LANES = 128
DENSE = HALF * MROW // LANES
OWNER_ROWS = NC * (DENSE + 1)
PER_FACE = 16
NAMED = FACES_PER_ELEM * PER_FACE
SHARE_ROWS = NAMED + 16
SLOT_BASE = 16
CHUNK = 16
MOST_PAIRED = 8
BIG = 62 << 20
SMALL = 12 << 20
PITCH = MROW + 8

BF16 = jnp.bfloat16
F32 = jnp.float32
I32 = jnp.int32

NT = (((1,), (1,)), ((), ()))
TN = (((0,), (0,)), ((), ()))


def iota(shape, dim):
    return lax.broadcasted_iota(I32, shape, dim)


def dot(left, right, dims=(((1,), (0,)), ((), ()))):
    return lax.dot_general(left, right, dims, preferred_element_type=F32)


def divided(value, by):
    shift = by.bit_length() - 1
    assert by == 1 << shift
    return value >> shift, value & (by - 1)


def place_rows(elem_count, face_count, capacity, owners, trace, slots):
    rows = owners.shape[1]
    earlier = (iota((rows, rows), 0) < iota((rows, rows), 1)).astype(BF16)
    hot = (iota((face_count, rows), 0) == owners).astype(F32)
    rank = jnp.sum(hot * dot(hot.astype(BF16), earlier), axis=0, keepdims=True).astype(I32)
    slot = iota((slots, rows), 0)
    wanted = divided(slot, elem_count * capacity)[0] * capacity + divided(slot, capacity)[1]
    place = (wanted == owners * capacity + rank).astype(BF16)
    return dot(place, trace).astype(BF16)


def turn_rhs(rhs_ref, wide_ref, rhs_turned_ref):
    wide_ref[...] = jnp.zeros_like(wide_ref)
    wide_ref[0 : rhs_ref.shape[0], :] = rhs_ref[...].astype(F32)
    rhs_turned_ref[...] = wide_ref[...].T.astype(BF16)


def gram_kernel(
    elem_count,
    face_count,
    capacity,
    paired,
    owner_hbm,
    coarse_hbm,
    tiles_hbm,
    new_owner_hbm,
    trace_hbm,
    placed_ref,
    *refs,
):
    out_refs, refs = refs[:-11], refs[-11:]
    owner_ref, coarse_ref, tiles_ref, rows_ref = refs[:4]
    accs, diags = refs[4:6], refs[6:8]
    new_owner_ref, trace_ref, sems = refs[8:]

    def place_of(owner):
        if not paired:
            return owner
        other = owner ^ lax.axis_index("face")
        return (other & 1) * (face_count // 2) + (other >> 1)

    tiles = tiles_ref.shape[0]
    copies = [
        pltpu.make_async_copy(owner_hbm, owner_ref, sems.at[0]),
        pltpu.make_async_copy(coarse_hbm, coarse_ref, sems.at[1]),
        pltpu.make_async_copy(new_owner_hbm, new_owner_ref, sems.at[2]),
        pltpu.make_async_copy(trace_hbm, trace_ref, sems.at[3]),
        pltpu.make_async_copy(tiles_hbm, tiles_ref, sems.at[4]),
    ]
    for copy in copies:
        copy.start()
    for ref in (*accs, *diags):
        ref[...] = jnp.zeros_like(ref)
    for copy in copies:
        copy.wait()
    placed_ref[...] = place_rows(
        elem_count, face_count, capacity, new_owner_ref[...], trace_ref[...], placed_ref.shape[0]
    )

    lane = iota((CHUNK, LANES), 1)
    inside = lane < MCOL
    row = iota((HALF, LANES), 0)
    column = divided(iota((HALF, LANES), 1), MROW)[1]
    swapped = (column > row) & (column < HALF)
    diagonal = column == row
    low = iota((DENSE, LANES), 1) < MROW
    low_wide = iota((MROW, LANES), 1) < MROW
    low_row = iota((1, LANES), 1) < MROW

    for chunk in range(tiles // CHUNK):
        first_tile = chunk * CHUNK
        for group in range(MROW // 4):
            base = group * 3 * LANES
            one, two, three = (
                tiles_ref[
                    first_tile : first_tile + CHUNK, base + k * LANES : base + (k + 1) * LANES
                ].astype(F32)
                for k in range(3)
            )
            rolled = (
                one,
                pltpu.roll(jnp.where(lane < 64, two, one), 32, 1),
                pltpu.roll(jnp.where(lane < 32, three, two), 64, 1),
                pltpu.roll(three, 96, 1),
            )
            for k in range(4):
                rows_ref[pl.ds(first_tile * PITCH + 4 * group + k, CHUNK, stride=PITCH), :] = (
                    jnp.where(inside, rolled[k], 0.0)
                )
        for tile in range(first_tile, first_tile + CHUNK, 2):
            both = jnp.concatenate(
                [
                    rows_ref[t * PITCH : t * PITCH + MROW, :].astype(BF16)
                    for t in (tile, tile + 1)
                ],
                axis=0,
            )
            gram = dot(both, both, NT)
            side = jnp.where(low_wide, gram[:MROW], gram[MROW:])
            lower = pltpu.roll(side[HALF:], LANES - HALF, 1)
            packed = jnp.where(swapped, lower, side[:HALF])
            diag = jnp.sum(jnp.where(diagonal, lower, 0.0), axis=0, keepdims=True)
            turned = pltpu.roll(packed, MROW, 1)
            dense = (
                jnp.where(low, packed[:DENSE], turned[DENSE:]),
                jnp.where(low, turned[:DENSE], packed[DENSE:]),
            )
            own = (jnp.where(low_row, diag, 0.0), jnp.where(low_row, 0.0, diag))
            for k in range(2):
                block = place_of(owner_ref[tile + k]) * NC + coarse_ref[tile + k]
                here = pl.ds(pl.multiple_of(block * DENSE, DENSE), DENSE)
                accs[k][here, :] += dense[k]
                diags[k][pl.ds(block, 1), :] += own[k]
    size = NC * DENSE
    each = face_count // len(out_refs)
    for owner in range(face_count):
        out_ref, start = out_refs[owner // each], owner % each * OWNER_ROWS
        here = slice(owner * size, (owner + 1) * size)
        out_ref[start : start + size, :] = (accs[0][here, :] + accs[1][here, :]).astype(BF16)
        here = slice(owner * NC, (owner + 1) * NC)
        out_ref[start + size : start + size + NC, :] = (
            diags[0][here, :] + diags[1][here, :]
        ).astype(BF16)


def join_kernel(kept_ref, came_ref, *out_refs):
    for k, out_ref in enumerate(out_refs):
        here = slice(k * OWNER_ROWS, (k + 1) * OWNER_ROWS)
        total = kept_ref[here, :].astype(F32) + came_ref[here, :].astype(F32)
        out_ref[...] = total.astype(BF16)


def main_kernel(
    elem_count,
    face_count,
    table_hbm,
    conn_hbm,
    rhs_hbm,
    inverse_hbm,
    coupling_hbm,
    schur_hbm,
    share_ref,
    left_ref,
    conn_ref,
    rhs_ref,
    table_ref,
    inverse_ref,
    coupling_ref,
    schur_ref,
    wide_ref,
    rhs_turned_ref,
    vector_ref,
    sum_ref,
    turned_a_ref,
    turned_b_ref,
    product_a_ref,
    product_b_ref,
    small_sems,
    block_sems,
    schur_sems,
):
    elements = rhs_ref.shape[0]
    modes = rhs_ref.shape[1]
    trace = FACES_PER_ELEM * FACE_COEFFS
    slots = table_ref.shape[0]
    own = left_ref.shape[0]
    capacity = own // face_count
    my_elem = lax.axis_index("elem")
    small = [
        pltpu.make_async_copy(rhs_hbm, rhs_ref, small_sems.at[0]),
        pltpu.make_async_copy(conn_hbm, conn_ref, small_sems.at[1]),
        pltpu.make_async_copy(table_hbm, table_ref, small_sems.at[2]),
    ]

    def coupling_copy(e):
        return pltpu.make_async_copy(coupling_hbm.at[e], coupling_ref.at[e], block_sems.at[0, e])

    def inverse_copy(e):
        return pltpu.make_async_copy(inverse_hbm.at[e], inverse_ref.at[e], block_sems.at[1, e])

    def leave(e):
        return pltpu.make_async_copy(schur_ref.at[e], schur_hbm.at[e], schur_sems.at[e])

    coupling_copy(0).start()
    for copy in small:
        copy.start()
    inverse_copy(0).start()
    coupling_copy(1).start()
    inverse_copy(1).start()
    coupling_copy(2).start()

    def turn(e, turned_ref):
        turned_ref[...] = coupling_ref[e].T

    def first(e, turned_ref, product_ref):
        for half in range(2):
            here = slice(half * modes // 2, (half + 1) * modes // 2)
            product_ref[:, here] = dot(turned_ref[...], inverse_ref[e, :, here]).astype(BF16)

    def second(e, product_ref):
        split = 2 * LANES
        one = dot(product_ref[...], coupling_ref[e, :, :split])
        wide = jnp.concatenate([coupling_ref[e, :, split:], rhs_turned_ref[...]], axis=1)
        two = dot(product_ref[...], wide)
        schur_ref[e, :, :split] = (-one).astype(BF16)
        schur_ref[e, :, split:] = (-two[:, : trace - split]).astype(BF16)
        vector = vector_ref[pl.ds(e, 1), :]
        one = one * vector[:, :split]
        two = two * vector[:, split:]
        total = (one[:, :LANES] + one[:, LANES:]) + (two[:, :LANES] + two[:, LANES:])
        sums = jnp.sum(total, axis=1, keepdims=True)
        sum_ref[...] = jnp.where(iota((trace, LANES), 1) == e, sums, sum_ref[...])

    turned = (turned_a_ref, turned_b_ref)
    product = (product_a_ref, product_b_ref)

    def advance(e, parity, turning=True, finishing=True):
        if turning:
            @pl.when(e + 2 < elements)
            def _():
                inverse_copy(e + 2).start()

            @pl.when(e + 3 < elements)
            def _():
                coupling_copy(e + 3).start()

            coupling_copy(e + 1).wait()
        inverse_copy(e).wait()
        if turning:
            turn(e + 1, turned[1 - parity])
        first(e, turned[parity], product[parity])
        if finishing:
            second(e - 1, product[1 - parity])
            leave(e - 1).start()

    coupling_copy(0).wait()
    turn(0, turned[0])
    for copy in small:
        copy.wait()
    sum_ref[...] = jnp.zeros_like(sum_ref)
    turn_rhs(rhs_ref, wide_ref, rhs_turned_ref)
    row = iota((PER_FACE, LANES), 0)
    lane = iota((PER_FACE, LANES), 1)

    def position(elem, inner):
        face, rank = divided(inner, capacity)
        return (face * elem_count + elem) * capacity + rank

    first_lane = iota((1, LANES), 1)
    high = jnp.full((1, LANES), -1, I32)
    rest = jnp.zeros((1, LANES), I32)
    for a in range(FACES_PER_ELEM):
        positions = jnp.full((PER_FACE, LANES), -1, I32)
        for e in range(elements):
            slot = conn_ref[a, e]
            positions = jnp.where(row == e, position(*divided(slot, own)), positions)
            here = first_lane == a * PER_FACE + e
            quotient, remainder = divided(slot, SLOT_BASE)
            high = jnp.where(here, quotient, high)
            rest = jnp.where(here, remainder, rest)
        hot = jnp.concatenate([positions == lane + k for k in range(0, slots, LANES)], axis=1)
        lam = dot(hot.astype(BF16), table_ref[...])
        vector_ref[:, a * LANES : (a + 1) * LANES] = -lam
    vector_ref[:, trace:] = (row == lane).astype(F32)
    names = jnp.where(row == 0, high, jnp.where(row == 1, rest, 0))
    share_ref[NAMED:, :] = names.astype(F32).astype(BF16)
    place = position(my_elem, iota((own, slots), 0))
    pick = (iota((own, slots), 1) == place).astype(BF16)
    left_ref[...] = dot(pick, table_ref[...])

    advance(0, 0, finishing=False)

    def two(index, carry):
        advance(2 * index + 1, 1)
        advance(2 * index + 2, 0)
        return carry

    pairs = (elements - 2) // 2
    lax.fori_loop(0, pairs, two, 0)
    for e in range(2 * pairs + 1, elements):
        advance(e, e % 2, turning=e + 1 < elements)
    second(elements - 1, product[(elements - 1) % 2])
    leave(elements - 1).start()

    for a in range(FACES_PER_ELEM):
        shares = sum_ref[a * LANES : (a + 1) * LANES, :].T
        share_ref[a * PER_FACE : (a + 1) * PER_FACE, :] = shares[:PER_FACE].astype(BF16)
    left_ref[...] = less_shares(left_ref[...], share_ref)
    for e in range(elements):
        leave(e).wait()


def less_shares(left, share_ref):
    own = left.shape[0]
    slot = (iota((own, SHARE_ROWS), 0) + lax.axis_index("elem") * own).astype(F32)
    names = share_ref[NAMED:, :].astype(F32)
    named = (names[0:1] * SLOT_BASE + names[1:2])[:, :SHARE_ROWS]
    return left - dot((slot == named).astype(BF16), share_ref[...])


def residual_kernel(left_ref, *refs):
    share_refs, residual_ref = refs[:-1], refs[-1]
    left = left_ref[...]
    for share_ref in share_refs:
        left = less_shares(left, share_ref)
    residual_ref[...] = left


def coarse_kernel(*refs):
    got_refs, (out_ref, sum_ref, full_ref) = refs[:-3], refs[-3:]
    sum_ref[...] = sum(
        got_ref[k : k + OWNER_ROWS, :].astype(F32)
        for got_ref in got_refs
        for k in range(0, got_ref.shape[0], OWNER_ROWS)
    )

    lane = iota((HALF, LANES), 1)
    row = iota((HALF, LANES), 0)
    wide_row = iota((MROW, LANES), 0)
    wide_lane = iota((MROW, LANES), 1)
    top = wide_row < HALF
    held = (top & ((wide_lane <= wide_row) | (wide_lane >= HALF))) | (
        (~top) & (wide_lane >= wide_row)
    )
    for block in range(NC):
        dense = sum_ref[block * DENSE : (block + 1) * DENSE, :]
        upper = jnp.concatenate([dense, pltpu.roll(dense, MROW, 1)], axis=0)
        diag = sum_ref[NC * DENSE + block : NC * DENSE + block + 1, :]
        diag = pltpu.roll(diag + pltpu.roll(diag, MROW, 1), HALF, 1)
        lower = jnp.where(lane == row + HALF, diag, pltpu.roll(upper, HALF, 1))
        given = jnp.concatenate([upper, lower], axis=0)
        turned = jnp.concatenate([given, given], axis=0).T[:MROW]
        full_ref[block * MROW : (block + 1) * MROW, :] = jnp.where(held, given, turned)
    low = iota((NC, LANES), 1) < MROW
    for chunk in range(HALF):
        left = full_ref[pl.ds(2 * chunk, NC, stride=MROW), :]
        right = full_ref[pl.ds(2 * chunk + 1, NC, stride=MROW), :]
        out_ref[:, chunk * LANES : (chunk + 1) * LANES] = jnp.where(
            low, left, pltpu.roll(right, MROW, 1)
        )


ANY = pl.BlockSpec(memory_space=pl.ANY)
VMEM = pl.BlockSpec(memory_space=pltpu.VMEM)


def cost(flops, bytes_accessed):
    return pl.CostEstimate(flops=flops, bytes_accessed=bytes_accessed, transcendentals=0)


def params(limit):
    return pltpu.CompilerParams(vmem_limit_bytes=limit)


def around(block, axis):
    count = lax.axis_size(axis)
    return [block] + [
        lax.ppermute(block, axis, [(i, i ^ k) for i in range(count)]) for k in range(1, count)
    ]


def shards(
    trace_old,
    new_owner,
    mortar_tiles,
    mortar_owner,
    mortar_coarse,
    interior_rhs,
    local_inverse,
    coupling,
    connectivity,
):
    face_count = lax.axis_size("face")
    elem_count = lax.axis_size("elem")
    row_count = trace_old.shape[0]
    tile_count = mortar_tiles.shape[0]
    elements, modes = interior_rhs.shape
    trace = FACES_PER_ELEM * FACE_COEFFS
    capacity = max(2, 2 * row_count // face_count)
    own = face_count * capacity

    slots = own * elem_count
    devices = face_count * elem_count
    paired = face_count <= MOST_PAIRED
    sides = 2 if paired else 1

    blocks = face_count * NC
    sums_shape = (blocks * DENSE, LANES)
    placed, *half_grams = pl.pallas_call(
        functools.partial(gram_kernel, elem_count, face_count, capacity, paired),
        out_shape=[jax.ShapeDtypeStruct((slots, FACE_COEFFS), BF16)]
        + [jax.ShapeDtypeStruct((blocks * (DENSE + 1) // sides, LANES), BF16)] * sides,
        in_specs=[ANY] * 5,
        out_specs=[VMEM] * (1 + sides),
        scratch_shapes=[
            pltpu.SMEM((tile_count,), I32),
            pltpu.SMEM((tile_count,), I32),
            pltpu.VMEM(mortar_tiles.shape, BF16),
            pltpu.VMEM((tile_count * PITCH, LANES), F32),
            pltpu.VMEM(sums_shape, F32),
            pltpu.VMEM(sums_shape, F32),
            pltpu.VMEM((blocks, LANES), F32),
            pltpu.VMEM((blocks, LANES), F32),
            pltpu.VMEM((1, row_count), I32),
            pltpu.VMEM(trace_old.shape, BF16),
            pltpu.SemaphoreType.DMA((5,)),
        ],
        compiler_params=params(BIG),
        cost_estimate=cost(4 * tile_count * MROW * MROW * LANES, 12 << 20),
        name="gram",
    )(
        mortar_owner.reshape(tile_count),
        mortar_coarse,
        mortar_tiles,
        new_owner.reshape(1, row_count),
        trace_old,
    )
    if paired:
        came = lax.ppermute(half_grams[1], "face", [(i, i ^ 1) for i in range(face_count)])
    table = lax.all_to_all(
        placed.reshape(devices, capacity, FACE_COEFFS), ("face", "elem"), 0, 0, tiled=True
    ).reshape(slots, FACE_COEFFS)

    if paired:
        joined = pl.pallas_call(
            join_kernel,
            out_shape=[jax.ShapeDtypeStruct((OWNER_ROWS, LANES), BF16)] * (face_count // 2),
            in_specs=[VMEM] * 2,
            out_specs=[VMEM] * (face_count // 2),
            compiler_params=params(SMALL),
            cost_estimate=cost(0, 4 << 20),
            name="join",
        )(half_grams[0], came)
        got = [joined[0]] + [
            lax.ppermute(joined[k], "face", [(i, i ^ (2 * k)) for i in range(face_count)])
            for k in range(1, face_count // 2)
        ]
        before = joined[0]
    else:
        blocked = half_grams[0].reshape(face_count, OWNER_ROWS, LANES)
        got = [lax.all_to_all(blocked, "face", 0, 0, tiled=True).reshape(-1, LANES)]
        before = half_grams[0]

    rhs, _ = lax.optimization_barrier((interior_rhs, before))
    schur_blocks, shares, left = pl.pallas_call(
        functools.partial(main_kernel, elem_count, face_count),
        out_shape=(
            jax.ShapeDtypeStruct((elements, trace, trace), BF16),
            jax.ShapeDtypeStruct((SHARE_ROWS, LANES), BF16),
            jax.ShapeDtypeStruct((own, FACE_COEFFS), F32),
        ),
        in_specs=[ANY] * 5,
        out_specs=(ANY, VMEM, VMEM),
        scratch_shapes=[
            pltpu.SMEM((FACES_PER_ELEM, elements), I32),
            pltpu.VMEM((elements, modes), BF16),
            pltpu.VMEM((slots, FACE_COEFFS), BF16),
            pltpu.VMEM((elements, modes, modes), BF16),
            pltpu.VMEM((elements, modes, trace), BF16),
            pltpu.VMEM((elements, trace, trace), BF16),
            pltpu.VMEM((LANES, modes), F32),
            pltpu.VMEM((modes, LANES), BF16),
            pltpu.VMEM((PER_FACE, trace + LANES), F32),
            pltpu.VMEM((trace, LANES), F32),
            pltpu.VMEM((trace, modes), BF16),
            pltpu.VMEM((trace, modes), BF16),
            pltpu.VMEM((trace, modes), BF16),
            pltpu.VMEM((trace, modes), BF16),
            pltpu.SemaphoreType.DMA((3,)),
            pltpu.SemaphoreType.DMA((2, elements)),
            pltpu.SemaphoreType.DMA((elements,)),
        ],
        compiler_params=params(BIG),
        cost_estimate=cost(
            2 * elements * modes * trace * (modes + trace),
            2 * elements * (modes * (modes + trace) + trace * trace),
        ),
        name="condense",
    )(table, connectivity.T, rhs, local_inverse, coupling)

    all_shares = around(shares, "elem")
    coarse_blocks = pl.pallas_call(
        coarse_kernel,
        out_shape=jax.ShapeDtypeStruct((NC, MROW * MROW), F32),
        in_specs=[VMEM] * len(got),
        out_specs=VMEM,
        scratch_shapes=[
            pltpu.VMEM((OWNER_ROWS, LANES), F32),
            pltpu.VMEM((NC * MROW, LANES), F32),
        ],
        compiler_params=params(SMALL),
        cost_estimate=cost(0, 8 << 20),
        name="coarse",
    )(*got)
    left, coarse_blocks = lax.optimization_barrier((left, coarse_blocks))
    slot_residual = pl.pallas_call(
        residual_kernel,
        out_shape=jax.ShapeDtypeStruct((own, FACE_COEFFS), F32),
        in_specs=[VMEM] * elem_count,
        out_specs=VMEM,
        compiler_params=params(SMALL),
        name="residual",
    )(left, *all_shares[1:])
    return schur_blocks, slot_residual, coarse_blocks


def solution(mesh):
    return jax.shard_map(
        shards,
        mesh=mesh,
        in_specs=(
            P(("face", "elem"), None),
            P(("face", "elem"), None),
            P(("face", "elem"), None),
            P(("face", "elem"), None),
            P(("face", "elem")),
            P(("face", "elem"), None),
            P(("face", "elem"), None, None),
            P(("face", "elem"), None, None),
            P(("face", "elem"), None),
        ),
        out_specs=(
            P(("face", "elem"), None, None),
            P(("face", "elem"), None),
            P(("face", "elem"), None),
        ),
        check_vma=False,
    )
```

```python
import functools

import jax
import jax.numpy as jnp
from jax import lax
from jax.experimental import pallas as pl
from jax.experimental.pallas import tpu as pltpu
from jax.sharding import PartitionSpec as P

FACE_COEFFS = 128
FACES_PER_ELEM = 3
MROW = 64
MCOL = 96
NC = 16
HALF = MROW // 2
LANES = 128
DENSE = HALF * MROW // LANES
OWNER_ROWS = NC * (DENSE + 1)
PER_FACE = 16
NAMED = FACES_PER_ELEM * PER_FACE
SHARE_ROWS = NAMED + 16
SLOT_BASE = 16
CHUNK = 16
AHEAD = 5
MOST_PAIRED = 8
BIG = 62 << 20
SMALL = 12 << 20
PITCH = MROW + 8

BF16 = jnp.bfloat16
F32 = jnp.float32
I32 = jnp.int32

NT = (((1,), (1,)), ((), ()))
TN = (((0,), (0,)), ((), ()))


def iota(shape, dim):
    return lax.broadcasted_iota(I32, shape, dim)


def dot(left, right, dims=(((1,), (0,)), ((), ()))):
    return lax.dot_general(left, right, dims, preferred_element_type=F32)


def divided(value, by):
    shift = by.bit_length() - 1
    assert by == 1 << shift
    return value >> shift, value & (by - 1)


def place_rows(elem_count, face_count, capacity, owners, trace, slots):
    rows = owners.shape[1]
    earlier = (iota((rows, rows), 0) < iota((rows, rows), 1)).astype(BF16)
    hot = (iota((face_count, rows), 0) == owners).astype(F32)
    rank = jnp.sum(hot * dot(hot.astype(BF16), earlier), axis=0, keepdims=True).astype(I32)
    slot = iota((slots, rows), 0)
    wanted = divided(slot, elem_count * capacity)[0] * capacity + divided(slot, capacity)[1]
    place = (wanted == owners * capacity + rank).astype(BF16)
    return dot(place, trace).astype(BF16)


def turn_rhs(rhs_ref, wide_ref, rhs_turned_ref):
    wide_ref[...] = jnp.zeros_like(wide_ref)
    wide_ref[0 : rhs_ref.shape[0], :] = rhs_ref[...].astype(F32)
    rhs_turned_ref[...] = wide_ref[...].T.astype(BF16)


def gram_kernel(
    elem_count,
    face_count,
    capacity,
    paired,
    owner_hbm,
    coarse_hbm,
    tiles_hbm,
    new_owner_hbm,
    trace_hbm,
    placed_ref,
    *refs,
):
    out_refs, refs = refs[:-11], refs[-11:]
    owner_ref, coarse_ref, tiles_ref, rows_ref = refs[:4]
    accs, diags = refs[4:6], refs[6:8]
    new_owner_ref, trace_ref, sems = refs[8:]

    def place_of(owner):
        if not paired:
            return owner
        other = owner ^ lax.axis_index("face")
        return (other & 1) * (face_count // 2) + (other >> 1)

    tiles = tiles_ref.shape[0]
    copies = [
        pltpu.make_async_copy(owner_hbm, owner_ref, sems.at[0]),
        pltpu.make_async_copy(coarse_hbm, coarse_ref, sems.at[1]),
        pltpu.make_async_copy(new_owner_hbm, new_owner_ref, sems.at[2]),
        pltpu.make_async_copy(trace_hbm, trace_ref, sems.at[3]),
        pltpu.make_async_copy(tiles_hbm, tiles_ref, sems.at[4]),
    ]
    for copy in copies:
        copy.start()
    for ref in (*accs, *diags):
        ref[...] = jnp.zeros_like(ref)
    for copy in copies:
        copy.wait()
    placed_ref[...] = place_rows(
        elem_count, face_count, capacity, new_owner_ref[...], trace_ref[...], placed_ref.shape[0]
    )

    lane = iota((CHUNK, LANES), 1)
    inside = lane < MCOL
    row = iota((HALF, LANES), 0)
    column = divided(iota((HALF, LANES), 1), MROW)[1]
    swapped = (column > row) & (column < HALF)
    diagonal = column == row
    low = iota((DENSE, LANES), 1) < MROW
    low_wide = iota((MROW, LANES), 1) < MROW
    low_row = iota((1, LANES), 1) < MROW

    for chunk in range(tiles // CHUNK):
        first_tile = chunk * CHUNK
        for group in range(MROW // 4):
            base = group * 3 * LANES
            one, two, three = (
                tiles_ref[
                    first_tile : first_tile + CHUNK, base + k * LANES : base + (k + 1) * LANES
                ].astype(F32)
                for k in range(3)
            )
            rolled = (
                one,
                pltpu.roll(jnp.where(lane < 64, two, one), 32, 1),
                pltpu.roll(jnp.where(lane < 32, three, two), 64, 1),
                pltpu.roll(three, 96, 1),
            )
            for k in range(4):
                rows_ref[pl.ds(first_tile * PITCH + 4 * group + k, CHUNK, stride=PITCH), :] = (
                    jnp.where(inside, rolled[k], 0.0)
                )
        for tile in range(first_tile, first_tile + CHUNK, 2):
            both = jnp.concatenate(
                [
                    rows_ref[t * PITCH : t * PITCH + MROW, :].astype(BF16)
                    for t in (tile, tile + 1)
                ],
                axis=0,
            )
            gram = dot(both, both, NT)
            side = jnp.where(low_wide, gram[:MROW], gram[MROW:])
            lower = pltpu.roll(side[HALF:], LANES - HALF, 1)
            packed = jnp.where(swapped, lower, side[:HALF])
            diag = jnp.sum(jnp.where(diagonal, lower, 0.0), axis=0, keepdims=True)
            turned = pltpu.roll(packed, MROW, 1)
            dense = (
                jnp.where(low, packed[:DENSE], turned[DENSE:]),
                jnp.where(low, turned[:DENSE], packed[DENSE:]),
            )
            own = (jnp.where(low_row, diag, 0.0), jnp.where(low_row, 0.0, diag))
            for k in range(2):
                block = place_of(owner_ref[tile + k]) * NC + coarse_ref[tile + k]
                here = pl.ds(pl.multiple_of(block * DENSE, DENSE), DENSE)
                accs[k][here, :] += dense[k]
                diags[k][pl.ds(block, 1), :] += own[k]
    size = NC * DENSE
    each = face_count // len(out_refs)
    for owner in range(face_count):
        out_ref, start = out_refs[owner // each], owner % each * OWNER_ROWS
        here = slice(owner * size, (owner + 1) * size)
        out_ref[start : start + size, :] = (accs[0][here, :] + accs[1][here, :]).astype(BF16)
        here = slice(owner * NC, (owner + 1) * NC)
        out_ref[start + size : start + size + NC, :] = (
            diags[0][here, :] + diags[1][here, :]
        ).astype(BF16)


def join_kernel(kept_ref, came_ref, *out_refs):
    for k, out_ref in enumerate(out_refs):
        here = slice(k * OWNER_ROWS, (k + 1) * OWNER_ROWS)
        total = kept_ref[here, :].astype(F32) + came_ref[here, :].astype(F32)
        out_ref[...] = total.astype(BF16)


def main_kernel(
    elem_count,
    face_count,
    table_hbm,
    conn_hbm,
    rhs_hbm,
    inverse_hbm,
    coupling_hbm,
    schur_hbm,
    share_ref,
    left_ref,
    conn_ref,
    rhs_ref,
    table_ref,
    inverse_ref,
    coupling_ref,
    schur_ref,
    wide_ref,
    rhs_turned_ref,
    vector_ref,
    sum_ref,
    turned_a_ref,
    turned_b_ref,
    product_a_ref,
    product_b_ref,
    small_sems,
    block_sems,
    schur_sems,
):
    elements = rhs_ref.shape[0]
    modes = rhs_ref.shape[1]
    trace = FACES_PER_ELEM * FACE_COEFFS
    slots = table_ref.shape[0]
    own = left_ref.shape[0]
    capacity = own // face_count
    my_elem = lax.axis_index("elem")
    small = [
        pltpu.make_async_copy(rhs_hbm, rhs_ref, small_sems.at[0]),
        pltpu.make_async_copy(conn_hbm, conn_ref, small_sems.at[1]),
        pltpu.make_async_copy(table_hbm, table_ref, small_sems.at[2]),
    ]

    def coupling_copy(e):
        return pltpu.make_async_copy(coupling_hbm.at[e], coupling_ref.at[e], block_sems.at[0, e])

    def inverse_copy(e):
        return pltpu.make_async_copy(inverse_hbm.at[e], inverse_ref.at[e], block_sems.at[1, e])

    def leave(e):
        return pltpu.make_async_copy(schur_ref.at[e], schur_hbm.at[e], schur_sems.at[e])

    def bring(first, last):
        for e in range(first, min(last, elements)):
            coupling_copy(e).start()
            inverse_copy(e).start()

    coupling_copy(0).start()
    for copy in small:
        copy.start()
    inverse_copy(0).start()
    bring(1, 2)

    def turn(e, turned_ref):
        turned_ref[...] = coupling_ref[e].T

    def first(e, turned_ref, product_ref):
        for half in range(2):
            here = slice(half * modes // 2, (half + 1) * modes // 2)
            product_ref[:, here] = dot(turned_ref[...], inverse_ref[e, :, here]).astype(BF16)

    def second(e, product_ref):
        split = 2 * LANES
        one = dot(product_ref[...], coupling_ref[e, :, :split])
        wide = jnp.concatenate([coupling_ref[e, :, split:], rhs_turned_ref[...]], axis=1)
        two = dot(product_ref[...], wide)
        schur_ref[e, :, :split] = (-one).astype(BF16)
        schur_ref[e, :, split:] = (-two[:, : trace - split]).astype(BF16)
        vector = vector_ref[pl.ds(e, 1), :]
        one = one * vector[:, :split]
        two = two * vector[:, split:]
        total = (one[:, :LANES] + one[:, LANES:]) + (two[:, :LANES] + two[:, LANES:])
        sums = jnp.sum(total, axis=1, keepdims=True)
        sum_ref[...] = jnp.where(iota((trace, LANES), 1) == e, sums, sum_ref[...])

    turned = (turned_a_ref, turned_b_ref)
    product = (product_a_ref, product_b_ref)

    def advance(e, parity, turning=True, finishing=True):
        if turning:

            @pl.when(e + AHEAD < elements)
            def _():
                coupling_copy(e + AHEAD).start()
                inverse_copy(e + AHEAD).start()

            coupling_copy(e + 1).wait()
        inverse_copy(e).wait()
        if turning:
            turn(e + 1, turned[1 - parity])
        first(e, turned[parity], product[parity])
        if finishing:
            second(e - 1, product[1 - parity])
            leave(e - 1).start()

    coupling_copy(0).wait()
    bring(2, 3)
    turn(0, turned[0])
    for copy in small:
        copy.wait()
    bring(3, AHEAD)
    sum_ref[...] = jnp.zeros_like(sum_ref)
    turn_rhs(rhs_ref, wide_ref, rhs_turned_ref)
    row = iota((PER_FACE, LANES), 0)
    lane = iota((PER_FACE, LANES), 1)

    def position(elem, inner):
        face, rank = divided(inner, capacity)
        return (face * elem_count + elem) * capacity + rank

    first_lane = iota((1, LANES), 1)
    high = jnp.full((1, LANES), -1, I32)
    rest = jnp.zeros((1, LANES), I32)
    for a in range(FACES_PER_ELEM):
        positions = jnp.full((PER_FACE, LANES), -1, I32)
        for e in range(elements):
            slot = conn_ref[a, e]
            positions = jnp.where(row == e, position(*divided(slot, own)), positions)
            here = first_lane == a * PER_FACE + e
            quotient, remainder = divided(slot, SLOT_BASE)
            high = jnp.where(here, quotient, high)
            rest = jnp.where(here, remainder, rest)
        hot = jnp.concatenate([positions == lane + k for k in range(0, slots, LANES)], axis=1)
        lam = dot(hot.astype(BF16), table_ref[...])
        vector_ref[:, a * LANES : (a + 1) * LANES] = -lam
    vector_ref[:, trace:] = (row == lane).astype(F32)
    names = jnp.where(row == 0, high, jnp.where(row == 1, rest, 0))
    share_ref[NAMED:, :] = names.astype(F32).astype(BF16)
    place = position(my_elem, iota((own, slots), 0))
    pick = (iota((own, slots), 1) == place).astype(BF16)
    left_ref[...] = dot(pick, table_ref[...])

    advance(0, 0, finishing=False)

    def two(index, carry):
        advance(2 * index + 1, 1)
        advance(2 * index + 2, 0)
        return carry

    pairs = (elements - 2) // 2
    lax.fori_loop(0, pairs, two, 0)
    for e in range(2 * pairs + 1, elements):
        advance(e, e % 2, turning=e + 1 < elements)
    second(elements - 1, product[(elements - 1) % 2])
    leave(elements - 1).start()

    for a in range(FACES_PER_ELEM):
        shares = sum_ref[a * LANES : (a + 1) * LANES, :].T
        share_ref[a * PER_FACE : (a + 1) * PER_FACE, :] = shares[:PER_FACE].astype(BF16)
    left_ref[...] = less_shares(left_ref[...], share_ref)
    for e in range(elements):
        leave(e).wait()


def less_shares(left, share_ref):
    own = left.shape[0]
    slot = (iota((own, SHARE_ROWS), 0) + lax.axis_index("elem") * own).astype(F32)
    names = share_ref[NAMED:, :].astype(F32)
    named = (names[0:1] * SLOT_BASE + names[1:2])[:, :SHARE_ROWS]
    return left - dot((slot == named).astype(BF16), share_ref[...])


def residual_kernel(left_ref, *refs):
    share_refs, residual_ref = refs[:-1], refs[-1]
    left = left_ref[...]
    for share_ref in share_refs:
        left = less_shares(left, share_ref)
    residual_ref[...] = left


def coarse_kernel(*refs):
    got_refs, (out_ref, sum_ref, full_ref) = refs[:-3], refs[-3:]
    sum_ref[...] = sum(
        got_ref[k : k + OWNER_ROWS, :].astype(F32)
        for got_ref in got_refs
        for k in range(0, got_ref.shape[0], OWNER_ROWS)
    )

    lane = iota((HALF, LANES), 1)
    row = iota((HALF, LANES), 0)
    wide_row = iota((MROW, LANES), 0)
    wide_lane = iota((MROW, LANES), 1)
    top = wide_row < HALF
    held = (top & ((wide_lane <= wide_row) | (wide_lane >= HALF))) | (
        (~top) & (wide_lane >= wide_row)
    )
    for block in range(NC):
        dense = sum_ref[block * DENSE : (block + 1) * DENSE, :]
        upper = jnp.concatenate([dense, pltpu.roll(dense, MROW, 1)], axis=0)
        diag = sum_ref[NC * DENSE + block : NC * DENSE + block + 1, :]
        diag = pltpu.roll(diag + pltpu.roll(diag, MROW, 1), HALF, 1)
        lower = jnp.where(lane == row + HALF, diag, pltpu.roll(upper, HALF, 1))
        given = jnp.concatenate([upper, lower], axis=0)
        turned = jnp.concatenate([given, given], axis=0).T[:MROW]
        full_ref[block * MROW : (block + 1) * MROW, :] = jnp.where(held, given, turned)
    low = iota((NC, LANES), 1) < MROW
    for chunk in range(HALF):
        left = full_ref[pl.ds(2 * chunk, NC, stride=MROW), :]
        right = full_ref[pl.ds(2 * chunk + 1, NC, stride=MROW), :]
        out_ref[:, chunk * LANES : (chunk + 1) * LANES] = jnp.where(
            low, left, pltpu.roll(right, MROW, 1)
        )


ANY = pl.BlockSpec(memory_space=pl.ANY)
VMEM = pl.BlockSpec(memory_space=pltpu.VMEM)


def cost(flops, bytes_accessed):
    return pl.CostEstimate(flops=flops, bytes_accessed=bytes_accessed, transcendentals=0)


def params(limit):
    return pltpu.CompilerParams(vmem_limit_bytes=limit)


def around(block, axis):
    count = lax.axis_size(axis)
    return [block] + [
        lax.ppermute(block, axis, [(i, i ^ k) for i in range(count)]) for k in range(1, count)
    ]


def shards(
    trace_old,
    new_owner,
    mortar_tiles,
    mortar_owner,
    mortar_coarse,
    interior_rhs,
    local_inverse,
    coupling,
    connectivity,
):
    face_count = lax.axis_size("face")
    elem_count = lax.axis_size("elem")
    row_count = trace_old.shape[0]
    tile_count = mortar_tiles.shape[0]
    elements, modes = interior_rhs.shape
    trace = FACES_PER_ELEM * FACE_COEFFS
    capacity = max(2, 2 * row_count // face_count)
    own = face_count * capacity

    slots = own * elem_count
    devices = face_count * elem_count
    paired = face_count <= MOST_PAIRED
    sides = 2 if paired else 1

    blocks = face_count * NC
    sums_shape = (blocks * DENSE, LANES)
    placed, *half_grams = pl.pallas_call(
        functools.partial(gram_kernel, elem_count, face_count, capacity, paired),
        out_shape=[jax.ShapeDtypeStruct((slots, FACE_COEFFS), BF16)]
        + [jax.ShapeDtypeStruct((blocks * (DENSE + 1) // sides, LANES), BF16)] * sides,
        in_specs=[ANY] * 5,
        out_specs=[VMEM] * (1 + sides),
        scratch_shapes=[
            pltpu.SMEM((tile_count,), I32),
            pltpu.SMEM((tile_count,), I32),
            pltpu.VMEM(mortar_tiles.shape, BF16),
            pltpu.VMEM((tile_count * PITCH, LANES), F32),
            pltpu.VMEM(sums_shape, F32),
            pltpu.VMEM(sums_shape, F32),
            pltpu.VMEM((blocks, LANES), F32),
            pltpu.VMEM((blocks, LANES), F32),
            pltpu.VMEM((1, row_count), I32),
            pltpu.VMEM(trace_old.shape, BF16),
            pltpu.SemaphoreType.DMA((5,)),
        ],
        compiler_params=params(BIG),
        cost_estimate=cost(4 * tile_count * MROW * MROW * LANES, 12 << 20),
        name="gram",
    )(
        mortar_owner.reshape(tile_count),
        mortar_coarse,
        mortar_tiles,
        new_owner.reshape(1, row_count),
        trace_old,
    )
    if paired:
        came = lax.ppermute(half_grams[1], "face", [(i, i ^ 1) for i in range(face_count)])
    table = lax.all_to_all(
        placed.reshape(devices, capacity, FACE_COEFFS), ("face", "elem"), 0, 0, tiled=True
    ).reshape(slots, FACE_COEFFS)

    if paired:
        joined = pl.pallas_call(
            join_kernel,
            out_shape=[jax.ShapeDtypeStruct((OWNER_ROWS, LANES), BF16)] * (face_count // 2),
            in_specs=[VMEM] * 2,
            out_specs=[VMEM] * (face_count // 2),
            compiler_params=params(SMALL),
            cost_estimate=cost(0, 4 << 20),
            name="join",
        )(half_grams[0], came)
        got = [joined[0]] + [
            lax.ppermute(joined[k], "face", [(i, i ^ (2 * k)) for i in range(face_count)])
            for k in range(1, face_count // 2)
        ]
        before = joined[0]
    else:
        blocked = half_grams[0].reshape(face_count, OWNER_ROWS, LANES)
        got = [lax.all_to_all(blocked, "face", 0, 0, tiled=True).reshape(-1, LANES)]
        before = half_grams[0]

    rhs, _ = lax.optimization_barrier((interior_rhs, before))
    schur_blocks, shares, left = pl.pallas_call(
        functools.partial(main_kernel, elem_count, face_count),
        out_shape=(
            jax.ShapeDtypeStruct((elements, trace, trace), BF16),
            jax.ShapeDtypeStruct((SHARE_ROWS, LANES), BF16),
            jax.ShapeDtypeStruct((own, FACE_COEFFS), F32),
        ),
        in_specs=[ANY] * 5,
        out_specs=(ANY, VMEM, VMEM),
        scratch_shapes=[
            pltpu.SMEM((FACES_PER_ELEM, elements), I32),
            pltpu.VMEM((elements, modes), BF16),
            pltpu.VMEM((slots, FACE_COEFFS), BF16),
            pltpu.VMEM((elements, modes, modes), BF16),
            pltpu.VMEM((elements, modes, trace), BF16),
            pltpu.VMEM((elements, trace, trace), BF16),
            pltpu.VMEM((LANES, modes), F32),
            pltpu.VMEM((modes, LANES), BF16),
            pltpu.VMEM((PER_FACE, trace + LANES), F32),
            pltpu.VMEM((trace, LANES), F32),
            pltpu.VMEM((trace, modes), BF16),
            pltpu.VMEM((trace, modes), BF16),
            pltpu.VMEM((trace, modes), BF16),
            pltpu.VMEM((trace, modes), BF16),
            pltpu.SemaphoreType.DMA((3,)),
            pltpu.SemaphoreType.DMA((2, elements)),
            pltpu.SemaphoreType.DMA((elements,)),
        ],
        compiler_params=params(BIG),
        cost_estimate=cost(
            2 * elements * modes * trace * (modes + trace),
            2 * elements * (modes * (modes + trace) + trace * trace),
        ),
        name="condense",
    )(table, connectivity.T, rhs, local_inverse, coupling)

    all_shares = around(shares, "elem")
    coarse_blocks = pl.pallas_call(
        coarse_kernel,
        out_shape=jax.ShapeDtypeStruct((NC, MROW * MROW), F32),
        in_specs=[VMEM] * len(got),
        out_specs=VMEM,
        scratch_shapes=[
            pltpu.VMEM((OWNER_ROWS, LANES), F32),
            pltpu.VMEM((NC * MROW, LANES), F32),
        ],
        compiler_params=params(SMALL),
        cost_estimate=cost(0, 8 << 20),
        name="coarse",
    )(*got)
    left, coarse_blocks = lax.optimization_barrier((left, coarse_blocks))
    slot_residual = pl.pallas_call(
        residual_kernel,
        out_shape=jax.ShapeDtypeStruct((own, FACE_COEFFS), F32),
        in_specs=[VMEM] * elem_count,
        out_specs=VMEM,
        compiler_params=params(SMALL),
        name="residual",
    )(left, *all_shares[1:])
    return schur_blocks, slot_residual, coarse_blocks


def solution(mesh):
    return jax.shard_map(
        shards,
        mesh=mesh,
        in_specs=(
            P(("face", "elem"), None),
            P(("face", "elem"), None),
            P(("face", "elem"), None),
            P(("face", "elem"), None),
            P(("face", "elem")),
            P(("face", "elem"), None),
            P(("face", "elem"), None, None),
            P(("face", "elem"), None, None),
            P(("face", "elem"), None),
        ),
        out_specs=(
            P(("face", "elem"), None, None),
            P(("face", "elem"), None),
            P(("face", "elem"), None),
        ),
        check_vma=False,
    )
```

```python
import functools

import jax
import jax.numpy as jnp
from jax import lax
from jax.experimental import pallas as pl
from jax.experimental.pallas import tpu as pltpu
from jax.sharding import PartitionSpec as P

FACE_COEFFS = 128
FACES_PER_ELEM = 3
MROW = 64
MCOL = 96
NC = 16
HALF = MROW // 2
LANES = 128
DENSE = HALF * MROW // LANES
OWNER_ROWS = NC * (DENSE + 1)
PER_FACE = 16
NAMED = FACES_PER_ELEM * PER_FACE
SHARE_ROWS = NAMED + 16
SLOT_BASE = 16
CHUNK = 16
MOST_PAIRED = 8
BIG = 62 << 20
SMALL = 12 << 20
PITCH = MROW + 8

BF16 = jnp.bfloat16
F32 = jnp.float32
I32 = jnp.int32

NT = (((1,), (1,)), ((), ()))
TN = (((0,), (0,)), ((), ()))


def iota(shape, dim):
    return lax.broadcasted_iota(I32, shape, dim)


def dot(left, right, dims=(((1,), (0,)), ((), ()))):
    return lax.dot_general(left, right, dims, preferred_element_type=F32)


def divided(value, by):
    shift = by.bit_length() - 1
    assert by == 1 << shift
    return value >> shift, value & (by - 1)


def place_rows(elem_count, face_count, capacity, owners, trace, slots):
    rows = owners.shape[1]
    earlier = (iota((rows, rows), 0) < iota((rows, rows), 1)).astype(BF16)
    hot = (iota((face_count, rows), 0) == owners).astype(F32)
    rank = jnp.sum(hot * dot(hot.astype(BF16), earlier), axis=0, keepdims=True).astype(I32)
    slot = iota((slots, rows), 0)
    wanted = divided(slot, elem_count * capacity)[0] * capacity + divided(slot, capacity)[1]
    place = (wanted == owners * capacity + rank).astype(BF16)
    return dot(place, trace).astype(BF16)


def turn_rhs(rhs_ref, wide_ref, rhs_turned_ref):
    wide_ref[...] = jnp.zeros_like(wide_ref)
    wide_ref[0 : rhs_ref.shape[0], :] = rhs_ref[...].astype(F32)
    rhs_turned_ref[...] = wide_ref[...].T.astype(BF16)


def gram_kernel(
    elem_count,
    face_count,
    capacity,
    paired,
    owner_hbm,
    coarse_hbm,
    tiles_hbm,
    new_owner_hbm,
    trace_hbm,
    placed_ref,
    *refs,
):
    out_refs, refs = refs[:-11], refs[-11:]
    owner_ref, coarse_ref, tiles_ref, rows_ref = refs[:4]
    accs, diags = refs[4:6], refs[6:8]
    new_owner_ref, trace_ref, sems = refs[8:]

    def place_of(owner):
        if not paired:
            return owner
        other = owner ^ lax.axis_index("face")
        bits = face_count.bit_length() - 1
        return sum(((other >> k) & 1) << (bits - 1 - k) for k in range(bits))

    tiles = tiles_ref.shape[0]
    copies = [
        pltpu.make_async_copy(owner_hbm, owner_ref, sems.at[0]),
        pltpu.make_async_copy(coarse_hbm, coarse_ref, sems.at[1]),
        pltpu.make_async_copy(new_owner_hbm, new_owner_ref, sems.at[2]),
        pltpu.make_async_copy(trace_hbm, trace_ref, sems.at[3]),
        pltpu.make_async_copy(tiles_hbm, tiles_ref, sems.at[4]),
    ]
    for copy in copies:
        copy.start()
    for ref in (*accs, *diags):
        ref[...] = jnp.zeros_like(ref)
    for copy in copies:
        copy.wait()
    placed_ref[...] = place_rows(
        elem_count, face_count, capacity, new_owner_ref[...], trace_ref[...], placed_ref.shape[0]
    )

    lane = iota((CHUNK, LANES), 1)
    inside = lane < MCOL
    row = iota((HALF, LANES), 0)
    column = divided(iota((HALF, LANES), 1), MROW)[1]
    swapped = (column > row) & (column < HALF)
    diagonal = column == row
    low = iota((DENSE, LANES), 1) < MROW
    low_wide = iota((MROW, LANES), 1) < MROW
    low_row = iota((1, LANES), 1) < MROW

    for chunk in range(tiles // CHUNK):
        first_tile = chunk * CHUNK
        for group in range(MROW // 4):
            base = group * 3 * LANES
            one, two, three = (
                tiles_ref[
                    first_tile : first_tile + CHUNK, base + k * LANES : base + (k + 1) * LANES
                ].astype(F32)
                for k in range(3)
            )
            rolled = (
                one,
                pltpu.roll(jnp.where(lane < 64, two, one), 32, 1),
                pltpu.roll(jnp.where(lane < 32, three, two), 64, 1),
                pltpu.roll(three, 96, 1),
            )
            for k in range(4):
                rows_ref[pl.ds(first_tile * PITCH + 4 * group + k, CHUNK, stride=PITCH), :] = (
                    jnp.where(inside, rolled[k], 0.0)
                )
        for tile in range(first_tile, first_tile + CHUNK, 2):
            both = jnp.concatenate(
                [
                    rows_ref[t * PITCH : t * PITCH + MROW, :].astype(BF16)
                    for t in (tile, tile + 1)
                ],
                axis=0,
            )
            gram = dot(both, both, NT)
            side = jnp.where(low_wide, gram[:MROW], gram[MROW:])
            lower = pltpu.roll(side[HALF:], LANES - HALF, 1)
            packed = jnp.where(swapped, lower, side[:HALF])
            diag = jnp.sum(jnp.where(diagonal, lower, 0.0), axis=0, keepdims=True)
            turned = pltpu.roll(packed, MROW, 1)
            dense = (
                jnp.where(low, packed[:DENSE], turned[DENSE:]),
                jnp.where(low, turned[:DENSE], packed[DENSE:]),
            )
            own = (jnp.where(low_row, diag, 0.0), jnp.where(low_row, 0.0, diag))
            for k in range(2):
                block = place_of(owner_ref[tile + k]) * NC + coarse_ref[tile + k]
                here = pl.ds(pl.multiple_of(block * DENSE, DENSE), DENSE)
                accs[k][here, :] += dense[k]
                diags[k][pl.ds(block, 1), :] += own[k]
    size = NC * DENSE
    each = face_count // len(out_refs)
    for owner in range(face_count):
        out_ref, start = out_refs[owner // each], owner % each * OWNER_ROWS
        here = slice(owner * size, (owner + 1) * size)
        out_ref[start : start + size, :] = (accs[0][here, :] + accs[1][here, :]).astype(BF16)
        here = slice(owner * NC, (owner + 1) * NC)
        out_ref[start + size : start + size + NC, :] = (
            diags[0][here, :] + diags[1][here, :]
        ).astype(BF16)


def join_kernel(kept_ref, came_ref, keep_ref, send_ref):
    half = keep_ref.shape[0]
    for out_ref, here in ((keep_ref, slice(0, half)), (send_ref, slice(half, 2 * half))):
        total = kept_ref[here, :].astype(F32) + came_ref[here, :].astype(F32)
        out_ref[...] = total.astype(BF16)


def main_kernel(
    rhs_hbm,
    inverse_hbm,
    coupling_hbm,
    schur_hbm,
    solved_ref,
    rhs_ref,
    inverse_ref,
    coupling_ref,
    schur_ref,
    wide_ref,
    rhs_turned_ref,
    turned_a_ref,
    turned_b_ref,
    product_a_ref,
    product_b_ref,
    small_sem,
    block_sems,
    schur_sems,
):
    elements = rhs_ref.shape[0]
    trace = FACES_PER_ELEM * FACE_COEFFS
    wide_lane = iota((trace, LANES), 1)
    small = pltpu.make_async_copy(rhs_hbm, rhs_ref, small_sem)

    def coupling_copy(e):
        return pltpu.make_async_copy(coupling_hbm.at[e], coupling_ref.at[e], block_sems.at[0, e])

    def inverse_copy(e):
        return pltpu.make_async_copy(inverse_hbm.at[e], inverse_ref.at[e], block_sems.at[1, e])

    def leave(e):
        return pltpu.make_async_copy(schur_ref.at[e], schur_hbm.at[e], schur_sems.at[e])

    coupling_copy(0).start()
    small.start()
    inverse_copy(0).start()
    coupling_copy(1).start()
    inverse_copy(1).start()
    coupling_copy(2).start()

    def turn(e, turned_ref):
        turned_ref[...] = coupling_ref[e].T

    def first(e, turned_ref, product_ref):
        product_ref[...] = dot(turned_ref[...], inverse_ref[e]).astype(BF16)

    def second(e, product_ref):
        wide = jnp.concatenate([coupling_ref[e], rhs_turned_ref[...]], axis=1)
        condensed = dot(product_ref[...], wide)
        schur_ref[e] = (-condensed[:, :trace]).astype(BF16)
        solved_ref[...] = jnp.where(wide_lane == e, condensed[:, trace:], solved_ref[...])

    turned = (turned_a_ref, turned_b_ref)
    product = (product_a_ref, product_b_ref)

    def advance(e, parity, turning=True, finishing=True):
        if turning:

            @pl.when(e + 2 < elements)
            def _():
                inverse_copy(e + 2).start()

            @pl.when(e + 3 < elements)
            def _():
                coupling_copy(e + 3).start()

            coupling_copy(e + 1).wait()
        inverse_copy(e).wait()
        if turning:
            turn(e + 1, turned[1 - parity])
        first(e, turned[parity], product[parity])
        if finishing:
            second(e - 1, product[1 - parity])
            leave(e - 1).start()

    solved_ref[...] = jnp.zeros_like(solved_ref)
    coupling_copy(0).wait()
    small.wait()
    turn(0, turned[0])
    turn_rhs(rhs_ref, wide_ref, rhs_turned_ref)
    advance(0, 0, finishing=False)

    def two(index, carry):
        advance(2 * index + 1, 1)
        advance(2 * index + 2, 0)
        return carry

    pairs = (elements - 2) // 2
    lax.fori_loop(0, pairs, two, 0)
    for e in range(2 * pairs + 1, elements):
        advance(e, e % 2, turning=e + 1 < elements)
    second(elements - 1, product[(elements - 1) % 2])
    leave(elements - 1).start()
    for e in range(elements):
        leave(e).wait()


def share_kernel(
    elem_count,
    face_count,
    table_hbm,
    conn_hbm,
    schur_hbm,
    solved_hbm,
    share_ref,
    left_ref,
    table_ref,
    conn_ref,
    schur_ref,
    vector_ref,
    sum_ref,
    sems,
    schur_sems,
):
    elements = schur_ref.shape[0]
    trace = FACES_PER_ELEM * FACE_COEFFS
    slots = table_ref.shape[0]
    own = left_ref.shape[0]
    capacity = own // face_count
    my_elem = lax.axis_index("elem")
    copies = [
        pltpu.make_async_copy(conn_hbm, conn_ref, sems.at[0]),
        pltpu.make_async_copy(table_hbm, table_ref, sems.at[1]),
        pltpu.make_async_copy(solved_hbm, sum_ref, sems.at[2]),
    ]
    parts = [
        pltpu.make_async_copy(schur_hbm.at[e], schur_ref.at[e], schur_sems.at[e])
        for e in range(elements)
    ]
    for copy in copies + parts:
        copy.start()
    copies[0].wait()

    row = iota((PER_FACE, LANES), 0)
    lane = iota((PER_FACE, LANES), 1)
    first_lane = iota((1, LANES), 1)
    wide_lane = iota((trace, LANES), 1)

    def position(elem, inner):
        face, rank = divided(inner, capacity)
        return (face * elem_count + elem) * capacity + rank

    high = jnp.full((1, LANES), -1, I32)
    rest = jnp.zeros((1, LANES), I32)
    hots = []
    for a in range(FACES_PER_ELEM):
        positions = jnp.full((PER_FACE, LANES), -1, I32)
        for e in range(elements):
            slot = conn_ref[a, e]
            positions = jnp.where(row == e, position(*divided(slot, own)), positions)
            here = first_lane == a * PER_FACE + e
            quotient, remainder = divided(slot, SLOT_BASE)
            high = jnp.where(here, quotient, high)
            rest = jnp.where(here, remainder, rest)
        hot = jnp.concatenate([positions == lane + k for k in range(0, slots, LANES)], axis=1)
        hots.append(hot.astype(BF16))
    names = jnp.where(row == 0, high, jnp.where(row == 1, rest, 0))
    share_ref[NAMED:, :] = names.astype(F32).astype(BF16)
    place = position(my_elem, iota((own, slots), 0))
    pick = (iota((own, slots), 1) == place).astype(BF16)
    for copy in copies[1:]:
        copy.wait()
    for a, hot in enumerate(hots):
        vector_ref[:, a * LANES : (a + 1) * LANES] = dot(hot, table_ref[...])
    left_ref[...] = dot(pick, table_ref[...])

    columns = sum_ref[...]
    for e in range(elements):
        parts[e].wait()
        total = sum(
            schur_ref[e, :, a * LANES : (a + 1) * LANES].astype(F32)
            * vector_ref[e : e + 1, a * LANES : (a + 1) * LANES]
            for a in range(FACES_PER_ELEM)
        )
        sums = jnp.sum(total, axis=1, keepdims=True)
        columns = jnp.where(wide_lane == e, columns + sums, columns)
    for a in range(FACES_PER_ELEM):
        shares = columns[a * LANES : (a + 1) * LANES, :].T
        share_ref[a * PER_FACE : (a + 1) * PER_FACE, :] = shares[:PER_FACE].astype(BF16)
    left_ref[...] = less_shares(left_ref[...], share_ref)


def less_shares(left, share_ref):
    own = left.shape[0]
    slot = (iota((own, SHARE_ROWS), 0) + lax.axis_index("elem") * own).astype(F32)
    names = share_ref[NAMED:, :].astype(F32)
    named = (names[0:1] * SLOT_BASE + names[1:2])[:, :SHARE_ROWS]
    return left - dot((slot == named).astype(BF16), share_ref[...])


def residual_kernel(left_ref, *refs):
    share_refs, residual_ref = refs[:-1], refs[-1]
    left = left_ref[...]
    for share_ref in share_refs:
        left = less_shares(left, share_ref)
    residual_ref[...] = left


def coarse_kernel(*refs):
    got_refs, (out_ref, sum_ref, full_ref) = refs[:-3], refs[-3:]
    sum_ref[...] = sum(
        got_ref[k : k + OWNER_ROWS, :].astype(F32)
        for got_ref in got_refs
        for k in range(0, got_ref.shape[0], OWNER_ROWS)
    )

    lane = iota((HALF, LANES), 1)
    row = iota((HALF, LANES), 0)
    wide_row = iota((MROW, LANES), 0)
    wide_lane = iota((MROW, LANES), 1)
    top = wide_row < HALF
    held = (top & ((wide_lane <= wide_row) | (wide_lane >= HALF))) | (
        (~top) & (wide_lane >= wide_row)
    )
    for block in range(NC):
        dense = sum_ref[block * DENSE : (block + 1) * DENSE, :]
        upper = jnp.concatenate([dense, pltpu.roll(dense, MROW, 1)], axis=0)
        diag = sum_ref[NC * DENSE + block : NC * DENSE + block + 1, :]
        diag = pltpu.roll(diag + pltpu.roll(diag, MROW, 1), HALF, 1)
        lower = jnp.where(lane == row + HALF, diag, pltpu.roll(upper, HALF, 1))
        given = jnp.concatenate([upper, lower], axis=0)
        turned = jnp.concatenate([given, given], axis=0).T[:MROW]
        full_ref[block * MROW : (block + 1) * MROW, :] = jnp.where(held, given, turned)
    low = iota((NC, LANES), 1) < MROW
    for chunk in range(HALF):
        left = full_ref[pl.ds(2 * chunk, NC, stride=MROW), :]
        right = full_ref[pl.ds(2 * chunk + 1, NC, stride=MROW), :]
        out_ref[:, chunk * LANES : (chunk + 1) * LANES] = jnp.where(
            low, left, pltpu.roll(right, MROW, 1)
        )


ANY = pl.BlockSpec(memory_space=pl.ANY)
VMEM = pl.BlockSpec(memory_space=pltpu.VMEM)


def cost(flops, bytes_accessed):
    return pl.CostEstimate(flops=flops, bytes_accessed=bytes_accessed, transcendentals=0)


def params(limit):
    return pltpu.CompilerParams(vmem_limit_bytes=limit)


def around(block, axis):
    count = lax.axis_size(axis)
    return [block] + [
        lax.ppermute(block, axis, [(i, i ^ k) for i in range(count)]) for k in range(1, count)
    ]


def trade(block, distance):
    count = lax.axis_size("face")
    return lax.ppermute(block, "face", [(i, i ^ distance) for i in range(count)])


def join(kept, came):
    half = jax.ShapeDtypeStruct((kept.shape[0] // 2, LANES), BF16)
    return pl.pallas_call(
        join_kernel,
        out_shape=(half, half),
        in_specs=[VMEM] * 2,
        out_specs=(VMEM, VMEM),
        compiler_params=params(SMALL),
        cost_estimate=cost(0, 4 << 20),
        name="join",
    )(kept, came)


def shards(
    trace_old,
    new_owner,
    mortar_tiles,
    mortar_owner,
    mortar_coarse,
    interior_rhs,
    local_inverse,
    coupling,
    connectivity,
):
    face_count = lax.axis_size("face")
    elem_count = lax.axis_size("elem")
    row_count = trace_old.shape[0]
    tile_count = mortar_tiles.shape[0]
    elements, modes = interior_rhs.shape
    trace = FACES_PER_ELEM * FACE_COEFFS
    capacity = max(2, 2 * row_count // face_count)
    own = face_count * capacity

    slots = own * elem_count
    devices = face_count * elem_count
    paired = face_count <= MOST_PAIRED
    sides = 2 if paired else 1

    blocks = face_count * NC
    sums_shape = (blocks * DENSE, LANES)
    placed, *half_grams = pl.pallas_call(
        functools.partial(gram_kernel, elem_count, face_count, capacity, paired),
        out_shape=[jax.ShapeDtypeStruct((slots, FACE_COEFFS), BF16)]
        + [jax.ShapeDtypeStruct((blocks * (DENSE + 1) // sides, LANES), BF16)] * sides,
        in_specs=[ANY] * 5,
        out_specs=[VMEM] * (1 + sides),
        scratch_shapes=[
            pltpu.SMEM((tile_count,), I32),
            pltpu.SMEM((tile_count,), I32),
            pltpu.VMEM(mortar_tiles.shape, BF16),
            pltpu.VMEM((tile_count * PITCH, LANES), F32),
            pltpu.VMEM(sums_shape, F32),
            pltpu.VMEM(sums_shape, F32),
            pltpu.VMEM((blocks, LANES), F32),
            pltpu.VMEM((blocks, LANES), F32),
            pltpu.VMEM((1, row_count), I32),
            pltpu.VMEM(trace_old.shape, BF16),
            pltpu.SemaphoreType.DMA((5,)),
        ],
        compiler_params=params(BIG),
        cost_estimate=cost(4 * tile_count * MROW * MROW * LANES, 12 << 20),
        name="gram",
    )(
        mortar_owner.reshape(tile_count),
        mortar_coarse,
        mortar_tiles,
        new_owner.reshape(1, row_count),
        trace_old,
    )
    if paired:
        kept, came = half_grams[0], trade(half_grams[1], 1)
    table = lax.all_to_all(
        placed.reshape(devices, capacity, FACE_COEFFS), ("face", "elem"), 0, 0, tiled=True
    ).reshape(slots, FACE_COEFFS)

    if not paired:
        blocked = half_grams[0].reshape(face_count, OWNER_ROWS, LANES)
        got = [lax.all_to_all(blocked, "face", 0, 0, tiled=True).reshape(-1, LANES)]

    rhs, _ = lax.optimization_barrier((interior_rhs, half_grams[0]))
    schur_blocks, solved = pl.pallas_call(
        main_kernel,
        out_shape=(
            jax.ShapeDtypeStruct((elements, trace, trace), BF16),
            jax.ShapeDtypeStruct((trace, LANES), F32),
        ),
        in_specs=[ANY] * 3,
        out_specs=(ANY, VMEM),
        scratch_shapes=[
            pltpu.VMEM((elements, modes), BF16),
            pltpu.VMEM((elements, modes, modes), BF16),
            pltpu.VMEM((elements, modes, trace), BF16),
            pltpu.VMEM((elements, trace, trace), BF16),
            pltpu.VMEM((LANES, modes), F32),
            pltpu.VMEM((modes, LANES), BF16),
            pltpu.VMEM((trace, modes), BF16),
            pltpu.VMEM((trace, modes), BF16),
            pltpu.VMEM((trace, modes), BF16),
            pltpu.VMEM((trace, modes), BF16),
            pltpu.SemaphoreType.DMA,
            pltpu.SemaphoreType.DMA((2, elements)),
            pltpu.SemaphoreType.DMA((elements,)),
        ],
        compiler_params=params(BIG),
        cost_estimate=cost(
            2 * elements * modes * trace * (modes + trace),
            2 * elements * (modes * (modes + trace) + trace * trace),
        ),
        name="condense",
    )(rhs, local_inverse, coupling)

    names = connectivity.T
    if paired and face_count > 2:
        kept, _ = lax.optimization_barrier((kept, solved))
        kept, sent = join(kept, came)
        came = trade(sent, 2)
        names, kept = lax.optimization_barrier((names, kept))
    shares, left = pl.pallas_call(
        functools.partial(share_kernel, elem_count, face_count),
        out_shape=(
            jax.ShapeDtypeStruct((SHARE_ROWS, LANES), BF16),
            jax.ShapeDtypeStruct((own, FACE_COEFFS), F32),
        ),
        in_specs=[ANY] * 4,
        out_specs=(VMEM, VMEM),
        scratch_shapes=[
            pltpu.VMEM((slots, FACE_COEFFS), BF16),
            pltpu.SMEM((FACES_PER_ELEM, elements), I32),
            pltpu.VMEM((elements, trace, trace), BF16),
            pltpu.VMEM((PER_FACE, trace), F32),
            pltpu.VMEM((trace, LANES), F32),
            pltpu.SemaphoreType.DMA((3,)),
            pltpu.SemaphoreType.DMA((elements,)),
        ],
        compiler_params=params(BIG),
        cost_estimate=cost(0, 8 << 20),
        name="share",
    )(table, names, schur_blocks, solved)

    if paired:
        for distance in (1 << k for k in range(2, face_count.bit_length() - 1)):
            kept, _ = lax.optimization_barrier((kept, shares))
            kept, sent = join(kept, came)
            came = trade(sent, distance)
        got = [kept, came]

    all_shares = around(shares, "elem")
    slot_residual = pl.pallas_call(
        residual_kernel,
        out_shape=jax.ShapeDtypeStruct((own, FACE_COEFFS), F32),
        in_specs=[VMEM] * elem_count,
        out_specs=VMEM,
        compiler_params=params(SMALL),
        name="residual",
    )(left, *all_shares[1:])

    first, slot_residual = lax.optimization_barrier((got[0], slot_residual))
    coarse_blocks = pl.pallas_call(
        coarse_kernel,
        out_shape=jax.ShapeDtypeStruct((NC, MROW * MROW), F32),
        in_specs=[VMEM] * len(got),
        out_specs=VMEM,
        scratch_shapes=[
            pltpu.VMEM((OWNER_ROWS, LANES), F32),
            pltpu.VMEM((NC * MROW, LANES), F32),
        ],
        compiler_params=params(SMALL),
        cost_estimate=cost(0, 8 << 20),
        name="coarse",
    )(first, *got[1:])
    return schur_blocks, slot_residual, coarse_blocks


def solution(mesh):
    return jax.shard_map(
        shards,
        mesh=mesh,
        in_specs=(
            P(("face", "elem"), None),
            P(("face", "elem"), None),
            P(("face", "elem"), None),
            P(("face", "elem"), None),
            P(("face", "elem")),
            P(("face", "elem"), None),
            P(("face", "elem"), None, None),
            P(("face", "elem"), None, None),
            P(("face", "elem"), None),
        ),
        out_specs=(
            P(("face", "elem"), None, None),
            P(("face", "elem"), None),
            P(("face", "elem"), None),
        ),
        check_vma=False,
    )
```

```python
import functools

import jax
import jax.numpy as jnp
from jax import lax
from jax.experimental import pallas as pl
from jax.experimental.pallas import tpu as pltpu
from jax.sharding import PartitionSpec as P

FACE_COEFFS = 128
FACES_PER_ELEM = 3
MROW = 64
MCOL = 96
NC = 16
HALF = MROW // 2
LANES = 128
DENSE = HALF * MROW // LANES
OWNER_ROWS = NC * (DENSE + 1)
PER_FACE = 16
NAMED = FACES_PER_ELEM * PER_FACE
SHARE_ROWS = NAMED + 16
SLOT_BASE = 16
CHUNK = 16
MOST_PAIRED = 8
BIG = 62 << 20
SMALL = 12 << 20
PITCH = MROW + 8

BF16 = jnp.bfloat16
F32 = jnp.float32
I32 = jnp.int32

NT = (((1,), (1,)), ((), ()))
TN = (((0,), (0,)), ((), ()))


def iota(shape, dim):
    return lax.broadcasted_iota(I32, shape, dim)


def dot(left, right, dims=(((1,), (0,)), ((), ()))):
    return lax.dot_general(left, right, dims, preferred_element_type=F32)


def divided(value, by):
    shift = by.bit_length() - 1
    assert by == 1 << shift
    return value >> shift, value & (by - 1)


def place_rows(elem_count, face_count, capacity, owners, trace, slots):
    rows = owners.shape[1]
    earlier = (iota((rows, rows), 0) < iota((rows, rows), 1)).astype(BF16)
    hot = (iota((face_count, rows), 0) == owners).astype(F32)
    rank = jnp.sum(hot * dot(hot.astype(BF16), earlier), axis=0, keepdims=True).astype(I32)
    slot = iota((slots, rows), 0)
    wanted = divided(slot, elem_count * capacity)[0] * capacity + divided(slot, capacity)[1]
    place = (wanted == owners * capacity + rank).astype(BF16)
    return dot(place, trace).astype(BF16)


def turn_rhs(rhs_ref, wide_ref, rhs_turned_ref):
    wide_ref[...] = jnp.zeros_like(wide_ref)
    wide_ref[0 : rhs_ref.shape[0], :] = rhs_ref[...].astype(F32)
    rhs_turned_ref[...] = wide_ref[...].T.astype(BF16)


def gram_kernel(
    elem_count,
    face_count,
    capacity,
    paired,
    owner_hbm,
    coarse_hbm,
    tiles_hbm,
    new_owner_hbm,
    trace_hbm,
    placed_ref,
    *refs,
):
    out_refs, refs = refs[:-11], refs[-11:]
    owner_ref, coarse_ref, tiles_ref, rows_ref = refs[:4]
    accs, diags = refs[4:6], refs[6:8]
    new_owner_ref, trace_ref, sems = refs[8:]

    def place_of(owner):
        if not paired:
            return owner
        other = owner ^ lax.axis_index("face")
        bits = face_count.bit_length() - 1
        odd = lax.axis_index("elem") & 1
        place = [(other >> k) & 1 for k in range(bits)]
        if bits > 1:
            place[:2] = (jnp.where(odd == 1, place[1 - k], place[k]) for k in range(2))
        return sum(bit << (bits - 1 - k) for k, bit in enumerate(place))

    tiles = tiles_ref.shape[0]
    copies = [
        pltpu.make_async_copy(owner_hbm, owner_ref, sems.at[0]),
        pltpu.make_async_copy(coarse_hbm, coarse_ref, sems.at[1]),
        pltpu.make_async_copy(new_owner_hbm, new_owner_ref, sems.at[2]),
        pltpu.make_async_copy(trace_hbm, trace_ref, sems.at[3]),
        pltpu.make_async_copy(tiles_hbm, tiles_ref, sems.at[4]),
    ]
    for copy in copies:
        copy.start()
    for ref in (*accs, *diags):
        ref[...] = jnp.zeros_like(ref)
    for copy in copies:
        copy.wait()
    placed_ref[...] = place_rows(
        elem_count, face_count, capacity, new_owner_ref[...], trace_ref[...], placed_ref.shape[0]
    )

    lane = iota((CHUNK, LANES), 1)
    inside = lane < MCOL
    row = iota((HALF, LANES), 0)
    column = divided(iota((HALF, LANES), 1), MROW)[1]
    swapped = (column > row) & (column < HALF)
    diagonal = column == row
    low = iota((DENSE, LANES), 1) < MROW
    low_wide = iota((MROW, LANES), 1) < MROW
    low_row = iota((1, LANES), 1) < MROW

    for chunk in range(tiles // CHUNK):
        first_tile = chunk * CHUNK
        for group in range(MROW // 4):
            base = group * 3 * LANES
            one, two, three = (
                tiles_ref[
                    first_tile : first_tile + CHUNK, base + k * LANES : base + (k + 1) * LANES
                ].astype(F32)
                for k in range(3)
            )
            rolled = (
                one,
                pltpu.roll(jnp.where(lane < 64, two, one), 32, 1),
                pltpu.roll(jnp.where(lane < 32, three, two), 64, 1),
                pltpu.roll(three, 96, 1),
            )
            for k in range(4):
                rows_ref[pl.ds(first_tile * PITCH + 4 * group + k, CHUNK, stride=PITCH), :] = (
                    jnp.where(inside, rolled[k], 0.0)
                )
        for tile in range(first_tile, first_tile + CHUNK, 2):
            both = jnp.concatenate(
                [
                    rows_ref[t * PITCH : t * PITCH + MROW, :].astype(BF16)
                    for t in (tile, tile + 1)
                ],
                axis=0,
            )
            gram = dot(both, both, NT)
            side = jnp.where(low_wide, gram[:MROW], gram[MROW:])
            lower = pltpu.roll(side[HALF:], LANES - HALF, 1)
            packed = jnp.where(swapped, lower, side[:HALF])
            diag = jnp.sum(jnp.where(diagonal, lower, 0.0), axis=0, keepdims=True)
            turned = pltpu.roll(packed, MROW, 1)
            dense = (
                jnp.where(low, packed[:DENSE], turned[DENSE:]),
                jnp.where(low, turned[:DENSE], packed[DENSE:]),
            )
            own = (jnp.where(low_row, diag, 0.0), jnp.where(low_row, 0.0, diag))
            for k in range(2):
                block = place_of(owner_ref[tile + k]) * NC + coarse_ref[tile + k]
                here = pl.ds(pl.multiple_of(block * DENSE, DENSE), DENSE)
                accs[k][here, :] += dense[k]
                diags[k][pl.ds(block, 1), :] += own[k]
    size = NC * DENSE
    each = face_count // len(out_refs)
    for owner in range(face_count):
        out_ref, start = out_refs[owner // each], owner % each * OWNER_ROWS
        here = slice(owner * size, (owner + 1) * size)
        out_ref[start : start + size, :] = (accs[0][here, :] + accs[1][here, :]).astype(BF16)
        here = slice(owner * NC, (owner + 1) * NC)
        out_ref[start + size : start + size + NC, :] = (
            diags[0][here, :] + diags[1][here, :]
        ).astype(BF16)


def join_kernel(kept_ref, came_ref, keep_ref, send_ref):
    half = keep_ref.shape[0]
    for out_ref, here in ((keep_ref, slice(0, half)), (send_ref, slice(half, 2 * half))):
        total = kept_ref[here, :].astype(F32) + came_ref[here, :].astype(F32)
        out_ref[...] = total.astype(BF16)


def main_kernel(
    elem_count,
    face_count,
    table_hbm,
    conn_hbm,
    rhs_hbm,
    inverse_hbm,
    coupling_hbm,
    schur_hbm,
    share_ref,
    left_ref,
    conn_ref,
    rhs_ref,
    table_ref,
    inverse_ref,
    coupling_ref,
    schur_ref,
    wide_ref,
    rhs_turned_ref,
    vector_ref,
    sum_ref,
    turned_a_ref,
    turned_b_ref,
    product_a_ref,
    product_b_ref,
    small_sems,
    block_sems,
    schur_sems,
):
    elements = rhs_ref.shape[0]
    modes = rhs_ref.shape[1]
    trace = FACES_PER_ELEM * FACE_COEFFS
    slots = table_ref.shape[0]
    own = left_ref.shape[0]
    capacity = own // face_count
    my_elem = lax.axis_index("elem")
    small = [
        pltpu.make_async_copy(rhs_hbm, rhs_ref, small_sems.at[0]),
        pltpu.make_async_copy(conn_hbm, conn_ref, small_sems.at[1]),
        pltpu.make_async_copy(table_hbm, table_ref, small_sems.at[2]),
    ]

    def coupling_copy(e):
        return pltpu.make_async_copy(coupling_hbm.at[e], coupling_ref.at[e], block_sems.at[0, e])

    def inverse_copy(e):
        return pltpu.make_async_copy(inverse_hbm.at[e], inverse_ref.at[e], block_sems.at[1, e])

    def leave(e):
        return pltpu.make_async_copy(schur_ref.at[e], schur_hbm.at[e], schur_sems.at[e])

    coupling_copy(0).start()
    for copy in small:
        copy.start()
    inverse_copy(0).start()
    coupling_copy(1).start()
    inverse_copy(1).start()
    coupling_copy(2).start()

    def turn(e, turned_ref):
        turned_ref[...] = coupling_ref[e].T

    def first(e, turned_ref, product_ref):
        for half in range(2):
            here = slice(half * modes // 2, (half + 1) * modes // 2)
            product_ref[:, here] = dot(turned_ref[...], inverse_ref[e, :, here]).astype(BF16)

    def second(e, product_ref):
        split = 2 * LANES
        one = dot(product_ref[...], coupling_ref[e, :, :split])
        wide = jnp.concatenate([coupling_ref[e, :, split:], rhs_turned_ref[...]], axis=1)
        two = dot(product_ref[...], wide)
        schur_ref[e, :, :split] = (-one).astype(BF16)
        schur_ref[e, :, split:] = (-two[:, : trace - split]).astype(BF16)
        vector = vector_ref[pl.ds(e, 1), :]
        one = one * vector[:, :split]
        two = two * vector[:, split:]
        total = (one[:, :LANES] + one[:, LANES:]) + (two[:, :LANES] + two[:, LANES:])
        sums = jnp.sum(total, axis=1, keepdims=True)
        sum_ref[...] = jnp.where(iota((trace, LANES), 1) == e, sums, sum_ref[...])

    turned = (turned_a_ref, turned_b_ref)
    product = (product_a_ref, product_b_ref)

    def advance(e, parity, turning=True, finishing=True):
        if turning:
            @pl.when(e + 2 < elements)
            def _():
                inverse_copy(e + 2).start()

            @pl.when(e + 3 < elements)
            def _():
                coupling_copy(e + 3).start()

            coupling_copy(e + 1).wait()
        inverse_copy(e).wait()
        if turning:
            turn(e + 1, turned[1 - parity])
        first(e, turned[parity], product[parity])
        if finishing:
            second(e - 1, product[1 - parity])
            leave(e - 1).start()

    coupling_copy(0).wait()
    turn(0, turned[0])
    for copy in small:
        copy.wait()
    sum_ref[...] = jnp.zeros_like(sum_ref)
    turn_rhs(rhs_ref, wide_ref, rhs_turned_ref)
    row = iota((PER_FACE, LANES), 0)
    lane = iota((PER_FACE, LANES), 1)

    def position(elem, inner):
        face, rank = divided(inner, capacity)
        return (face * elem_count + elem) * capacity + rank

    first_lane = iota((1, LANES), 1)
    high = jnp.full((1, LANES), -1, I32)
    rest = jnp.zeros((1, LANES), I32)
    for a in range(FACES_PER_ELEM):
        positions = jnp.full((PER_FACE, LANES), -1, I32)
        for e in range(elements):
            slot = conn_ref[a, e]
            positions = jnp.where(row == e, position(*divided(slot, own)), positions)
            here = first_lane == a * PER_FACE + e
            quotient, remainder = divided(slot, SLOT_BASE)
            high = jnp.where(here, quotient, high)
            rest = jnp.where(here, remainder, rest)
        hot = jnp.concatenate([positions == lane + k for k in range(0, slots, LANES)], axis=1)
        lam = dot(hot.astype(BF16), table_ref[...])
        vector_ref[:, a * LANES : (a + 1) * LANES] = -lam
    vector_ref[:, trace:] = (row == lane).astype(F32)
    names = jnp.where(row == 0, high, jnp.where(row == 1, rest, 0))
    share_ref[NAMED:, :] = names.astype(F32).astype(BF16)
    place = position(my_elem, iota((own, slots), 0))
    pick = (iota((own, slots), 1) == place).astype(BF16)
    left_ref[...] = dot(pick, table_ref[...])

    advance(0, 0, finishing=False)

    def two(index, carry):
        advance(2 * index + 1, 1)
        advance(2 * index + 2, 0)
        return carry

    pairs = (elements - 2) // 2
    lax.fori_loop(0, pairs, two, 0)
    for e in range(2 * pairs + 1, elements):
        advance(e, e % 2, turning=e + 1 < elements)
    second(elements - 1, product[(elements - 1) % 2])
    leave(elements - 1).start()

    for a in range(FACES_PER_ELEM):
        shares = sum_ref[a * LANES : (a + 1) * LANES, :].T
        share_ref[a * PER_FACE : (a + 1) * PER_FACE, :] = shares[:PER_FACE].astype(BF16)
    left_ref[...] = less_shares(left_ref[...], share_ref)
    for e in range(elements):
        leave(e).wait()


def less_shares(left, share_ref):
    own = left.shape[0]
    slot = (iota((own, SHARE_ROWS), 0) + lax.axis_index("elem") * own).astype(F32)
    names = share_ref[NAMED:, :].astype(F32)
    named = (names[0:1] * SLOT_BASE + names[1:2])[:, :SHARE_ROWS]
    return left - dot((slot == named).astype(BF16), share_ref[...])


def residual_kernel(left_ref, *refs):
    share_refs, residual_ref = refs[:-1], refs[-1]
    left = left_ref[...]
    for share_ref in share_refs:
        left = less_shares(left, share_ref)
    residual_ref[...] = left


def coarse_kernel(*refs):
    got_refs, (out_ref, sum_ref, full_ref) = refs[:-3], refs[-3:]
    sum_ref[...] = sum(
        got_ref[k : k + OWNER_ROWS, :].astype(F32)
        for got_ref in got_refs
        for k in range(0, got_ref.shape[0], OWNER_ROWS)
    )

    lane = iota((HALF, LANES), 1)
    row = iota((HALF, LANES), 0)
    wide_row = iota((MROW, LANES), 0)
    wide_lane = iota((MROW, LANES), 1)
    top = wide_row < HALF
    held = (top & ((wide_lane <= wide_row) | (wide_lane >= HALF))) | (
        (~top) & (wide_lane >= wide_row)
    )
    for block in range(NC):
        dense = sum_ref[block * DENSE : (block + 1) * DENSE, :]
        upper = jnp.concatenate([dense, pltpu.roll(dense, MROW, 1)], axis=0)
        diag = sum_ref[NC * DENSE + block : NC * DENSE + block + 1, :]
        diag = pltpu.roll(diag + pltpu.roll(diag, MROW, 1), HALF, 1)
        lower = jnp.where(lane == row + HALF, diag, pltpu.roll(upper, HALF, 1))
        given = jnp.concatenate([upper, lower], axis=0)
        turned = jnp.concatenate([given, given], axis=0).T[:MROW]
        full_ref[block * MROW : (block + 1) * MROW, :] = jnp.where(held, given, turned)
    low = iota((NC, LANES), 1) < MROW
    for chunk in range(HALF):
        left = full_ref[pl.ds(2 * chunk, NC, stride=MROW), :]
        right = full_ref[pl.ds(2 * chunk + 1, NC, stride=MROW), :]
        out_ref[:, chunk * LANES : (chunk + 1) * LANES] = jnp.where(
            low, left, pltpu.roll(right, MROW, 1)
        )


ANY = pl.BlockSpec(memory_space=pl.ANY)
VMEM = pl.BlockSpec(memory_space=pltpu.VMEM)


def cost(flops, bytes_accessed):
    return pl.CostEstimate(flops=flops, bytes_accessed=bytes_accessed, transcendentals=0)


def params(limit):
    return pltpu.CompilerParams(vmem_limit_bytes=limit)


def around(block, axis):
    count = lax.axis_size(axis)
    return [block] + [
        lax.ppermute(block, axis, [(i, i ^ k) for i in range(count)]) for k in range(1, count)
    ]


def trade(block, stage):
    face_count, elem_count = lax.axis_size("face"), lax.axis_size("elem")
    bits = face_count.bit_length() - 1
    pairs = []
    for face in range(face_count):
        for elem in range(elem_count):
            swapped = bits > 1 and elem % 2 == 1 and stage < 2
            other = face ^ (1 << (1 - stage if swapped else stage))
            pairs.append((face * elem_count + elem, other * elem_count + elem))
    return lax.ppermute(block, ("face", "elem"), pairs)


def join(kept, came):
    half = jax.ShapeDtypeStruct((kept.shape[0] // 2, LANES), BF16)
    return pl.pallas_call(
        join_kernel,
        out_shape=(half, half),
        in_specs=[VMEM] * 2,
        out_specs=(VMEM, VMEM),
        compiler_params=params(SMALL),
        cost_estimate=cost(0, 4 << 20),
        name="join",
    )(kept, came)


def shards(
    trace_old,
    new_owner,
    mortar_tiles,
    mortar_owner,
    mortar_coarse,
    interior_rhs,
    local_inverse,
    coupling,
    connectivity,
):
    face_count = lax.axis_size("face")
    elem_count = lax.axis_size("elem")
    row_count = trace_old.shape[0]
    tile_count = mortar_tiles.shape[0]
    elements, modes = interior_rhs.shape
    trace = FACES_PER_ELEM * FACE_COEFFS
    capacity = max(2, 2 * row_count // face_count)
    own = face_count * capacity

    slots = own * elem_count
    devices = face_count * elem_count
    paired = face_count <= MOST_PAIRED
    sides = 2 if paired else 1

    blocks = face_count * NC
    sums_shape = (blocks * DENSE, LANES)
    placed, *half_grams = pl.pallas_call(
        functools.partial(gram_kernel, elem_count, face_count, capacity, paired),
        out_shape=[jax.ShapeDtypeStruct((slots, FACE_COEFFS), BF16)]
        + [jax.ShapeDtypeStruct((blocks * (DENSE + 1) // sides, LANES), BF16)] * sides,
        in_specs=[ANY] * 5,
        out_specs=[VMEM] * (1 + sides),
        scratch_shapes=[
            pltpu.SMEM((tile_count,), I32),
            pltpu.SMEM((tile_count,), I32),
            pltpu.VMEM(mortar_tiles.shape, BF16),
            pltpu.VMEM((tile_count * PITCH, LANES), F32),
            pltpu.VMEM(sums_shape, F32),
            pltpu.VMEM(sums_shape, F32),
            pltpu.VMEM((blocks, LANES), F32),
            pltpu.VMEM((blocks, LANES), F32),
            pltpu.VMEM((1, row_count), I32),
            pltpu.VMEM(trace_old.shape, BF16),
            pltpu.SemaphoreType.DMA((5,)),
        ],
        compiler_params=params(BIG),
        cost_estimate=cost(4 * tile_count * MROW * MROW * LANES, 12 << 20),
        name="gram",
    )(
        mortar_owner.reshape(tile_count),
        mortar_coarse,
        mortar_tiles,
        new_owner.reshape(1, row_count),
        trace_old,
    )
    if paired:
        kept, came = half_grams[0], trade(half_grams[1], 0)
    table = lax.all_to_all(
        placed.reshape(devices, capacity, FACE_COEFFS), ("face", "elem"), 0, 0, tiled=True
    ).reshape(slots, FACE_COEFFS)

    if paired:
        for stage in range(1, face_count.bit_length() - 1):
            kept, sent = join(kept, came)
            came = trade(sent, stage)
        got = [kept, came]
    else:
        blocked = half_grams[0].reshape(face_count, OWNER_ROWS, LANES)
        got = [lax.all_to_all(blocked, "face", 0, 0, tiled=True).reshape(-1, LANES)]
        kept = half_grams[0]

    rhs, _ = lax.optimization_barrier((interior_rhs, kept))
    schur_blocks, shares, left = pl.pallas_call(
        functools.partial(main_kernel, elem_count, face_count),
        out_shape=(
            jax.ShapeDtypeStruct((elements, trace, trace), BF16),
            jax.ShapeDtypeStruct((SHARE_ROWS, LANES), BF16),
            jax.ShapeDtypeStruct((own, FACE_COEFFS), F32),
        ),
        in_specs=[ANY] * 5,
        out_specs=(ANY, VMEM, VMEM),
        scratch_shapes=[
            pltpu.SMEM((FACES_PER_ELEM, elements), I32),
            pltpu.VMEM((elements, modes), BF16),
            pltpu.VMEM((slots, FACE_COEFFS), BF16),
            pltpu.VMEM((elements, modes, modes), BF16),
            pltpu.VMEM((elements, modes, trace), BF16),
            pltpu.VMEM((elements, trace, trace), BF16),
            pltpu.VMEM((LANES, modes), F32),
            pltpu.VMEM((modes, LANES), BF16),
            pltpu.VMEM((PER_FACE, trace + LANES), F32),
            pltpu.VMEM((trace, LANES), F32),
            pltpu.VMEM((trace, modes), BF16),
            pltpu.VMEM((trace, modes), BF16),
            pltpu.VMEM((trace, modes), BF16),
            pltpu.VMEM((trace, modes), BF16),
            pltpu.SemaphoreType.DMA((3,)),
            pltpu.SemaphoreType.DMA((2, elements)),
            pltpu.SemaphoreType.DMA((elements,)),
        ],
        compiler_params=params(BIG),
        cost_estimate=cost(
            2 * elements * modes * trace * (modes + trace),
            2 * elements * (modes * (modes + trace) + trace * trace),
        ),
        name="condense",
    )(table, connectivity.T, rhs, local_inverse, coupling)

    all_shares = around(shares, "elem")
    coarse_blocks = pl.pallas_call(
        coarse_kernel,
        out_shape=jax.ShapeDtypeStruct((NC, MROW * MROW), F32),
        in_specs=[VMEM] * len(got),
        out_specs=VMEM,
        scratch_shapes=[
            pltpu.VMEM((OWNER_ROWS, LANES), F32),
            pltpu.VMEM((NC * MROW, LANES), F32),
        ],
        compiler_params=params(SMALL),
        cost_estimate=cost(0, 8 << 20),
        name="coarse",
    )(*got)
    left, coarse_blocks = lax.optimization_barrier((left, coarse_blocks))
    slot_residual = pl.pallas_call(
        residual_kernel,
        out_shape=jax.ShapeDtypeStruct((own, FACE_COEFFS), F32),
        in_specs=[VMEM] * elem_count,
        out_specs=VMEM,
        compiler_params=params(SMALL),
        name="residual",
    )(left, *all_shares[1:])
    return schur_blocks, slot_residual, coarse_blocks


def solution(mesh):
    return jax.shard_map(
        shards,
        mesh=mesh,
        in_specs=(
            P(("face", "elem"), None),
            P(("face", "elem"), None),
            P(("face", "elem"), None),
            P(("face", "elem"), None),
            P(("face", "elem")),
            P(("face", "elem"), None),
            P(("face", "elem"), None, None),
            P(("face", "elem"), None, None),
            P(("face", "elem"), None),
        ),
        out_specs=(
            P(("face", "elem"), None, None),
            P(("face", "elem"), None),
            P(("face", "elem"), None),
        ),
        check_vma=False,
    )
```

```python
import functools

import jax
import jax.numpy as jnp
from jax import lax
from jax.experimental import pallas as pl
from jax.experimental.pallas import tpu as pltpu
from jax.sharding import PartitionSpec as P

FACE_COEFFS = 128
FACES_PER_ELEM = 3
MROW = 64
MCOL = 96
NC = 16
HALF = MROW // 2
LANES = 128
DENSE = HALF * MROW // LANES
OWNER_ROWS = NC * (DENSE + 1)
PER_FACE = 16
NAMED = FACES_PER_ELEM * PER_FACE
SHARE_ROWS = NAMED + 16
SLOT_BASE = 16
CHUNK = 16
MOST_PAIRED = 8
BIG = 62 << 20
SMALL = 12 << 20
PITCH = MROW + 8

BF16 = jnp.bfloat16
F32 = jnp.float32
I32 = jnp.int32

NT = (((1,), (1,)), ((), ()))
TN = (((0,), (0,)), ((), ()))


def iota(shape, dim):
    return lax.broadcasted_iota(I32, shape, dim)


def dot(left, right, dims=(((1,), (0,)), ((), ()))):
    return lax.dot_general(left, right, dims, preferred_element_type=F32)


def divided(value, by):
    shift = by.bit_length() - 1
    assert by == 1 << shift
    return value >> shift, value & (by - 1)


def place_rows(elem_count, face_count, capacity, owners, trace, slots):
    rows = owners.shape[1]
    earlier = (iota((rows, rows), 0) < iota((rows, rows), 1)).astype(BF16)
    hot = (iota((face_count, rows), 0) == owners).astype(F32)
    rank = jnp.sum(hot * dot(hot.astype(BF16), earlier), axis=0, keepdims=True).astype(I32)
    slot = iota((slots, rows), 0)
    wanted = divided(slot, elem_count * capacity)[0] * capacity + divided(slot, capacity)[1]
    place = (wanted == owners * capacity + rank).astype(BF16)
    return dot(place, trace).astype(BF16)


def turn_rhs(rhs_ref, wide_ref, rhs_turned_ref):
    wide_ref[...] = jnp.zeros_like(wide_ref)
    wide_ref[0 : rhs_ref.shape[0], :] = rhs_ref[...].astype(F32)
    rhs_turned_ref[...] = wide_ref[...].T.astype(BF16)


def gram_kernel(
    elem_count,
    face_count,
    capacity,
    paired,
    owner_hbm,
    coarse_hbm,
    tiles_hbm,
    new_owner_hbm,
    trace_hbm,
    placed_ref,
    *refs,
):
    out_refs, refs = refs[:-11], refs[-11:]
    owner_ref, coarse_ref, tiles_ref, rows_ref = refs[:4]
    accs, diags = refs[4:6], refs[6:8]
    new_owner_ref, trace_ref, sems = refs[8:]

    def place_of(owner):
        if not paired:
            return owner
        other = owner ^ lax.axis_index("face")
        bits = face_count.bit_length() - 1
        odd = lax.axis_index("elem") & 1
        place = [(other >> k) & 1 for k in range(bits)]
        if bits > 1:
            place[:2] = (jnp.where(odd == 1, place[1 - k], place[k]) for k in range(2))
        return sum(bit << (bits - 1 - k) for k, bit in enumerate(place))

    tiles = tiles_ref.shape[0]
    copies = [
        pltpu.make_async_copy(owner_hbm, owner_ref, sems.at[0]),
        pltpu.make_async_copy(coarse_hbm, coarse_ref, sems.at[1]),
        pltpu.make_async_copy(new_owner_hbm, new_owner_ref, sems.at[2]),
        pltpu.make_async_copy(trace_hbm, trace_ref, sems.at[3]),
        pltpu.make_async_copy(tiles_hbm, tiles_ref, sems.at[4]),
    ]
    for copy in copies:
        copy.start()
    for ref in (*accs, *diags):
        ref[...] = jnp.zeros_like(ref)
    for copy in copies:
        copy.wait()
    placed_ref[...] = place_rows(
        elem_count, face_count, capacity, new_owner_ref[...], trace_ref[...], placed_ref.shape[0]
    )

    lane = iota((CHUNK, LANES), 1)
    inside = lane < MCOL
    row = iota((HALF, LANES), 0)
    column = divided(iota((HALF, LANES), 1), MROW)[1]
    swapped = (column > row) & (column < HALF)
    diagonal = column == row
    low = iota((DENSE, LANES), 1) < MROW
    low_wide = iota((MROW, LANES), 1) < MROW
    low_row = iota((1, LANES), 1) < MROW

    for chunk in range(tiles // CHUNK):
        first_tile = chunk * CHUNK
        for group in range(MROW // 4):
            base = group * 3 * LANES
            one, two, three = (
                tiles_ref[
                    first_tile : first_tile + CHUNK, base + k * LANES : base + (k + 1) * LANES
                ].astype(F32)
                for k in range(3)
            )
            rolled = (
                one,
                pltpu.roll(jnp.where(lane < 64, two, one), 32, 1),
                pltpu.roll(jnp.where(lane < 32, three, two), 64, 1),
                pltpu.roll(three, 96, 1),
            )
            for k in range(4):
                rows_ref[pl.ds(first_tile * PITCH + 4 * group + k, CHUNK, stride=PITCH), :] = (
                    jnp.where(inside, rolled[k], 0.0)
                )
        for tile in range(first_tile, first_tile + CHUNK, 2):
            both = jnp.concatenate(
                [
                    rows_ref[t * PITCH : t * PITCH + MROW, :].astype(BF16)
                    for t in (tile, tile + 1)
                ],
                axis=0,
            )
            gram = dot(both, both, NT)
            side = jnp.where(low_wide, gram[:MROW], gram[MROW:])
            lower = pltpu.roll(side[HALF:], LANES - HALF, 1)
            packed = jnp.where(swapped, lower, side[:HALF])
            diag = jnp.sum(jnp.where(diagonal, lower, 0.0), axis=0, keepdims=True)
            turned = pltpu.roll(packed, MROW, 1)
            dense = (
                jnp.where(low, packed[:DENSE], turned[DENSE:]),
                jnp.where(low, turned[:DENSE], packed[DENSE:]),
            )
            own = (jnp.where(low_row, diag, 0.0), jnp.where(low_row, 0.0, diag))
            for k in range(2):
                block = place_of(owner_ref[tile + k]) * NC + coarse_ref[tile + k]
                here = pl.ds(pl.multiple_of(block * DENSE, DENSE), DENSE)
                accs[k][here, :] += dense[k]
                diags[k][pl.ds(block, 1), :] += own[k]
    size = NC * DENSE
    each = face_count // len(out_refs)
    for owner in range(face_count):
        out_ref, start = out_refs[owner // each], owner % each * OWNER_ROWS
        here = slice(owner * size, (owner + 1) * size)
        out_ref[start : start + size, :] = (accs[0][here, :] + accs[1][here, :]).astype(BF16)
        here = slice(owner * NC, (owner + 1) * NC)
        out_ref[start + size : start + size + NC, :] = (
            diags[0][here, :] + diags[1][here, :]
        ).astype(BF16)


def join_kernel(kept_ref, came_ref, *out_refs):
    for k, out_ref in enumerate(out_refs):
        here = slice(k * OWNER_ROWS, (k + 1) * OWNER_ROWS)
        total = kept_ref[here, :].astype(F32) + came_ref[here, :].astype(F32)
        out_ref[...] = total.astype(BF16)


def main_kernel(
    elem_count,
    face_count,
    table_hbm,
    conn_hbm,
    rhs_hbm,
    inverse_hbm,
    coupling_hbm,
    schur_hbm,
    share_ref,
    left_ref,
    conn_ref,
    rhs_ref,
    table_ref,
    inverse_ref,
    coupling_ref,
    schur_ref,
    wide_ref,
    rhs_turned_ref,
    vector_ref,
    sum_ref,
    turned_a_ref,
    turned_b_ref,
    product_a_ref,
    product_b_ref,
    small_sems,
    block_sems,
    schur_sems,
):
    elements = rhs_ref.shape[0]
    modes = rhs_ref.shape[1]
    trace = FACES_PER_ELEM * FACE_COEFFS
    slots = table_ref.shape[0]
    own = left_ref.shape[0]
    capacity = own // face_count
    my_elem = lax.axis_index("elem")
    small = [
        pltpu.make_async_copy(rhs_hbm, rhs_ref, small_sems.at[0]),
        pltpu.make_async_copy(conn_hbm, conn_ref, small_sems.at[1]),
        pltpu.make_async_copy(table_hbm, table_ref, small_sems.at[2]),
    ]

    def coupling_copy(e):
        return pltpu.make_async_copy(coupling_hbm.at[e], coupling_ref.at[e], block_sems.at[0, e])

    def inverse_copy(e):
        return pltpu.make_async_copy(inverse_hbm.at[e], inverse_ref.at[e], block_sems.at[1, e])

    def leave(e):
        return pltpu.make_async_copy(schur_ref.at[e], schur_hbm.at[e], schur_sems.at[e])

    coupling_copy(0).start()
    for copy in small:
        copy.start()
    inverse_copy(0).start()

    def turn(e, turned_ref):
        turned_ref[...] = coupling_ref[e].T

    def first(e, turned_ref, product_ref):
        for half in range(2):
            here = slice(half * modes // 2, (half + 1) * modes // 2)
            product_ref[:, here] = dot(turned_ref[...], inverse_ref[e, :, here]).astype(BF16)

    def second(e, product_ref):
        split = 2 * LANES
        one = dot(product_ref[...], coupling_ref[e, :, :split])
        wide = jnp.concatenate([coupling_ref[e, :, split:], rhs_turned_ref[...]], axis=1)
        two = dot(product_ref[...], wide)
        schur_ref[e, :, :split] = (-one).astype(BF16)
        schur_ref[e, :, split:] = (-two[:, : trace - split]).astype(BF16)
        vector = vector_ref[pl.ds(e, 1), :]
        one = one * vector[:, :split]
        two = two * vector[:, split:]
        total = (one[:, :LANES] + one[:, LANES:]) + (two[:, :LANES] + two[:, LANES:])
        sums = jnp.sum(total, axis=1, keepdims=True)
        sum_ref[...] = jnp.where(iota((trace, LANES), 1) == e, sums, sum_ref[...])

    turned = (turned_a_ref, turned_b_ref)
    product = (product_a_ref, product_b_ref)

    def advance(e, parity, turning=True, finishing=True):
        if turning:
            @pl.when(e + 2 < elements)
            def _():
                inverse_copy(e + 2).start()

            @pl.when(e + 3 < elements)
            def _():
                coupling_copy(e + 3).start()

            coupling_copy(e + 1).wait()
        inverse_copy(e).wait()
        if turning:
            turn(e + 1, turned[1 - parity])
        first(e, turned[parity], product[parity])
        if finishing:
            second(e - 1, product[1 - parity])
            leave(e - 1).start()

    coupling_copy(0).wait()
    coupling_copy(1).start()
    inverse_copy(1).start()
    coupling_copy(2).start()
    turn(0, turned[0])
    for copy in small:
        copy.wait()
    sum_ref[...] = jnp.zeros_like(sum_ref)
    turn_rhs(rhs_ref, wide_ref, rhs_turned_ref)
    row = iota((PER_FACE, LANES), 0)
    lane = iota((PER_FACE, LANES), 1)

    def position(elem, inner):
        face, rank = divided(inner, capacity)
        return (face * elem_count + elem) * capacity + rank

    first_lane = iota((1, LANES), 1)
    high = jnp.full((1, LANES), -1, I32)
    rest = jnp.zeros((1, LANES), I32)
    for a in range(FACES_PER_ELEM):
        positions = jnp.full((PER_FACE, LANES), -1, I32)
        for e in range(elements):
            slot = conn_ref[a, e]
            positions = jnp.where(row == e, position(*divided(slot, own)), positions)
            here = first_lane == a * PER_FACE + e
            quotient, remainder = divided(slot, SLOT_BASE)
            high = jnp.where(here, quotient, high)
            rest = jnp.where(here, remainder, rest)
        hot = jnp.concatenate([positions == lane + k for k in range(0, slots, LANES)], axis=1)
        lam = dot(hot.astype(BF16), table_ref[...])
        vector_ref[:, a * LANES : (a + 1) * LANES] = -lam
    vector_ref[:, trace:] = (row == lane).astype(F32)
    names = jnp.where(row == 0, high, jnp.where(row == 1, rest, 0))
    share_ref[NAMED:, :] = names.astype(F32).astype(BF16)
    place = position(my_elem, iota((own, slots), 0))
    pick = (iota((own, slots), 1) == place).astype(BF16)
    left_ref[...] = dot(pick, table_ref[...])

    advance(0, 0, finishing=False)

    def two(index, carry):
        advance(2 * index + 1, 1)
        advance(2 * index + 2, 0)
        return carry

    pairs = (elements - 2) // 2
    lax.fori_loop(0, pairs, two, 0)
    for e in range(2 * pairs + 1, elements):
        advance(e, e % 2, turning=e + 1 < elements)
    second(elements - 1, product[(elements - 1) % 2])
    leave(elements - 1).start()

    for a in range(FACES_PER_ELEM):
        shares = sum_ref[a * LANES : (a + 1) * LANES, :].T
        share_ref[a * PER_FACE : (a + 1) * PER_FACE, :] = shares[:PER_FACE].astype(BF16)
    left_ref[...] = less_shares(left_ref[...], share_ref)
    for e in range(elements):
        leave(e).wait()


def less_shares(left, share_ref):
    own = left.shape[0]
    slot = (iota((own, SHARE_ROWS), 0) + lax.axis_index("elem") * own).astype(F32)
    names = share_ref[NAMED:, :].astype(F32)
    named = (names[0:1] * SLOT_BASE + names[1:2])[:, :SHARE_ROWS]
    return left - dot((slot == named).astype(BF16), share_ref[...])


def residual_kernel(left_ref, *refs):
    share_refs, residual_ref = refs[:-1], refs[-1]
    left = left_ref[...]
    for share_ref in share_refs:
        left = less_shares(left, share_ref)
    residual_ref[...] = left


def coarse_kernel(*refs):
    got_refs, (out_ref, sum_ref, full_ref) = refs[:-3], refs[-3:]
    sum_ref[...] = sum(
        got_ref[k : k + OWNER_ROWS, :].astype(F32)
        for got_ref in got_refs
        for k in range(0, got_ref.shape[0], OWNER_ROWS)
    )

    lane = iota((HALF, LANES), 1)
    row = iota((HALF, LANES), 0)
    wide_row = iota((MROW, LANES), 0)
    wide_lane = iota((MROW, LANES), 1)
    top = wide_row < HALF
    held = (top & ((wide_lane <= wide_row) | (wide_lane >= HALF))) | (
        (~top) & (wide_lane >= wide_row)
    )
    for block in range(NC):
        dense = sum_ref[block * DENSE : (block + 1) * DENSE, :]
        upper = jnp.concatenate([dense, pltpu.roll(dense, MROW, 1)], axis=0)
        diag = sum_ref[NC * DENSE + block : NC * DENSE + block + 1, :]
        diag = pltpu.roll(diag + pltpu.roll(diag, MROW, 1), HALF, 1)
        lower = jnp.where(lane == row + HALF, diag, pltpu.roll(upper, HALF, 1))
        given = jnp.concatenate([upper, lower], axis=0)
        turned = jnp.concatenate([given, given], axis=0).T[:MROW]
        full_ref[block * MROW : (block + 1) * MROW, :] = jnp.where(held, given, turned)
    low = iota((NC, LANES), 1) < MROW
    for chunk in range(HALF):
        left = full_ref[pl.ds(2 * chunk, NC, stride=MROW), :]
        right = full_ref[pl.ds(2 * chunk + 1, NC, stride=MROW), :]
        out_ref[:, chunk * LANES : (chunk + 1) * LANES] = jnp.where(
            low, left, pltpu.roll(right, MROW, 1)
        )


ANY = pl.BlockSpec(memory_space=pl.ANY)
VMEM = pl.BlockSpec(memory_space=pltpu.VMEM)


def cost(flops, bytes_accessed):
    return pl.CostEstimate(flops=flops, bytes_accessed=bytes_accessed, transcendentals=0)


def params(limit):
    return pltpu.CompilerParams(vmem_limit_bytes=limit)


def around(block, axis):
    count = lax.axis_size(axis)
    return [block] + [
        lax.ppermute(block, axis, [(i, i ^ k) for i in range(count)]) for k in range(1, count)
    ]


def trade(block, place, face_count):
    elem_count = lax.axis_size("elem")
    bits = face_count.bit_length() - 1
    pairs = []
    for face in range(face_count):
        for elem in range(elem_count):
            other = face
            for k in range(bits):
                swapped = bits > 1 and elem % 2 == 1 and k < 2
                if place >> (bits - 1 - k) & 1:
                    other ^= 1 << (1 - k if swapped else k)
            pairs.append((face * elem_count + elem, other * elem_count + elem))
    return lax.ppermute(block, ("face", "elem"), pairs)


def shards(
    trace_old,
    new_owner,
    mortar_tiles,
    mortar_owner,
    mortar_coarse,
    interior_rhs,
    local_inverse,
    coupling,
    connectivity,
):
    face_count = lax.axis_size("face")
    elem_count = lax.axis_size("elem")
    row_count = trace_old.shape[0]
    tile_count = mortar_tiles.shape[0]
    elements, modes = interior_rhs.shape
    trace = FACES_PER_ELEM * FACE_COEFFS
    capacity = max(2, 2 * row_count // face_count)
    own = face_count * capacity

    slots = own * elem_count
    devices = face_count * elem_count
    paired = face_count <= MOST_PAIRED
    sides = 2 if paired else 1

    blocks = face_count * NC
    sums_shape = (blocks * DENSE, LANES)
    placed, *half_grams = pl.pallas_call(
        functools.partial(gram_kernel, elem_count, face_count, capacity, paired),
        out_shape=[jax.ShapeDtypeStruct((slots, FACE_COEFFS), BF16)]
        + [jax.ShapeDtypeStruct((blocks * (DENSE + 1) // sides, LANES), BF16)] * sides,
        in_specs=[ANY] * 5,
        out_specs=[VMEM] * (1 + sides),
        scratch_shapes=[
            pltpu.SMEM((tile_count,), I32),
            pltpu.SMEM((tile_count,), I32),
            pltpu.VMEM(mortar_tiles.shape, BF16),
            pltpu.VMEM((tile_count * PITCH, LANES), F32),
            pltpu.VMEM(sums_shape, F32),
            pltpu.VMEM(sums_shape, F32),
            pltpu.VMEM((blocks, LANES), F32),
            pltpu.VMEM((blocks, LANES), F32),
            pltpu.VMEM((1, row_count), I32),
            pltpu.VMEM(trace_old.shape, BF16),
            pltpu.SemaphoreType.DMA((5,)),
        ],
        compiler_params=params(BIG),
        cost_estimate=cost(4 * tile_count * MROW * MROW * LANES, 12 << 20),
        name="gram",
    )(
        mortar_owner.reshape(tile_count),
        mortar_coarse,
        mortar_tiles,
        new_owner.reshape(1, row_count),
        trace_old,
    )
    if paired:
        came = trade(half_grams[1], face_count // 2, face_count)
    table = lax.all_to_all(
        placed.reshape(devices, capacity, FACE_COEFFS), ("face", "elem"), 0, 0, tiled=True
    ).reshape(slots, FACE_COEFFS)

    if paired:
        joined = pl.pallas_call(
            join_kernel,
            out_shape=[jax.ShapeDtypeStruct((OWNER_ROWS, LANES), BF16)] * (face_count // 2),
            in_specs=[VMEM] * 2,
            out_specs=[VMEM] * (face_count // 2),
            compiler_params=params(SMALL),
            cost_estimate=cost(0, 4 << 20),
            name="join",
        )(half_grams[0], came)
        got = [joined[0]] + [
            trade(joined[k], k, face_count) for k in range(face_count // 2 - 1, 0, -1)
        ]
        before = joined[0]
    else:
        blocked = half_grams[0].reshape(face_count, OWNER_ROWS, LANES)
        got = [lax.all_to_all(blocked, "face", 0, 0, tiled=True).reshape(-1, LANES)]
        before = half_grams[0]

    rhs, _ = lax.optimization_barrier((interior_rhs, before))
    schur_blocks, shares, left = pl.pallas_call(
        functools.partial(main_kernel, elem_count, face_count),
        out_shape=(
            jax.ShapeDtypeStruct((elements, trace, trace), BF16),
            jax.ShapeDtypeStruct((SHARE_ROWS, LANES), BF16),
            jax.ShapeDtypeStruct((own, FACE_COEFFS), F32),
        ),
        in_specs=[ANY] * 5,
        out_specs=(ANY, VMEM, VMEM),
        scratch_shapes=[
            pltpu.SMEM((FACES_PER_ELEM, elements), I32),
            pltpu.VMEM((elements, modes), BF16),
            pltpu.VMEM((slots, FACE_COEFFS), BF16),
            pltpu.VMEM((elements, modes, modes), BF16),
            pltpu.VMEM((elements, modes, trace), BF16),
            pltpu.VMEM((elements, trace, trace), BF16),
            pltpu.VMEM((LANES, modes), F32),
            pltpu.VMEM((modes, LANES), BF16),
            pltpu.VMEM((PER_FACE, trace + LANES), F32),
            pltpu.VMEM((trace, LANES), F32),
            pltpu.VMEM((trace, modes), BF16),
            pltpu.VMEM((trace, modes), BF16),
            pltpu.VMEM((trace, modes), BF16),
            pltpu.VMEM((trace, modes), BF16),
            pltpu.SemaphoreType.DMA((3,)),
            pltpu.SemaphoreType.DMA((2, elements)),
            pltpu.SemaphoreType.DMA((elements,)),
        ],
        compiler_params=params(BIG),
        cost_estimate=cost(
            2 * elements * modes * trace * (modes + trace),
            2 * elements * (modes * (modes + trace) + trace * trace),
        ),
        name="condense",
    )(table, connectivity.T, rhs, local_inverse, coupling)

    all_shares = around(shares, "elem")
    coarse_blocks = pl.pallas_call(
        coarse_kernel,
        out_shape=jax.ShapeDtypeStruct((NC, MROW * MROW), F32),
        in_specs=[VMEM] * len(got),
        out_specs=VMEM,
        scratch_shapes=[
            pltpu.VMEM((OWNER_ROWS, LANES), F32),
            pltpu.VMEM((NC * MROW, LANES), F32),
        ],
        compiler_params=params(SMALL),
        cost_estimate=cost(0, 8 << 20),
        name="coarse",
    )(*got)
    left, coarse_blocks = lax.optimization_barrier((left, coarse_blocks))
    slot_residual = pl.pallas_call(
        residual_kernel,
        out_shape=jax.ShapeDtypeStruct((own, FACE_COEFFS), F32),
        in_specs=[VMEM] * elem_count,
        out_specs=VMEM,
        compiler_params=params(SMALL),
        name="residual",
    )(left, *all_shares[1:])
    return schur_blocks, slot_residual, coarse_blocks


def solution(mesh):
    return jax.shard_map(
        shards,
        mesh=mesh,
        in_specs=(
            P(("face", "elem"), None),
            P(("face", "elem"), None),
            P(("face", "elem"), None),
            P(("face", "elem"), None),
            P(("face", "elem")),
            P(("face", "elem"), None),
            P(("face", "elem"), None, None),
            P(("face", "elem"), None, None),
            P(("face", "elem"), None),
        ),
        out_specs=(
            P(("face", "elem"), None, None),
            P(("face", "elem"), None),
            P(("face", "elem"), None),
        ),
        check_vma=False,
    )
```

```python
import functools

import jax
import jax.numpy as jnp
from jax import lax
from jax.experimental import pallas as pl
from jax.experimental.pallas import tpu as pltpu
from jax.sharding import PartitionSpec as P

FACE_COEFFS = 128
FACES_PER_ELEM = 3
MROW = 64
MCOL = 96
NC = 16
HALF = MROW // 2
LANES = 128
DENSE = HALF * MROW // LANES
OWNER_ROWS = NC * (DENSE + 1)
PER_FACE = 16
NAMED = FACES_PER_ELEM * PER_FACE
SHARE_ROWS = NAMED + 16
SLOT_BASE = 16
CHUNK = 16
MOST_PAIRED = 8
BIG = 62 << 20
SMALL = 12 << 20
PITCH = MROW + 8

BF16 = jnp.bfloat16
F32 = jnp.float32
I32 = jnp.int32

NT = (((1,), (1,)), ((), ()))
TN = (((0,), (0,)), ((), ()))


def iota(shape, dim):
    return lax.broadcasted_iota(I32, shape, dim)


def dot(left, right, dims=(((1,), (0,)), ((), ()))):
    return lax.dot_general(left, right, dims, preferred_element_type=F32)


def divided(value, by):
    shift = by.bit_length() - 1
    assert by == 1 << shift
    return value >> shift, value & (by - 1)


def place_rows(elem_count, face_count, capacity, owners, trace, slots):
    rows = owners.shape[1]
    earlier = (iota((rows, rows), 0) < iota((rows, rows), 1)).astype(BF16)
    hot = (iota((face_count, rows), 0) == owners).astype(F32)
    rank = jnp.sum(hot * dot(hot.astype(BF16), earlier), axis=0, keepdims=True).astype(I32)
    slot = iota((slots, rows), 0)
    wanted = divided(slot, elem_count * capacity)[0] * capacity + divided(slot, capacity)[1]
    place = (wanted == owners * capacity + rank).astype(BF16)
    return dot(place, trace).astype(BF16)


def position(elem, inner, elem_count, capacity):
    face, rank = divided(inner, capacity)
    return (face * elem_count + elem) * capacity + rank


def name_slots(elem_count, face_count, capacity, conn_ref, named_ref):
    elements = conn_ref.shape[1]
    slots = named_ref.shape[1]
    row = iota((PER_FACE, LANES), 0)
    lane = iota((PER_FACE, LANES), 1)
    first_lane = iota((1, LANES), 1)
    high = jnp.full((1, LANES), -1, I32)
    rest = jnp.zeros((1, LANES), I32)
    for a in range(FACES_PER_ELEM):
        positions = jnp.full((PER_FACE, LANES), -1, I32)
        for e in range(elements):
            slot = conn_ref[a, e]
            place = position(*divided(slot, face_count * capacity), elem_count, capacity)
            positions = jnp.where(row == e, place, positions)
            here = first_lane == a * PER_FACE + e
            quotient, remainder = divided(slot, SLOT_BASE)
            high = jnp.where(here, quotient, high)
            rest = jnp.where(here, remainder, rest)
        hot = jnp.concatenate([positions == lane + k for k in range(0, slots, LANES)], axis=1)
        named_ref[a * PER_FACE : (a + 1) * PER_FACE, :] = hot.astype(BF16)
    names = jnp.where(row == 0, high, jnp.where(row == 1, rest, 0)).astype(F32)
    named_ref[NAMED:, :] = jnp.concatenate([names] * (slots // LANES), axis=1).astype(BF16)


def turn_rhs(rhs_ref, wide_ref, rhs_turned_ref):
    wide_ref[...] = jnp.zeros_like(wide_ref)
    wide_ref[0 : rhs_ref.shape[0], :] = rhs_ref[...].astype(F32)
    rhs_turned_ref[...] = wide_ref[...].T.astype(BF16)


def gram_kernel(
    elem_count,
    face_count,
    capacity,
    paired,
    owner_hbm,
    coarse_hbm,
    tiles_hbm,
    new_owner_hbm,
    trace_hbm,
    conn_hbm,
    placed_ref,
    named_ref,
    *refs,
):
    out_refs, refs = refs[:-12], refs[-12:]
    owner_ref, coarse_ref, tiles_ref, rows_ref = refs[:4]
    accs, diags = refs[4:6], refs[6:8]
    new_owner_ref, trace_ref, conn_ref, sems = refs[8:]

    def place_of(owner):
        if not paired:
            return owner
        other = owner ^ lax.axis_index("face")
        bits = face_count.bit_length() - 1
        odd = lax.axis_index("elem") & 1
        place = [(other >> k) & 1 for k in range(bits)]
        if bits > 1:
            place[:2] = (jnp.where(odd == 1, place[1 - k], place[k]) for k in range(2))
        return sum(bit << (bits - 1 - k) for k, bit in enumerate(place))

    tiles = tiles_ref.shape[0]
    copies = [
        pltpu.make_async_copy(owner_hbm, owner_ref, sems.at[0]),
        pltpu.make_async_copy(coarse_hbm, coarse_ref, sems.at[1]),
        pltpu.make_async_copy(new_owner_hbm, new_owner_ref, sems.at[2]),
        pltpu.make_async_copy(trace_hbm, trace_ref, sems.at[3]),
        pltpu.make_async_copy(tiles_hbm, tiles_ref, sems.at[4]),
    ]
    names = pltpu.make_async_copy(conn_hbm, conn_ref, sems.at[5])
    names.start()
    for copy in copies:
        copy.start()
    for ref in (*accs, *diags):
        ref[...] = jnp.zeros_like(ref)
    names.wait()
    name_slots(elem_count, face_count, capacity, conn_ref, named_ref)
    for copy in copies:
        copy.wait()
    placed_ref[...] = place_rows(
        elem_count, face_count, capacity, new_owner_ref[...], trace_ref[...], placed_ref.shape[0]
    )

    lane = iota((CHUNK, LANES), 1)
    inside = lane < MCOL
    row = iota((HALF, LANES), 0)
    column = divided(iota((HALF, LANES), 1), MROW)[1]
    swapped = (column > row) & (column < HALF)
    diagonal = column == row
    low = iota((DENSE, LANES), 1) < MROW
    low_wide = iota((MROW, LANES), 1) < MROW
    low_row = iota((1, LANES), 1) < MROW

    for chunk in range(tiles // CHUNK):
        first_tile = chunk * CHUNK
        for group in range(MROW // 4):
            base = group * 3 * LANES
            one, two, three = (
                tiles_ref[
                    first_tile : first_tile + CHUNK, base + k * LANES : base + (k + 1) * LANES
                ].astype(F32)
                for k in range(3)
            )
            rolled = (
                one,
                pltpu.roll(jnp.where(lane < 64, two, one), 32, 1),
                pltpu.roll(jnp.where(lane < 32, three, two), 64, 1),
                pltpu.roll(three, 96, 1),
            )
            for k in range(4):
                rows_ref[pl.ds(first_tile * PITCH + 4 * group + k, CHUNK, stride=PITCH), :] = (
                    jnp.where(inside, rolled[k], 0.0)
                )
        for tile in range(first_tile, first_tile + CHUNK, 2):
            both = jnp.concatenate(
                [
                    rows_ref[t * PITCH : t * PITCH + MROW, :].astype(BF16)
                    for t in (tile, tile + 1)
                ],
                axis=0,
            )
            gram = dot(both, both, NT)
            side = jnp.where(low_wide, gram[:MROW], gram[MROW:])
            lower = pltpu.roll(side[HALF:], LANES - HALF, 1)
            packed = jnp.where(swapped, lower, side[:HALF])
            diag = jnp.sum(jnp.where(diagonal, lower, 0.0), axis=0, keepdims=True)
            turned = pltpu.roll(packed, MROW, 1)
            dense = (
                jnp.where(low, packed[:DENSE], turned[DENSE:]),
                jnp.where(low, turned[:DENSE], packed[DENSE:]),
            )
            own = (jnp.where(low_row, diag, 0.0), jnp.where(low_row, 0.0, diag))
            for k in range(2):
                block = place_of(owner_ref[tile + k]) * NC + coarse_ref[tile + k]
                here = pl.ds(pl.multiple_of(block * DENSE, DENSE), DENSE)
                accs[k][here, :] += dense[k]
                diags[k][pl.ds(block, 1), :] += own[k]
    size = NC * DENSE
    each = face_count // len(out_refs)
    for owner in range(face_count):
        out_ref, start = out_refs[owner // each], owner % each * OWNER_ROWS
        here = slice(owner * size, (owner + 1) * size)
        out_ref[start : start + size, :] = (accs[0][here, :] + accs[1][here, :]).astype(BF16)
        here = slice(owner * NC, (owner + 1) * NC)
        out_ref[start + size : start + size + NC, :] = (
            diags[0][here, :] + diags[1][here, :]
        ).astype(BF16)


def join_kernel(kept_ref, came_ref, *out_refs):
    for k, out_ref in enumerate(out_refs):
        here = slice(k * OWNER_ROWS, (k + 1) * OWNER_ROWS)
        total = kept_ref[here, :].astype(F32) + came_ref[here, :].astype(F32)
        out_ref[...] = total.astype(BF16)


def main_kernel(
    elem_count,
    face_count,
    table_hbm,
    named_hbm,
    rhs_hbm,
    inverse_hbm,
    coupling_hbm,
    schur_hbm,
    share_ref,
    left_ref,
    named_ref,
    rhs_ref,
    table_ref,
    inverse_ref,
    coupling_ref,
    schur_ref,
    wide_ref,
    rhs_turned_ref,
    vector_ref,
    sum_ref,
    turned_a_ref,
    turned_b_ref,
    product_a_ref,
    product_b_ref,
    small_sems,
    block_sems,
    schur_sems,
):
    elements = rhs_ref.shape[0]
    modes = rhs_ref.shape[1]
    trace = FACES_PER_ELEM * FACE_COEFFS
    slots = table_ref.shape[0]
    own = left_ref.shape[0]
    capacity = own // face_count
    my_elem = lax.axis_index("elem")
    small = [
        pltpu.make_async_copy(rhs_hbm, rhs_ref, small_sems.at[0]),
        pltpu.make_async_copy(named_hbm, named_ref, small_sems.at[1]),
        pltpu.make_async_copy(table_hbm, table_ref, small_sems.at[2]),
    ]

    def coupling_copy(e):
        return pltpu.make_async_copy(coupling_hbm.at[e], coupling_ref.at[e], block_sems.at[0, e])

    def inverse_copy(e):
        return pltpu.make_async_copy(inverse_hbm.at[e], inverse_ref.at[e], block_sems.at[1, e])

    def leave(e):
        return pltpu.make_async_copy(schur_ref.at[e], schur_hbm.at[e], schur_sems.at[e])

    coupling_copy(0).start()
    for copy in small:
        copy.start()
    inverse_copy(0).start()
    coupling_copy(1).start()
    inverse_copy(1).start()
    coupling_copy(2).start()

    def turn(e, turned_ref):
        turned_ref[...] = coupling_ref[e].T

    def first(e, turned_ref, product_ref):
        for half in range(2):
            here = slice(half * modes // 2, (half + 1) * modes // 2)
            product_ref[:, here] = dot(turned_ref[...], inverse_ref[e, :, here]).astype(BF16)

    def second(e, product_ref):
        split = 2 * LANES
        one = dot(product_ref[...], coupling_ref[e, :, :split])
        wide = jnp.concatenate([coupling_ref[e, :, split:], rhs_turned_ref[...]], axis=1)
        two = dot(product_ref[...], wide)
        schur_ref[e, :, :split] = (-one).astype(BF16)
        schur_ref[e, :, split:] = (-two[:, : trace - split]).astype(BF16)
        vector = vector_ref[pl.ds(e, 1), :]
        one = one * vector[:, :split]
        two = two * vector[:, split:]
        total = (one[:, :LANES] + one[:, LANES:]) + (two[:, :LANES] + two[:, LANES:])
        sums = jnp.sum(total, axis=1, keepdims=True)
        sum_ref[...] = jnp.where(iota((trace, LANES), 1) == e, sums, sum_ref[...])

    turned = (turned_a_ref, turned_b_ref)
    product = (product_a_ref, product_b_ref)

    def advance(e, parity, turning=True, finishing=True):
        if turning:
            @pl.when(e + 2 < elements)
            def _():
                inverse_copy(e + 2).start()

            @pl.when(e + 3 < elements)
            def _():
                coupling_copy(e + 3).start()

            coupling_copy(e + 1).wait()
        inverse_copy(e).wait()
        if turning:
            turn(e + 1, turned[1 - parity])
        first(e, turned[parity], product[parity])
        if finishing:
            second(e - 1, product[1 - parity])
            leave(e - 1).start()

    coupling_copy(0).wait()
    turn(0, turned[0])
    for copy in small:
        copy.wait()
    sum_ref[...] = jnp.zeros_like(sum_ref)
    turn_rhs(rhs_ref, wide_ref, rhs_turned_ref)
    row = iota((PER_FACE, LANES), 0)
    lane = iota((PER_FACE, LANES), 1)

    for a in range(FACES_PER_ELEM):
        hot = named_ref[a * PER_FACE : (a + 1) * PER_FACE, :]
        vector_ref[:, a * LANES : (a + 1) * LANES] = -dot(hot, table_ref[...])
    vector_ref[:, trace:] = (row == lane).astype(F32)
    share_ref[NAMED:, :] = named_ref[NAMED:, :LANES]
    place = position(my_elem, iota((own, slots), 0), elem_count, capacity)
    pick = (iota((own, slots), 1) == place).astype(BF16)
    left_ref[...] = dot(pick, table_ref[...])

    advance(0, 0, finishing=False)

    def two(index, carry):
        advance(2 * index + 1, 1)
        advance(2 * index + 2, 0)
        return carry

    pairs = (elements - 2) // 2
    lax.fori_loop(0, pairs, two, 0)
    for e in range(2 * pairs + 1, elements):
        advance(e, e % 2, turning=e + 1 < elements)
    second(elements - 1, product[(elements - 1) % 2])
    leave(elements - 1).start()

    for a in range(FACES_PER_ELEM):
        shares = sum_ref[a * LANES : (a + 1) * LANES, :].T
        share_ref[a * PER_FACE : (a + 1) * PER_FACE, :] = shares[:PER_FACE].astype(BF16)
    left_ref[...] = less_shares(left_ref[...], share_ref)
    for e in range(elements):
        leave(e).wait()


def less_shares(left, share_ref):
    own = left.shape[0]
    slot = (iota((own, SHARE_ROWS), 0) + lax.axis_index("elem") * own).astype(F32)
    names = share_ref[NAMED:, :].astype(F32)
    named = (names[0:1] * SLOT_BASE + names[1:2])[:, :SHARE_ROWS]
    return left - dot((slot == named).astype(BF16), share_ref[...])


def residual_kernel(left_ref, *refs):
    share_refs, residual_ref = refs[:-1], refs[-1]
    left = left_ref[...]
    for share_ref in share_refs:
        left = less_shares(left, share_ref)
    residual_ref[...] = left


def coarse_kernel(*refs):
    got_refs, (out_ref, sum_ref, full_ref) = refs[:-3], refs[-3:]
    sum_ref[...] = sum(
        got_ref[k : k + OWNER_ROWS, :].astype(F32)
        for got_ref in got_refs
        for k in range(0, got_ref.shape[0], OWNER_ROWS)
    )

    lane = iota((HALF, LANES), 1)
    row = iota((HALF, LANES), 0)
    wide_row = iota((MROW, LANES), 0)
    wide_lane = iota((MROW, LANES), 1)
    top = wide_row < HALF
    held = (top & ((wide_lane <= wide_row) | (wide_lane >= HALF))) | (
        (~top) & (wide_lane >= wide_row)
    )
    for block in range(NC):
        dense = sum_ref[block * DENSE : (block + 1) * DENSE, :]
        upper = jnp.concatenate([dense, pltpu.roll(dense, MROW, 1)], axis=0)
        diag = sum_ref[NC * DENSE + block : NC * DENSE + block + 1, :]
        diag = pltpu.roll(diag + pltpu.roll(diag, MROW, 1), HALF, 1)
        lower = jnp.where(lane == row + HALF, diag, pltpu.roll(upper, HALF, 1))
        given = jnp.concatenate([upper, lower], axis=0)
        turned = jnp.concatenate([given, given], axis=0).T[:MROW]
        full_ref[block * MROW : (block + 1) * MROW, :] = jnp.where(held, given, turned)
    low = iota((NC, LANES), 1) < MROW
    for chunk in range(HALF):
        left = full_ref[pl.ds(2 * chunk, NC, stride=MROW), :]
        right = full_ref[pl.ds(2 * chunk + 1, NC, stride=MROW), :]
        out_ref[:, chunk * LANES : (chunk + 1) * LANES] = jnp.where(
            low, left, pltpu.roll(right, MROW, 1)
        )


ANY = pl.BlockSpec(memory_space=pl.ANY)
VMEM = pl.BlockSpec(memory_space=pltpu.VMEM)


def cost(flops, bytes_accessed):
    return pl.CostEstimate(flops=flops, bytes_accessed=bytes_accessed, transcendentals=0)


def params(limit):
    return pltpu.CompilerParams(vmem_limit_bytes=limit)


def around(block, axis):
    count = lax.axis_size(axis)
    return [block] + [
        lax.ppermute(block, axis, [(i, i ^ k) for i in range(count)]) for k in range(1, count)
    ]


def trade(block, place, face_count):
    elem_count = lax.axis_size("elem")
    bits = face_count.bit_length() - 1
    pairs = []
    for face in range(face_count):
        for elem in range(elem_count):
            other = face
            for k in range(bits):
                swapped = bits > 1 and elem % 2 == 1 and k < 2
                if place >> (bits - 1 - k) & 1:
                    other ^= 1 << (1 - k if swapped else k)
            pairs.append((face * elem_count + elem, other * elem_count + elem))
    return lax.ppermute(block, ("face", "elem"), pairs)


def shards(
    trace_old,
    new_owner,
    mortar_tiles,
    mortar_owner,
    mortar_coarse,
    interior_rhs,
    local_inverse,
    coupling,
    connectivity,
):
    face_count = lax.axis_size("face")
    elem_count = lax.axis_size("elem")
    row_count = trace_old.shape[0]
    tile_count = mortar_tiles.shape[0]
    elements, modes = interior_rhs.shape
    trace = FACES_PER_ELEM * FACE_COEFFS
    capacity = max(2, 2 * row_count // face_count)
    own = face_count * capacity

    slots = own * elem_count
    devices = face_count * elem_count
    paired = face_count <= MOST_PAIRED
    sides = 2 if paired else 1

    blocks = face_count * NC
    sums_shape = (blocks * DENSE, LANES)
    placed, named, *half_grams = pl.pallas_call(
        functools.partial(gram_kernel, elem_count, face_count, capacity, paired),
        out_shape=[
            jax.ShapeDtypeStruct((slots, FACE_COEFFS), BF16),
            jax.ShapeDtypeStruct((SHARE_ROWS, slots), BF16),
        ]
        + [jax.ShapeDtypeStruct((blocks * (DENSE + 1) // sides, LANES), BF16)] * sides,
        in_specs=[ANY] * 6,
        out_specs=[VMEM] * (2 + sides),
        scratch_shapes=[
            pltpu.SMEM((tile_count,), I32),
            pltpu.SMEM((tile_count,), I32),
            pltpu.VMEM(mortar_tiles.shape, BF16),
            pltpu.VMEM((tile_count * PITCH, LANES), F32),
            pltpu.VMEM(sums_shape, F32),
            pltpu.VMEM(sums_shape, F32),
            pltpu.VMEM((blocks, LANES), F32),
            pltpu.VMEM((blocks, LANES), F32),
            pltpu.VMEM((1, row_count), I32),
            pltpu.VMEM(trace_old.shape, BF16),
            pltpu.SMEM((FACES_PER_ELEM, elements), I32),
            pltpu.SemaphoreType.DMA((6,)),
        ],
        compiler_params=params(BIG),
        cost_estimate=cost(4 * tile_count * MROW * MROW * LANES, 12 << 20),
        name="gram",
    )(
        mortar_owner.reshape(tile_count),
        mortar_coarse,
        mortar_tiles,
        new_owner.reshape(1, row_count),
        trace_old,
        connectivity.T,
    )
    if paired:
        came = trade(half_grams[1], face_count // 2, face_count)
    table = lax.all_to_all(
        placed.reshape(devices, capacity, FACE_COEFFS), ("face", "elem"), 0, 0, tiled=True
    ).reshape(slots, FACE_COEFFS)

    if paired:
        joined = pl.pallas_call(
            join_kernel,
            out_shape=[jax.ShapeDtypeStruct((OWNER_ROWS, LANES), BF16)] * (face_count // 2),
            in_specs=[VMEM] * 2,
            out_specs=[VMEM] * (face_count // 2),
            compiler_params=params(SMALL),
            cost_estimate=cost(0, 4 << 20),
            name="join",
        )(half_grams[0], came)
        got = [joined[0]] + [
            trade(joined[k], k, face_count) for k in range(face_count // 2 - 1, 0, -1)
        ]
        before = joined[0]
    else:
        blocked = half_grams[0].reshape(face_count, OWNER_ROWS, LANES)
        got = [lax.all_to_all(blocked, "face", 0, 0, tiled=True).reshape(-1, LANES)]
        before = half_grams[0]

    rhs, _ = lax.optimization_barrier((interior_rhs, before))
    schur_blocks, shares, left = pl.pallas_call(
        functools.partial(main_kernel, elem_count, face_count),
        out_shape=(
            jax.ShapeDtypeStruct((elements, trace, trace), BF16),
            jax.ShapeDtypeStruct((SHARE_ROWS, LANES), BF16),
            jax.ShapeDtypeStruct((own, FACE_COEFFS), F32),
        ),
        in_specs=[ANY] * 5,
        out_specs=(ANY, VMEM, VMEM),
        scratch_shapes=[
            pltpu.VMEM((SHARE_ROWS, slots), BF16),
            pltpu.VMEM((elements, modes), BF16),
            pltpu.VMEM((slots, FACE_COEFFS), BF16),
            pltpu.VMEM((elements, modes, modes), BF16),
            pltpu.VMEM((elements, modes, trace), BF16),
            pltpu.VMEM((elements, trace, trace), BF16),
            pltpu.VMEM((LANES, modes), F32),
            pltpu.VMEM((modes, LANES), BF16),
            pltpu.VMEM((PER_FACE, trace + LANES), F32),
            pltpu.VMEM((trace, LANES), F32),
            pltpu.VMEM((trace, modes), BF16),
            pltpu.VMEM((trace, modes), BF16),
            pltpu.VMEM((trace, modes), BF16),
            pltpu.VMEM((trace, modes), BF16),
            pltpu.SemaphoreType.DMA((3,)),
            pltpu.SemaphoreType.DMA((2, elements)),
            pltpu.SemaphoreType.DMA((elements,)),
        ],
        compiler_params=params(BIG),
        cost_estimate=cost(
            2 * elements * modes * trace * (modes + trace),
            2 * elements * (modes * (modes + trace) + trace * trace),
        ),
        name="condense",
    )(table, named, rhs, local_inverse, coupling)

    all_shares = around(shares, "elem")
    coarse_blocks = pl.pallas_call(
        coarse_kernel,
        out_shape=jax.ShapeDtypeStruct((NC, MROW * MROW), F32),
        in_specs=[VMEM] * len(got),
        out_specs=VMEM,
        scratch_shapes=[
            pltpu.VMEM((OWNER_ROWS, LANES), F32),
            pltpu.VMEM((NC * MROW, LANES), F32),
        ],
        compiler_params=params(SMALL),
        cost_estimate=cost(0, 8 << 20),
        name="coarse",
    )(*got)
    last, coarse_blocks = lax.optimization_barrier((all_shares[-1], coarse_blocks))
    slot_residual = pl.pallas_call(
        residual_kernel,
        out_shape=jax.ShapeDtypeStruct((own, FACE_COEFFS), F32),
        in_specs=[VMEM] * elem_count,
        out_specs=VMEM,
        compiler_params=params(SMALL),
        name="residual",
    )(left, *all_shares[1:-1], last)
    return schur_blocks, slot_residual, coarse_blocks


def solution(mesh):
    return jax.shard_map(
        shards,
        mesh=mesh,
        in_specs=(
            P(("face", "elem"), None),
            P(("face", "elem"), None),
            P(("face", "elem"), None),
            P(("face", "elem"), None),
            P(("face", "elem")),
            P(("face", "elem"), None),
            P(("face", "elem"), None, None),
            P(("face", "elem"), None, None),
            P(("face", "elem"), None),
        ),
        out_specs=(
            P(("face", "elem"), None, None),
            P(("face", "elem"), None),
            P(("face", "elem"), None),
        ),
        check_vma=False,
    )
```

```python
import functools

import jax
import jax.numpy as jnp
from jax import lax
from jax.experimental import pallas as pl
from jax.experimental.pallas import tpu as pltpu
from jax.sharding import PartitionSpec as P

FACE_COEFFS = 128
FACES_PER_ELEM = 3
MROW = 64
MCOL = 96
NC = 16
HALF = MROW // 2
LANES = 128
DENSE = HALF * MROW // LANES
OWNER_ROWS = NC * (DENSE + 1)
PER_FACE = 16
NAMED = FACES_PER_ELEM * PER_FACE
SHARE_ROWS = NAMED + 16
SLOT_BASE = 16
CHUNK = 16
MOST_PAIRED = 8
BIG = 62 << 20
MIDDLE = 52 << 20
SMALL = 12 << 20
PITCH = MROW + 8

BF16 = jnp.bfloat16
F32 = jnp.float32
I32 = jnp.int32

NT = (((1,), (1,)), ((), ()))
TN = (((0,), (0,)), ((), ()))


def iota(shape, dim):
    return lax.broadcasted_iota(I32, shape, dim)


def dot(left, right, dims=(((1,), (0,)), ((), ()))):
    return lax.dot_general(left, right, dims, preferred_element_type=F32)


def divided(value, by):
    shift = by.bit_length() - 1
    assert by == 1 << shift
    return value >> shift, value & (by - 1)


def place_rows(elem_count, face_count, capacity, owners, trace, slots):
    rows = owners.shape[1]
    earlier = (iota((rows, rows), 0) < iota((rows, rows), 1)).astype(BF16)
    hot = (iota((face_count, rows), 0) == owners).astype(F32)
    rank = jnp.sum(hot * dot(hot.astype(BF16), earlier), axis=0, keepdims=True).astype(I32)
    slot = iota((slots, rows), 0)
    wanted = divided(slot, elem_count * capacity)[0] * capacity + divided(slot, capacity)[1]
    place = (wanted == owners * capacity + rank).astype(BF16)
    return dot(place, trace).astype(BF16)


def position(elem, inner, elem_count, capacity):
    face, rank = divided(inner, capacity)
    return (face * elem_count + elem) * capacity + rank


def name_slots(elem_count, face_count, capacity, conn_ref, named_ref):
    elements = conn_ref.shape[1]
    slots = elem_count * face_count * capacity
    row = iota((PER_FACE, LANES), 0)
    lane = iota((PER_FACE, LANES), 1)
    first_lane = iota((1, LANES), 1)
    high = jnp.full((1, LANES), -1, I32)
    rest = jnp.zeros((1, LANES), I32)
    for a in range(FACES_PER_ELEM):
        positions = jnp.full((PER_FACE, LANES), -1, I32)
        for e in range(elements):
            slot = conn_ref[a, e]
            place = position(*divided(slot, face_count * capacity), elem_count, capacity)
            positions = jnp.where(row == e, place, positions)
            here = first_lane == a * PER_FACE + e
            quotient, remainder = divided(slot, SLOT_BASE)
            high = jnp.where(here, quotient, high)
            rest = jnp.where(here, remainder, rest)
        hot = jnp.concatenate([positions == lane + k for k in range(0, slots, LANES)], axis=1)
        named_ref[a * PER_FACE : (a + 1) * PER_FACE, :slots] = hot.astype(BF16)
    names = jnp.where(row == 0, high, jnp.where(row == 1, rest, 0)).astype(F32)
    named_ref[NAMED:SHARE_ROWS, :LANES] = names.astype(BF16)


def gram_kernel(
    elem_count,
    face_count,
    capacity,
    paired,
    owner_hbm,
    coarse_hbm,
    tiles_hbm,
    new_owner_hbm,
    trace_hbm,
    conn_hbm,
    rhs_hbm,
    placed_ref,
    named_ref,
    *refs,
):
    out_refs, refs = refs[:-14], refs[-14:]
    owner_ref, coarse_ref, tiles_ref, rows_ref = refs[:4]
    accs, diags = refs[4:6], refs[6:8]
    new_owner_ref, trace_ref, conn_ref, rhs_ref, wide_ref, sems = refs[8:]

    def place_of(owner):
        if not paired:
            return owner
        other = owner ^ lax.axis_index("face")
        bits = face_count.bit_length() - 1
        odd = lax.axis_index("elem") & 1
        place = [(other >> k) & 1 for k in range(bits)]
        if bits > 1:
            place[:2] = (jnp.where(odd == 1, place[1 - k], place[k]) for k in range(2))
        return sum(bit << (bits - 1 - k) for k, bit in enumerate(place))

    tiles = tiles_ref.shape[0]
    copies = [
        pltpu.make_async_copy(owner_hbm, owner_ref, sems.at[0]),
        pltpu.make_async_copy(coarse_hbm, coarse_ref, sems.at[1]),
        pltpu.make_async_copy(new_owner_hbm, new_owner_ref, sems.at[2]),
        pltpu.make_async_copy(trace_hbm, trace_ref, sems.at[3]),
        pltpu.make_async_copy(tiles_hbm, tiles_ref, sems.at[4]),
    ]
    names = pltpu.make_async_copy(conn_hbm, conn_ref, sems.at[5])
    names.start()
    copies.append(pltpu.make_async_copy(rhs_hbm, rhs_ref, sems.at[6]))
    for copy in copies:
        copy.start()
    for ref in (*accs, *diags):
        ref[...] = jnp.zeros_like(ref)
    names.wait()
    name_slots(elem_count, face_count, capacity, conn_ref, named_ref)
    for copy in copies:
        copy.wait()
    wide_ref[...] = jnp.zeros_like(wide_ref)
    wide_ref[0 : rhs_ref.shape[0], :] = rhs_ref[...].astype(F32)
    named_ref[SHARE_ROWS:, : wide_ref.shape[1]] = wide_ref[...].astype(BF16)
    placed_ref[...] = place_rows(
        elem_count, face_count, capacity, new_owner_ref[...], trace_ref[...], placed_ref.shape[0]
    )

    lane = iota((CHUNK, LANES), 1)
    inside = lane < MCOL
    row = iota((HALF, LANES), 0)
    column = divided(iota((HALF, LANES), 1), MROW)[1]
    swapped = (column > row) & (column < HALF)
    diagonal = column == row
    low = iota((DENSE, LANES), 1) < MROW
    low_wide = iota((MROW, LANES), 1) < MROW
    low_row = iota((1, LANES), 1) < MROW

    for chunk in range(tiles // CHUNK):
        first_tile = chunk * CHUNK
        for group in range(MROW // 4):
            base = group * 3 * LANES
            one, two, three = (
                tiles_ref[
                    first_tile : first_tile + CHUNK, base + k * LANES : base + (k + 1) * LANES
                ].astype(F32)
                for k in range(3)
            )
            rolled = (
                one,
                pltpu.roll(jnp.where(lane < 64, two, one), 32, 1),
                pltpu.roll(jnp.where(lane < 32, three, two), 64, 1),
                pltpu.roll(three, 96, 1),
            )
            for k in range(4):
                rows_ref[pl.ds(first_tile * PITCH + 4 * group + k, CHUNK, stride=PITCH), :] = (
                    jnp.where(inside, rolled[k], 0.0)
                )
        for tile in range(first_tile, first_tile + CHUNK, 2):
            both = jnp.concatenate(
                [
                    rows_ref[t * PITCH : t * PITCH + MROW, :].astype(BF16)
                    for t in (tile, tile + 1)
                ],
                axis=0,
            )
            gram = dot(both, both, NT)
            side = jnp.where(low_wide, gram[:MROW], gram[MROW:])
            lower = pltpu.roll(side[HALF:], LANES - HALF, 1)
            packed = jnp.where(swapped, lower, side[:HALF])
            diag = jnp.sum(jnp.where(diagonal, lower, 0.0), axis=0, keepdims=True)
            turned = pltpu.roll(packed, MROW, 1)
            dense = (
                jnp.where(low, packed[:DENSE], turned[DENSE:]),
                jnp.where(low, turned[:DENSE], packed[DENSE:]),
            )
            own = (jnp.where(low_row, diag, 0.0), jnp.where(low_row, 0.0, diag))
            for k in range(2):
                block = place_of(owner_ref[tile + k]) * NC + coarse_ref[tile + k]
                here = pl.ds(pl.multiple_of(block * DENSE, DENSE), DENSE)
                accs[k][here, :] += dense[k]
                diags[k][pl.ds(block, 1), :] += own[k]
    size = NC * DENSE
    each = face_count // len(out_refs)
    for owner in range(face_count):
        out_ref, start = out_refs[owner // each], owner % each * OWNER_ROWS
        here = slice(owner * size, (owner + 1) * size)
        out_ref[start : start + size, :] = (accs[0][here, :] + accs[1][here, :]).astype(BF16)
        here = slice(owner * NC, (owner + 1) * NC)
        out_ref[start + size : start + size + NC, :] = (
            diags[0][here, :] + diags[1][here, :]
        ).astype(BF16)


def join_kernel(kept_ref, came_ref, *out_refs):
    for k, out_ref in enumerate(out_refs):
        here = slice(k * OWNER_ROWS, (k + 1) * OWNER_ROWS)
        total = kept_ref[here, :].astype(F32) + came_ref[here, :].astype(F32)
        out_ref[...] = total.astype(BF16)


def main_kernel(
    elem_count,
    face_count,
    table_hbm,
    named_hbm,
    inverse_hbm,
    coupling_hbm,
    schur_hbm,
    share_ref,
    left_ref,
    named_ref,
    table_ref,
    inverse_ref,
    coupling_ref,
    schur_ref,
    wide_ref,
    rhs_turned_ref,
    vector_ref,
    sum_ref,
    turned_a_ref,
    turned_b_ref,
    product_a_ref,
    product_b_ref,
    small_sems,
    block_sems,
    schur_sems,
):
    elements, modes = inverse_ref.shape[:2]
    trace = FACES_PER_ELEM * FACE_COEFFS
    slots = table_ref.shape[0]
    own = left_ref.shape[0]
    capacity = own // face_count
    my_elem = lax.axis_index("elem")
    small = [
        pltpu.make_async_copy(named_hbm, named_ref, small_sems.at[0]),
        pltpu.make_async_copy(table_hbm, table_ref, small_sems.at[1]),
    ]

    def coupling_copy(e):
        return pltpu.make_async_copy(coupling_hbm.at[e], coupling_ref.at[e], block_sems.at[0, e])

    def inverse_copy(e):
        return pltpu.make_async_copy(inverse_hbm.at[e], inverse_ref.at[e], block_sems.at[1, e])

    def leave(e):
        return pltpu.make_async_copy(schur_ref.at[e], schur_hbm.at[e], schur_sems.at[e])

    coupling_copy(0).start()
    for copy in small:
        copy.start()
    inverse_copy(0).start()
    coupling_copy(1).start()
    inverse_copy(1).start()
    coupling_copy(2).start()

    def turn(e, turned_ref):
        turned_ref[...] = coupling_ref[e].T

    def first(e, turned_ref, product_ref):
        for half in range(2):
            here = slice(half * modes // 2, (half + 1) * modes // 2)
            product_ref[:, here] = dot(turned_ref[...], inverse_ref[e, :, here]).astype(BF16)

    def second(e, product_ref):
        split = 2 * LANES
        one = dot(product_ref[...], coupling_ref[e, :, :split])
        wide = jnp.concatenate([coupling_ref[e, :, split:], rhs_turned_ref[...]], axis=1)
        two = dot(product_ref[...], wide)
        schur_ref[e, :, :split] = (-one).astype(BF16)
        schur_ref[e, :, split:] = (-two[:, : trace - split]).astype(BF16)
        vector = vector_ref[pl.ds(e, 1), :]
        one = one * vector[:, :split]
        two = two * vector[:, split:]
        total = (one[:, :LANES] + one[:, LANES:]) + (two[:, :LANES] + two[:, LANES:])
        sums = jnp.sum(total, axis=1, keepdims=True)
        sum_ref[...] = jnp.where(iota((trace, LANES), 1) == e, sums, sum_ref[...])

    turned = (turned_a_ref, turned_b_ref)
    product = (product_a_ref, product_b_ref)

    def advance(e, parity, turning=True, finishing=True):
        if turning:
            @pl.when(e + 2 < elements)
            def _():
                inverse_copy(e + 2).start()

            @pl.when(e + 3 < elements)
            def _():
                coupling_copy(e + 3).start()

            coupling_copy(e + 1).wait()
        inverse_copy(e).wait()
        if turning:
            turn(e + 1, turned[1 - parity])
        first(e, turned[parity], product[parity])
        if finishing:
            second(e - 1, product[1 - parity])
            leave(e - 1).start()

    coupling_copy(0).wait()
    turn(0, turned[0])
    for copy in small:
        copy.wait()
    sum_ref[...] = jnp.zeros_like(sum_ref)
    wide_ref[...] = jnp.zeros_like(wide_ref)
    wide_ref[0:PER_FACE, :] = named_ref[SHARE_ROWS:, :modes].astype(F32)
    rhs_turned_ref[...] = wide_ref[...].T.astype(BF16)
    row = iota((PER_FACE, LANES), 0)
    lane = iota((PER_FACE, LANES), 1)

    for a in range(FACES_PER_ELEM):
        hot = named_ref[a * PER_FACE : (a + 1) * PER_FACE, :slots]
        vector_ref[:, a * LANES : (a + 1) * LANES] = -dot(hot, table_ref[...])
    vector_ref[:, trace:] = (row == lane).astype(F32)
    share_ref[NAMED:, :] = named_ref[NAMED:SHARE_ROWS, :LANES]
    place = position(my_elem, iota((own, slots), 0), elem_count, capacity)
    pick = (iota((own, slots), 1) == place).astype(BF16)
    left_ref[...] = dot(pick, table_ref[...])

    advance(0, 0, finishing=False)

    def two(index, carry):
        advance(2 * index + 1, 1)
        advance(2 * index + 2, 0)
        return carry

    pairs = (elements - 2) // 2
    lax.fori_loop(0, pairs, two, 0)
    for e in range(2 * pairs + 1, elements):
        advance(e, e % 2, turning=e + 1 < elements)
    second(elements - 1, product[(elements - 1) % 2])
    leave(elements - 1).start()

    for a in range(FACES_PER_ELEM):
        shares = sum_ref[a * LANES : (a + 1) * LANES, :].T
        share_ref[a * PER_FACE : (a + 1) * PER_FACE, :] = shares[:PER_FACE].astype(BF16)
    left_ref[...] = less_shares(left_ref[...], share_ref)
    for e in range(elements):
        leave(e).wait()


def less_shares(left, share_ref):
    own = left.shape[0]
    slot = (iota((own, SHARE_ROWS), 0) + lax.axis_index("elem") * own).astype(F32)
    names = share_ref[NAMED:, :].astype(F32)
    named = (names[0:1] * SLOT_BASE + names[1:2])[:, :SHARE_ROWS]
    return left - dot((slot == named).astype(BF16), share_ref[...])


def residual_kernel(left_ref, *refs):
    share_refs, residual_ref = refs[:-1], refs[-1]
    left = left_ref[...]
    for share_ref in share_refs:
        left = less_shares(left, share_ref)
    residual_ref[...] = left


def coarse_kernel(*refs):
    got_refs, (out_ref, sum_ref, full_ref) = refs[:-3], refs[-3:]
    sum_ref[...] = sum(
        got_ref[k : k + OWNER_ROWS, :].astype(F32)
        for got_ref in got_refs
        for k in range(0, got_ref.shape[0], OWNER_ROWS)
    )

    lane = iota((HALF, LANES), 1)
    row = iota((HALF, LANES), 0)
    wide_row = iota((MROW, LANES), 0)
    wide_lane = iota((MROW, LANES), 1)
    top = wide_row < HALF
    held = (top & ((wide_lane <= wide_row) | (wide_lane >= HALF))) | (
        (~top) & (wide_lane >= wide_row)
    )
    for block in range(NC):
        dense = sum_ref[block * DENSE : (block + 1) * DENSE, :]
        upper = jnp.concatenate([dense, pltpu.roll(dense, MROW, 1)], axis=0)
        diag = sum_ref[NC * DENSE + block : NC * DENSE + block + 1, :]
        diag = pltpu.roll(diag + pltpu.roll(diag, MROW, 1), HALF, 1)
        lower = jnp.where(lane == row + HALF, diag, pltpu.roll(upper, HALF, 1))
        given = jnp.concatenate([upper, lower], axis=0)
        turned = jnp.concatenate([given, given], axis=0).T[:MROW]
        full_ref[block * MROW : (block + 1) * MROW, :] = jnp.where(held, given, turned)
    low = iota((NC, LANES), 1) < MROW
    for chunk in range(HALF):
        left = full_ref[pl.ds(2 * chunk, NC, stride=MROW), :]
        right = full_ref[pl.ds(2 * chunk + 1, NC, stride=MROW), :]
        out_ref[:, chunk * LANES : (chunk + 1) * LANES] = jnp.where(
            low, left, pltpu.roll(right, MROW, 1)
        )


ANY = pl.BlockSpec(memory_space=pl.ANY)
VMEM = pl.BlockSpec(memory_space=pltpu.VMEM)


def cost(flops, bytes_accessed):
    return pl.CostEstimate(flops=flops, bytes_accessed=bytes_accessed, transcendentals=0)


def params(limit):
    return pltpu.CompilerParams(vmem_limit_bytes=limit)


def around(block, axis):
    count = lax.axis_size(axis)
    return [block] + [
        lax.ppermute(block, axis, [(i, i ^ k) for i in range(count)]) for k in range(1, count)
    ]


def trade(block, place, face_count):
    elem_count = lax.axis_size("elem")
    bits = face_count.bit_length() - 1
    pairs = []
    for face in range(face_count):
        for elem in range(elem_count):
            other = face
            for k in range(bits):
                swapped = bits > 1 and elem % 2 == 1 and k < 2
                if place >> (bits - 1 - k) & 1:
                    other ^= 1 << (1 - k if swapped else k)
            pairs.append((face * elem_count + elem, other * elem_count + elem))
    return lax.ppermute(block, ("face", "elem"), pairs)


def shards(
    trace_old,
    new_owner,
    mortar_tiles,
    mortar_owner,
    mortar_coarse,
    interior_rhs,
    local_inverse,
    coupling,
    connectivity,
):
    face_count = lax.axis_size("face")
    elem_count = lax.axis_size("elem")
    row_count = trace_old.shape[0]
    tile_count = mortar_tiles.shape[0]
    elements, modes = interior_rhs.shape
    trace = FACES_PER_ELEM * FACE_COEFFS
    capacity = max(2, 2 * row_count // face_count)
    own = face_count * capacity

    slots = own * elem_count
    devices = face_count * elem_count
    paired = face_count <= MOST_PAIRED
    named_shape = (SHARE_ROWS + PER_FACE, max(slots, modes))
    sides = 2 if paired else 1

    blocks = face_count * NC
    sums_shape = (blocks * DENSE, LANES)
    placed, named, *half_grams = pl.pallas_call(
        functools.partial(gram_kernel, elem_count, face_count, capacity, paired),
        out_shape=[
            jax.ShapeDtypeStruct((slots, FACE_COEFFS), BF16),
            jax.ShapeDtypeStruct(named_shape, BF16),
        ]
        + [jax.ShapeDtypeStruct((blocks * (DENSE + 1) // sides, LANES), BF16)] * sides,
        in_specs=[ANY] * 7,
        out_specs=[VMEM] * (2 + sides),
        scratch_shapes=[
            pltpu.SMEM((tile_count,), I32),
            pltpu.SMEM((tile_count,), I32),
            pltpu.VMEM(mortar_tiles.shape, BF16),
            pltpu.VMEM((tile_count * PITCH, LANES), F32),
            pltpu.VMEM(sums_shape, F32),
            pltpu.VMEM(sums_shape, F32),
            pltpu.VMEM((blocks, LANES), F32),
            pltpu.VMEM((blocks, LANES), F32),
            pltpu.VMEM((1, row_count), I32),
            pltpu.VMEM(trace_old.shape, BF16),
            pltpu.SMEM((FACES_PER_ELEM, elements), I32),
            pltpu.VMEM((elements, modes), BF16),
            pltpu.VMEM((PER_FACE, modes), F32),
            pltpu.SemaphoreType.DMA((7,)),
        ],
        compiler_params=params(BIG),
        cost_estimate=cost(4 * tile_count * MROW * MROW * LANES, 12 << 20),
        name="gram",
    )(
        mortar_owner.reshape(tile_count),
        mortar_coarse,
        mortar_tiles,
        new_owner.reshape(1, row_count),
        trace_old,
        connectivity.T,
        interior_rhs,
    )
    if paired:
        came = trade(half_grams[1], face_count // 2, face_count)
    table = lax.all_to_all(
        placed.reshape(devices, capacity, FACE_COEFFS), ("face", "elem"), 0, 0, tiled=True
    ).reshape(slots, FACE_COEFFS)

    if paired:
        joined = pl.pallas_call(
            join_kernel,
            out_shape=[jax.ShapeDtypeStruct((OWNER_ROWS, LANES), BF16)] * (face_count // 2),
            in_specs=[VMEM] * 2,
            out_specs=[VMEM] * (face_count // 2),
            compiler_params=params(SMALL),
            cost_estimate=cost(0, 4 << 20),
            name="join",
        )(half_grams[0], came)
        got = [joined[0]] + [
            trade(joined[k], k, face_count) for k in range(face_count // 2 - 1, 0, -1)
        ]
        before = joined[0]
    else:
        blocked = half_grams[0].reshape(face_count, OWNER_ROWS, LANES)
        got = [lax.all_to_all(blocked, "face", 0, 0, tiled=True).reshape(-1, LANES)]
        before = half_grams[0]

    named, _ = lax.optimization_barrier((named, before))
    schur_blocks, shares, left = pl.pallas_call(
        functools.partial(main_kernel, elem_count, face_count),
        out_shape=(
            jax.ShapeDtypeStruct((elements, trace, trace), BF16),
            jax.ShapeDtypeStruct((SHARE_ROWS, LANES), BF16),
            jax.ShapeDtypeStruct((own, FACE_COEFFS), F32),
        ),
        in_specs=[ANY] * 4,
        out_specs=(ANY, VMEM, VMEM),
        scratch_shapes=[
            pltpu.VMEM(named_shape, BF16),
            pltpu.VMEM((slots, FACE_COEFFS), BF16),
            pltpu.VMEM((elements, modes, modes), BF16),
            pltpu.VMEM((elements, modes, trace), BF16),
            pltpu.VMEM((elements, trace, trace), BF16),
            pltpu.VMEM((LANES, modes), F32),
            pltpu.VMEM((modes, LANES), BF16),
            pltpu.VMEM((PER_FACE, trace + LANES), F32),
            pltpu.VMEM((trace, LANES), F32),
            pltpu.VMEM((trace, modes), BF16),
            pltpu.VMEM((trace, modes), BF16),
            pltpu.VMEM((trace, modes), BF16),
            pltpu.VMEM((trace, modes), BF16),
            pltpu.SemaphoreType.DMA((2,)),
            pltpu.SemaphoreType.DMA((2, elements)),
            pltpu.SemaphoreType.DMA((elements,)),
        ],
        compiler_params=params(MIDDLE),
        cost_estimate=cost(
            2 * elements * modes * trace * (modes + trace),
            2 * elements * (modes * (modes + trace) + trace * trace),
        ),
        name="condense",
    )(table, named, local_inverse, coupling)

    all_shares = around(shares, "elem")
    coarse_blocks = pl.pallas_call(
        coarse_kernel,
        out_shape=jax.ShapeDtypeStruct((NC, MROW * MROW), F32),
        in_specs=[VMEM] * len(got),
        out_specs=VMEM,
        scratch_shapes=[
            pltpu.VMEM((OWNER_ROWS, LANES), F32),
            pltpu.VMEM((NC * MROW, LANES), F32),
        ],
        compiler_params=params(SMALL),
        cost_estimate=cost(0, 8 << 20),
        name="coarse",
    )(*got)
    last, coarse_blocks = lax.optimization_barrier((all_shares[-1], coarse_blocks))
    slot_residual = pl.pallas_call(
        residual_kernel,
        out_shape=jax.ShapeDtypeStruct((own, FACE_COEFFS), F32),
        in_specs=[VMEM] * elem_count,
        out_specs=VMEM,
        compiler_params=params(SMALL),
        name="residual",
    )(left, *all_shares[1:-1], last)
    return schur_blocks, slot_residual, coarse_blocks


def solution(mesh):
    return jax.shard_map(
        shards,
        mesh=mesh,
        in_specs=(
            P(("face", "elem"), None),
            P(("face", "elem"), None),
            P(("face", "elem"), None),
            P(("face", "elem"), None),
            P(("face", "elem")),
            P(("face", "elem"), None),
            P(("face", "elem"), None, None),
            P(("face", "elem"), None, None),
            P(("face", "elem"), None),
        ),
        out_specs=(
            P(("face", "elem"), None, None),
            P(("face", "elem"), None),
            P(("face", "elem"), None),
        ),
        check_vma=False,
    )
```

```python
import functools

import jax
import jax.numpy as jnp
from jax import lax
from jax.experimental import pallas as pl
from jax.experimental.pallas import tpu as pltpu
from jax.sharding import PartitionSpec as P

FACE_COEFFS = 128
FACES_PER_ELEM = 3
MROW = 64
MCOL = 96
NC = 16
HALF = MROW // 2
LANES = 128
DENSE = HALF * MROW // LANES
OWNER_ROWS = NC * (DENSE + 1)
PER_FACE = 16
NAMED = FACES_PER_ELEM * PER_FACE
SHARE_ROWS = NAMED + 16
SLOT_BASE = 16
CHUNK = 16
MOST_PAIRED = 8
BIG = 62 << 20
MIDDLE = 52 << 20
SMALL = 12 << 20
PITCH = MROW + 8

BF16 = jnp.bfloat16
F32 = jnp.float32
I32 = jnp.int32

NT = (((1,), (1,)), ((), ()))
TN = (((0,), (0,)), ((), ()))


def iota(shape, dim):
    return lax.broadcasted_iota(I32, shape, dim)


def dot(left, right, dims=(((1,), (0,)), ((), ()))):
    return lax.dot_general(left, right, dims, preferred_element_type=F32)


def divided(value, by):
    shift = by.bit_length() - 1
    assert by == 1 << shift
    return value >> shift, value & (by - 1)


def place_rows(elem_count, face_count, capacity, owners, trace, slots):
    rows = owners.shape[1]
    earlier = (iota((rows, rows), 0) < iota((rows, rows), 1)).astype(BF16)
    hot = (iota((face_count, rows), 0) == owners).astype(F32)
    rank = jnp.sum(hot * dot(hot.astype(BF16), earlier), axis=0, keepdims=True).astype(I32)
    slot = iota((slots, rows), 0)
    wanted = divided(slot, elem_count * capacity)[0] * capacity + divided(slot, capacity)[1]
    place = (wanted == owners * capacity + rank).astype(BF16)
    return dot(place, trace).astype(BF16)


def position(elem, inner, elem_count, capacity):
    face, rank = divided(inner, capacity)
    return (face * elem_count + elem) * capacity + rank


def name_slots(elem_count, face_count, capacity, conn_ref, named_ref):
    elements = conn_ref.shape[1]
    slots = elem_count * face_count * capacity
    row = iota((PER_FACE, LANES), 0)
    lane = iota((PER_FACE, LANES), 1)
    first_lane = iota((1, LANES), 1)
    high = jnp.full((1, LANES), -1, I32)
    rest = jnp.zeros((1, LANES), I32)
    for a in range(FACES_PER_ELEM):
        positions = jnp.full((PER_FACE, LANES), -1, I32)
        for e in range(elements):
            slot = conn_ref[a, e]
            place = position(*divided(slot, face_count * capacity), elem_count, capacity)
            positions = jnp.where(row == e, place, positions)
            here = first_lane == a * PER_FACE + e
            quotient, remainder = divided(slot, SLOT_BASE)
            high = jnp.where(here, quotient, high)
            rest = jnp.where(here, remainder, rest)
        hot = jnp.concatenate([positions == lane + k for k in range(0, slots, LANES)], axis=1)
        named_ref[a * PER_FACE : (a + 1) * PER_FACE, :slots] = hot.astype(BF16)
    names = jnp.where(row == 0, high, jnp.where(row == 1, rest, 0)).astype(F32)
    named_ref[NAMED:SHARE_ROWS, :LANES] = names.astype(BF16)


def gram_kernel(
    elem_count,
    face_count,
    capacity,
    paired,
    owner_hbm,
    coarse_hbm,
    tiles_hbm,
    new_owner_hbm,
    trace_hbm,
    conn_hbm,
    rhs_hbm,
    placed_ref,
    *refs,
):
    if paired:
        *refs, named_ref = refs
    else:
        named_ref, *refs = refs
    out_refs, refs = refs[:-14], refs[-14:]
    owner_ref, coarse_ref, tiles_ref, rows_ref = refs[:4]
    accs, diags = refs[4:6], refs[6:8]
    new_owner_ref, trace_ref, conn_ref, rhs_ref, wide_ref, sems = refs[8:]

    def place_of(owner):
        if not paired:
            return owner
        other = owner ^ lax.axis_index("face")
        bits = face_count.bit_length() - 1
        odd = lax.axis_index("elem") & 1
        place = [(other >> k) & 1 for k in range(bits)]
        if bits > 1:
            place[:2] = (jnp.where(odd == 1, place[1 - k], place[k]) for k in range(2))
        return sum(bit << (bits - 1 - k) for k, bit in enumerate(place))

    tiles = tiles_ref.shape[0]
    copies = [
        pltpu.make_async_copy(owner_hbm, owner_ref, sems.at[0]),
        pltpu.make_async_copy(coarse_hbm, coarse_ref, sems.at[1]),
        pltpu.make_async_copy(new_owner_hbm, new_owner_ref, sems.at[2]),
        pltpu.make_async_copy(trace_hbm, trace_ref, sems.at[3]),
        pltpu.make_async_copy(tiles_hbm, tiles_ref, sems.at[4]),
    ]
    names = pltpu.make_async_copy(conn_hbm, conn_ref, sems.at[5])
    names.start()
    copies.append(pltpu.make_async_copy(rhs_hbm, rhs_ref, sems.at[6]))
    for copy in copies:
        copy.start()
    for ref in (*accs, *diags):
        ref[...] = jnp.zeros_like(ref)
    names.wait()
    name_slots(elem_count, face_count, capacity, conn_ref, named_ref)
    for copy in copies:
        copy.wait()
    wide_ref[...] = jnp.zeros_like(wide_ref)
    wide_ref[0 : rhs_ref.shape[0], :] = rhs_ref[...].astype(F32)
    named_ref[SHARE_ROWS:, : wide_ref.shape[1]] = wide_ref[...].astype(BF16)
    placed_ref[...] = place_rows(
        elem_count, face_count, capacity, new_owner_ref[...], trace_ref[...], placed_ref.shape[0]
    )

    lane = iota((CHUNK, LANES), 1)
    inside = lane < MCOL
    row = iota((HALF, LANES), 0)
    column = divided(iota((HALF, LANES), 1), MROW)[1]
    swapped = (column > row) & (column < HALF)
    diagonal = column == row
    low = iota((DENSE, LANES), 1) < MROW
    low_wide = iota((MROW, LANES), 1) < MROW
    low_row = iota((1, LANES), 1) < MROW

    for chunk in range(tiles // CHUNK):
        first_tile = chunk * CHUNK
        for group in range(MROW // 4):
            base = group * 3 * LANES
            one, two, three = (
                tiles_ref[
                    first_tile : first_tile + CHUNK, base + k * LANES : base + (k + 1) * LANES
                ].astype(F32)
                for k in range(3)
            )
            rolled = (
                one,
                pltpu.roll(jnp.where(lane < 64, two, one), 32, 1),
                pltpu.roll(jnp.where(lane < 32, three, two), 64, 1),
                pltpu.roll(three, 96, 1),
            )
            for k in range(4):
                rows_ref[pl.ds(first_tile * PITCH + 4 * group + k, CHUNK, stride=PITCH), :] = (
                    jnp.where(inside, rolled[k], 0.0)
                )
        for tile in range(first_tile, first_tile + CHUNK, 2):
            both = jnp.concatenate(
                [
                    rows_ref[t * PITCH : t * PITCH + MROW, :].astype(BF16)
                    for t in (tile, tile + 1)
                ],
                axis=0,
            )
            gram = dot(both, both, NT)
            side = jnp.where(low_wide, gram[:MROW], gram[MROW:])
            lower = pltpu.roll(side[HALF:], LANES - HALF, 1)
            packed = jnp.where(swapped, lower, side[:HALF])
            diag = jnp.sum(jnp.where(diagonal, lower, 0.0), axis=0, keepdims=True)
            turned = pltpu.roll(packed, MROW, 1)
            dense = (
                jnp.where(low, packed[:DENSE], turned[DENSE:]),
                jnp.where(low, turned[:DENSE], packed[DENSE:]),
            )
            own = (jnp.where(low_row, diag, 0.0), jnp.where(low_row, 0.0, diag))
            for k in range(2):
                block = place_of(owner_ref[tile + k]) * NC + coarse_ref[tile + k]
                here = pl.ds(pl.multiple_of(block * DENSE, DENSE), DENSE)
                accs[k][here, :] += dense[k]
                diags[k][pl.ds(block, 1), :] += own[k]
    size = NC * DENSE
    each = face_count // len(out_refs)
    for owner in range(face_count):
        out_ref, start = out_refs[owner // each], owner % each * OWNER_ROWS
        here = slice(owner * size, (owner + 1) * size)
        out_ref[start : start + size, :] = (accs[0][here, :] + accs[1][here, :]).astype(BF16)
        here = slice(owner * NC, (owner + 1) * NC)
        out_ref[start + size : start + size + NC, :] = (
            diags[0][here, :] + diags[1][here, :]
        ).astype(BF16)
    if paired:
        rows = named_ref.shape[0]
        for k in range(named_ref.shape[1] // LANES):
            start = each * OWNER_ROWS + k * rows
            out_refs[0][start : start + rows, :] = named_ref[:, k * LANES : (k + 1) * LANES]


def join_kernel(kept_ref, came_ref, named_ref, *out_refs):
    for k, out_ref in enumerate(out_refs):
        here = slice(k * OWNER_ROWS, (k + 1) * OWNER_ROWS)
        total = kept_ref[here, :].astype(F32) + came_ref[here, :].astype(F32)
        out_ref[...] = total.astype(BF16)
    rows = named_ref.shape[0]
    for k in range(named_ref.shape[1] // LANES):
        start = came_ref.shape[0] + k * rows
        named_ref[:, k * LANES : (k + 1) * LANES] = kept_ref[start : start + rows, :]


def main_kernel(
    elem_count,
    face_count,
    table_hbm,
    named_hbm,
    inverse_hbm,
    coupling_hbm,
    schur_hbm,
    share_ref,
    left_ref,
    named_ref,
    table_ref,
    inverse_ref,
    coupling_ref,
    schur_ref,
    wide_ref,
    rhs_turned_ref,
    vector_ref,
    sum_ref,
    turned_a_ref,
    turned_b_ref,
    product_a_ref,
    product_b_ref,
    small_sems,
    block_sems,
    schur_sems,
):
    elements, modes = inverse_ref.shape[:2]
    trace = FACES_PER_ELEM * FACE_COEFFS
    slots = table_ref.shape[0]
    own = left_ref.shape[0]
    capacity = own // face_count
    my_elem = lax.axis_index("elem")
    small = [
        pltpu.make_async_copy(named_hbm, named_ref, small_sems.at[0]),
        pltpu.make_async_copy(table_hbm, table_ref, small_sems.at[1]),
    ]

    def coupling_copy(e):
        return pltpu.make_async_copy(coupling_hbm.at[e], coupling_ref.at[e], block_sems.at[0, e])

    def inverse_copy(e):
        return pltpu.make_async_copy(inverse_hbm.at[e], inverse_ref.at[e], block_sems.at[1, e])

    def leave(e):
        return pltpu.make_async_copy(schur_ref.at[e], schur_hbm.at[e], schur_sems.at[e])

    coupling_copy(0).start()
    for copy in small:
        copy.start()
    inverse_copy(0).start()
    coupling_copy(1).start()
    inverse_copy(1).start()
    coupling_copy(2).start()

    def turn(e, turned_ref):
        turned_ref[...] = coupling_ref[e].T

    def first(e, turned_ref, product_ref):
        for half in range(2):
            here = slice(half * modes // 2, (half + 1) * modes // 2)
            product_ref[:, here] = dot(turned_ref[...], inverse_ref[e, :, here]).astype(BF16)

    def second(e, product_ref):
        split = 2 * LANES
        one = dot(product_ref[...], coupling_ref[e, :, :split])
        wide = jnp.concatenate([coupling_ref[e, :, split:], rhs_turned_ref[...]], axis=1)
        two = dot(product_ref[...], wide)
        schur_ref[e, :, :split] = (-one).astype(BF16)
        schur_ref[e, :, split:] = (-two[:, : trace - split]).astype(BF16)
        vector = vector_ref[pl.ds(e, 1), :]
        one = one * vector[:, :split]
        two = two * vector[:, split:]
        total = (one[:, :LANES] + one[:, LANES:]) + (two[:, :LANES] + two[:, LANES:])
        sums = jnp.sum(total, axis=1, keepdims=True)
        sum_ref[...] = jnp.where(iota((trace, LANES), 1) == e, sums, sum_ref[...])

    turned = (turned_a_ref, turned_b_ref)
    product = (product_a_ref, product_b_ref)

    def advance(e, parity, turning=True, finishing=True):
        if turning:
            @pl.when(e + 2 < elements)
            def _():
                inverse_copy(e + 2).start()

            @pl.when(e + 3 < elements)
            def _():
                coupling_copy(e + 3).start()

            coupling_copy(e + 1).wait()
        inverse_copy(e).wait()
        if turning:
            turn(e + 1, turned[1 - parity])
        first(e, turned[parity], product[parity])
        if finishing:
            second(e - 1, product[1 - parity])
            leave(e - 1).start()

    coupling_copy(0).wait()
    turn(0, turned[0])
    for copy in small:
        copy.wait()
    sum_ref[...] = jnp.zeros_like(sum_ref)
    wide_ref[...] = jnp.zeros_like(wide_ref)
    wide_ref[0:PER_FACE, :] = named_ref[SHARE_ROWS:, :modes].astype(F32)
    rhs_turned_ref[...] = wide_ref[...].T.astype(BF16)
    row = iota((PER_FACE, LANES), 0)
    lane = iota((PER_FACE, LANES), 1)

    for a in range(FACES_PER_ELEM):
        hot = named_ref[a * PER_FACE : (a + 1) * PER_FACE, :slots]
        vector_ref[:, a * LANES : (a + 1) * LANES] = -dot(hot, table_ref[...])
    vector_ref[:, trace:] = (row == lane).astype(F32)
    share_ref[NAMED:, :] = named_ref[NAMED:SHARE_ROWS, :LANES]
    place = position(my_elem, iota((own, slots), 0), elem_count, capacity)
    pick = (iota((own, slots), 1) == place).astype(BF16)
    left_ref[...] = dot(pick, table_ref[...])

    advance(0, 0, finishing=False)

    def two(index, carry):
        advance(2 * index + 1, 1)
        advance(2 * index + 2, 0)
        return carry

    pairs = (elements - 2) // 2
    lax.fori_loop(0, pairs, two, 0)
    for e in range(2 * pairs + 1, elements):
        advance(e, e % 2, turning=e + 1 < elements)
    second(elements - 1, product[(elements - 1) % 2])
    leave(elements - 1).start()

    for a in range(FACES_PER_ELEM):
        shares = sum_ref[a * LANES : (a + 1) * LANES, :].T
        share_ref[a * PER_FACE : (a + 1) * PER_FACE, :] = shares[:PER_FACE].astype(BF16)
    left_ref[...] = less_shares(left_ref[...], share_ref)
    for e in range(elements):
        leave(e).wait()


def less_shares(left, share_ref):
    own = left.shape[0]
    slot = (iota((own, SHARE_ROWS), 0) + lax.axis_index("elem") * own).astype(F32)
    names = share_ref[NAMED:, :].astype(F32)
    named = (names[0:1] * SLOT_BASE + names[1:2])[:, :SHARE_ROWS]
    return left - dot((slot == named).astype(BF16), share_ref[...])


def residual_kernel(left_ref, *refs):
    share_refs, residual_ref = refs[:-1], refs[-1]
    left = left_ref[...]
    for share_ref in share_refs:
        left = less_shares(left, share_ref)
    residual_ref[...] = left


def coarse_kernel(*refs):
    got_refs, (out_ref, sum_ref, full_ref) = refs[:-3], refs[-3:]
    sum_ref[...] = sum(
        got_ref[k : k + OWNER_ROWS, :].astype(F32)
        for got_ref in got_refs
        for k in range(0, got_ref.shape[0], OWNER_ROWS)
    )

    lane = iota((HALF, LANES), 1)
    row = iota((HALF, LANES), 0)
    wide_row = iota((MROW, LANES), 0)
    wide_lane = iota((MROW, LANES), 1)
    top = wide_row < HALF
    held = (top & ((wide_lane <= wide_row) | (wide_lane >= HALF))) | (
        (~top) & (wide_lane >= wide_row)
    )
    for block in range(NC):
        dense = sum_ref[block * DENSE : (block + 1) * DENSE, :]
        upper = jnp.concatenate([dense, pltpu.roll(dense, MROW, 1)], axis=0)
        diag = sum_ref[NC * DENSE + block : NC * DENSE + block + 1, :]
        diag = pltpu.roll(diag + pltpu.roll(diag, MROW, 1), HALF, 1)
        lower = jnp.where(lane == row + HALF, diag, pltpu.roll(upper, HALF, 1))
        given = jnp.concatenate([upper, lower], axis=0)
        turned = jnp.concatenate([given, given], axis=0).T[:MROW]
        full_ref[block * MROW : (block + 1) * MROW, :] = jnp.where(held, given, turned)
    low = iota((NC, LANES), 1) < MROW
    for chunk in range(HALF):
        left = full_ref[pl.ds(2 * chunk, NC, stride=MROW), :]
        right = full_ref[pl.ds(2 * chunk + 1, NC, stride=MROW), :]
        out_ref[:, chunk * LANES : (chunk + 1) * LANES] = jnp.where(
            low, left, pltpu.roll(right, MROW, 1)
        )


ANY = pl.BlockSpec(memory_space=pl.ANY)
VMEM = pl.BlockSpec(memory_space=pltpu.VMEM)


def cost(flops, bytes_accessed):
    return pl.CostEstimate(flops=flops, bytes_accessed=bytes_accessed, transcendentals=0)


def params(limit):
    return pltpu.CompilerParams(vmem_limit_bytes=limit)


def around(block, axis):
    count = lax.axis_size(axis)
    return [block] + [
        lax.ppermute(block, axis, [(i, i ^ k) for i in range(count)]) for k in range(1, count)
    ]


def trade(block, place, face_count):
    elem_count = lax.axis_size("elem")
    bits = face_count.bit_length() - 1
    pairs = []
    for face in range(face_count):
        for elem in range(elem_count):
            other = face
            for k in range(bits):
                swapped = bits > 1 and elem % 2 == 1 and k < 2
                if place >> (bits - 1 - k) & 1:
                    other ^= 1 << (1 - k if swapped else k)
            pairs.append((face * elem_count + elem, other * elem_count + elem))
    return lax.ppermute(block, ("face", "elem"), pairs)


def shards(
    trace_old,
    new_owner,
    mortar_tiles,
    mortar_owner,
    mortar_coarse,
    interior_rhs,
    local_inverse,
    coupling,
    connectivity,
):
    face_count = lax.axis_size("face")
    elem_count = lax.axis_size("elem")
    row_count = trace_old.shape[0]
    tile_count = mortar_tiles.shape[0]
    elements, modes = interior_rhs.shape
    trace = FACES_PER_ELEM * FACE_COEFFS
    capacity = max(2, 2 * row_count // face_count)
    own = face_count * capacity

    slots = own * elem_count
    devices = face_count * elem_count
    paired = face_count <= MOST_PAIRED
    named_shape = (SHARE_ROWS + PER_FACE, max(slots, modes))
    sides = 2 if paired else 1

    blocks = face_count * NC
    sums_shape = (blocks * DENSE, LANES)
    half = (blocks * (DENSE + 1) // sides, LANES)
    named_out = jax.ShapeDtypeStruct(named_shape, BF16)
    if paired:
        more = named_shape[0] * named_shape[1] // LANES
        outs = [jax.ShapeDtypeStruct((half[0] + more, LANES), BF16), jax.ShapeDtypeStruct(half, BF16)]
    else:
        outs = [named_out, jax.ShapeDtypeStruct(half, BF16)]
    placed, *half_grams = pl.pallas_call(
        functools.partial(gram_kernel, elem_count, face_count, capacity, paired),
        out_shape=[jax.ShapeDtypeStruct((slots, FACE_COEFFS), BF16)] + outs,
        in_specs=[ANY] * 7,
        out_specs=[VMEM] * (1 + len(outs)),
        scratch_shapes=[
            pltpu.SMEM((tile_count,), I32),
            pltpu.SMEM((tile_count,), I32),
            pltpu.VMEM(mortar_tiles.shape, BF16),
            pltpu.VMEM((tile_count * PITCH, LANES), F32),
            pltpu.VMEM(sums_shape, F32),
            pltpu.VMEM(sums_shape, F32),
            pltpu.VMEM((blocks, LANES), F32),
            pltpu.VMEM((blocks, LANES), F32),
            pltpu.VMEM((1, row_count), I32),
            pltpu.VMEM(trace_old.shape, BF16),
            pltpu.SMEM((FACES_PER_ELEM, elements), I32),
            pltpu.VMEM((elements, modes), BF16),
            pltpu.VMEM((PER_FACE, modes), F32),
            pltpu.SemaphoreType.DMA((7,)),
        ]
        + [pltpu.VMEM(named_shape, BF16)] * paired,
        compiler_params=params(BIG),
        cost_estimate=cost(4 * tile_count * MROW * MROW * LANES, 12 << 20),
        name="gram",
    )(
        mortar_owner.reshape(tile_count),
        mortar_coarse,
        mortar_tiles,
        new_owner.reshape(1, row_count),
        trace_old,
        connectivity.T,
        interior_rhs,
    )
    if paired:
        came = trade(half_grams[1], face_count // 2, face_count)
    table = lax.all_to_all(
        placed.reshape(devices, capacity, FACE_COEFFS), ("face", "elem"), 0, 0, tiled=True
    ).reshape(slots, FACE_COEFFS)

    if paired:
        named, *joined = pl.pallas_call(
            join_kernel,
            out_shape=[named_out]
            + [jax.ShapeDtypeStruct((OWNER_ROWS, LANES), BF16)] * (face_count // 2),
            in_specs=[VMEM] * 2,
            out_specs=[VMEM] * (1 + face_count // 2),
            compiler_params=params(SMALL),
            cost_estimate=cost(0, 4 << 20),
            name="join",
        )(half_grams[0], came)
        got = [joined[0]] + [
            trade(joined[k], k, face_count) for k in range(face_count // 2 - 1, 0, -1)
        ]
    else:
        named, blocked = half_grams
        blocked = blocked.reshape(face_count, OWNER_ROWS, LANES)
        got = [lax.all_to_all(blocked, "face", 0, 0, tiled=True).reshape(-1, LANES)]

    schur_blocks, shares, left = pl.pallas_call(
        functools.partial(main_kernel, elem_count, face_count),
        out_shape=(
            jax.ShapeDtypeStruct((elements, trace, trace), BF16),
            jax.ShapeDtypeStruct((SHARE_ROWS, LANES), BF16),
            jax.ShapeDtypeStruct((own, FACE_COEFFS), F32),
        ),
        in_specs=[ANY] * 4,
        out_specs=(ANY, VMEM, VMEM),
        scratch_shapes=[
            pltpu.VMEM(named_shape, BF16),
            pltpu.VMEM((slots, FACE_COEFFS), BF16),
            pltpu.VMEM((elements, modes, modes), BF16),
            pltpu.VMEM((elements, modes, trace), BF16),
            pltpu.VMEM((elements, trace, trace), BF16),
            pltpu.VMEM((LANES, modes), F32),
            pltpu.VMEM((modes, LANES), BF16),
            pltpu.VMEM((PER_FACE, trace + LANES), F32),
            pltpu.VMEM((trace, LANES), F32),
            pltpu.VMEM((trace, modes), BF16),
            pltpu.VMEM((trace, modes), BF16),
            pltpu.VMEM((trace, modes), BF16),
            pltpu.VMEM((trace, modes), BF16),
            pltpu.SemaphoreType.DMA((2,)),
            pltpu.SemaphoreType.DMA((2, elements)),
            pltpu.SemaphoreType.DMA((elements,)),
        ],
        compiler_params=params(MIDDLE),
        cost_estimate=cost(
            2 * elements * modes * trace * (modes + trace),
            2 * elements * (modes * (modes + trace) + trace * trace),
        ),
        name="condense",
    )(table, named, local_inverse, coupling)

    all_shares = around(shares, "elem")
    coarse_blocks = pl.pallas_call(
        coarse_kernel,
        out_shape=jax.ShapeDtypeStruct((NC, MROW * MROW), F32),
        in_specs=[VMEM] * len(got),
        out_specs=VMEM,
        scratch_shapes=[
            pltpu.VMEM((OWNER_ROWS, LANES), F32),
            pltpu.VMEM((NC * MROW, LANES), F32),
        ],
        compiler_params=params(SMALL),
        cost_estimate=cost(0, 8 << 20),
        name="coarse",
    )(*got)
    last, coarse_blocks = lax.optimization_barrier((all_shares[-1], coarse_blocks))
    slot_residual = pl.pallas_call(
        residual_kernel,
        out_shape=jax.ShapeDtypeStruct((own, FACE_COEFFS), F32),
        in_specs=[VMEM] * elem_count,
        out_specs=VMEM,
        compiler_params=params(SMALL),
        name="residual",
    )(left, *all_shares[1:-1], last)
    return schur_blocks, slot_residual, coarse_blocks


def solution(mesh):
    return jax.shard_map(
        shards,
        mesh=mesh,
        in_specs=(
            P(("face", "elem"), None),
            P(("face", "elem"), None),
            P(("face", "elem"), None),
            P(("face", "elem"), None),
            P(("face", "elem")),
            P(("face", "elem"), None),
            P(("face", "elem"), None, None),
            P(("face", "elem"), None, None),
            P(("face", "elem"), None),
        ),
        out_specs=(
            P(("face", "elem"), None, None),
            P(("face", "elem"), None),
            P(("face", "elem"), None),
        ),
        check_vma=False,
    )
```

```python
import functools

import jax
import jax.numpy as jnp
from jax import lax
from jax.experimental import pallas as pl
from jax.experimental.pallas import tpu as pltpu
from jax.sharding import PartitionSpec as P

FACE_COEFFS = 128
FACES_PER_ELEM = 3
MROW = 64
MCOL = 96
NC = 16
HALF = MROW // 2
LANES = 128
DENSE = HALF * MROW // LANES
OWNER_ROWS = NC * (DENSE + 1)
PER_FACE = 16
NAMED = FACES_PER_ELEM * PER_FACE
SHARE_ROWS = NAMED + 16
SLOT_BASE = 16
ROWS = 8
CHUNK = 16
MOST_PAIRED = 8
BIG = 62 << 20
MIDDLE = 52 << 20
SMALL = 12 << 20
PITCH = MROW + 8

BF16 = jnp.bfloat16
F32 = jnp.float32
I32 = jnp.int32

NT = (((1,), (1,)), ((), ()))
TN = (((0,), (0,)), ((), ()))


def iota(shape, dim):
    return lax.broadcasted_iota(I32, shape, dim)


def dot(left, right, dims=(((1,), (0,)), ((), ()))):
    return lax.dot_general(left, right, dims, preferred_element_type=F32)


def divided(value, by):
    shift = by.bit_length() - 1
    assert by == 1 << shift
    return value >> shift, value & (by - 1)


def place_rows(elem_count, face_count, capacity, owners, trace, slots):
    rows = owners.shape[1]
    earlier = (iota((rows, rows), 0) < iota((rows, rows), 1)).astype(BF16)
    hot = (iota((face_count, rows), 0) == owners).astype(F32)
    rank = jnp.sum(hot * dot(hot.astype(BF16), earlier), axis=0, keepdims=True).astype(I32)
    slot = iota((slots, rows), 0)
    wanted = divided(slot, elem_count * capacity)[0] * capacity + divided(slot, capacity)[1]
    place = (wanted == owners * capacity + rank).astype(BF16)
    return dot(place, trace).astype(BF16)


def position(elem, inner, elem_count, capacity):
    face, rank = divided(inner, capacity)
    return (face * elem_count + elem) * capacity + rank


def name_slots(elem_count, face_count, capacity, conn_ref, named_ref):
    elements = conn_ref.shape[1]
    slots = elem_count * face_count * capacity
    row = iota((PER_FACE, LANES), 0)
    lane = iota((PER_FACE, LANES), 1)
    first_lane = iota((1, LANES), 1)
    high = jnp.full((1, LANES), -1, I32)
    rest = jnp.zeros((1, LANES), I32)
    for a in range(FACES_PER_ELEM):
        positions = jnp.full((PER_FACE, LANES), -1, I32)
        for e in range(elements):
            slot = conn_ref[a, e]
            place = position(*divided(slot, face_count * capacity), elem_count, capacity)
            positions = jnp.where(row == e, place, positions)
            here = first_lane == a * PER_FACE + e
            quotient, remainder = divided(slot, SLOT_BASE)
            high = jnp.where(here, quotient, high)
            rest = jnp.where(here, remainder, rest)
        hot = jnp.concatenate([positions == lane + k for k in range(0, slots, LANES)], axis=1)
        named_ref[a * PER_FACE : (a + 1) * PER_FACE, :slots] = hot.astype(BF16)
    names = jnp.where(row == 0, high, jnp.where(row == 1, rest, 0)).astype(F32)
    named_ref[NAMED:SHARE_ROWS, :LANES] = names.astype(BF16)


def gram_kernel(
    elem_count,
    face_count,
    capacity,
    paired,
    owner_hbm,
    coarse_hbm,
    tiles_hbm,
    new_owner_hbm,
    trace_hbm,
    conn_hbm,
    rhs_hbm,
    placed_ref,
    *refs,
):
    if paired:
        *refs, named_ref = refs
    else:
        named_ref, *refs = refs
    out_refs, refs = refs[:-14], refs[-14:]
    owner_ref, coarse_ref, tiles_ref, rows_ref = refs[:4]
    accs, diags = refs[4:6], refs[6:8]
    new_owner_ref, trace_ref, conn_ref, rhs_ref, wide_ref, sems = refs[8:]

    def place_of(owner):
        if not paired:
            return owner
        other = owner ^ lax.axis_index("face")
        bits = face_count.bit_length() - 1
        odd = lax.axis_index("elem") & 1
        place = [(other >> k) & 1 for k in range(bits)]
        if bits > 1:
            place[:2] = (jnp.where(odd == 1, place[1 - k], place[k]) for k in range(2))
        return sum(bit << (bits - 1 - k) for k, bit in enumerate(place))

    tiles = tiles_ref.shape[0]
    copies = [
        pltpu.make_async_copy(owner_hbm, owner_ref, sems.at[0]),
        pltpu.make_async_copy(coarse_hbm, coarse_ref, sems.at[1]),
        pltpu.make_async_copy(new_owner_hbm, new_owner_ref, sems.at[2]),
        pltpu.make_async_copy(trace_hbm, trace_ref, sems.at[3]),
        pltpu.make_async_copy(tiles_hbm, tiles_ref, sems.at[4]),
    ]
    names = pltpu.make_async_copy(conn_hbm, conn_ref, sems.at[5])
    names.start()
    copies.append(pltpu.make_async_copy(rhs_hbm, rhs_ref, sems.at[6]))
    for copy in copies:
        copy.start()
    for ref in (*accs, *diags):
        ref[...] = jnp.zeros_like(ref)
    names.wait()
    name_slots(elem_count, face_count, capacity, conn_ref, named_ref)
    for copy in copies:
        copy.wait()
    wide_ref[...] = jnp.zeros_like(wide_ref)
    wide_ref[0 : rhs_ref.shape[0], :] = rhs_ref[...].astype(F32)
    named_ref[SHARE_ROWS:, : wide_ref.shape[1]] = wide_ref[...].astype(BF16)
    placed_ref[...] = place_rows(
        elem_count, face_count, capacity, new_owner_ref[...], trace_ref[...], placed_ref.shape[0]
    )

    lane = iota((CHUNK, LANES), 1)
    inside = lane < MCOL
    row = iota((HALF, LANES), 0)
    column = divided(iota((HALF, LANES), 1), MROW)[1]
    swapped = (column > row) & (column < HALF)
    diagonal = column == row
    low = iota((DENSE, LANES), 1) < MROW
    low_wide = iota((MROW, LANES), 1) < MROW
    low_row = iota((1, LANES), 1) < MROW

    for chunk in range(tiles // CHUNK):
        first_tile = chunk * CHUNK
        for group in range(MROW // 4):
            base = group * 3 * LANES
            one, two, three = (
                tiles_ref[
                    first_tile : first_tile + CHUNK, base + k * LANES : base + (k + 1) * LANES
                ].astype(F32)
                for k in range(3)
            )
            rolled = (
                one,
                pltpu.roll(jnp.where(lane < 64, two, one), 32, 1),
                pltpu.roll(jnp.where(lane < 32, three, two), 64, 1),
                pltpu.roll(three, 96, 1),
            )
            for k in range(4):
                rows_ref[pl.ds(first_tile * PITCH + 4 * group + k, CHUNK, stride=PITCH), :] = (
                    jnp.where(inside, rolled[k], 0.0)
                )
        for tile in range(first_tile, first_tile + CHUNK, 2):
            both = jnp.concatenate(
                [
                    rows_ref[t * PITCH : t * PITCH + MROW, :].astype(BF16)
                    for t in (tile, tile + 1)
                ],
                axis=0,
            )
            gram = dot(both, both, NT)
            side = jnp.where(low_wide, gram[:MROW], gram[MROW:])
            lower = pltpu.roll(side[HALF:], LANES - HALF, 1)
            packed = jnp.where(swapped, lower, side[:HALF])
            diag = jnp.sum(jnp.where(diagonal, lower, 0.0), axis=0, keepdims=True)
            turned = pltpu.roll(packed, MROW, 1)
            dense = (
                jnp.where(low, packed[:DENSE], turned[DENSE:]),
                jnp.where(low, turned[:DENSE], packed[DENSE:]),
            )
            own = (jnp.where(low_row, diag, 0.0), jnp.where(low_row, 0.0, diag))
            for k in range(2):
                block = place_of(owner_ref[tile + k]) * NC + coarse_ref[tile + k]
                here = pl.ds(pl.multiple_of(block * DENSE, DENSE), DENSE)
                accs[k][here, :] += dense[k]
                diags[k][pl.ds(block, 1), :] += own[k]
    size = NC * DENSE
    each = face_count // len(out_refs)
    for owner in range(face_count):
        out_ref, start = out_refs[owner // each], owner % each * OWNER_ROWS
        here = slice(owner * size, (owner + 1) * size)
        out_ref[start : start + size, :] = (accs[0][here, :] + accs[1][here, :]).astype(BF16)
        here = slice(owner * NC, (owner + 1) * NC)
        out_ref[start + size : start + size + NC, :] = (
            diags[0][here, :] + diags[1][here, :]
        ).astype(BF16)
    if paired:
        rows = named_ref.shape[0]
        for k in range(named_ref.shape[1] // LANES):
            start = each * OWNER_ROWS + k * rows
            out_refs[0][start : start + rows, :] = named_ref[:, k * LANES : (k + 1) * LANES]


def join_kernel(kept_ref, came_ref, named_ref, *out_refs):
    for k, out_ref in enumerate(out_refs):
        here = slice(k * OWNER_ROWS, (k + 1) * OWNER_ROWS)
        total = kept_ref[here, :].astype(F32) + came_ref[here, :].astype(F32)
        out_ref[...] = total.astype(BF16)
    rows = named_ref.shape[0]
    for k in range(named_ref.shape[1] // LANES):
        start = came_ref.shape[0] + k * rows
        named_ref[:, k * LANES : (k + 1) * LANES] = kept_ref[start : start + rows, :]


def main_kernel(
    elem_count,
    face_count,
    table_hbm,
    named_hbm,
    inverse_hbm,
    coupling_hbm,
    schur_hbm,
    share_ref,
    left_ref,
    named_ref,
    table_ref,
    inverse_ref,
    coupling_ref,
    schur_ref,
    wide_ref,
    rhs_turned_ref,
    vector_ref,
    sum_ref,
    turned_a_ref,
    turned_b_ref,
    product_a_ref,
    product_b_ref,
    small_sems,
    block_sems,
    schur_sems,
):
    elements, modes = inverse_ref.shape[:2]
    trace = FACES_PER_ELEM * FACE_COEFFS
    slots = table_ref.shape[0]
    own = left_ref.shape[0]
    capacity = own // face_count
    my_elem = lax.axis_index("elem")
    small = [
        pltpu.make_async_copy(named_hbm, named_ref, small_sems.at[0]),
        pltpu.make_async_copy(table_hbm, table_ref, small_sems.at[1]),
    ]

    def coupling_copy(e):
        return pltpu.make_async_copy(coupling_hbm.at[e], coupling_ref.at[e], block_sems.at[0, e])

    def inverse_copy(e):
        return pltpu.make_async_copy(inverse_hbm.at[e], inverse_ref.at[e], block_sems.at[1, e])

    def leave(e):
        return pltpu.make_async_copy(schur_ref.at[e], schur_hbm.at[e], schur_sems.at[e])

    coupling_copy(0).start()
    for copy in small:
        copy.start()
    inverse_copy(0).start()
    coupling_copy(1).start()
    inverse_copy(1).start()
    coupling_copy(2).start()

    def turn(e, turned_ref):
        turned_ref[...] = coupling_ref[e].T

    def first(e, turned_ref, product_ref):
        for half in range(2):
            here = slice(half * modes // 2, (half + 1) * modes // 2)
            product_ref[:, here] = dot(turned_ref[...], inverse_ref[e, :, here]).astype(BF16)

    def second(e, product_ref):
        split = 2 * LANES
        one = dot(product_ref[...], coupling_ref[e, :, :split])
        wide = jnp.concatenate([coupling_ref[e, :, split:], rhs_turned_ref[...]], axis=1)
        two = dot(product_ref[...], wide)
        schur_ref[e, :, :split] = (-one).astype(BF16)
        schur_ref[e, :, split:] = (-two[:, : trace - split]).astype(BF16)
        vector = vector_ref[pl.ds(e, 1), :]
        one = one * vector[:, :split]
        two = two * vector[:, split:]
        total = (one[:, :LANES] + one[:, LANES:]) + (two[:, :LANES] + two[:, LANES:])
        sums = jnp.sum(total, axis=1, keepdims=True)
        sum_ref[...] = jnp.where(iota((trace, LANES), 1) == e, sums, sum_ref[...])

    turned = (turned_a_ref, turned_b_ref)
    product = (product_a_ref, product_b_ref)

    def advance(e, parity, turning=True, finishing=True):
        if turning:
            @pl.when(e + 2 < elements)
            def _():
                inverse_copy(e + 2).start()

            @pl.when(e + 3 < elements)
            def _():
                coupling_copy(e + 3).start()

            coupling_copy(e + 1).wait()
        inverse_copy(e).wait()
        if turning:
            turn(e + 1, turned[1 - parity])
        first(e, turned[parity], product[parity])
        if finishing:
            second(e - 1, product[1 - parity])
            leave(e - 1).start()

    coupling_copy(0).wait()
    turn(0, turned[0])
    for copy in small:
        copy.wait()
    sum_ref[...] = jnp.zeros_like(sum_ref)
    wide_ref[...] = jnp.zeros_like(wide_ref)
    wide_ref[0:PER_FACE, :] = named_ref[SHARE_ROWS:, :modes].astype(F32)
    rhs_turned_ref[...] = wide_ref[...].T.astype(BF16)
    row = iota((PER_FACE, LANES), 0)
    lane = iota((PER_FACE, LANES), 1)

    for a in range(FACES_PER_ELEM):
        hot = named_ref[a * PER_FACE : (a + 1) * PER_FACE, :slots]
        vector_ref[:, a * LANES : (a + 1) * LANES] = -dot(hot, table_ref[...])
    vector_ref[:, trace:] = (row == lane).astype(F32)
    share_ref[NAMED:, :] = named_ref[NAMED:SHARE_ROWS, :LANES]
    place = position(my_elem, iota((own, slots), 0), elem_count, capacity)
    pick = (iota((own, slots), 1) == place).astype(BF16)
    left_ref[...] = dot(pick, table_ref[...])

    advance(0, 0, finishing=False)

    def two(index, carry):
        advance(2 * index + 1, 1)
        advance(2 * index + 2, 0)
        return carry

    pairs = (elements - 2) // 2
    lax.fori_loop(0, pairs, two, 0)
    for e in range(2 * pairs + 1, elements):
        advance(e, e % 2, turning=e + 1 < elements)
    second(elements - 1, product[(elements - 1) % 2])
    leave(elements - 1).start()

    for a in range(FACES_PER_ELEM):
        shares = sum_ref[a * LANES : (a + 1) * LANES, :].T
        share_ref[a * PER_FACE : (a + 1) * PER_FACE, :] = shares[:PER_FACE].astype(BF16)
    left_ref[...] = less_shares(left_ref[...], share_ref)
    for e in range(elements):
        leave(e).wait()


def less_shares(left, share_ref):
    own = left.shape[0]
    slot = (iota((own, SHARE_ROWS), 0) + lax.axis_index("elem") * own).astype(F32)
    names = share_ref[NAMED:, :].astype(F32)
    named = (names[0:1] * SLOT_BASE + names[1:2])[:, :SHARE_ROWS]
    return left - dot((slot == named).astype(BF16), share_ref[...])


def residual_kernel(left_ref, *refs):
    share_refs, residual_ref = refs[:-1], refs[-1]
    left = left_ref[...]
    for share_ref in share_refs:
        left = less_shares(left, share_ref)
    residual_ref[...] = left


def coarse_kernel(*refs):
    got_refs, (out_hbm, out_ref, sum_ref, full_ref, sems) = refs[:-5], refs[-5:]
    sum_ref[...] = sum(
        got_ref[k : k + OWNER_ROWS, :].astype(F32)
        for got_ref in got_refs
        for k in range(0, got_ref.shape[0], OWNER_ROWS)
    )

    lane = iota((HALF, LANES), 1)
    row = iota((HALF, LANES), 0)
    wide_row = iota((MROW, LANES), 0)
    wide_lane = iota((MROW, LANES), 1)
    top = wide_row < HALF
    held = (top & ((wide_lane <= wide_row) | (wide_lane >= HALF))) | (
        (~top) & (wide_lane >= wide_row)
    )
    low = iota((ROWS, LANES), 1) < MROW
    copies = []
    for start in range(0, NC, ROWS):
        for block in range(start, start + ROWS):
            dense = sum_ref[block * DENSE : (block + 1) * DENSE, :]
            upper = jnp.concatenate([dense, pltpu.roll(dense, MROW, 1)], axis=0)
            diag = sum_ref[NC * DENSE + block : NC * DENSE + block + 1, :]
            diag = pltpu.roll(diag + pltpu.roll(diag, MROW, 1), HALF, 1)
            lower = jnp.where(lane == row + HALF, diag, pltpu.roll(upper, HALF, 1))
            given = jnp.concatenate([upper, lower], axis=0)
            turned = jnp.concatenate([given, given], axis=0).T[:MROW]
            full_ref[block * MROW : (block + 1) * MROW, :] = jnp.where(held, given, turned)
        for chunk in range(HALF):
            first = start * MROW + 2 * chunk
            left = full_ref[pl.ds(first, ROWS, stride=MROW), :]
            right = full_ref[pl.ds(first + 1, ROWS, stride=MROW), :]
            out_ref[start : start + ROWS, chunk * LANES : (chunk + 1) * LANES] = jnp.where(
                low, left, pltpu.roll(right, MROW, 1)
            )
        here = pl.ds(start, ROWS)
        copies.append(
            pltpu.make_async_copy(out_ref.at[here], out_hbm.at[here], sems.at[start // ROWS])
        )
        copies[-1].start()
    for copy in copies:
        copy.wait()


ANY = pl.BlockSpec(memory_space=pl.ANY)
VMEM = pl.BlockSpec(memory_space=pltpu.VMEM)


def cost(flops, bytes_accessed):
    return pl.CostEstimate(flops=flops, bytes_accessed=bytes_accessed, transcendentals=0)


def params(limit):
    return pltpu.CompilerParams(vmem_limit_bytes=limit)


def around(block, axis):
    count = lax.axis_size(axis)
    return [block] + [
        lax.ppermute(block, axis, [(i, i ^ k) for i in range(count)]) for k in range(1, count)
    ]


def trade(block, place, face_count):
    elem_count = lax.axis_size("elem")
    bits = face_count.bit_length() - 1
    pairs = []
    for face in range(face_count):
        for elem in range(elem_count):
            other = face
            for k in range(bits):
                swapped = bits > 1 and elem % 2 == 1 and k < 2
                if place >> (bits - 1 - k) & 1:
                    other ^= 1 << (1 - k if swapped else k)
            pairs.append((face * elem_count + elem, other * elem_count + elem))
    return lax.ppermute(block, ("face", "elem"), pairs)


def shards(
    trace_old,
    new_owner,
    mortar_tiles,
    mortar_owner,
    mortar_coarse,
    interior_rhs,
    local_inverse,
    coupling,
    connectivity,
):
    face_count = lax.axis_size("face")
    elem_count = lax.axis_size("elem")
    row_count = trace_old.shape[0]
    tile_count = mortar_tiles.shape[0]
    elements, modes = interior_rhs.shape
    trace = FACES_PER_ELEM * FACE_COEFFS
    capacity = max(2, 2 * row_count // face_count)
    own = face_count * capacity

    slots = own * elem_count
    devices = face_count * elem_count
    paired = face_count <= MOST_PAIRED
    named_shape = (SHARE_ROWS + PER_FACE, max(slots, modes))
    sides = 2 if paired else 1

    blocks = face_count * NC
    sums_shape = (blocks * DENSE, LANES)
    half = (blocks * (DENSE + 1) // sides, LANES)
    named_out = jax.ShapeDtypeStruct(named_shape, BF16)
    if paired:
        more = named_shape[0] * named_shape[1] // LANES
        outs = [jax.ShapeDtypeStruct((half[0] + more, LANES), BF16), jax.ShapeDtypeStruct(half, BF16)]
    else:
        outs = [named_out, jax.ShapeDtypeStruct(half, BF16)]
    placed, *half_grams = pl.pallas_call(
        functools.partial(gram_kernel, elem_count, face_count, capacity, paired),
        out_shape=[jax.ShapeDtypeStruct((slots, FACE_COEFFS), BF16)] + outs,
        in_specs=[ANY] * 7,
        out_specs=[VMEM] * (1 + len(outs)),
        scratch_shapes=[
            pltpu.SMEM((tile_count,), I32),
            pltpu.SMEM((tile_count,), I32),
            pltpu.VMEM(mortar_tiles.shape, BF16),
            pltpu.VMEM((tile_count * PITCH, LANES), F32),
            pltpu.VMEM(sums_shape, F32),
            pltpu.VMEM(sums_shape, F32),
            pltpu.VMEM((blocks, LANES), F32),
            pltpu.VMEM((blocks, LANES), F32),
            pltpu.VMEM((1, row_count), I32),
            pltpu.VMEM(trace_old.shape, BF16),
            pltpu.SMEM((FACES_PER_ELEM, elements), I32),
            pltpu.VMEM((elements, modes), BF16),
            pltpu.VMEM((PER_FACE, modes), F32),
            pltpu.SemaphoreType.DMA((7,)),
        ]
        + [pltpu.VMEM(named_shape, BF16)] * paired,
        compiler_params=params(BIG),
        cost_estimate=cost(4 * tile_count * MROW * MROW * LANES, 12 << 20),
        name="gram",
    )(
        mortar_owner.reshape(tile_count),
        mortar_coarse,
        mortar_tiles,
        new_owner.reshape(1, row_count),
        trace_old,
        connectivity.T,
        interior_rhs,
    )
    if paired:
        came = trade(half_grams[1], face_count // 2, face_count)
    table = lax.all_to_all(
        placed.reshape(devices, capacity, FACE_COEFFS), ("face", "elem"), 0, 0, tiled=True
    ).reshape(slots, FACE_COEFFS)

    if paired:
        named, *joined = pl.pallas_call(
            join_kernel,
            out_shape=[named_out]
            + [jax.ShapeDtypeStruct((OWNER_ROWS, LANES), BF16)] * (face_count // 2),
            in_specs=[VMEM] * 2,
            out_specs=[VMEM] * (1 + face_count // 2),
            compiler_params=params(SMALL),
            cost_estimate=cost(0, 4 << 20),
            name="join",
        )(half_grams[0], came)
        got = [joined[0]] + [
            trade(joined[k], k, face_count) for k in range(face_count // 2 - 1, 0, -1)
        ]
    else:
        named, blocked = half_grams
        blocked = blocked.reshape(face_count, OWNER_ROWS, LANES)
        got = [lax.all_to_all(blocked, "face", 0, 0, tiled=True).reshape(-1, LANES)]

    schur_blocks, shares, left = pl.pallas_call(
        functools.partial(main_kernel, elem_count, face_count),
        out_shape=(
            jax.ShapeDtypeStruct((elements, trace, trace), BF16),
            jax.ShapeDtypeStruct((SHARE_ROWS, LANES), BF16),
            jax.ShapeDtypeStruct((own, FACE_COEFFS), F32),
        ),
        in_specs=[ANY] * 4,
        out_specs=(ANY, VMEM, VMEM),
        scratch_shapes=[
            pltpu.VMEM(named_shape, BF16),
            pltpu.VMEM((slots, FACE_COEFFS), BF16),
            pltpu.VMEM((elements, modes, modes), BF16),
            pltpu.VMEM((elements, modes, trace), BF16),
            pltpu.VMEM((elements, trace, trace), BF16),
            pltpu.VMEM((LANES, modes), F32),
            pltpu.VMEM((modes, LANES), BF16),
            pltpu.VMEM((PER_FACE, trace + LANES), F32),
            pltpu.VMEM((trace, LANES), F32),
            pltpu.VMEM((trace, modes), BF16),
            pltpu.VMEM((trace, modes), BF16),
            pltpu.VMEM((trace, modes), BF16),
            pltpu.VMEM((trace, modes), BF16),
            pltpu.SemaphoreType.DMA((2,)),
            pltpu.SemaphoreType.DMA((2, elements)),
            pltpu.SemaphoreType.DMA((elements,)),
        ],
        compiler_params=params(MIDDLE),
        cost_estimate=cost(
            2 * elements * modes * trace * (modes + trace),
            2 * elements * (modes * (modes + trace) + trace * trace),
        ),
        name="condense",
    )(table, named, local_inverse, coupling)

    all_shares = around(shares, "elem")
    coarse_blocks = pl.pallas_call(
        coarse_kernel,
        out_shape=jax.ShapeDtypeStruct((NC, MROW * MROW), F32),
        in_specs=[VMEM] * len(got),
        out_specs=ANY,
        scratch_shapes=[
            pltpu.VMEM((NC, MROW * MROW), F32),
            pltpu.VMEM((OWNER_ROWS, LANES), F32),
            pltpu.VMEM((NC * MROW, LANES), F32),
            pltpu.SemaphoreType.DMA((NC // ROWS,)),
        ],
        compiler_params=params(SMALL),
        cost_estimate=cost(0, 8 << 20),
        name="coarse",
    )(*got)
    last, coarse_blocks = lax.optimization_barrier((all_shares[-1], coarse_blocks))
    slot_residual = pl.pallas_call(
        residual_kernel,
        out_shape=jax.ShapeDtypeStruct((own, FACE_COEFFS), F32),
        in_specs=[VMEM] * elem_count,
        out_specs=VMEM,
        compiler_params=params(SMALL),
        name="residual",
    )(left, *all_shares[1:-1], last)
    return schur_blocks, slot_residual, coarse_blocks


def solution(mesh):
    return jax.shard_map(
        shards,
        mesh=mesh,
        in_specs=(
            P(("face", "elem"), None),
            P(("face", "elem"), None),
            P(("face", "elem"), None),
            P(("face", "elem"), None),
            P(("face", "elem")),
            P(("face", "elem"), None),
            P(("face", "elem"), None, None),
            P(("face", "elem"), None, None),
            P(("face", "elem"), None),
        ),
        out_specs=(
            P(("face", "elem"), None, None),
            P(("face", "elem"), None),
            P(("face", "elem"), None),
        ),
        check_vma=False,
    )
```

```python
import functools

import jax
import jax.numpy as jnp
from jax import lax
from jax.experimental import pallas as pl
from jax.experimental.pallas import tpu as pltpu
from jax.sharding import PartitionSpec as P

FACE_COEFFS = 128
FACES_PER_ELEM = 3
MROW = 64
MCOL = 96
NC = 16
HALF = MROW // 2
LANES = 128
DENSE = HALF * MROW // LANES
OWNER_ROWS = NC * (DENSE + 1)
PER_FACE = 16
NAMED = FACES_PER_ELEM * PER_FACE
SHARE_ROWS = NAMED + 16
SLOT_BASE = 16
CHUNK = 16
MOST_PAIRED = 8
BIG = 62 << 20
MIDDLE = 52 << 20
SMALL = 12 << 20
PITCH = MROW + 8

BF16 = jnp.bfloat16
F32 = jnp.float32
I32 = jnp.int32

NT = (((1,), (1,)), ((), ()))
TN = (((0,), (0,)), ((), ()))


def iota(shape, dim):
    return lax.broadcasted_iota(I32, shape, dim)


def dot(left, right, dims=(((1,), (0,)), ((), ()))):
    return lax.dot_general(left, right, dims, preferred_element_type=F32)


def divided(value, by):
    shift = by.bit_length() - 1
    assert by == 1 << shift
    return value >> shift, value & (by - 1)


def place_rows(elem_count, face_count, capacity, owners, trace, slots):
    rows = owners.shape[1]
    earlier = (iota((rows, rows), 0) < iota((rows, rows), 1)).astype(BF16)
    hot = (iota((face_count, rows), 0) == owners).astype(F32)
    rank = jnp.sum(hot * dot(hot.astype(BF16), earlier), axis=0, keepdims=True).astype(I32)
    slot = iota((slots, rows), 0)
    wanted = divided(slot, elem_count * capacity)[0] * capacity + divided(slot, capacity)[1]
    place = (wanted == owners * capacity + rank).astype(BF16)
    return dot(place, trace).astype(BF16)


def position(elem, inner, elem_count, capacity):
    face, rank = divided(inner, capacity)
    return (face * elem_count + elem) * capacity + rank


def name_slots(elem_count, face_count, capacity, conn_ref, named_ref):
    elements = conn_ref.shape[1]
    slots = elem_count * face_count * capacity
    row = iota((PER_FACE, LANES), 0)
    lane = iota((PER_FACE, LANES), 1)
    first_lane = iota((1, LANES), 1)
    high = jnp.full((1, LANES), -1, I32)
    rest = jnp.zeros((1, LANES), I32)
    for a in range(FACES_PER_ELEM):
        positions = jnp.full((PER_FACE, LANES), -1, I32)
        for e in range(elements):
            slot = conn_ref[a, e]
            place = position(*divided(slot, face_count * capacity), elem_count, capacity)
            positions = jnp.where(row == e, place, positions)
            here = first_lane == a * PER_FACE + e
            quotient, remainder = divided(slot, SLOT_BASE)
            high = jnp.where(here, quotient, high)
            rest = jnp.where(here, remainder, rest)
        hot = jnp.concatenate([positions == lane + k for k in range(0, slots, LANES)], axis=1)
        named_ref[a * PER_FACE : (a + 1) * PER_FACE, :slots] = hot.astype(BF16)
    names = jnp.where(row == 0, high, jnp.where(row == 1, rest, 0)).astype(F32)
    named_ref[NAMED:SHARE_ROWS, :LANES] = names.astype(BF16)


def gram_kernel(
    elem_count,
    face_count,
    capacity,
    paired,
    owner_hbm,
    coarse_hbm,
    tiles_hbm,
    new_owner_hbm,
    trace_hbm,
    conn_hbm,
    rhs_hbm,
    placed_ref,
    *refs,
):
    if paired:
        *refs, named_ref = refs
    else:
        named_ref, *refs = refs
    out_refs, refs = refs[:-14], refs[-14:]
    owner_ref, coarse_ref, tiles_ref, rows_ref = refs[:4]
    accs, diags = refs[4:6], refs[6:8]
    new_owner_ref, trace_ref, conn_ref, rhs_ref, wide_ref, sems = refs[8:]

    def place_of(owner):
        if not paired:
            return owner
        other = owner ^ lax.axis_index("face")
        bits = face_count.bit_length() - 1
        odd = lax.axis_index("elem") & 1
        place = [(other >> k) & 1 for k in range(bits)]
        if bits > 1:
            place[:2] = (jnp.where(odd == 1, place[1 - k], place[k]) for k in range(2))
        return sum(bit << (bits - 1 - k) for k, bit in enumerate(place))

    tiles = tiles_ref.shape[0]
    copies = []
    for k in range(2):
        here = pl.ds(k * tiles // 2, tiles // 2)
        copies.append(
            pltpu.make_async_copy(tiles_hbm.at[here], tiles_ref.at[here], sems.at[4 + k])
        )
        copies[-1].start()
    names = pltpu.make_async_copy(conn_hbm, conn_ref, sems.at[6])
    names.start()
    copies += [
        pltpu.make_async_copy(owner_hbm, owner_ref, sems.at[0]),
        pltpu.make_async_copy(coarse_hbm, coarse_ref, sems.at[1]),
        pltpu.make_async_copy(new_owner_hbm, new_owner_ref, sems.at[2]),
        pltpu.make_async_copy(trace_hbm, trace_ref, sems.at[3]),
        pltpu.make_async_copy(rhs_hbm, rhs_ref, sems.at[7]),
    ]
    for copy in copies[2:]:
        copy.start()
    for ref in (*accs, *diags):
        ref[...] = jnp.zeros_like(ref)
    names.wait()
    name_slots(elem_count, face_count, capacity, conn_ref, named_ref)
    for copy in copies:
        copy.wait()
    wide_ref[...] = jnp.zeros_like(wide_ref)
    wide_ref[0 : rhs_ref.shape[0], :] = rhs_ref[...].astype(F32)
    named_ref[SHARE_ROWS:, : wide_ref.shape[1]] = wide_ref[...].astype(BF16)
    placed_ref[...] = place_rows(
        elem_count, face_count, capacity, new_owner_ref[...], trace_ref[...], placed_ref.shape[0]
    )

    lane = iota((CHUNK, LANES), 1)
    inside = lane < MCOL
    row = iota((HALF, LANES), 0)
    column = divided(iota((HALF, LANES), 1), MROW)[1]
    swapped = (column > row) & (column < HALF)
    diagonal = column == row
    low = iota((DENSE, LANES), 1) < MROW
    low_wide = iota((MROW, LANES), 1) < MROW
    low_row = iota((1, LANES), 1) < MROW

    for chunk in range(tiles // CHUNK):
        first_tile = chunk * CHUNK
        for group in range(MROW // 4):
            base = group * 3 * LANES
            one, two, three = (
                tiles_ref[
                    first_tile : first_tile + CHUNK, base + k * LANES : base + (k + 1) * LANES
                ].astype(F32)
                for k in range(3)
            )
            rolled = (
                one,
                pltpu.roll(jnp.where(lane < 64, two, one), 32, 1),
                pltpu.roll(jnp.where(lane < 32, three, two), 64, 1),
                pltpu.roll(three, 96, 1),
            )
            for k in range(4):
                rows_ref[pl.ds(first_tile * PITCH + 4 * group + k, CHUNK, stride=PITCH), :] = (
                    jnp.where(inside, rolled[k], 0.0)
                )
        for tile in range(first_tile, first_tile + CHUNK, 2):
            both = jnp.concatenate(
                [
                    rows_ref[t * PITCH : t * PITCH + MROW, :].astype(BF16)
                    for t in (tile, tile + 1)
                ],
                axis=0,
            )
            gram = dot(both, both, NT)
            side = jnp.where(low_wide, gram[:MROW], gram[MROW:])
            lower = pltpu.roll(side[HALF:], LANES - HALF, 1)
            packed = jnp.where(swapped, lower, side[:HALF])
            diag = jnp.sum(jnp.where(diagonal, lower, 0.0), axis=0, keepdims=True)
            turned = pltpu.roll(packed, MROW, 1)
            dense = (
                jnp.where(low, packed[:DENSE], turned[DENSE:]),
                jnp.where(low, turned[:DENSE], packed[DENSE:]),
            )
            own = (jnp.where(low_row, diag, 0.0), jnp.where(low_row, 0.0, diag))
            for k in range(2):
                block = place_of(owner_ref[tile + k]) * NC + coarse_ref[tile + k]
                here = pl.ds(pl.multiple_of(block * DENSE, DENSE), DENSE)
                accs[k][here, :] += dense[k]
                diags[k][pl.ds(block, 1), :] += own[k]
    size = NC * DENSE
    each = face_count // len(out_refs)
    for owner in range(face_count):
        out_ref, start = out_refs[owner // each], owner % each * OWNER_ROWS
        here = slice(owner * size, (owner + 1) * size)
        out_ref[start : start + size, :] = (accs[0][here, :] + accs[1][here, :]).astype(BF16)
        here = slice(owner * NC, (owner + 1) * NC)
        out_ref[start + size : start + size + NC, :] = (
            diags[0][here, :] + diags[1][here, :]
        ).astype(BF16)
    if paired:
        rows = named_ref.shape[0]
        for k in range(named_ref.shape[1] // LANES):
            start = each * OWNER_ROWS + k * rows
            out_refs[0][start : start + rows, :] = named_ref[:, k * LANES : (k + 1) * LANES]


def join_kernel(kept_ref, came_ref, named_ref, *out_refs):
    for k, out_ref in enumerate(out_refs):
        here = slice(k * OWNER_ROWS, (k + 1) * OWNER_ROWS)
        total = kept_ref[here, :].astype(F32) + came_ref[here, :].astype(F32)
        out_ref[...] = total.astype(BF16)
    rows = named_ref.shape[0]
    for k in range(named_ref.shape[1] // LANES):
        start = came_ref.shape[0] + k * rows
        named_ref[:, k * LANES : (k + 1) * LANES] = kept_ref[start : start + rows, :]


def main_kernel(
    elem_count,
    face_count,
    table_hbm,
    named_hbm,
    inverse_hbm,
    coupling_hbm,
    schur_hbm,
    share_ref,
    left_ref,
    named_ref,
    table_ref,
    inverse_ref,
    coupling_ref,
    schur_ref,
    wide_ref,
    rhs_turned_ref,
    vector_ref,
    sum_ref,
    turned_a_ref,
    turned_b_ref,
    product_a_ref,
    product_b_ref,
    small_sems,
    block_sems,
    schur_sems,
):
    elements, modes = inverse_ref.shape[:2]
    trace = FACES_PER_ELEM * FACE_COEFFS
    slots = table_ref.shape[0]
    own = left_ref.shape[0]
    capacity = own // face_count
    my_elem = lax.axis_index("elem")
    small = [
        pltpu.make_async_copy(named_hbm, named_ref, small_sems.at[0]),
        pltpu.make_async_copy(table_hbm, table_ref, small_sems.at[1]),
    ]

    def coupling_copy(e):
        return pltpu.make_async_copy(coupling_hbm.at[e], coupling_ref.at[e], block_sems.at[0, e])

    def inverse_copy(e):
        return pltpu.make_async_copy(inverse_hbm.at[e], inverse_ref.at[e], block_sems.at[1, e])

    def leave(e):
        return pltpu.make_async_copy(schur_ref.at[e], schur_hbm.at[e], schur_sems.at[e])

    coupling_copy(0).start()
    inverse_copy(0).start()
    for copy in small:
        copy.start()
    coupling_copy(1).start()
    inverse_copy(1).start()
    coupling_copy(2).start()

    def turn(e, turned_ref):
        turned_ref[...] = coupling_ref[e].T

    def first(e, turned_ref, product_ref):
        for half in range(2):
            here = slice(half * modes // 2, (half + 1) * modes // 2)
            product_ref[:, here] = dot(turned_ref[...], inverse_ref[e, :, here]).astype(BF16)

    def second(e, product_ref):
        split = 2 * LANES
        one = dot(product_ref[...], coupling_ref[e, :, :split])
        wide = jnp.concatenate([coupling_ref[e, :, split:], rhs_turned_ref[...]], axis=1)
        two = dot(product_ref[...], wide)
        schur_ref[e, :, :split] = (-one).astype(BF16)
        schur_ref[e, :, split:] = (-two[:, : trace - split]).astype(BF16)
        vector = vector_ref[pl.ds(e, 1), :]
        one = one * vector[:, :split]
        two = two * vector[:, split:]
        total = (one[:, :LANES] + one[:, LANES:]) + (two[:, :LANES] + two[:, LANES:])
        sums = jnp.sum(total, axis=1, keepdims=True)
        sum_ref[...] = jnp.where(iota((trace, LANES), 1) == e, sums, sum_ref[...])

    turned = (turned_a_ref, turned_b_ref)
    product = (product_a_ref, product_b_ref)

    def advance(e, parity, turning=True, finishing=True):
        if turning:
            @pl.when(e + 2 < elements)
            def _():
                inverse_copy(e + 2).start()

            @pl.when(e + 3 < elements)
            def _():
                coupling_copy(e + 3).start()

            coupling_copy(e + 1).wait()
        inverse_copy(e).wait()
        if turning:
            turn(e + 1, turned[1 - parity])
        first(e, turned[parity], product[parity])
        if finishing:
            second(e - 1, product[1 - parity])
            leave(e - 1).start()

    coupling_copy(0).wait()
    turn(0, turned[0])
    for copy in small:
        copy.wait()
    sum_ref[...] = jnp.zeros_like(sum_ref)
    wide_ref[...] = jnp.zeros_like(wide_ref)
    wide_ref[0:PER_FACE, :] = named_ref[SHARE_ROWS:, :modes].astype(F32)
    rhs_turned_ref[...] = wide_ref[...].T.astype(BF16)
    row = iota((PER_FACE, LANES), 0)
    lane = iota((PER_FACE, LANES), 1)

    for a in range(FACES_PER_ELEM):
        hot = named_ref[a * PER_FACE : (a + 1) * PER_FACE, :slots]
        vector_ref[:, a * LANES : (a + 1) * LANES] = -dot(hot, table_ref[...])
    vector_ref[:, trace:] = (row == lane).astype(F32)
    share_ref[NAMED:, :] = named_ref[NAMED:SHARE_ROWS, :LANES]
    place = position(my_elem, iota((own, slots), 0), elem_count, capacity)
    pick = (iota((own, slots), 1) == place).astype(BF16)
    left_ref[...] = dot(pick, table_ref[...])

    advance(0, 0, finishing=False)

    def two(index, carry):
        advance(2 * index + 1, 1)
        advance(2 * index + 2, 0)
        return carry

    pairs = (elements - 2) // 2
    lax.fori_loop(0, pairs, two, 0)
    for e in range(2 * pairs + 1, elements):
        advance(e, e % 2, turning=e + 1 < elements)
    second(elements - 1, product[(elements - 1) % 2])
    leave(elements - 1).start()

    for a in range(FACES_PER_ELEM):
        shares = sum_ref[a * LANES : (a + 1) * LANES, :].T
        share_ref[a * PER_FACE : (a + 1) * PER_FACE, :] = shares[:PER_FACE].astype(BF16)
    left_ref[...] = less_shares(left_ref[...], share_ref)
    for e in range(elements):
        leave(e).wait()


def less_shares(left, share_ref):
    own = left.shape[0]
    slot = (iota((own, SHARE_ROWS), 0) + lax.axis_index("elem") * own).astype(F32)
    names = share_ref[NAMED:, :].astype(F32)
    named = (names[0:1] * SLOT_BASE + names[1:2])[:, :SHARE_ROWS]
    return left - dot((slot == named).astype(BF16), share_ref[...])


def residual_kernel(left_ref, *refs):
    share_refs, residual_ref = refs[:-1], refs[-1]
    left = left_ref[...]
    for share_ref in share_refs:
        left = less_shares(left, share_ref)
    residual_ref[...] = left


def coarse_kernel(*refs):
    got_refs, (out_ref, sum_ref, full_ref) = refs[:-3], refs[-3:]
    sum_ref[...] = sum(
        got_ref[k : k + OWNER_ROWS, :].astype(F32)
        for got_ref in got_refs
        for k in range(0, got_ref.shape[0], OWNER_ROWS)
    )

    lane = iota((HALF, LANES), 1)
    row = iota((HALF, LANES), 0)
    wide_row = iota((MROW, LANES), 0)
    wide_lane = iota((MROW, LANES), 1)
    top = wide_row < HALF
    held = (top & ((wide_lane <= wide_row) | (wide_lane >= HALF))) | (
        (~top) & (wide_lane >= wide_row)
    )
    for block in range(NC):
        dense = sum_ref[block * DENSE : (block + 1) * DENSE, :]
        upper = jnp.concatenate([dense, pltpu.roll(dense, MROW, 1)], axis=0)
        diag = sum_ref[NC * DENSE + block : NC * DENSE + block + 1, :]
        diag = pltpu.roll(diag + pltpu.roll(diag, MROW, 1), HALF, 1)
        lower = jnp.where(lane == row + HALF, diag, pltpu.roll(upper, HALF, 1))
        given = jnp.concatenate([upper, lower], axis=0)
        turned = jnp.concatenate([given, given], axis=0).T[:MROW]
        full_ref[block * MROW : (block + 1) * MROW, :] = jnp.where(held, given, turned)
    low = iota((NC, LANES), 1) < MROW
    for chunk in range(HALF):
        left = full_ref[pl.ds(2 * chunk, NC, stride=MROW), :]
        right = full_ref[pl.ds(2 * chunk + 1, NC, stride=MROW), :]
        out_ref[:, chunk * LANES : (chunk + 1) * LANES] = jnp.where(
            low, left, pltpu.roll(right, MROW, 1)
        )


ANY = pl.BlockSpec(memory_space=pl.ANY)
VMEM = pl.BlockSpec(memory_space=pltpu.VMEM)


def cost(flops, bytes_accessed):
    return pl.CostEstimate(flops=flops, bytes_accessed=bytes_accessed, transcendentals=0)


def params(limit):
    return pltpu.CompilerParams(vmem_limit_bytes=limit)


def around(block, axis):
    count = lax.axis_size(axis)
    return [block] + [
        lax.ppermute(block, axis, [(i, i ^ k) for i in range(count)]) for k in range(1, count)
    ]


def trade(block, place, face_count):
    elem_count = lax.axis_size("elem")
    bits = face_count.bit_length() - 1
    pairs = []
    for face in range(face_count):
        for elem in range(elem_count):
            other = face
            for k in range(bits):
                swapped = bits > 1 and elem % 2 == 1 and k < 2
                if place >> (bits - 1 - k) & 1:
                    other ^= 1 << (1 - k if swapped else k)
            pairs.append((face * elem_count + elem, other * elem_count + elem))
    return lax.ppermute(block, ("face", "elem"), pairs)


def shards(
    trace_old,
    new_owner,
    mortar_tiles,
    mortar_owner,
    mortar_coarse,
    interior_rhs,
    local_inverse,
    coupling,
    connectivity,
):
    face_count = lax.axis_size("face")
    elem_count = lax.axis_size("elem")
    row_count = trace_old.shape[0]
    tile_count = mortar_tiles.shape[0]
    elements, modes = interior_rhs.shape
    trace = FACES_PER_ELEM * FACE_COEFFS
    capacity = max(2, 2 * row_count // face_count)
    own = face_count * capacity

    slots = own * elem_count
    devices = face_count * elem_count
    paired = face_count <= MOST_PAIRED
    named_shape = (SHARE_ROWS + PER_FACE, max(slots, modes))
    sides = 2 if paired else 1

    blocks = face_count * NC
    sums_shape = (blocks * DENSE, LANES)
    half = (blocks * (DENSE + 1) // sides, LANES)
    named_out = jax.ShapeDtypeStruct(named_shape, BF16)
    if paired:
        more = named_shape[0] * named_shape[1] // LANES
        outs = [jax.ShapeDtypeStruct((half[0] + more, LANES), BF16), jax.ShapeDtypeStruct(half, BF16)]
    else:
        outs = [named_out, jax.ShapeDtypeStruct(half, BF16)]
    placed, *half_grams = pl.pallas_call(
        functools.partial(gram_kernel, elem_count, face_count, capacity, paired),
        out_shape=[jax.ShapeDtypeStruct((slots, FACE_COEFFS), BF16)] + outs,
        in_specs=[ANY] * 7,
        out_specs=[VMEM] * (1 + len(outs)),
        scratch_shapes=[
            pltpu.SMEM((tile_count,), I32),
            pltpu.SMEM((tile_count,), I32),
            pltpu.VMEM(mortar_tiles.shape, BF16),
            pltpu.VMEM((tile_count * PITCH, LANES), F32),
            pltpu.VMEM(sums_shape, F32),
            pltpu.VMEM(sums_shape, F32),
            pltpu.VMEM((blocks, LANES), F32),
            pltpu.VMEM((blocks, LANES), F32),
            pltpu.VMEM((1, row_count), I32),
            pltpu.VMEM(trace_old.shape, BF16),
            pltpu.SMEM((FACES_PER_ELEM, elements), I32),
            pltpu.VMEM((elements, modes), BF16),
            pltpu.VMEM((PER_FACE, modes), F32),
            pltpu.SemaphoreType.DMA((8,)),
        ]
        + [pltpu.VMEM(named_shape, BF16)] * paired,
        compiler_params=params(BIG),
        cost_estimate=cost(4 * tile_count * MROW * MROW * LANES, 12 << 20),
        name="gram",
    )(
        mortar_owner.reshape(tile_count),
        mortar_coarse,
        mortar_tiles,
        new_owner.reshape(1, row_count),
        trace_old,
        connectivity.T,
        interior_rhs,
    )
    if paired:
        came = trade(half_grams[1], face_count // 2, face_count)
    table = lax.all_to_all(
        placed.reshape(devices, capacity, FACE_COEFFS), ("face", "elem"), 0, 0, tiled=True
    ).reshape(slots, FACE_COEFFS)

    if paired:
        named, *joined = pl.pallas_call(
            join_kernel,
            out_shape=[named_out]
            + [jax.ShapeDtypeStruct((OWNER_ROWS, LANES), BF16)] * (face_count // 2),
            in_specs=[VMEM] * 2,
            out_specs=[VMEM] * (1 + face_count // 2),
            compiler_params=params(SMALL),
            cost_estimate=cost(0, 4 << 20),
            name="join",
        )(half_grams[0], came)
        got = [joined[0]] + [
            trade(joined[k], k, face_count) for k in range(face_count // 2 - 1, 0, -1)
        ]
    else:
        named, blocked = half_grams
        blocked = blocked.reshape(face_count, OWNER_ROWS, LANES)
        got = [lax.all_to_all(blocked, "face", 0, 0, tiled=True).reshape(-1, LANES)]

    schur_blocks, shares, left = pl.pallas_call(
        functools.partial(main_kernel, elem_count, face_count),
        out_shape=(
            jax.ShapeDtypeStruct((elements, trace, trace), BF16),
            jax.ShapeDtypeStruct((SHARE_ROWS, LANES), BF16),
            jax.ShapeDtypeStruct((own, FACE_COEFFS), F32),
        ),
        in_specs=[ANY] * 4,
        out_specs=(ANY, VMEM, VMEM),
        scratch_shapes=[
            pltpu.VMEM(named_shape, BF16),
            pltpu.VMEM((slots, FACE_COEFFS), BF16),
            pltpu.VMEM((elements, modes, modes), BF16),
            pltpu.VMEM((elements, modes, trace), BF16),
            pltpu.VMEM((elements, trace, trace), BF16),
            pltpu.VMEM((LANES, modes), F32),
            pltpu.VMEM((modes, LANES), BF16),
            pltpu.VMEM((PER_FACE, trace + LANES), F32),
            pltpu.VMEM((trace, LANES), F32),
            pltpu.VMEM((trace, modes), BF16),
            pltpu.VMEM((trace, modes), BF16),
            pltpu.VMEM((trace, modes), BF16),
            pltpu.VMEM((trace, modes), BF16),
            pltpu.SemaphoreType.DMA((2,)),
            pltpu.SemaphoreType.DMA((2, elements)),
            pltpu.SemaphoreType.DMA((elements,)),
        ],
        compiler_params=params(MIDDLE),
        cost_estimate=cost(
            2 * elements * modes * trace * (modes + trace),
            2 * elements * (modes * (modes + trace) + trace * trace),
        ),
        name="condense",
    )(table, named, local_inverse, coupling)

    all_shares = around(shares, "elem")
    coarse_blocks = pl.pallas_call(
        coarse_kernel,
        out_shape=jax.ShapeDtypeStruct((NC, MROW * MROW), F32),
        in_specs=[VMEM] * len(got),
        out_specs=VMEM,
        scratch_shapes=[
            pltpu.VMEM((OWNER_ROWS, LANES), F32),
            pltpu.VMEM((NC * MROW, LANES), F32),
        ],
        compiler_params=params(SMALL),
        cost_estimate=cost(0, 8 << 20),
        name="coarse",
    )(*got)
    last, coarse_blocks = lax.optimization_barrier((all_shares[-1], coarse_blocks))
    slot_residual = pl.pallas_call(
        residual_kernel,
        out_shape=jax.ShapeDtypeStruct((own, FACE_COEFFS), F32),
        in_specs=[VMEM] * elem_count,
        out_specs=VMEM,
        compiler_params=params(SMALL),
        name="residual",
    )(left, *all_shares[1:-1], last)
    return schur_blocks, slot_residual, coarse_blocks


def solution(mesh):
    return jax.shard_map(
        shards,
        mesh=mesh,
        in_specs=(
            P(("face", "elem"), None),
            P(("face", "elem"), None),
            P(("face", "elem"), None),
            P(("face", "elem"), None),
            P(("face", "elem")),
            P(("face", "elem"), None),
            P(("face", "elem"), None, None),
            P(("face", "elem"), None, None),
            P(("face", "elem"), None),
        ),
        out_specs=(
            P(("face", "elem"), None, None),
            P(("face", "elem"), None),
            P(("face", "elem"), None),
        ),
        check_vma=False,
    )
```

```python
import functools

import jax
import jax.numpy as jnp
from jax import lax
from jax.experimental import pallas as pl
from jax.experimental.pallas import tpu as pltpu
from jax.sharding import PartitionSpec as P

FACE_COEFFS = 128
FACES_PER_ELEM = 3
MROW = 64
MCOL = 96
NC = 16
HALF = MROW // 2
LANES = 128
DENSE = HALF * MROW // LANES
OWNER_ROWS = NC * (DENSE + 1)
PER_FACE = 16
NAMED = FACES_PER_ELEM * PER_FACE
SHARE_ROWS = NAMED + 16
SLOT_BASE = 16
CHUNK = 16
MOST_PAIRED = 8
BIG = 62 << 20
MIDDLE = 52 << 20
SMALL = 12 << 20
PITCH = MROW + 8

BF16 = jnp.bfloat16
F32 = jnp.float32
I32 = jnp.int32

NT = (((1,), (1,)), ((), ()))
TN = (((0,), (0,)), ((), ()))


def iota(shape, dim):
    return lax.broadcasted_iota(I32, shape, dim)


def dot(left, right, dims=(((1,), (0,)), ((), ()))):
    return lax.dot_general(left, right, dims, preferred_element_type=F32)


def divided(value, by):
    shift = by.bit_length() - 1
    assert by == 1 << shift
    return value >> shift, value & (by - 1)


def place_rows(elem_count, face_count, capacity, owners, trace, slots):
    rows = owners.shape[1]
    earlier = (iota((rows, rows), 0) < iota((rows, rows), 1)).astype(BF16)
    hot = (iota((face_count, rows), 0) == owners).astype(F32)
    rank = jnp.sum(hot * dot(hot.astype(BF16), earlier), axis=0, keepdims=True).astype(I32)
    slot = iota((slots, rows), 0)
    wanted = divided(slot, elem_count * capacity)[0] * capacity + divided(slot, capacity)[1]
    place = (wanted == owners * capacity + rank).astype(BF16)
    return dot(place, trace).astype(BF16)


def position(elem, inner, elem_count, capacity):
    face, rank = divided(inner, capacity)
    return (face * elem_count + elem) * capacity + rank


def name_slots(elem_count, face_count, capacity, conn_ref, named_ref):
    elements = conn_ref.shape[1]
    slots = elem_count * face_count * capacity
    row = iota((PER_FACE, LANES), 0)
    lane = iota((PER_FACE, LANES), 1)
    first_lane = iota((1, LANES), 1)
    high = jnp.full((1, LANES), -1, I32)
    rest = jnp.zeros((1, LANES), I32)
    for a in range(FACES_PER_ELEM):
        positions = jnp.full((PER_FACE, LANES), -1, I32)
        for e in range(elements):
            slot = conn_ref[a, e]
            place = position(*divided(slot, face_count * capacity), elem_count, capacity)
            positions = jnp.where(row == e, place, positions)
            here = first_lane == a * PER_FACE + e
            quotient, remainder = divided(slot, SLOT_BASE)
            high = jnp.where(here, quotient, high)
            rest = jnp.where(here, remainder, rest)
        hot = jnp.concatenate([positions == lane + k for k in range(0, slots, LANES)], axis=1)
        named_ref[a * PER_FACE : (a + 1) * PER_FACE, :slots] = hot.astype(BF16)
    names = jnp.where(row == 0, high, jnp.where(row == 1, rest, 0)).astype(F32)
    named_ref[NAMED:SHARE_ROWS, :LANES] = names.astype(BF16)


def gram_kernel(
    elem_count,
    face_count,
    capacity,
    paired,
    owner_hbm,
    coarse_hbm,
    tiles_hbm,
    new_owner_hbm,
    trace_hbm,
    conn_hbm,
    rhs_hbm,
    placed_ref,
    *refs,
):
    if paired:
        *refs, named_ref = refs
    else:
        named_ref, *refs = refs
    out_refs, refs = refs[:-14], refs[-14:]
    owner_ref, coarse_ref, tiles_ref, rows_ref = refs[:4]
    accs, diags = refs[4:6], refs[6:8]
    new_owner_ref, trace_ref, conn_ref, rhs_ref, wide_ref, sems = refs[8:]

    def place_of(owner):
        if not paired:
            return owner
        other = owner ^ lax.axis_index("face")
        bits = face_count.bit_length() - 1
        odd = lax.axis_index("elem") & 1
        place = [(other >> k) & 1 for k in range(bits)]
        if bits > 1:
            place[:2] = (jnp.where(odd == 1, place[1 - k], place[k]) for k in range(2))
        return sum(bit << (bits - 1 - k) for k, bit in enumerate(place))

    tiles = tiles_ref.shape[0]
    copies = []
    for k in range(2):
        here = pl.ds(k * tiles // 2, tiles // 2)
        copies.append(
            pltpu.make_async_copy(tiles_hbm.at[here], tiles_ref.at[here], sems.at[4 + k])
        )
        copies[-1].start()
    names = pltpu.make_async_copy(conn_hbm, conn_ref, sems.at[6])
    names.start()
    copies += [
        pltpu.make_async_copy(owner_hbm, owner_ref, sems.at[0]),
        pltpu.make_async_copy(coarse_hbm, coarse_ref, sems.at[1]),
        pltpu.make_async_copy(new_owner_hbm, new_owner_ref, sems.at[2]),
        pltpu.make_async_copy(trace_hbm, trace_ref, sems.at[3]),
        pltpu.make_async_copy(rhs_hbm, rhs_ref, sems.at[7]),
    ]
    for copy in copies[2:]:
        copy.start()
    for ref in (*accs, *diags):
        ref[...] = jnp.zeros_like(ref)
    names.wait()
    name_slots(elem_count, face_count, capacity, conn_ref, named_ref)
    for copy in copies:
        copy.wait()
    wide_ref[...] = jnp.zeros_like(wide_ref)
    wide_ref[0 : rhs_ref.shape[0], :] = rhs_ref[...].astype(F32)
    named_ref[SHARE_ROWS:, : wide_ref.shape[1]] = wide_ref[...].astype(BF16)
    placed_ref[...] = place_rows(
        elem_count, face_count, capacity, new_owner_ref[...], trace_ref[...], placed_ref.shape[0]
    )

    lane = iota((CHUNK, LANES), 1)
    inside = lane < MCOL
    row = iota((HALF, LANES), 0)
    column = divided(iota((HALF, LANES), 1), MROW)[1]
    swapped = (column > row) & (column < HALF)
    diagonal = column == row
    low = iota((DENSE, LANES), 1) < MROW
    low_wide = iota((MROW, LANES), 1) < MROW
    low_row = iota((1, LANES), 1) < MROW

    for chunk in range(tiles // CHUNK):
        first_tile = chunk * CHUNK
        for group in range(MROW // 4):
            base = group * 3 * LANES
            one, two, three = (
                tiles_ref[
                    first_tile : first_tile + CHUNK, base + k * LANES : base + (k + 1) * LANES
                ].astype(F32)
                for k in range(3)
            )
            rolled = (
                one,
                pltpu.roll(jnp.where(lane < 64, two, one), 32, 1),
                pltpu.roll(jnp.where(lane < 32, three, two), 64, 1),
                pltpu.roll(three, 96, 1),
            )
            for k in range(4):
                rows_ref[pl.ds(first_tile * PITCH + 4 * group + k, CHUNK, stride=PITCH), :] = (
                    jnp.where(inside, rolled[k], 0.0)
                )
        for tile in range(first_tile, first_tile + CHUNK, 2):
            both = jnp.concatenate(
                [
                    rows_ref[t * PITCH : t * PITCH + MROW, :].astype(BF16)
                    for t in (tile, tile + 1)
                ],
                axis=0,
            )
            gram = dot(both, both, NT)
            side = jnp.where(low_wide, gram[:MROW], gram[MROW:])
            lower = pltpu.roll(side[HALF:], LANES - HALF, 1)
            packed = jnp.where(swapped, lower, side[:HALF])
            diag = jnp.sum(jnp.where(diagonal, lower, 0.0), axis=0, keepdims=True)
            turned = pltpu.roll(packed, MROW, 1)
            dense = (
                jnp.where(low, packed[:DENSE], turned[DENSE:]),
                jnp.where(low, turned[:DENSE], packed[DENSE:]),
            )
            own = (jnp.where(low_row, diag, 0.0), jnp.where(low_row, 0.0, diag))
            for k in range(2):
                block = place_of(owner_ref[tile + k]) * NC + coarse_ref[tile + k]
                here = pl.ds(pl.multiple_of(block * DENSE, DENSE), DENSE)
                accs[k][here, :] += dense[k]
                diags[k][pl.ds(block, 1), :] += own[k]
    size = NC * DENSE
    each = face_count // len(out_refs)
    for owner in range(face_count):
        out_ref, start = out_refs[owner // each], owner % each * OWNER_ROWS
        here = slice(owner * size, (owner + 1) * size)
        out_ref[start : start + size, :] = (accs[0][here, :] + accs[1][here, :]).astype(BF16)
        here = slice(owner * NC, (owner + 1) * NC)
        out_ref[start + size : start + size + NC, :] = (
            diags[0][here, :] + diags[1][here, :]
        ).astype(BF16)
    if paired:
        rows = named_ref.shape[0]
        for k in range(named_ref.shape[1] // LANES):
            start = each * OWNER_ROWS + k * rows
            out_refs[0][start : start + rows, :] = named_ref[:, k * LANES : (k + 1) * LANES]


def join_kernel(kept_ref, came_ref, named_ref, *out_refs):
    for k, out_ref in enumerate(out_refs):
        here = slice(k * OWNER_ROWS, (k + 1) * OWNER_ROWS)
        total = kept_ref[here, :].astype(F32) + came_ref[here, :].astype(F32)
        out_ref[...] = total.astype(BF16)
    rows = named_ref.shape[0]
    for k in range(named_ref.shape[1] // LANES):
        start = came_ref.shape[0] + k * rows
        named_ref[:, k * LANES : (k + 1) * LANES] = kept_ref[start : start + rows, :]


def main_kernel(
    elem_count,
    face_count,
    table_hbm,
    named_hbm,
    inverse_hbm,
    coupling_hbm,
    schur_hbm,
    share_ref,
    left_ref,
    named_ref,
    table_ref,
    inverse_ref,
    coupling_ref,
    schur_ref,
    wide_ref,
    rhs_turned_ref,
    vector_ref,
    sum_ref,
    turned_a_ref,
    turned_b_ref,
    product_a_ref,
    product_b_ref,
    small_sems,
    block_sems,
    schur_sems,
):
    elements, modes = inverse_ref.shape[:2]
    trace = FACES_PER_ELEM * FACE_COEFFS
    slots = table_ref.shape[0]
    own = left_ref.shape[0]
    capacity = own // face_count
    my_elem = lax.axis_index("elem")
    small = [
        pltpu.make_async_copy(named_hbm, named_ref, small_sems.at[0]),
        pltpu.make_async_copy(table_hbm, table_ref, small_sems.at[1]),
    ]

    def coupling_copy(e):
        return pltpu.make_async_copy(coupling_hbm.at[e], coupling_ref.at[e], block_sems.at[0, e])

    def inverse_copy(e):
        return pltpu.make_async_copy(inverse_hbm.at[e], inverse_ref.at[e], block_sems.at[1, e])

    def leave(e):
        return pltpu.make_async_copy(schur_ref.at[e], schur_hbm.at[e], schur_sems.at[e])

    coupling_copy(0).start()
    inverse_copy(0).start()
    for copy in small:
        copy.start()
    coupling_copy(1).start()
    inverse_copy(1).start()
    coupling_copy(2).start()

    def turn(e, turned_ref):
        turned_ref[...] = coupling_ref[e].T

    def first(e, turned_ref, product_ref):
        for half in range(2):
            here = slice(half * modes // 2, (half + 1) * modes // 2)
            product_ref[:, here] = dot(turned_ref[...], inverse_ref[e, :, here]).astype(BF16)

    def second(e, product_ref):
        split = 2 * LANES
        one = dot(product_ref[...], coupling_ref[e, :, :split])
        wide = jnp.concatenate([coupling_ref[e, :, split:], rhs_turned_ref[...]], axis=1)
        two = dot(product_ref[...], wide)
        schur_ref[e, :, :split] = (-one).astype(BF16)
        schur_ref[e, :, split:] = (-two[:, : trace - split]).astype(BF16)
        vector = vector_ref[pl.ds(e, 1), :]
        one = one * vector[:, :split]
        two = two * vector[:, split:]
        total = (one[:, :LANES] + one[:, LANES:]) + (two[:, :LANES] + two[:, LANES:])
        sums = jnp.sum(total, axis=1, keepdims=True)
        sum_ref[...] = jnp.where(iota((trace, LANES), 1) == e, sums, sum_ref[...])

    turned = (turned_a_ref, turned_b_ref)
    product = (product_a_ref, product_b_ref)

    def advance(e, parity, turning=True, finishing=True):
        if turning:
            @pl.when(e + 2 < elements)
            def _():
                inverse_copy(e + 2).start()

            @pl.when(e + 3 < elements)
            def _():
                coupling_copy(e + 3).start()

            coupling_copy(e + 1).wait()
        inverse_copy(e).wait()
        if turning:
            turn(e + 1, turned[1 - parity])
        first(e, turned[parity], product[parity])
        if finishing:
            second(e - 1, product[1 - parity])
            leave(e - 1).start()

    coupling_copy(0).wait()
    turn(0, turned[0])
    for copy in small:
        copy.wait()
    sum_ref[...] = jnp.zeros_like(sum_ref)
    wide_ref[...] = jnp.zeros_like(wide_ref)
    wide_ref[0:PER_FACE, :] = named_ref[SHARE_ROWS:, :modes].astype(F32)
    rhs_turned_ref[...] = wide_ref[...].T.astype(BF16)
    row = iota((PER_FACE, LANES), 0)
    lane = iota((PER_FACE, LANES), 1)

    for a in range(FACES_PER_ELEM):
        hot = named_ref[a * PER_FACE : (a + 1) * PER_FACE, :slots]
        vector_ref[:, a * LANES : (a + 1) * LANES] = -dot(hot, table_ref[...])
    vector_ref[:, trace:] = (row == lane).astype(F32)
    share_ref[NAMED:, :] = named_ref[NAMED:SHARE_ROWS, :LANES]
    place = position(my_elem, iota((own, slots), 0), elem_count, capacity)
    pick = (iota((own, slots), 1) == place).astype(BF16)
    left_ref[...] = dot(pick, table_ref[...])

    advance(0, 0, finishing=False)

    def two(index, carry):
        advance(2 * index + 1, 1)
        advance(2 * index + 2, 0)
        return carry

    pairs = (elements - 2) // 2
    lax.fori_loop(0, pairs, two, 0)
    for e in range(2 * pairs + 1, elements):
        advance(e, e % 2, turning=e + 1 < elements)
    second(elements - 1, product[(elements - 1) % 2])
    leave(elements - 1).start()

    for a in range(FACES_PER_ELEM):
        shares = sum_ref[a * LANES : (a + 1) * LANES, :].T
        share_ref[a * PER_FACE : (a + 1) * PER_FACE, :] = shares[:PER_FACE].astype(BF16)
    left_ref[...] = less_shares(left_ref[...], share_ref)
    for e in range(elements):
        leave(e).wait()


def less_shares(left, share_ref):
    own = left.shape[0]
    slot = (iota((own, SHARE_ROWS), 0) + lax.axis_index("elem") * own).astype(F32)
    names = share_ref[NAMED:, :].astype(F32)
    named = (names[0:1] * SLOT_BASE + names[1:2])[:, :SHARE_ROWS]
    return left - dot((slot == named).astype(BF16), share_ref[...])


def residual_kernel(left_ref, *refs):
    share_refs, residual_ref = refs[:-1], refs[-1]
    left = left_ref[...]
    for share_ref in share_refs:
        left = less_shares(left, share_ref)
    residual_ref[...] = left


def coarse_kernel(*refs):
    got_refs, (out_ref, sum_ref, full_ref) = refs[:-3], refs[-3:]
    sum_ref[...] = sum(
        got_ref[k : k + OWNER_ROWS, :].astype(F32)
        for got_ref in got_refs
        for k in range(0, got_ref.shape[0], OWNER_ROWS)
    )

    lane = iota((HALF, LANES), 1)
    row = iota((HALF, LANES), 0)
    wide_row = iota((MROW, LANES), 0)
    wide_lane = iota((MROW, LANES), 1)
    top = wide_row < HALF
    held = (top & ((wide_lane <= wide_row) | (wide_lane >= HALF))) | (
        (~top) & (wide_lane >= wide_row)
    )
    for block in range(NC):
        dense = sum_ref[block * DENSE : (block + 1) * DENSE, :]
        upper = jnp.concatenate([dense, pltpu.roll(dense, MROW, 1)], axis=0)
        diag = sum_ref[NC * DENSE + block : NC * DENSE + block + 1, :]
        diag = pltpu.roll(diag + pltpu.roll(diag, MROW, 1), HALF, 1)
        lower = jnp.where(lane == row + HALF, diag, pltpu.roll(upper, HALF, 1))
        given = jnp.concatenate([upper, lower], axis=0)
        turned = jnp.concatenate([given, given], axis=0).T[:MROW]
        full_ref[block * MROW : (block + 1) * MROW, :] = jnp.where(held, given, turned)
    low = iota((NC, LANES), 1) < MROW
    for chunk in range(HALF):
        left = full_ref[pl.ds(2 * chunk, NC, stride=MROW), :]
        right = full_ref[pl.ds(2 * chunk + 1, NC, stride=MROW), :]
        out_ref[:, chunk * LANES : (chunk + 1) * LANES] = jnp.where(
            low, left, pltpu.roll(right, MROW, 1)
        )


ANY = pl.BlockSpec(memory_space=pl.ANY)
VMEM = pl.BlockSpec(memory_space=pltpu.VMEM)


def cost(flops, bytes_accessed):
    return pl.CostEstimate(flops=flops, bytes_accessed=bytes_accessed, transcendentals=0)


def params(limit):
    return pltpu.CompilerParams(vmem_limit_bytes=limit)


def around(block, axis):
    count = lax.axis_size(axis)
    return [block] + [
        lax.ppermute(block, axis, [(i, i ^ k) for i in range(count)]) for k in range(1, count)
    ]


def trade(block, place, face_count):
    elem_count = lax.axis_size("elem")
    bits = face_count.bit_length() - 1
    pairs = []
    for face in range(face_count):
        for elem in range(elem_count):
            other = face
            for k in range(bits):
                swapped = bits > 1 and elem % 2 == 1 and k < 2
                if place >> (bits - 1 - k) & 1:
                    other ^= 1 << (1 - k if swapped else k)
            pairs.append((face * elem_count + elem, other * elem_count + elem))
    return lax.ppermute(block, ("face", "elem"), pairs)


def shards(
    trace_old,
    new_owner,
    mortar_tiles,
    mortar_owner,
    mortar_coarse,
    interior_rhs,
    local_inverse,
    coupling,
    connectivity,
):
    face_count = lax.axis_size("face")
    elem_count = lax.axis_size("elem")
    row_count = trace_old.shape[0]
    tile_count = mortar_tiles.shape[0]
    elements, modes = interior_rhs.shape
    trace = FACES_PER_ELEM * FACE_COEFFS
    capacity = max(2, 2 * row_count // face_count)
    own = face_count * capacity

    slots = own * elem_count
    devices = face_count * elem_count
    paired = face_count <= MOST_PAIRED
    named_shape = (SHARE_ROWS + PER_FACE, max(slots, modes))
    sides = 2 if paired else 1

    blocks = face_count * NC
    sums_shape = (blocks * DENSE, LANES)
    half = (blocks * (DENSE + 1) // sides, LANES)
    named_out = jax.ShapeDtypeStruct(named_shape, BF16)
    if paired:
        more = named_shape[0] * named_shape[1] // LANES
        outs = [jax.ShapeDtypeStruct((half[0] + more, LANES), BF16), jax.ShapeDtypeStruct(half, BF16)]
    else:
        outs = [named_out, jax.ShapeDtypeStruct(half, BF16)]
    placed, *half_grams = pl.pallas_call(
        functools.partial(gram_kernel, elem_count, face_count, capacity, paired),
        out_shape=[jax.ShapeDtypeStruct((slots, FACE_COEFFS), BF16)] + outs,
        in_specs=[ANY] * 7,
        out_specs=[VMEM] * (1 + len(outs)),
        scratch_shapes=[
            pltpu.SMEM((tile_count,), I32),
            pltpu.SMEM((tile_count,), I32),
            pltpu.VMEM(mortar_tiles.shape, BF16),
            pltpu.VMEM(((tile_count + 1) * PITCH, LANES), F32),
            pltpu.VMEM(sums_shape, F32),
            pltpu.VMEM(sums_shape, F32),
            pltpu.VMEM((blocks, LANES), F32),
            pltpu.VMEM((blocks, LANES), F32),
            pltpu.VMEM((1, row_count), I32),
            pltpu.VMEM(trace_old.shape, BF16),
            pltpu.SMEM((FACES_PER_ELEM, elements), I32),
            pltpu.VMEM((elements, modes), BF16),
            pltpu.VMEM((PER_FACE, modes), F32),
            pltpu.SemaphoreType.DMA((8,)),
        ]
        + [pltpu.VMEM(named_shape, BF16)] * paired,
        compiler_params=params(BIG),
        cost_estimate=cost(4 * tile_count * MROW * MROW * LANES, 12 << 20),
        name="gram",
    )(
        mortar_owner.reshape(tile_count),
        mortar_coarse,
        mortar_tiles,
        new_owner.reshape(1, row_count),
        trace_old,
        connectivity.T,
        interior_rhs,
    )
    if paired:
        came = trade(half_grams[1], face_count // 2, face_count)
    table = lax.all_to_all(
        placed.reshape(devices, capacity, FACE_COEFFS), ("face", "elem"), 0, 0, tiled=True
    ).reshape(slots, FACE_COEFFS)

    if paired:
        named, *joined = pl.pallas_call(
            join_kernel,
            out_shape=[named_out]
            + [jax.ShapeDtypeStruct((OWNER_ROWS, LANES), BF16)] * (face_count // 2),
            in_specs=[VMEM] * 2,
            out_specs=[VMEM] * (1 + face_count // 2),
            compiler_params=params(SMALL),
            cost_estimate=cost(0, 4 << 20),
            name="join",
        )(half_grams[0], came)
        got = [joined[0]] + [
            trade(joined[k], k, face_count) for k in range(face_count // 2 - 1, 0, -1)
        ]
    else:
        named, blocked = half_grams
        blocked = blocked.reshape(face_count, OWNER_ROWS, LANES)
        got = [lax.all_to_all(blocked, "face", 0, 0, tiled=True).reshape(-1, LANES)]

    schur_blocks, shares, left = pl.pallas_call(
        functools.partial(main_kernel, elem_count, face_count),
        out_shape=(
            jax.ShapeDtypeStruct((elements, trace, trace), BF16),
            jax.ShapeDtypeStruct((SHARE_ROWS, LANES), BF16),
            jax.ShapeDtypeStruct((own, FACE_COEFFS), F32),
        ),
        in_specs=[ANY] * 4,
        out_specs=(ANY, VMEM, VMEM),
        scratch_shapes=[
            pltpu.VMEM(named_shape, BF16),
            pltpu.VMEM((slots, FACE_COEFFS), BF16),
            pltpu.VMEM((elements, modes, modes), BF16),
            pltpu.VMEM((elements, modes, trace), BF16),
            pltpu.VMEM((elements, trace, trace), BF16),
            pltpu.VMEM((LANES, modes), F32),
            pltpu.VMEM((modes, LANES), BF16),
            pltpu.VMEM((PER_FACE, trace + LANES), F32),
            pltpu.VMEM((trace, LANES), F32),
            pltpu.VMEM((trace, modes), BF16),
            pltpu.VMEM((trace, modes), BF16),
            pltpu.VMEM((trace, modes), BF16),
            pltpu.VMEM((trace, modes), BF16),
            pltpu.SemaphoreType.DMA((2,)),
            pltpu.SemaphoreType.DMA((2, elements)),
            pltpu.SemaphoreType.DMA((elements,)),
        ],
        compiler_params=params(MIDDLE),
        cost_estimate=cost(
            2 * elements * modes * trace * (modes + trace),
            2 * elements * (modes * (modes + trace) + trace * trace),
        ),
        name="condense",
    )(table, named, local_inverse, coupling)

    all_shares = around(shares, "elem")
    coarse_blocks = pl.pallas_call(
        coarse_kernel,
        out_shape=jax.ShapeDtypeStruct((NC, MROW * MROW), F32),
        in_specs=[VMEM] * len(got),
        out_specs=VMEM,
        scratch_shapes=[
            pltpu.VMEM((OWNER_ROWS, LANES), F32),
            pltpu.VMEM(((NC + 1) * MROW, LANES), F32),
        ],
        compiler_params=params(SMALL),
        cost_estimate=cost(0, 8 << 20),
        name="coarse",
    )(*got)
    last, coarse_blocks = lax.optimization_barrier((all_shares[-1], coarse_blocks))
    slot_residual = pl.pallas_call(
        residual_kernel,
        out_shape=jax.ShapeDtypeStruct((own, FACE_COEFFS), F32),
        in_specs=[VMEM] * elem_count,
        out_specs=VMEM,
        compiler_params=params(SMALL),
        name="residual",
    )(left, *all_shares[1:-1], last)
    return schur_blocks, slot_residual, coarse_blocks


def solution(mesh):
    return jax.shard_map(
        shards,
        mesh=mesh,
        in_specs=(
            P(("face", "elem"), None),
            P(("face", "elem"), None),
            P(("face", "elem"), None),
            P(("face", "elem"), None),
            P(("face", "elem")),
            P(("face", "elem"), None),
            P(("face", "elem"), None, None),
            P(("face", "elem"), None, None),
            P(("face", "elem"), None),
        ),
        out_specs=(
            P(("face", "elem"), None, None),
            P(("face", "elem"), None),
            P(("face", "elem"), None),
        ),
        check_vma=False,
    )
```
